32 devices in a mesh: dp: 8 (over z, x), chan: 4 (over y, core).
Axes of the slice: x: 2, y: 2, z: 4, core: 2. Of those that a mesh axis runs over, the one named last changes fastest.
Arguments:
- block_in: bfloat16 [12544, 2048], P('dp', 'chan'), may hold values from -6 to 6
- weight_in: bfloat16 [2048, 512], P('dp', 'chan'), may hold values from -0.125 to 0.125
- weight_mid: bfloat16 [4608, 512], P('dp', 'chan'), may hold values from -0.09375 to 0.09375
- weight_out: bfloat16 [512, 2048], P('dp', 'chan'), may hold values from -0.25 to 0.25
- gain_in: float32 [512], P('chan'), may hold values from 0.1 to 1.9
- bias_in: float32 [512], P('chan'), may hold values from -3 to 3
- gain_mid: float32 [512], P('chan'), may hold values from 0.1 to 1.9
- bias_mid: float32 [512], P('chan'), may hold values from -3 to 3
- gain_out: float32 [2048], P('chan'), may hold values from 0.1 to 1.9
- bias_out: float32 [2048], P('chan'), may hold values from -3 to 3
- kernel_near: float32 [9, 512], P(None, 'chan'), may hold values from -2 to 2
- kernel_far: float32 [9, 512], P(None, 'chan'), may hold values from -2 to 2
- gate_bias: float32 [512], P('chan'), may hold values from -3 to 3
- same_video: int32 [32, 7], P('dp'), may hold values 0 or 1
- video: bfloat16 [256, 15, 1024], P('dp'), may hold values from -6 to 6
- stem_center: bfloat16 [147, 64], P(None, 'chan'), may hold values from -0.5 to 0.5
- stem_diff: bfloat16 [588, 64], P(None, 'chan'), may hold values from -0.1875 to 0.1875
- stem_gain: float32 [64], P('chan'), may hold values from 0.1 to 1.9
- stem_bias: float32 [64], P('chan'), may hold values from -3 to 3
- block_grad: bfloat16 [12544, 2048], P('dp', 'chan'), may hold values from -6 to 6
- stem_grad: bfloat16 [256, 64, 256], P('dp', 'chan'), may hold values from -6 to 6
Outputs:
- block_out: bfloat16 [12544, 2048], P('dp', 'chan')
- stem_out: bfloat16 [256, 64, 256], P('dp', 'chan')
- grad_block_in: bfloat16 [12544, 2048], P('dp', 'chan')
- grad_weight_in: float32 [2048, 512], P('dp', 'chan')
- grad_weight_mid: float32 [4608, 512], P('dp', 'chan')
- grad_weight_out: float32 [512, 2048], P('dp', 'chan')
- grad_gain_in: float32 [512], P('chan')
- grad_bias_in: float32 [512], P('chan')
- grad_gain_mid: float32 [512], P('chan')
- grad_bias_mid: float32 [512], P('chan')
- grad_gain_out: float32 [2048], P('chan')
- grad_bias_out: float32 [2048], P('chan')
- grad_kernel_near: float32 [9, 512], P(None, 'chan')
- grad_kernel_far: float32 [9, 512], P(None, 'chan')
- grad_gate_bias: float32 [512], P('chan')
- grad_stem_center: float32 [147, 64], P(None, 'chan')
- grad_stem_diff: float32 [588, 64], P(None, 'chan')
- grad_stem_gain: float32 [64], P('chan')
- grad_stem_bias: float32 [64], P('chan')
The draws below stay inside these ranges and needn't reach their ends.
All inputs are finite; a program needn't handle non-finite values. No bound on the sum of `same_video` on one device may be relied on, other than what follows from the above.
Results may differ from the reference program's by a relative error of at most 0.0085.
Values may be sent and summed in bfloat16 or wider, within the bound.
No kernel may reach another device: no remote copies, remote signals or barrier semaphores. Data moves between devices by JAX's collectives and lax.ppermute only.
A program may use at most 256 MiB of HBM per device.

```python
import jax
import jax.numpy as jnp
from jax import lax

FULL = 2048
MID = 512
STEM_CH = 64
SEG = 8
SIDE = 7
FRAMES = 5
CROP = 16
CLIPS = 32
SEGS = 256
ROWS = 12544


def touch_ends(result, rng, least, top_value):
    longest = result.shape.index(max(result.shape))
    spots = []
    for shift in (0, 1):
        where = [jax.random.randint(jax.random.fold_in(rng, axis), (), 0, length) for axis, length in enumerate(result.shape)]
        where[longest] = (where[longest] + shift) % result.shape[longest]
        spots.append(tuple(where))
    return result.at[spots[0]].set(least).at[spots[1]].set(top_value)


def levels(key, shape, cuts, low, top_value):
    def one(axis_at, parts):
        draws = jax.random.uniform(jax.random.fold_in(jax.random.fold_in(key, 6), axis_at), (parts,), jnp.float32, low / len(cuts), top_value / len(cuts))
        return jnp.repeat(jnp.exp(draws), shape[axis_at] // parts).reshape((-1,) + (1,) * (len(shape) - axis_at - 1))

    loudness = one(*cuts[0])
    for cut in cuts[1:]:
        loudness = loudness * one(*cut)
    return loudness


def bell_draw(rng, shape, scale, most, pieces=(), dtype=jnp.bfloat16):
    factor_of = levels(rng, shape, pieces, -0.22, 0.18) if pieces else 1.0
    drawn = jax.random.normal(rng, shape, jnp.float32) * scale * factor_of
    return jnp.minimum(jnp.maximum(drawn, -most), most).astype(dtype)


def setup_inputs(seed: int = 0) -> dict:
    splits = jax.random.split(jax.random.key(seed), 22)
    block_in = bell_draw(splits[0], (ROWS, FULL), 1.0, 6.0, ((0, 8), (1, 4)))
    weight_in = bell_draw(splits[1], (FULL, MID), FULL ** -0.5, 0.125, ((0, 8), (1, 4)))
    weight_mid = bell_draw(splits[2], (9 * MID, MID), (9 * MID) ** -0.5, 0.09375, ((0, 8), (1, 4)))
    weight_out = bell_draw(splits[3], (MID, FULL), MID ** -0.5, 0.25, ((0, 8), (1, 4)))
    gain_in = jnp.clip(1.0 + 0.18 * jax.random.normal(splits[4], (MID,), jnp.float32), 0.1, 1.9)
    bias_in = bell_draw(splits[5], (MID,), 0.5, 3.0, ((0, 4),), jnp.float32)
    gain_mid = jnp.clip(1.0 + 0.18 * jax.random.normal(splits[6], (MID,), jnp.float32), 0.1, 1.9)
    bias_mid = bell_draw(splits[7], (MID,), 0.5, 3.0, ((0, 4),), jnp.float32)
    gain_out = jnp.clip(1.0 + 0.18 * jax.random.normal(splits[8], (FULL,), jnp.float32), 0.1, 1.9)
    bias_out = bell_draw(splits[9], (FULL,), 0.5, 3.0, ((0, 4),), jnp.float32)
    kernel_near = bell_draw(splits[10], (9, MID), 0.3, 2.0, ((1, 4),), jnp.float32)
    kernel_far = bell_draw(splits[11], (9, MID), 0.3, 2.0, ((1, 4),), jnp.float32)
    gate_bias = bell_draw(splits[12], (MID,), 0.5, 3.0, ((0, 4),), jnp.float32)
    same_video = touch_ends((jax.random.randint(splits[13], (CLIPS, SEG - 1), 0, 4) < 3).astype(jnp.int32), jax.random.fold_in(splits[13], 1), 0, 1)
    video = bell_draw(splits[14], (SEGS, 3 * FRAMES, 4 * CROP * CROP), 1.0, 6.0, ((0, 8),))
    stem_center = bell_draw(splits[15], (147, STEM_CH), 147 ** -0.5, 0.5, ((1, 4),))
    stem_diff = bell_draw(splits[16], (588, STEM_CH), 1176 ** -0.5, 0.1875, ((1, 4),))
    stem_gain = jnp.clip(1.0 + 0.18 * jax.random.normal(splits[17], (STEM_CH,), jnp.float32), 0.1, 1.9)
    stem_bias = bell_draw(splits[18], (STEM_CH,), 0.5, 3.0, ((0, 4),), jnp.float32)
    block_grad = bell_draw(splits[19], (ROWS, FULL), 1.0, 6.0, ((0, 8), (1, 4)))
    stem_grad = bell_draw(splits[20], (SEGS, STEM_CH, CROP * CROP), 1.0, 6.0, ((0, 8), (1, 4)))
    return dict(block_in=block_in, weight_in=weight_in, weight_mid=weight_mid, weight_out=weight_out, gain_in=gain_in, bias_in=bias_in, gain_mid=gain_mid, bias_mid=bias_mid, gain_out=gain_out, bias_out=bias_out, kernel_near=kernel_near, kernel_far=kernel_far, gate_bias=gate_bias, same_video=same_video, video=video, stem_center=stem_center, stem_diff=stem_diff, stem_gain=stem_gain, stem_bias=stem_bias, block_grad=block_grad, stem_grad=stem_grad)


@jax.custom_vjp
def low(v):
    return lax.optimization_barrier(v.astype(jnp.bfloat16)).astype(jnp.float32)

@jax.custom_vjp
def low_back(v):
    return v

def low_keep(v):
    return (low(v), None)

def low_pass(kept, grad):
    return (grad,)

def back_keep(v):
    return (v, None)

def back_low(kept, grad):
    return (low(grad),)
low.defvjp(low_keep, low_pass)
low_back.defvjp(back_keep, back_low)
eps = 1e-05
top_precision = lax.Precision.HIGHEST

def norm_layer(value, gain, bias, axes):
    center = lax.optimization_barrier(jnp.mean(value, axis=axes, keepdims=True))
    spread = lax.optimization_barrier(jnp.mean(value * value, axis=axes, keepdims=True)) - center * center
    scaled = (value - center) * lax.rsqrt(spread + eps)
    return scaled * gain + bias

def depthwise(field, kernel, step):
    padded = jnp.pad(field, ((0, 0), (step, step), (step, step), (0, 0)))
    total = jnp.zeros_like(field)
    for tap in range(9):
        row_at = tap // 3 * step
        col_at = tap % 3 * step
        total = total + kernel[tap] * padded[:, row_at:row_at + SIDE, col_at:col_at + SIDE, :]
    return total

def temporal_gate(hidden, same_video, kernel_near, kernel_far, gate_bias):
    clips = same_video.shape[0]
    field = hidden.reshape(clips, SEG, SIDE * SIDE, hidden.shape[1])
    later = (field[:, 1:] - field[:, :-1]) * same_video.astype(jnp.float32)[:, :, None, None]
    change = jnp.concatenate([later, jnp.zeros_like(field[:, :1])], axis=1)
    change = change.reshape(clips * SEG, SIDE, SIDE, hidden.shape[1])
    score = depthwise(change, kernel_near, 1) + depthwise(change, kernel_far, 2) + gate_bias
    gate = jax.nn.sigmoid(score).reshape(hidden.shape)
    return hidden * (1.0 + gate)

def neighbours(values, clips):
    field = values.reshape(clips * SEG, SIDE, SIDE, values.shape[1])
    padded = jnp.pad(field, ((0, 0), (1, 1), (1, 1), (0, 0)))
    taps = [padded[:, row:row + SIDE, col:col + SIDE, :] for row in range(3) for col in range(3)]
    return jnp.concatenate(taps, axis=-1).reshape(values.shape[0], 9 * values.shape[1])

def stem_patches(planes):
    segs, chans = (planes.shape[0], planes.shape[1])
    field = planes.reshape(segs, chans, 2 * CROP, 2 * CROP)
    padded = jnp.pad(field, ((0, 0), (0, 0), (3, 3), (3, 3)))
    taps = [padded[:, :, row:row + 2 * CROP:2, col:col + 2 * CROP:2] for row in range(7) for col in range(7)]
    return jnp.stack(taps, axis=2).reshape(segs, chans * 49, CROP * CROP)

def block_forward(block_in, weight_in, weight_mid, weight_out, gain_in, bias_in, gain_mid, bias_mid, gain_out, bias_out, kernel_near, kernel_far, gate_bias, same_video):
    clips = same_video.shape[0]
    pre_in = low_back(jnp.dot(block_in, weight_in, preferred_element_type=jnp.float32, precision=top_precision))
    hidden = jax.nn.silu(norm_layer(pre_in, gain_in, bias_in, (0,)))
    mixed = low(temporal_gate(hidden, same_video, kernel_near, kernel_far, gate_bias))
    pre_mid = low_back(jnp.dot(neighbours(mixed, clips), weight_mid, preferred_element_type=jnp.float32, precision=top_precision))
    second = low(jax.nn.silu(norm_layer(pre_mid, gain_mid, bias_mid, (0,))))
    pre_out = low_back(jnp.dot(second, weight_out, preferred_element_type=jnp.float32, precision=top_precision))
    return jax.nn.silu(norm_layer(pre_out, gain_out, bias_out, (0,)) + block_in)

def stem_forward(video, stem_center, stem_diff, stem_gain, stem_bias):
    segs = video.shape[0]
    frames = video.reshape(segs, FRAMES, 3, video.shape[2])
    center = frames[:, FRAMES // 2]
    diffs = low((frames[:, 1:] - frames[:, :-1]).reshape(segs, 3 * (FRAMES - 1), video.shape[2]))
    pre_stem = jnp.einsum('ko,skp->sop', stem_center, stem_patches(center), precision=top_precision)
    pre_stem = pre_stem + jnp.einsum('ko,skp->sop', stem_diff, stem_patches(diffs), precision=top_precision)
    pre_stem = low_back(pre_stem)
    return jax.nn.silu(norm_layer(pre_stem, stem_gain[:, None], stem_bias[:, None], (0, 2)))

def reference(block_in, weight_in, weight_mid, weight_out, gain_in, bias_in, gain_mid, bias_mid, gain_out, bias_out, kernel_near, kernel_far, gate_bias, same_video, video, stem_center, stem_diff, stem_gain, stem_bias, block_grad, stem_grad):
    params = tuple((item.astype(jnp.float32) for item in (block_in, weight_in, weight_mid, weight_out, gain_in, bias_in, gain_mid, bias_mid, gain_out, bias_out, kernel_near, kernel_far, gate_bias, stem_center, stem_diff, stem_gain, stem_bias)))
    frames = video.astype(jnp.float32)

    def forward(*values):
        block_out = block_forward(*values[:13], same_video)
        stem_out = stem_forward(frames, *values[13:])
        return (block_out, stem_out)
    outputs, pullback = jax.vjp(forward, *params)
    grads = pullback((block_grad.astype(jnp.float32), stem_grad.astype(jnp.float32)))
    return (outputs[0].astype(jnp.bfloat16), outputs[1].astype(jnp.bfloat16), grads[0].astype(jnp.bfloat16), grads[1], grads[2], grads[3], grads[4], grads[5], grads[6], grads[7], grads[8], grads[9], grads[10], grads[11], grads[12], grads[13], grads[14], grads[15], grads[16])
```

```python
import functools

import jax
import jax.numpy as jnp
from jax import lax
from jax.experimental import pallas as pl
from jax.experimental.pallas import tpu as pltpu
from jax.sharding import PartitionSpec as P

SEG = 8
SIDE = 7
FRAMES = 5
PIXELS = SIDE * SIDE
BLOCK = 16
SPAN = SIDE + 2

eps = 1e-05
vmem_limit = 60 * 1024 * 1024

whole = pl.BlockSpec(memory_space=pltpu.VMEM)
scalars = pl.BlockSpec(memory_space=pltpu.SMEM)


def logistic(value):
    return 0.5 * jnp.tanh(0.5 * value) + 0.5


def silu_slope(value):
    part = logistic(value)
    return part * (1.0 + value * (1.0 - part))


def norm_stats(totals, squares, count):
    center = totals / count
    spread = squares / count - center * center
    return (center, lax.rsqrt(spread + eps))


def kernel_call(body, out_shape, in_specs, scratch=(), flops=0, moved=0):
    return pl.pallas_call(
        body,
        out_shape=out_shape,
        in_specs=in_specs,
        out_specs=jax.tree.map(lambda _: whole, out_shape),
        scratch_shapes=list(scratch),
        compiler_params=pltpu.CompilerParams(vmem_limit_bytes=vmem_limit),
        cost_estimate=pl.CostEstimate(flops=flops, bytes_accessed=moved, transcendentals=0),
    )


PAIRS = SEG // 2
CLIP = SEG * PIXELS


def pair_row(clip, pair):
    return pl.multiple_of(BLOCK * (2 + SPAN * (PAIRS * clip + pair)), BLOCK)


def clip_view(ref, clip, extra=0):
    return ref.at[pl.ds(pl.multiple_of(clip * CLIP, 8), CLIP + extra)]


def lane_mask(width):
    return lax.broadcasted_iota(jnp.int32, (1, 8, width), 1)


def load_map(ref, first, lanes):
    return jnp.stack([ref[pl.ds(first + SIDE * at, 8), lanes] for at in range(SIDE)])


def store_map(ref, first, lanes, value):
    for at in range(SIDE):
        ref[pl.ds(first + SIDE * at, SIDE), lanes] = value[at][:SIDE]


def two_maps(early, late):
    both = jnp.stack([early, late], axis=1)
    return both.reshape(SIDE * BLOCK, early.shape[-1])


def down(value, step):
    zeros = jnp.zeros((abs(step),) + value.shape[1:], value.dtype)
    if step > 0:
        return jnp.concatenate([value[step:], zeros])
    if step < 0:
        return jnp.concatenate([zeros, value[:step]])
    return value


def across(value, step, place):
    if step == 0:
        return value
    moved = pltpu.roll(value, (-step) % 8, 1)
    if step == 2:
        return jnp.where(place < 6, moved, 0.0)
    if step == -2:
        return jnp.where(place > 0, moved, 0.0)
    return moved


def taps_of(near, far):
    for step, kernel in ((1, near), (2, far)):
        for row in range(3):
            yield step, row, [kernel[row * 3 + col] for col in range(3)]


def gate_score(change, near, far, offset, place):
    views = {step: across(change, step, place) for step in (-2, -1, 0, 1, 2)}
    score = jnp.broadcast_to(offset, change.shape)
    for step, row, kernel in taps_of(near, far):
        term = sum(kernel[col] * views[step * (col - 1)] for col in range(3))
        score = score + down(term, step * (row - 1))
    return score, views


def conv_chunk(parts, weights, first, rows, sign):
    total = None
    for col in (1, 0, 2):
        acc = None
        for row in range(3):
            start = pl.multiple_of(first + BLOCK * (1 + sign * (row - 1)), BLOCK)
            for part, weight in zip(parts, weights, strict=True):
                left = part[pl.ds(start, rows), :]
                term = weight(left, row * 3 + col)
                acc = term if acc is None else acc + term
        acc = acc.reshape(rows // 8, 8, acc.shape[-1])
        shift = sign * (col - 1)
        if shift:
            acc = pltpu.roll(acc, (-shift) % 8, 1)
        total = acc if total is None else total + acc
    return total


def gate_mid_body(
    count,
    y_ref,
    same_ref,
    own_ref,
    oth_ref,
    stats_ref,
    par_own_ref,
    par_oth_ref,
    weight_ref,
    mixed_ref,
    mid_ref,
    mid16_ref,
    sums_ref,
    hidden_ref,
    par_ref,
    acc_ref,
):
    rows, width = own_ref.shape
    clips = rows // CLIP
    y = y_ref[0]
    mixed_ref[...] = jnp.zeros_like(mixed_ref)
    hidden_ref[pl.ds(rows, hidden_ref.shape[0] - rows), :] = jnp.zeros(
        (hidden_ref.shape[0] - rows, 2 * width), jnp.float32
    )
    for side, (pre, par) in enumerate(((own_ref, par_own_ref), (oth_ref, par_oth_ref))):
        place = pl.multiple_of(width * (y if side == 0 else 1 - y), width)
        center, rate = norm_stats(
            stats_ref[2 * side : 2 * side + 1], stats_ref[2 * side + 1 : 2 * side + 2], count
        )
        scaled = (pre[...].astype(jnp.float32) - center) * rate
        normed = scaled * par[0:1] + par[1:2]
        hidden_ref[pl.ds(0, rows), pl.ds(place, width)] = normed * logistic(normed)
        par_ref[:, pl.ds(place, width)] = par[...]
    at = lane_mask(128)

    def lanes_step(chunk, _):
        lanes = pl.ds(pl.multiple_of(chunk * 128, 128), 128)
        near = [par_ref[5 + tap : 6 + tap, lanes].reshape(1, 1, 128) for tap in range(9)]
        far = [par_ref[14 + tap : 15 + tap, lanes].reshape(1, 1, 128) for tap in range(9)]
        offset = par_ref[4:5, lanes].reshape(1, 1, 128)

        def clip_step(clip, _):
            view = clip_view(hidden_ref, clip, 56)
            for pair in range(PAIRS):
                maps = [
                    load_map(view, PIXELS * (2 * pair + seg), lanes) for seg in range(3)
                ]
                results = []
                for seg in range(2):
                    same = same_ref[clip, 2 * pair + seg].astype(jnp.float32)
                    change = jnp.where(at < SIDE, same * (maps[seg + 1] - maps[seg]), 0.0)
                    score, _ = gate_score(change, near, far, offset, at)
                    mixed = maps[seg] * (1.0 + logistic(score))
                    results.append(jnp.where(at < SIDE, mixed, 0.0))
                place = pl.ds(pair_row(clip, pair), SIDE * BLOCK)
                mixed_ref[place, lanes] = two_maps(*results).astype(jnp.bfloat16)
            return 0

        return lax.fori_loop(0, clips, clip_step, 0)

    lax.fori_loop(0, 2 * width // 128, lanes_step, 0)
    depth = 2 * width

    def tap_dot(left, tap):
        return jnp.dot(
            left, weight_ref[tap * depth : (tap + 1) * depth], preferred_element_type=jnp.float32
        )

    def conv_step(clip, _):
        span = PAIRS * SPAN * BLOCK
        total = conv_chunk([mixed_ref], [tap_dot], clip * span, span, 1)
        view = clip_view(acc_ref, clip)
        for seg in range(SEG):
            value = [total[2 * (SPAN * (seg // 2) + 1 + row) + seg % 2] for row in range(SIDE)]
            store_map(view, seg * PIXELS, slice(None), value)
        return 0

    lax.fori_loop(0, clips, conv_step, 0)
    result = acc_ref[pl.ds(0, rows), :]
    mid_ref[...] = result
    mid16_ref[...] = result.astype(jnp.bfloat16)
    sums_ref[...] = jnp.zeros_like(sums_ref)
    sums_ref[0:1, :] = jnp.sum(result, 0, keepdims=True)
    sums_ref[1:2, :] = jnp.sum(result * result, 0, keepdims=True)


def map_rows(rows):
    return (rows // (2 * PIXELS) * SPAN + 2) * BLOCK


def gate_mid(count, y, same, own, oth, stats, par_own, par_oth, weight):
    rows, width = own.shape
    spread = map_rows(rows)
    return kernel_call(
        functools.partial(gate_mid_body, count),
        (
            jax.ShapeDtypeStruct((spread, 2 * width), jnp.bfloat16),
            jax.ShapeDtypeStruct((rows, width), jnp.float32),
            jax.ShapeDtypeStruct((rows, width), jnp.bfloat16),
            jax.ShapeDtypeStruct((8, width), jnp.float32),
        ),
        [scalars, scalars] + [whole] * 6,
        (
            pltpu.VMEM((rows + 56, 2 * width), jnp.float32),
            pltpu.VMEM((24, 2 * width), jnp.float32),
            pltpu.VMEM((rows + 8, width), jnp.float32),
        ),
        flops=2 * rows * weight.shape[0] * width,
        moved=weight.size * 2 + rows * width * 12,
    )(y, same, own, oth, stats, par_own, par_oth, weight)


def mid_back_body(
    count,
    y_ref,
    same_ref,
    d_own_ref,
    d_oth_ref,
    mid_own_ref,
    mid_oth_ref,
    stats_ref,
    back_ref,
    pre_ref,
    stats_in_ref,
    par_own_ref,
    par_oth_ref,
    weight_ref,
    weight_oth_ref,
    slopes_ref,
    d_in_ref,
    d_in16_ref,
    sums_ref,
    grads_ref,
    flat_ref,
    oth_ref,
    dmix_ref,
    scaled_ref,
    parts_ref,
):
    rows, width = d_own_ref.shape
    clips = rows // CLIP
    y = y_ref[0]
    everything = slice(None)
    slopes_ref[...] = jnp.zeros_like(slopes_ref)
    oth_ref[...] = jnp.zeros_like(oth_ref)
    flat_ref[pl.ds(rows, flat_ref.shape[0] - rows), :] = jnp.zeros(
        (flat_ref.shape[0] - rows, width), jnp.float32
    )
    at_wide = lane_mask(width)
    for side, (grad, pre, par) in enumerate(
        ((d_own_ref, mid_own_ref, par_own_ref), (d_oth_ref, mid_oth_ref, par_oth_ref))
    ):
        lo = 2 * side
        center, rate = norm_stats(stats_ref[lo : lo + 1], stats_ref[lo + 1 : lo + 2], count)
        scaled = (pre[...].astype(jnp.float32) - center) * rate
        flat_ref[pl.ds(0, rows), :] = (par[2:3] * rate) * (
            grad[...].astype(jnp.float32)
            - back_ref[lo : lo + 1] / count
            - scaled * (back_ref[lo + 1 : lo + 2] / count)
        )

        def spread_step(clip, _, side=side):
            view = clip_view(flat_ref, clip, 8)
            for pair in range(PAIRS):
                maps = [
                    jnp.where(
                        at_wide < SIDE, load_map(view, PIXELS * (2 * pair + seg), everything), 0.0
                    )
                    for seg in range(2)
                ]
                place = pl.ds(pair_row(clip, pair), SIDE * BLOCK)
                if side:
                    oth_ref[place, :] = two_maps(*maps).astype(jnp.bfloat16)
                else:
                    for col in range(3):
                        slopes_ref[col, place, :] = two_maps(
                            *[across(value, 1 - col, at_wide) for value in maps]
                        ).astype(jnp.bfloat16)
            return 0

        lax.fori_loop(0, clips, spread_step, 0)

    depth = 2 * width
    turned = (((1,), (1,)), ((), ()))

    def own_dot(left, tap):
        start = pl.multiple_of(tap * depth + y * width, width)
        return lax.dot_general(
            left, weight_ref[pl.ds(start, width), :], turned, preferred_element_type=jnp.float32
        )

    def oth_dot(left, tap):
        return lax.dot_general(
            left,
            weight_oth_ref[tap * width : (tap + 1) * width],
            turned,
            preferred_element_type=jnp.float32,
        )

    def conv_step(clip, _):
        span = PAIRS * SPAN * BLOCK
        total = conv_chunk([slopes_ref.at[1], oth_ref], [own_dot, oth_dot], clip * span, span, -1)
        dmix_ref[pl.ds(clip * (span // 8), span // 8)] = total
        return 0

    lax.fori_loop(0, clips, conv_step, 0)

    center, rate = norm_stats(stats_in_ref[0:1], stats_in_ref[1:2], count)
    scaled_ref[pl.ds(0, rows), :] = (pre_ref[...] - center) * rate
    scaled_ref[pl.ds(rows, scaled_ref.shape[0] - rows), :] = jnp.zeros(
        (scaled_ref.shape[0] - rows, width), jnp.float32
    )
    parts_ref[...] = jnp.zeros_like(parts_ref)
    at = lane_mask(128)

    def lanes_step(chunk, _):
        lanes = pl.ds(pl.multiple_of(chunk * 128, 128), 128)

        def row_of(index):
            return par_own_ref[index : index + 1, lanes].reshape(1, 1, 128)

        near = [row_of(5 + tap) for tap in range(9)]
        far = [row_of(14 + tap) for tap in range(9)]
        offset, gain, bias = row_of(4), row_of(0), row_of(1)

        def add_part(index, value):
            here = pl.ds(8 * index, 8)
            parts_ref[here, lanes] += jnp.sum(value, 0)

        def clip_step(clip, carry):
            view = clip_view(scaled_ref, clip, 56)
            target = clip_view(flat_ref, clip)
            for pair in range(PAIRS):
                carry = pair_step(clip, pair, carry, view, target)
            return carry

        def pair_step(clip, pair, carry, view, target):
            normed = [
                load_map(view, PIXELS * (2 * pair + seg), lanes) * gain + bias for seg in range(3)
            ]
            parts = [logistic(value) for value in normed]
            hidden = [value * part for value, part in zip(normed, parts, strict=True)]
            for seg in range(2):
                same = same_ref[clip, 2 * pair + seg].astype(jnp.float32)
                change = jnp.where(at < SIDE, same * (hidden[seg + 1] - hidden[seg]), 0.0)
                score, views = gate_score(change, near, far, offset, at)
                gate = logistic(score)
                start = 2 * (SPAN * (PAIRS * clip + pair) + 1) + seg
                d_mixed = jnp.stack([dmix_ref[start + 2 * row, :, lanes] for row in range(SIDE)])
                d_mixed = jnp.where(at < SIDE, d_mixed, 0.0)
                d_score = d_mixed * hidden[seg] * (gate * (1.0 - gate))
                add_part(0, d_score)
                backs = {step: across(d_score, step, at) for step in (-2, -1, 0, 1, 2)}
                d_change = None
                for index, (step, row, kernel) in enumerate(taps_of(near, far)):
                    here = down(d_score, -step * (row - 1))
                    for col in range(3):
                        add_part(1 + 3 * index + col, here * views[step * (col - 1)])
                    term = sum(kernel[col] * backs[-step * (col - 1)] for col in range(3))
                    term = down(term, -step * (row - 1))
                    d_change = term if d_change is None else d_change + term
                d_change = jnp.where(at < SIDE, same * d_change, 0.0)
                d_hidden = d_mixed * (1.0 + gate) - d_change + carry
                carry = d_change
                slope = parts[seg] * (1.0 + normed[seg] * (1.0 - parts[seg]))
                store_map(target, PIXELS * (2 * pair + seg), lanes, d_hidden * slope)
            return carry

        lax.fori_loop(0, clips, clip_step, jnp.zeros((SIDE, 8, 128), jnp.float32))
        return 0

    lax.fori_loop(0, width // 128, lanes_step, 0)
    result = flat_ref[pl.ds(0, rows), :]
    d_in_ref[...] = result
    d_in16_ref[...] = result.astype(jnp.bfloat16)
    sums_ref[...] = jnp.zeros_like(sums_ref)
    sums_ref[0:1, :] = jnp.sum(result, 0, keepdims=True)
    sums_ref[1:2, :] = jnp.sum(result * scaled_ref[pl.ds(0, rows), :], 0, keepdims=True)
    grads_ref[...] = jnp.sum(parts_ref[...].reshape(24, 8, width), 1)


def mid_back(
    count, y, same, d_own, d_oth, mid_own, mid_oth, stats, back, pre, stats_in, par_own, par_oth,
    weight, weight_oth,
):
    rows, width = d_own.shape
    spread = map_rows(rows)
    return kernel_call(
        functools.partial(mid_back_body, count),
        (
            jax.ShapeDtypeStruct((3, spread, width), jnp.bfloat16),
            jax.ShapeDtypeStruct((rows, width), jnp.float32),
            jax.ShapeDtypeStruct((rows, width), jnp.bfloat16),
            jax.ShapeDtypeStruct((8, width), jnp.float32),
            jax.ShapeDtypeStruct((24, width), jnp.float32),
        ),
        [scalars, scalars] + [whole] * 12,
        (
            pltpu.VMEM((rows + 56, width), jnp.float32),
            pltpu.VMEM((spread, width), jnp.bfloat16),
            pltpu.VMEM((spread // 8, 8, width), jnp.float32),
            pltpu.VMEM((rows + 56, width), jnp.float32),
            pltpu.VMEM((24 * 8, width), jnp.float32),
        ),
        flops=2 * rows * weight.shape[0] * width,
        moved=weight.size * 3 + rows * width * 20,
    )(
        y, same, d_own, d_oth, mid_own, mid_oth, stats, back, pre, stats_in, par_own, par_oth,
        weight, weight_oth,
    )


def mid_weight_body(r_ref, mixed_ref, slopes_ref, keep_ref, send_ref, turned_ref):
    spread, depth = mixed_ref.shape
    rows = spread - 2 * BLOCK
    half = keep_ref.shape[1]
    first = r_ref[0] == 0
    turned_ref[...] = mixed_ref[pl.ds(BLOCK, rows), :].T
    for tap in range(9):
        row, col = tap // 3, tap % 3
        right = slopes_ref[col, pl.ds(BLOCK * (2 - row), rows), :]
        value = jnp.dot(turned_ref[...], right, preferred_element_type=jnp.float32)
        low, high = value[:, :half], value[:, half:]
        keep_ref[tap * depth : (tap + 1) * depth] = jnp.where(first, low, high)
        send_ref[tap * depth : (tap + 1) * depth] = jnp.where(first, high, low).astype(jnp.bfloat16)


def mid_weight(r, mixed, slopes):
    spread, depth = mixed.shape
    width = slopes.shape[2]
    return kernel_call(
        mid_weight_body,
        (
            jax.ShapeDtypeStruct((9 * depth, width // 2), jnp.float32),
            jax.ShapeDtypeStruct((9 * depth, width // 2), jnp.bfloat16),
        ),
        [scalars, whole, whole],
        (pltpu.VMEM((depth, spread - 2 * BLOCK), jnp.bfloat16),),
        flops=2 * spread * 9 * depth * width,
        moved=spread * (2 * depth + 6 * width) + 9 * depth * width * 3,
    )(r, mixed, slopes)


def stem_conv(planes, kernel):
    segs, chans = (planes.shape[0], planes.shape[1])
    side = planes.shape[2]
    width = int(round(side**0.5))
    field = planes.reshape(segs, chans, width, width)
    weights = kernel.reshape(chans, 7, 7, kernel.shape[1])
    result = lax.conv_general_dilated(
        field,
        weights,
        (2, 2),
        ((3, 3), (3, 3)),
        dimension_numbers=("NCHW", "IHWO", "NCHW"),
        preferred_element_type=jnp.float32,
    )
    return result.reshape(segs, kernel.shape[1], width // 2 * (width // 2))


def stem_kernel_grad(planes, slopes):
    segs, chans = (planes.shape[0], planes.shape[1])
    width = int(round(planes.shape[2] ** 0.5))
    half = width // 2
    outputs = slopes.shape[1]
    field = planes.reshape(segs, chans, width, width)
    grads = slopes.reshape(segs, outputs, half, half)
    result = lax.conv_general_dilated(
        field,
        grads,
        (1, 1),
        ((3, 2), (3, 2)),
        rhs_dilation=(2, 2),
        dimension_numbers=("CNHW", "IOHW", "NCHW"),
        preferred_element_type=jnp.float32,
    )
    return jnp.transpose(result, (0, 2, 3, 1)).reshape(chans * 49, outputs)


def norm_back(upstream, scaled, gain, rate, bias_grad, gain_grad, count):
    return gain * rate * (upstream - bias_grad / count - scaled * gain_grad / count)


def swap(value, axis, bit):
    size = lax.axis_size(axis)
    return lax.ppermute(value, axis, [(at, at ^ bit) for at in range(size)])


def steps_of(axis):
    size = lax.axis_size(axis)
    assert size & (size - 1) == 0
    return [1 << at for at in range(size.bit_length() - 1)]


def sum_over(value, axis):
    for bit in steps_of(axis):
        value = value + swap(value, axis, bit)
    return value


def ordered(second, own, other, axis=0):
    return jnp.where(
        second, jnp.concatenate([other, own], axis), jnp.concatenate([own, other], axis)
    )


def gather_rows(value, axis):
    index = lax.axis_index(axis)
    full = value[None]
    bits = steps_of(axis)
    for bit in reversed(bits):
        other = swap(full, axis, bit)
        full = ordered((index & bit) != 0, full[None], other[None])
    full = full.reshape([2] * len(bits) + list(value.shape))
    order = list(reversed(range(len(bits))))
    full = full.transpose(order + [len(bits), len(bits) + 1])
    return full.reshape(-1, value.shape[1])


def scatter_rows(keep, send, axis):
    bits = steps_of(axis)
    index = lax.axis_index(axis)
    for place, bit in enumerate(bits):
        total = keep + swap(send, axis, bit).astype(jnp.float32)
        if place + 1 < len(bits):
            keep, send = split_rows(total, (index >> (place + 1)) & 1, len(bits) - place - 1)
        else:
            keep = total
    return keep


def split_rows(value, bit, left):
    rows, width = value.shape
    blocks = value.reshape(1 << (left - 1), 2, rows >> left, width)
    low, high = blocks[:, 0], blocks[:, 1]
    keep = jnp.where(bit == 0, low, high).reshape(-1, width)
    send = jnp.where(bit == 0, high, low).astype(jnp.bfloat16).reshape(-1, width)
    return keep, send


def reduce_rows(value, axis):
    bits = steps_of(axis)
    keep, send = split_rows(value, lax.axis_index(axis) & 1, len(bits))
    return scatter_rows(keep, send, axis)


def transposed(left, right):
    return lax.dot_general(
        left, right, (((1,), (1,)), ((), ())), preferred_element_type=jnp.float32
    )


def weight_grad(left, right):
    return lax.dot_general(
        left, right, (((0,), (0,)), ((), ())), preferred_element_type=jnp.float32
    )


def per_device(
    block_in,
    weight_in,
    weight_mid,
    weight_out,
    gain_in,
    bias_in,
    gain_mid,
    bias_mid,
    gain_out,
    bias_out,
    kernel_near,
    kernel_far,
    gate_bias,
    same_video,
    video,
    stem_center,
    stem_diff,
    stem_gain,
    stem_bias,
    block_grad,
    stem_grad,
):
    groups = lax.axis_size("dp")
    assert lax.axis_size("chan") == 4
    clips = same_video.shape[0]
    rows, quarter = block_in.shape
    half = rows // 2
    narrow = weight_in.shape[1]
    width = 2 * narrow
    count = float(rows * groups)
    segs = video.shape[0]
    stem_count = float(segs * stem_grad.shape[2] * groups)
    chan = lax.axis_index("chan")
    core, y = chan % 2, chan // 2
    y_scalar, core_scalar = y.reshape(1), core.reshape(1)

    def my_rows(value, which):
        return lax.dynamic_slice_in_dim(value, which * half, half, 0)

    mine, others = my_rows(block_in, core), my_rows(block_in, 1 - core)
    pieces = [mine, swap(others, "chan", 1), swap(mine, "chan", 2), swap(others, "chan", 3)]

    own_in = gather_rows(weight_in, "dp")
    full_in = ordered(core == 1, own_in, swap(own_in, "chan", 1), 1)
    packed = jnp.concatenate([weight_mid, weight_out.reshape(-1, narrow)], 0)
    gathered = lax.all_gather(packed, "dp", axis=0)
    own_mid = gathered[:, : weight_mid.shape[0]].reshape(-1, narrow)
    full_out = gathered[:, weight_mid.shape[0] :].reshape(-1, weight_out.shape[1])
    full_mid = ordered(core == 1, own_mid, swap(own_mid, "chan", 1), 1)
    slab = lax.dynamic_slice_in_dim(own_mid.reshape(9, 2, width, narrow), 1 - y, 1, 1)
    slab = swap(slab.reshape(9 * width, narrow), "chan", 2)
    oth_mid = ordered(core == 1, slab, swap(slab, "chan", 1), 1)
    away = lax.dynamic_slice_in_dim(full_in, (chan ^ 2) * quarter, quarter, 0)
    here = lax.dynamic_slice_in_dim(full_in, chan * quarter, quarter, 0)
    rows_in = ordered(y == 1, here, swap(away, "chan", 2), 1)

    params = jnp.concatenate(
        [
            jnp.stack([gain_in, bias_in, gain_mid, bias_mid, gate_bias]),
            kernel_near,
            kernel_far,
            jnp.zeros((1, narrow), jnp.float32),
        ]
    )
    par_own = ordered(core == 1, params, swap(params, "chan", 1), 1)
    par_oth = swap(par_own, "chan", 2)
    same = lax.dynamic_slice_in_dim(same_video, core * (clips // 2), clips // 2, 0)
    same = jnp.concatenate([same, jnp.zeros((clips // 2, 1), jnp.int32)], 1)

    frames = video.reshape(segs, FRAMES, 3, video.shape[2])
    center_frame = frames[:, FRAMES // 2]
    moving = frames[:, 1:].astype(jnp.float32) - frames[:, :-1].astype(jnp.float32)
    diff_frames = moving.reshape(segs, 3 * (FRAMES - 1), video.shape[2]).astype(jnp.bfloat16)
    pre_stem = stem_conv(center_frame, stem_center) + stem_conv(diff_frames, stem_diff)

    pre_in = sum(
        jnp.dot(
            piece,
            lax.dynamic_slice_in_dim(full_in, (chan ^ at) * quarter, quarter, 0),
            preferred_element_type=jnp.float32,
        )
        for at, piece in enumerate(pieces)
    )
    pre_in_oth = swap(pre_in.astype(jnp.bfloat16), "chan", 2)

    def both_sums(first, second, extra):
        own = jnp.stack([first, second])
        own = own + swap(own, "chan", 1)
        packed = jnp.concatenate([own] + extra)
        packed = sum_over(packed, "dp")
        own = packed[:2]
        oth = swap(own, "chan", 2)
        return jnp.concatenate([own, oth, jnp.zeros((4, width), jnp.float32)]), packed[2:]

    def stem_row(first, second):
        row = jnp.concatenate([first, second])
        return [jnp.pad(row, (0, width - row.shape[0]))[None]]

    outs = stem_grad.shape[1]
    stats_in, stem_stats = both_sums(
        jnp.sum(pre_in, 0),
        jnp.sum(pre_in * pre_in, 0),
        stem_row(jnp.sum(pre_stem, (0, 2)), jnp.sum(pre_stem * pre_stem, (0, 2))),
    )
    center_stem, rate_stem = norm_stats(stem_stats[0, :outs], stem_stats[0, outs : 2 * outs], stem_count)
    scaled_stem = (pre_stem - center_stem[:, None]) * rate_stem[:, None]
    normed_stem = scaled_stem * stem_gain[:, None] + stem_bias[:, None]
    stem_out = (normed_stem * logistic(normed_stem)).astype(jnp.bfloat16)
    grad_normed_stem = stem_grad.astype(jnp.float32) * silu_slope(normed_stem)
    stem_sums = stem_row(
        jnp.sum(grad_normed_stem, (0, 2)), jnp.sum(grad_normed_stem * scaled_stem, (0, 2))
    )

    mixed, pre_mid, pre_mid16, sums_mid = gate_mid(
        count, y_scalar, same, pre_in, pre_in_oth, stats_in, par_own, par_oth, full_mid
    )
    pre_mid_oth = swap(pre_mid16, "chan", 2)
    stats_mid, stem_back = both_sums(sums_mid[0], sums_mid[1], stem_sums)

    def mid_norm(value, stats, par):
        center, rate = norm_stats(stats[0], stats[1], count)
        scaled = (value.astype(jnp.float32) - center) * rate
        return scaled, scaled * par[2] + par[3]

    scaled_mid, normed_mid = mid_norm(pre_mid, stats_mid[:2], par_own)
    _, normed_oth = mid_norm(pre_mid_oth, stats_mid[2:4], par_oth)
    second_own = (normed_mid * logistic(normed_mid)).astype(jnp.bfloat16)
    second_oth = (normed_oth * logistic(normed_oth)).astype(jnp.bfloat16)
    second_half = ordered(y == 1, second_own, second_oth, 1)
    second = ordered(core == 1, second_half, swap(second_half, "chan", 1))

    pre_out = jnp.dot(second, full_out, preferred_element_type=jnp.float32)
    stats_out = sum_over(jnp.stack([jnp.sum(pre_out, 0), jnp.sum(pre_out * pre_out, 0)]), "dp")
    center_out, rate_out = norm_stats(stats_out[0], stats_out[1], count)
    scaled_out = (pre_out - center_out) * rate_out
    total = scaled_out * gain_out + bias_out + block_in.astype(jnp.float32)
    part = logistic(total)
    block_out = (total * part).astype(jnp.bfloat16)
    grad_total = block_grad.astype(jnp.float32) * (part * (1.0 + total * (1.0 - part)))
    back_out = sum_over(
        jnp.stack([jnp.sum(grad_total, 0), jnp.sum(grad_total * scaled_out, 0)]), "dp"
    )
    bias_out_grad, gain_out_grad = back_out[0], back_out[1]
    grad_pre_out = norm_back(
        grad_total, scaled_out, gain_out, rate_out, bias_out_grad, gain_out_grad, count
    ).astype(jnp.bfloat16)

    stem_bias_grad, stem_gain_grad = stem_back[0, :outs], stem_back[0, outs : 2 * outs]
    grad_pre_stem = norm_back(
        grad_normed_stem,
        scaled_stem,
        stem_gain[:, None],
        rate_stem[:, None],
        stem_bias_grad[:, None],
        stem_gain_grad[:, None],
        stem_count,
    ).astype(jnp.bfloat16)
    part_center = stem_kernel_grad(center_frame, grad_pre_stem)
    part_diff = stem_kernel_grad(diff_frames, grad_pre_stem)

    grad_second = transposed(grad_pre_out, full_out)
    keep, send = my_rows(grad_second, core), my_rows(grad_second, 1 - core)
    keep = keep + swap(send.astype(jnp.bfloat16), "chan", 1).astype(jnp.float32)
    send = lax.dynamic_slice_in_dim(keep, (1 - y) * width, width, 1)
    keep = lax.dynamic_slice_in_dim(keep, y * width, width, 1)
    grad_second = keep + swap(send.astype(jnp.bfloat16), "chan", 2).astype(jnp.float32)
    grad_normed_mid = grad_second * silu_slope(normed_mid)
    grad_mid_oth = swap(grad_normed_mid.astype(jnp.bfloat16), "chan", 2)
    back_mid, _ = both_sums(
        jnp.sum(grad_normed_mid, 0), jnp.sum(grad_normed_mid * scaled_mid, 0), []
    )
    sum_out = reduce_rows(weight_grad(second, grad_pre_out), "dp")

    slopes, grad_in, grad_in16, sums_in, gate_parts = mid_back(
        count, y_scalar, same, grad_normed_mid, grad_mid_oth, pre_mid, pre_mid_oth, stats_mid,
        back_mid, pre_in, stats_in, par_own, par_oth, full_mid, oth_mid,
    )
    grad_in_oth = swap(grad_in16, "chan", 2)
    back_in, _ = both_sums(sums_in[0], sums_in[1], [])
    keep, send = mid_weight(core_scalar, mixed, slopes)
    part_mid = keep + swap(send, "chan", 1).astype(jnp.float32)
    sum_mid = reduce_rows(part_mid, "dp")

    def in_back(value, pre, stats, par, back):
        center, rate = norm_stats(stats[0], stats[1], count)
        scaled = (pre.astype(jnp.float32) - center) * rate
        return norm_back(
            value.astype(jnp.float32), scaled, par[0], rate, back[0], back[1], count
        ).astype(jnp.bfloat16)

    pre_own = in_back(grad_in, pre_in, stats_in[:2], par_own, back_in[:2])
    pre_oth = in_back(grad_in_oth, pre_in_oth, stats_in[2:4], par_oth, back_in[2:4])
    grad_half = ordered(y == 1, pre_own, pre_oth, 1)
    grad_pre_in = ordered(core == 1, grad_half, swap(grad_half, "chan", 1))
    grad_block_in = (transposed(grad_pre_in, rows_in) + grad_total).astype(jnp.bfloat16)
    blocks = jnp.stack([weight_grad(piece, pre_own) for piece in pieces])
    blocks = jnp.where(core == 1, blocks[jnp.array([1, 0, 3, 2])], blocks)
    blocks = jnp.where(y == 1, blocks[jnp.array([2, 3, 0, 1])], blocks).reshape(-1, width)
    send = lax.dynamic_slice_in_dim(blocks, (1 - core) * narrow, narrow, 1)
    keep = lax.dynamic_slice_in_dim(blocks, core * narrow, narrow, 1)
    part_in = keep + swap(send.astype(jnp.bfloat16), "chan", 1).astype(jnp.float32)
    sum_in = reduce_rows(part_in, "dp")

    gate_parts = gate_parts + swap(gate_parts, "chan", 1)
    stem_flat = jnp.concatenate([part_center, part_diff]).reshape(-1)
    stem_size = stem_flat.shape[0]
    padded = -(-stem_size // width)
    stem_flat = jnp.pad(stem_flat, (0, padded * width - stem_size)).reshape(padded, width)
    small = sum_over(jnp.concatenate([gate_parts, stem_flat]), "dp")
    stem_flat = small[24:].reshape(-1)[:stem_size].reshape(-1, outs)
    split = part_center.shape[0]

    def my_columns(value):
        return lax.dynamic_slice_in_dim(value, core * narrow, narrow, value.ndim - 1)

    gate_grads = my_columns(small[:24])
    mid_grads, in_grads = my_columns(back_mid), my_columns(back_in)
    return (
        block_out,
        stem_out,
        grad_block_in,
        sum_in,
        sum_mid,
        sum_out,
        in_grads[1],
        in_grads[0],
        mid_grads[1],
        mid_grads[0],
        gain_out_grad,
        bias_out_grad,
        gate_grads[1:10],
        gate_grads[10:19],
        gate_grads[0],
        stem_flat[:split],
        stem_flat[split:],
        stem_gain_grad,
        stem_bias_grad,
    )


def solution(mesh):
    placed = (
        P("dp", "chan"),
        P("dp", "chan"),
        P("dp", "chan"),
        P("dp", "chan"),
        P("chan"),
        P("chan"),
        P("chan"),
        P("chan"),
        P("chan"),
        P("chan"),
        P(None, "chan"),
        P(None, "chan"),
        P("chan"),
        P("dp", None),
        P("dp", None, None),
        P(None, "chan"),
        P(None, "chan"),
        P("chan"),
        P("chan"),
        P("dp", "chan"),
        P("dp", "chan", None),
    )
    return jax.shard_map(
        per_device,
        mesh=mesh,
        in_specs=placed,
        out_specs=(
            P("dp", "chan"),
            P("dp", "chan", None),
            P("dp", "chan"),
            P("dp", "chan"),
            P("dp", "chan"),
            P("dp", "chan"),
            P("chan"),
            P("chan"),
            P("chan"),
            P("chan"),
            P("chan"),
            P("chan"),
            P(None, "chan"),
            P(None, "chan"),
            P("chan"),
            P(None, "chan"),
            P(None, "chan"),
            P("chan"),
            P("chan"),
        ),
        check_vma=False,
    )
```

```python
import functools

import jax
import jax.numpy as jnp
from jax import lax
from jax.experimental import pallas as pl
from jax.experimental.pallas import tpu as pltpu
from jax.sharding import PartitionSpec as P

SEG = 8
SIDE = 7
FRAMES = 5
PIXELS = SIDE * SIDE
BLOCK = 16
SPAN = SIDE + 2

eps = 1e-05
vmem_limit = 24 * 1024 * 1024

whole = pl.BlockSpec(memory_space=pltpu.VMEM)
remote = pl.BlockSpec(memory_space=pltpu.HBM)
scalars = pl.BlockSpec(memory_space=pltpu.SMEM)


def logistic(value):
    return 0.5 * jnp.tanh(0.5 * value) + 0.5


def silu_slope(value):
    part = logistic(value)
    return part * (1.0 + value * (1.0 - part))


def norm_stats(totals, squares, count):
    center = totals / count
    spread = squares / count - center * center
    return (center, lax.rsqrt(spread + eps))


def move(source, target, sems, at):
    copy = pltpu.make_async_copy(source, target, sems.at[at])
    copy.start()
    return copy


def kernel_call(body, out_shape, in_specs, scratch=(), flops=0, moved=0, away=(), held=()):
    several = isinstance(out_shape, tuple)
    shapes = list(out_shape) if several else [out_shape]
    specs = [remote if at in away else whole for at in range(len(shapes))]
    shapes = [
        (pltpu.HBM if at in away else pltpu.VMEM)(shape.shape, shape.dtype)
        if at in away or at in held
        else shape
        for at, shape in enumerate(shapes)
    ]
    call = pl.pallas_call(
        body,
        out_shape=tuple(shapes) if several else shapes[0],
        in_specs=in_specs,
        out_specs=tuple(specs) if several else specs[0],
        scratch_shapes=list(scratch),
        compiler_params=pltpu.CompilerParams(vmem_limit_bytes=vmem_limit),
        cost_estimate=pl.CostEstimate(flops=flops, bytes_accessed=moved, transcendentals=0),
    )

    def run(*args):
        return call(
            *[
                pltpu.with_memory_space_constraint(arg, pltpu.HBM) if spec is remote else arg
                for arg, spec in zip(args, in_specs, strict=True)
            ]
        )

    return run


PAIRS = SEG // 2
CLIP = SEG * PIXELS


def pair_row(clip, pair):
    return pl.multiple_of(BLOCK * (2 + SPAN * (PAIRS * clip + pair)), BLOCK)


def clip_view(ref, clip, extra=0):
    return ref.at[pl.ds(pl.multiple_of(clip * CLIP, 8), CLIP + extra)]


def lane_mask(width):
    return lax.broadcasted_iota(jnp.int32, (1, 8, width), 1)


def load_map(ref, first, lanes):
    return jnp.stack([ref[pl.ds(first + SIDE * at, 8), lanes] for at in range(SIDE)])


def store_map(ref, first, lanes, value):
    for at in range(SIDE):
        ref[pl.ds(first + SIDE * at, SIDE), lanes] = value[at][:SIDE]


def two_maps(early, late):
    both = jnp.stack([early, late], axis=1)
    return both.reshape(SIDE * BLOCK, early.shape[-1])


def down(value, step):
    zeros = jnp.zeros((abs(step),) + value.shape[1:], value.dtype)
    if step > 0:
        return jnp.concatenate([value[step:], zeros])
    if step < 0:
        return jnp.concatenate([zeros, value[:step]])
    return value


def across(value, step, place):
    if step == 0:
        return value
    moved = pltpu.roll(value, (-step) % 8, 1)
    if step == 2:
        return jnp.where(place < 6, moved, 0.0)
    if step == -2:
        return jnp.where(place > 0, moved, 0.0)
    return moved


def taps_of(near, far):
    for step, kernel in ((1, near), (2, far)):
        for row in range(3):
            yield step, row, [kernel[row * 3 + col] for col in range(3)]


def gate_score(change, near, far, offset, place):
    views = {step: across(change, step, place) for step in (-2, -1, 0, 1, 2)}
    score = jnp.broadcast_to(offset, change.shape)
    for step, row, kernel in taps_of(near, far):
        term = sum(kernel[col] * views[step * (col - 1)] for col in range(3))
        score = score + down(term, step * (row - 1))
    return score, views


def conv_chunk(parts, weights, first, rows, sign):
    total = None
    for col in (1, 0, 2):
        acc = None
        for row in range(3):
            start = pl.multiple_of(first + BLOCK * (1 + sign * (row - 1)), BLOCK)
            for part, weight in zip(parts, weights, strict=True):
                left = part[pl.ds(start, rows), :]
                term = weight(left, row * 3 + col)
                acc = term if acc is None else acc + term
        acc = acc.reshape(rows // 8, 8, acc.shape[-1])
        shift = sign * (col - 1)
        if shift:
            acc = pltpu.roll(acc, (-shift) % 8, 1)
        total = acc if total is None else total + acc
    return total


def lane_part(index, width=128):
    return pl.ds(pl.multiple_of(index * width, width), width)


def row_part(index, size):
    return pl.ds(pl.multiple_of(index * size, size), size)


def rows_of(stats_ref):
    return stats_ref[0:1], stats_ref[1:2]


def put_sums(sums_ref, first, second):
    sums_ref[...] = jnp.zeros_like(sums_ref)
    sums_ref[0:1, :] = first
    sums_ref[1:2, :] = second


def gate_mid_body(
    count,
    place_ref,
    same_ref,
    own_ref,
    oth_ref,
    stats_own_ref,
    stats_oth_ref,
    par_own_ref,
    par_oth_ref,
    weight_own_ref,
    weight_peer_ref,
    mixed_out_ref,
    mid_ref,
    mid16_ref,
    sums_ref,
    hidden_ref,
    par_ref,
    acc_ref,
    weight_ref,
    oth_here_ref,
    stats_here_ref,
    mixed_ref,
    sems,
):
    rows, width = own_ref.shape
    clips = rows // CLIP
    core, y = place_ref[0] % 2, place_ref[0] // 2
    arrivals = [
        move(stats_oth_ref, stats_here_ref, sems, 0),
        move(oth_ref, oth_here_ref, sems, 1),
    ]
    weight_moves = [
        move(weight_own_ref, weight_ref.at[:, lane_part(core)], sems, 2),
        move(weight_peer_ref, weight_ref.at[:, lane_part(1 - core)], sems, 3),
    ]
    mixed_ref[...] = jnp.zeros_like(mixed_ref)
    hidden_ref[pl.ds(rows, hidden_ref.shape[0] - rows), :] = jnp.zeros(
        (hidden_ref.shape[0] - rows, 2 * width), jnp.float32
    )
    for side, (pre, stats, par) in enumerate(
        (
            (own_ref, stats_own_ref, par_own_ref),
            (oth_here_ref, stats_here_ref, par_oth_ref),
        )
    ):
        place = pl.multiple_of(width * (y if side == 0 else 1 - y), width)
        if side:
            for copy in arrivals:
                copy.wait()
        center, rate = norm_stats(*rows_of(stats), count)
        scaled = (pre[...].astype(jnp.float32) - center) * rate
        normed = scaled * par[0:1] + par[1:2]
        hidden_ref[pl.ds(0, rows), pl.ds(place, width)] = normed * logistic(normed)
        par_ref[:, pl.ds(place, width)] = par[...]
    at = lane_mask(128)

    def lanes_step(chunk, _):
        lanes = pl.ds(pl.multiple_of(chunk * 128, 128), 128)
        near = [par_ref[5 + tap : 6 + tap, lanes].reshape(1, 1, 128) for tap in range(9)]
        far = [par_ref[14 + tap : 15 + tap, lanes].reshape(1, 1, 128) for tap in range(9)]
        offset = par_ref[4:5, lanes].reshape(1, 1, 128)

        def clip_step(clip, _):
            view = clip_view(hidden_ref, clip, 56)
            for pair in range(PAIRS):
                maps = [
                    load_map(view, PIXELS * (2 * pair + seg), lanes) for seg in range(3)
                ]
                results = []
                for seg in range(2):
                    same = same_ref[clip, 2 * pair + seg].astype(jnp.float32)
                    change = jnp.where(at < SIDE, same * (maps[seg + 1] - maps[seg]), 0.0)
                    score, _ = gate_score(change, near, far, offset, at)
                    mixed = maps[seg] * (1.0 + logistic(score))
                    results.append(jnp.where(at < SIDE, mixed, 0.0))
                place = pl.ds(pair_row(clip, pair), SIDE * BLOCK)
                mixed_ref[place, lanes] = two_maps(*results).astype(jnp.bfloat16)
            return 0

        return lax.fori_loop(0, clips, clip_step, 0)

    lax.fori_loop(0, 2 * width // 128, lanes_step, 0)
    depth = 2 * width
    mixed_move = move(mixed_ref, mixed_out_ref, sems, 4)
    for copy in weight_moves:
        copy.wait()

    def tap_dot(left, tap):
        return jnp.dot(
            left, weight_ref[tap * depth : (tap + 1) * depth], preferred_element_type=jnp.float32
        )

    def conv_step(clip, _):
        span = PAIRS * SPAN * BLOCK
        total = conv_chunk([mixed_ref], [tap_dot], clip * span, span, 1)
        view = clip_view(acc_ref, clip)
        for seg in range(SEG):
            value = [total[2 * (SPAN * (seg // 2) + 1 + row) + seg % 2] for row in range(SIDE)]
            store_map(view, seg * PIXELS, slice(None), value)
        return 0

    lax.fori_loop(0, clips, conv_step, 0)
    mid_move = move(acc_ref.at[pl.ds(0, rows)], mid_ref, sems, 5)
    result = acc_ref[pl.ds(0, rows), :]
    mid16_ref[...] = result.astype(jnp.bfloat16)
    put_sums(
        sums_ref, jnp.sum(result, 0, keepdims=True), jnp.sum(result * result, 0, keepdims=True)
    )
    mixed_move.wait()
    mid_move.wait()


def map_rows(rows):
    return (rows // (2 * PIXELS) * SPAN + 2) * BLOCK


def gate_mid(count, place, same, own, oth, stats_own, stats_oth, par_own, par_oth, weights):
    rows, width = own.shape
    spread = map_rows(rows)
    depth = weights[0].shape[0]
    return kernel_call(
        functools.partial(gate_mid_body, count),
        (
            jax.ShapeDtypeStruct((spread, 2 * width), jnp.bfloat16),
            jax.ShapeDtypeStruct((rows, width), jnp.float32),
            jax.ShapeDtypeStruct((rows, width), jnp.bfloat16),
            jax.ShapeDtypeStruct((8, width), jnp.float32),
        ),
        [scalars, scalars, whole, remote, whole, remote, whole, whole, remote, remote],
        (
            pltpu.VMEM((rows + 56, 2 * width), jnp.float32),
            pltpu.VMEM((24, 2 * width), jnp.float32),
            pltpu.VMEM((rows + 8, width), jnp.float32),
            pltpu.VMEM((depth, width), jnp.bfloat16),
            pltpu.VMEM((rows, width), jnp.bfloat16),
            pltpu.VMEM((8, width), jnp.float32),
            pltpu.VMEM((spread, 2 * width), jnp.bfloat16),
            pltpu.SemaphoreType.DMA((6,)),
        ),
        away=(0, 1),
        flops=2 * rows * depth * width,
        moved=depth * width * 2 + rows * width * 12,
    )(place, same, own, oth, stats_own, stats_oth, par_own, par_oth, *weights)


def mid_back_body(
    count,
    place_ref,
    same_ref,
    d_own_ref,
    d_oth_ref,
    mid_own_ref,
    mid_oth_ref,
    stats_own_ref,
    stats_oth_ref,
    back_own_ref,
    back_oth_ref,
    pre_ref,
    stats_in_ref,
    par_own_ref,
    par_oth_ref,
    weight_own_ref,
    weight_peer_ref,
    away_own_ref,
    away_peer_ref,
    slopes_ref,
    d_in_ref,
    d_in16_ref,
    sums_ref,
    flat_ref,
    oth_ref,
    dmix_ref,
    scaled_ref,
    parts_ref,
    weight_ref,
    weight_oth_ref,
    d_here_ref,
    mid_here_ref,
    back_here_ref,
    pre_here_ref,
    sems,
):
    rows, width = d_own_ref.shape
    clips = rows // CLIP
    core, y = place_ref[0] % 2, place_ref[0] // 2
    arrivals = [
        move(back_oth_ref, back_here_ref, sems, 0),
        move(d_oth_ref, d_here_ref, sems, 1),
        move(mid_oth_ref, mid_here_ref, sems, 2),
    ]
    weight_moves = [
        move(weight_own_ref, weight_ref.at[:, lane_part(core)], sems, 3),
        move(weight_peer_ref, weight_ref.at[:, lane_part(1 - core)], sems, 4),
        move(away_own_ref, weight_oth_ref.at[:, lane_part(core)], sems, 5),
        move(away_peer_ref, weight_oth_ref.at[:, lane_part(1 - core)], sems, 6),
    ]
    pre_move = move(pre_ref, pre_here_ref, sems, 7)
    everything = slice(None)
    slopes_ref[...] = jnp.zeros_like(slopes_ref)
    oth_ref[...] = jnp.zeros_like(oth_ref)
    flat_ref[pl.ds(rows, flat_ref.shape[0] - rows), :] = jnp.zeros(
        (flat_ref.shape[0] - rows, width), jnp.float32
    )
    at_wide = lane_mask(width)
    for side, (grad, pre, stats, back, par) in enumerate(
        (
            (d_own_ref, mid_own_ref, stats_own_ref, back_own_ref, par_own_ref),
            (d_here_ref, mid_here_ref, stats_oth_ref, back_here_ref, par_oth_ref),
        )
    ):
        if side:
            for copy in arrivals:
                copy.wait()
        center, rate = norm_stats(*rows_of(stats), count)
        scaled = (pre[...].astype(jnp.float32) - center) * rate
        flat_ref[pl.ds(0, rows), :] = (par[2:3] * rate) * (
            grad[...].astype(jnp.float32)
            - back[0:1] / count
            - scaled * (back[1:2] / count)
        )

        def spread_step(clip, _, side=side):
            view = clip_view(flat_ref, clip, 8)
            for pair in range(PAIRS):
                maps = [
                    jnp.where(
                        at_wide < SIDE, load_map(view, PIXELS * (2 * pair + seg), everything), 0.0
                    )
                    for seg in range(2)
                ]
                place = pl.ds(pair_row(clip, pair), SIDE * BLOCK)
                if side:
                    oth_ref[place, :] = two_maps(*maps).astype(jnp.bfloat16)
                else:
                    for col in range(3):
                        slopes_ref[col, place, :] = two_maps(
                            *[across(value, 1 - col, at_wide) for value in maps]
                        ).astype(jnp.bfloat16)
            return 0

        lax.fori_loop(0, clips, spread_step, 0)

    depth = 2 * width
    turned = (((1,), (1,)), ((), ()))
    for copy in weight_moves:
        copy.wait()

    def own_dot(left, tap):
        start = pl.multiple_of(tap * depth + y * width, width)
        return lax.dot_general(
            left, weight_ref[pl.ds(start, width), :], turned, preferred_element_type=jnp.float32
        )

    def oth_dot(left, tap):
        return lax.dot_general(
            left,
            weight_oth_ref[tap * width : (tap + 1) * width],
            turned,
            preferred_element_type=jnp.float32,
        )

    def conv_step(clip, _):
        span = PAIRS * SPAN * BLOCK
        total = conv_chunk([slopes_ref.at[1], oth_ref], [own_dot, oth_dot], clip * span, span, -1)
        dmix_ref[pl.ds(clip * (span // 8), span // 8)] = total
        return 0

    lax.fori_loop(0, clips, conv_step, 0)

    center, rate = norm_stats(*rows_of(stats_in_ref), count)
    pre_move.wait()
    scaled_ref[pl.ds(0, rows), :] = (pre_here_ref[...] - center) * rate
    scaled_ref[pl.ds(rows, scaled_ref.shape[0] - rows), :] = jnp.zeros(
        (scaled_ref.shape[0] - rows, width), jnp.float32
    )
    parts_ref[...] = jnp.zeros_like(parts_ref)
    at = lane_mask(128)

    def lanes_step(chunk, _):
        lanes = pl.ds(pl.multiple_of(chunk * 128, 128), 128)

        def row_of(index):
            return par_own_ref[index : index + 1, lanes].reshape(1, 1, 128)

        near = [row_of(5 + tap) for tap in range(9)]
        far = [row_of(14 + tap) for tap in range(9)]
        offset, gain, bias = row_of(4), row_of(0), row_of(1)

        def add_part(index, value):
            here = pl.ds(8 * index, 8)
            parts_ref[here, lanes] += jnp.sum(value, 0)

        def clip_step(clip, carry):
            view = clip_view(scaled_ref, clip, 56)
            target = clip_view(flat_ref, clip)
            for pair in range(PAIRS):
                carry = pair_step(clip, pair, carry, view, target)
            return carry

        def pair_step(clip, pair, carry, view, target):
            normed = [
                load_map(view, PIXELS * (2 * pair + seg), lanes) * gain + bias for seg in range(3)
            ]
            parts = [logistic(value) for value in normed]
            hidden = [value * part for value, part in zip(normed, parts, strict=True)]
            for seg in range(2):
                same = same_ref[clip, 2 * pair + seg].astype(jnp.float32)
                change = jnp.where(at < SIDE, same * (hidden[seg + 1] - hidden[seg]), 0.0)
                score, views = gate_score(change, near, far, offset, at)
                gate = logistic(score)
                start = 2 * (SPAN * (PAIRS * clip + pair) + 1) + seg
                d_mixed = jnp.stack([dmix_ref[start + 2 * row, :, lanes] for row in range(SIDE)])
                d_mixed = jnp.where(at < SIDE, d_mixed, 0.0)
                d_score = d_mixed * hidden[seg] * (gate * (1.0 - gate))
                add_part(0, d_score)
                backs = {step: across(d_score, step, at) for step in (-2, -1, 0, 1, 2)}
                d_change = None
                for index, (step, row, kernel) in enumerate(taps_of(near, far)):
                    here = down(d_score, -step * (row - 1))
                    for col in range(3):
                        add_part(1 + 3 * index + col, here * views[step * (col - 1)])
                    term = sum(kernel[col] * backs[-step * (col - 1)] for col in range(3))
                    term = down(term, -step * (row - 1))
                    d_change = term if d_change is None else d_change + term
                d_change = jnp.where(at < SIDE, same * d_change, 0.0)
                d_hidden = d_mixed * (1.0 + gate) - d_change + carry
                carry = d_change
                slope = parts[seg] * (1.0 + normed[seg] * (1.0 - parts[seg]))
                store_map(target, PIXELS * (2 * pair + seg), lanes, d_hidden * slope)
            return carry

        lax.fori_loop(0, clips, clip_step, jnp.zeros((SIDE, 8, 128), jnp.float32))
        return 0

    lax.fori_loop(0, width // 128, lanes_step, 0)
    result = flat_ref[pl.ds(0, rows), :]
    d_in_ref[...] = result
    d_in16_ref[...] = result.astype(jnp.bfloat16)
    put_sums(
        sums_ref,
        jnp.sum(result, 0, keepdims=True),
        jnp.sum(result * scaled_ref[pl.ds(0, rows), :], 0, keepdims=True),
    )
    sums_ref[8:32, :] = jnp.sum(parts_ref[...].reshape(24, 8, width), 1)


def mid_back(
    count, place, same, d_own, d_oth, mid_own, mid_oth, stats, back, pre, stats_in, pars, weights, aways,
):
    rows, width = d_own.shape
    spread = map_rows(rows)
    depth = weights[0].shape[0]
    return kernel_call(
        functools.partial(mid_back_body, count),
        (
            jax.ShapeDtypeStruct((3, spread, width), jnp.bfloat16),
            jax.ShapeDtypeStruct((rows, width), jnp.float32),
            jax.ShapeDtypeStruct((rows, width), jnp.bfloat16),
            jax.ShapeDtypeStruct((32, width), jnp.float32),
        ),
        [scalars, scalars, whole, remote, whole, remote, whole, whole, whole, remote, remote]
        + [whole] * 3
        + [remote] * 4,
        (
            pltpu.VMEM((rows + 56, width), jnp.float32),
            pltpu.VMEM((spread, width), jnp.bfloat16),
            pltpu.VMEM((spread // 8, 8, width), jnp.float32),
            pltpu.VMEM((rows + 56, width), jnp.float32),
            pltpu.VMEM((24 * 8, width), jnp.float32),
            pltpu.VMEM((depth, width), jnp.bfloat16),
            pltpu.VMEM((depth // 2, width), jnp.bfloat16),
            pltpu.VMEM((rows, width), jnp.bfloat16),
            pltpu.VMEM((rows, width), jnp.bfloat16),
            pltpu.VMEM((8, width), jnp.float32),
            pltpu.VMEM((rows, width), jnp.float32),
            pltpu.SemaphoreType.DMA((8,)),
        ),
        flops=2 * rows * depth * width,
        moved=depth * width * 3 + rows * width * 20,
        held=(0, 1),
    )(
        place, same, d_own, d_oth, mid_own, mid_oth, *stats, *back, pre, stats_in, *pars, *weights, *aways,
    )


def turn_body(mixed_ref, out_ref, mixed_here_ref, sems):
    move(mixed_ref, mixed_here_ref, sems, 0).wait()
    out_ref[...] = mixed_here_ref[pl.ds(BLOCK, out_ref.shape[1]), :].T


def turn(mixed):
    spread, depth = mixed.shape
    return kernel_call(
        turn_body,
        jax.ShapeDtypeStruct((depth, spread - 2 * BLOCK), jnp.bfloat16),
        [remote],
        (pltpu.VMEM(mixed.shape, jnp.bfloat16), pltpu.SemaphoreType.DMA((1,))),
        held=(0,),
    )(mixed)


def mid_weight_body(place_ref, turned_ref, slopes_ref, keep_ref, send_ref):
    depth, rows = turned_ref.shape
    half = keep_ref.shape[1]
    first = place_ref[0] % 2 == 0
    for tap in range(9):
        row, col = tap // 3, tap % 3
        right = slopes_ref[col, pl.ds(BLOCK * (2 - row), rows), :]
        value = jnp.dot(turned_ref[...], right, preferred_element_type=jnp.float32)
        low, high = value[:, :half], value[:, half:]
        here = pl.ds(tap * depth, depth)
        keep_ref[here, :] = jnp.where(first, low, high)
        send_ref[here, :] = jnp.where(first, high, low).astype(jnp.bfloat16)


def mid_weight(place, turned, slopes):
    depth, rows = turned.shape
    width = slopes.shape[2]
    return kernel_call(
        mid_weight_body,
        (
            jax.ShapeDtypeStruct((9 * depth, width // 2), jnp.float32),
            jax.ShapeDtypeStruct((9 * depth, width // 2), jnp.bfloat16),
        ),
        [scalars, whole, whole],
        flops=2 * rows * 9 * depth * width,
        moved=rows * (2 * depth + 6 * width) + 9 * depth * width * 3,
        held=(0,),
    )(place, turned, slopes)


def first_conv_body(
    order,
    place_ref,
    block_ref,
    peer_ref,
    across_ref,
    corner_ref,
    own_ref,
    other_ref,
    extra_ref,
    pre_out_ref,
    pre16_ref,
    sums_ref,
    weight_out_ref,
    pre_ref,
    weight_ref,
    sems,
):
    rows = peer_ref.shape[0]
    quarter = block_ref.shape[1]
    chan, group = place_ref[0], place_ref[1]
    core = chan % 2
    size = own_ref.shape[0] // len(order)
    for at, bits in enumerate(order):
        here = row_part(group ^ bits, size)
        weight_ref[here, lane_part(core)] = own_ref[at * size : (at + 1) * size]
        weight_ref[here, lane_part(1 - core)] = other_ref[at * size : (at + 1) * size]
    weight_move = move(weight_ref, weight_out_ref, sems, 0)
    mine = block_ref[row_part(core, rows), :]
    total = None
    for at, piece in enumerate((mine, peer_ref[...], across_ref[...], corner_ref[...])):
        weight = weight_ref[row_part(chan ^ at, quarter), :]
        term = jnp.dot(piece, weight, preferred_element_type=jnp.float32)
        total = term if total is None else total + term
    pre_ref[...] = total
    pre_move = move(pre_ref, pre_out_ref, sems, 1)
    pre16_ref[...] = total.astype(jnp.bfloat16)
    sums_ref[...] = extra_ref[...]
    sums_ref[0:1, :] = jnp.sum(total, 0, keepdims=True)
    sums_ref[1:2, :] = jnp.sum(total * total, 0, keepdims=True)
    weight_move.wait()
    pre_move.wait()


def first_conv(order, place, block, pieces, weights, extra):
    rows, quarter = pieces[0].shape
    width = 2 * weights[0].shape[1]
    return kernel_call(
        functools.partial(first_conv_body, order),
        (
            jax.ShapeDtypeStruct((rows, width), jnp.float32),
            jax.ShapeDtypeStruct((rows, width), jnp.bfloat16),
            jax.ShapeDtypeStruct((8, width), jnp.float32),
            jax.ShapeDtypeStruct((4 * quarter, width), jnp.bfloat16),
        ),
        [scalars] + [whole] * 7,
        (
            pltpu.VMEM((rows, width), jnp.float32),
            pltpu.VMEM((4 * quarter, width), jnp.bfloat16),
            pltpu.SemaphoreType.DMA((2,)),
        ),
        flops=8 * rows * quarter * width,
        moved=rows * quarter * 8,
        away=(0, 3),
    )(place, block, *pieces, *weights, extra)


def second_body(
    count, place_ref, own_ref, oth_ref, stats_own_ref, stats_oth_ref, par_own_ref, par_oth_ref, out_ref,
    oth_here_ref, stats_here_ref, sems,
):
    width = own_ref.shape[1]
    y = place_ref[0] // 2
    arrivals = [
        move(stats_oth_ref, stats_here_ref, sems, 0),
        move(oth_ref, oth_here_ref, sems, 1),
    ]
    for side, pre, stats, par in (
        (y, own_ref, stats_own_ref, par_own_ref),
        (1 - y, oth_here_ref, stats_here_ref, par_oth_ref),
    ):
        center, rate = norm_stats(*rows_of(stats), count)
        normed = (pre[...].astype(jnp.float32) - center) * rate * par[2:3] + par[3:4]
        out_ref[:, lane_part(side, width)] = (normed * logistic(normed)).astype(jnp.bfloat16)
        for copy in arrivals:
            copy.wait()
        arrivals = []


def second_half(count, place, own, oth, stats, pars):
    rows, width = own.shape
    return kernel_call(
        functools.partial(second_body, count),
        jax.ShapeDtypeStruct((rows, 2 * width), jnp.bfloat16),
        [scalars, whole, remote, whole, remote, whole, whole],
        (
            pltpu.VMEM((rows, width), jnp.bfloat16),
            pltpu.VMEM((8, width), jnp.float32),
            pltpu.SemaphoreType.DMA((2,)),
        ),
        moved=rows * width * 10,
    )(place, own, oth, *stats, *pars)


def last_conv_body(place_ref, mine_ref, peer_ref, weight_ref, extra_ref, out_ref, sums_ref):
    rows = mine_ref.shape[0]
    core = place_ref[0] % 2
    sums = squares = 0.0
    for side, part in ((core, mine_ref), (1 - core, peer_ref)):
        value = jnp.dot(part[...], weight_ref[...], preferred_element_type=jnp.float32)
        out_ref[row_part(side, rows), :] = value
        sums += jnp.sum(value, 0, keepdims=True)
        squares += jnp.sum(value * value, 0, keepdims=True)
    sums_ref[...] = extra_ref[...]
    sums_ref[0:1, :] = sums
    sums_ref[1:2, :] = squares


def last_conv(place, mine, peer, weight, extra):
    rows, depth = mine.shape
    width = weight.shape[1]
    return kernel_call(
        last_conv_body,
        (
            jax.ShapeDtypeStruct((2 * rows, width), jnp.float32),
            jax.ShapeDtypeStruct((8, width), jnp.float32),
        ),
        [scalars] + [whole] * 4,
        flops=4 * rows * depth * width,
        moved=rows * width * 12,
    )(place, mine, peer, weight, extra)


def out_back_body(
    count,
    place_ref,
    pre_ref,
    block_ref,
    grad_ref,
    stats_ref,
    gain_ref,
    bias_ref,
    weight_ref,
    out_ref,
    total_out_ref,
    sums_ref,
    keep_ref,
    send_ref,
    total_ref,
    sems,
):
    rows = keep_ref.shape[0]
    core = place_ref[0] % 2
    center, rate = norm_stats(*rows_of(stats_ref), count)
    gain, bias = gain_ref[...], bias_ref[...]
    step = rows // 7

    def add_step(at, sums):
        here = row_part(at, step)
        scaled = (pre_ref[here, :] - center) * rate
        total = scaled * gain + bias + block_ref[here, :].astype(jnp.float32)
        part = logistic(total)
        out_ref[here, :] = (total * part).astype(jnp.bfloat16)
        value = grad_ref[here, :].astype(jnp.float32) * (part * (1.0 + total * (1.0 - part)))
        total_ref[here, :] = value
        return (
            sums[0] + jnp.sum(value, 0, keepdims=True),
            sums[1] + jnp.sum(value * scaled, 0, keepdims=True),
        )

    zero = jnp.zeros((1, pre_ref.shape[1]), jnp.float32)
    sums, products = lax.fori_loop(0, 14, add_step, (zero, zero))
    put_sums(sums_ref, sums, products)
    total_move = move(total_ref, total_out_ref, sems, 0)
    local = 1.0 / (2 * rows)

    def slope_rows(side):
        here = row_part(side, rows)
        scaled = (pre_ref[here, :] - center) * rate
        value = gain * rate * (total_ref[here, :] - sums * local - scaled * (products * local))
        return lax.dot_general(
            value.astype(jnp.bfloat16),
            weight_ref[...],
            (((1,), (1,)), ((), ())),
            preferred_element_type=jnp.float32,
        )

    send_ref[...] = slope_rows(1 - core).astype(jnp.bfloat16)
    keep_ref[...] = slope_rows(core)
    total_move.wait()


def out_back(count, place, pre, block, grad, stats, gain, bias, weight):
    rows, width = pre.shape
    depth = weight.shape[0]
    return kernel_call(
        functools.partial(out_back_body, count),
        (
            jax.ShapeDtypeStruct((rows, width), jnp.bfloat16),
            jax.ShapeDtypeStruct((rows, width), jnp.float32),
            jax.ShapeDtypeStruct((8, width), jnp.float32),
            jax.ShapeDtypeStruct((rows // 2, depth), jnp.float32),
            jax.ShapeDtypeStruct((rows // 2, depth), jnp.bfloat16),
        ),
        [scalars] + [whole] * 7,
        (pltpu.VMEM((rows, width), jnp.float32), pltpu.SemaphoreType.DMA((1,))),
        flops=2 * rows * width * depth,
        moved=rows * width * 20,
        away=(1,),
    )(place, pre, block, grad, stats, gain, bias, weight)


def cross_body(place_ref, keep_ref, got_ref, own_ref, send_ref):
    width = own_ref.shape[1]
    y = place_ref[0] // 2
    for lanes, ref in ((1 - y, send_ref), (y, own_ref)):
        here = lane_part(lanes, width)
        value = keep_ref[:, here] + got_ref[:, here].astype(jnp.float32)
        ref[...] = value.astype(ref.dtype)


def cross_half(place, keep, got):
    rows, width = keep.shape[0], keep.shape[1] // 2
    return kernel_call(
        cross_body,
        (
            jax.ShapeDtypeStruct((rows, width), jnp.float32),
            jax.ShapeDtypeStruct((rows, width), jnp.bfloat16),
        ),
        [scalars, whole, whole],
        moved=rows * width * 18,
    )(place, keep, got)


def out_delta_body(count, local, stats_ref, sums_ref, back_ref, gain_ref, out_ref):
    center, rate = norm_stats(*rows_of(stats_ref), count)
    scale = gain_ref[...] * rate
    first = scale * (back_ref[0:1] / count - sums_ref[0:1] * local)
    second = scale * rate * (back_ref[1:2] / count - sums_ref[1:2] * local)
    put_sums(out_ref, first - second * center, second)


def out_delta(count, rows, stats, sums, back, gain):
    return kernel_call(
        functools.partial(out_delta_body, count, 1.0 / rows),
        jax.ShapeDtypeStruct(stats.shape, jnp.float32),
        [whole] * 4,
    )(stats, sums, back, gain)


def mid_slope_body(
    count,
    place_ref,
    keep_ref,
    got_ref,
    second_ref,
    mid_ref,
    stats_ref,
    par_ref,
    deltas0_ref,
    deltas1_ref,
    deltas2_ref,
    deltas3_ref,
    weights0_ref,
    weights1_ref,
    weights2_ref,
    weights3_ref,
    out_ref,
    out16_ref,
    sums_ref,
):
    width = mid_ref.shape[1]
    y = place_ref[0] // 2
    turned = (((1,), (1,)), ((), ()))
    factor, offset = None, None
    for deltas, weights in (
        (deltas0_ref, weights0_ref),
        (deltas1_ref, weights1_ref),
        (deltas2_ref, weights2_ref),
        (deltas3_ref, weights3_ref),
    ):
        own = weights[row_part(y, width), :]
        left = (weights[...].astype(jnp.float32) * deltas[1:2]).astype(jnp.bfloat16)
        term = lax.dot_general(left, own, turned, preferred_element_type=jnp.float32)
        factor = term if factor is None else factor + term
        term = lax.dot_general(
            deltas[...], own.astype(jnp.float32), turned, preferred_element_type=jnp.float32
        )[0:1]
        offset = term if offset is None else offset + term
    delta = jnp.dot(
        second_ref[...], factor.astype(jnp.bfloat16), preferred_element_type=jnp.float32
    )
    grad = keep_ref[...] + got_ref[...].astype(jnp.float32) - delta - offset
    center, rate = norm_stats(*rows_of(stats_ref), count)
    scaled = (mid_ref[...] - center) * rate
    normed = scaled * par_ref[2:3] + par_ref[3:4]
    result = grad * silu_slope(normed)
    out_ref[...] = result
    out16_ref[...] = result.astype(jnp.bfloat16)
    put_sums(
        sums_ref, jnp.sum(result, 0, keepdims=True), jnp.sum(result * scaled, 0, keepdims=True)
    )


def mid_slope(count, place, keep, got, second, mid, stats, par, deltas, weights):
    rows, width = mid.shape
    return kernel_call(
        functools.partial(mid_slope_body, count),
        (
            jax.ShapeDtypeStruct((rows, width), jnp.float32),
            jax.ShapeDtypeStruct((rows, width), jnp.bfloat16),
            jax.ShapeDtypeStruct((8, width), jnp.float32),
        ),
        [scalars] + [whole] * 14,
        flops=2 * rows * width * 2 * width,
        moved=rows * width * 20,
        held=(0,),
    )(place, keep, got, second, mid, stats, par, *deltas, *weights)


def out_weight_body(
    count, part, place_ref, rows_ref, pre_ref, total_ref, stats_ref, back_ref, gain_ref, *refs
):
    rows = rows_ref.shape[0]
    core = place_ref[0] % 2
    center, rate = norm_stats(*rows_of(stats_ref), count)
    here = row_part(1 - core if part else core, rows)
    scaled = (pre_ref[here, :] - center) * rate
    value = (gain_ref[...] * rate) * (
        total_ref[here, :] - back_ref[0:1] / count - scaled * (back_ref[1:2] / count)
    )
    result = exact(rows_ref[...], value.astype(jnp.bfloat16), ((0,), (0,)))
    refs[-1][...] = refs[0][...] + result if part else result


def out_weight(count, place, second, pre, total, stats, back, gain, start=None):
    rows, depth = second.shape
    width = pre.shape[1]
    part = 0 if start is None else 1
    return kernel_call(
        functools.partial(out_weight_body, count, part),
        jax.ShapeDtypeStruct((depth, width), jnp.float32),
        [scalars] + [whole] * (6 + part),
        flops=2 * rows * depth * width,
        moved=rows * width * 10,
    )(place, second, pre, total, stats, back, gain, *([start] if part else []))


def in_back_body(
    count,
    place_ref,
    d_own_ref,
    d_oth_ref,
    pre_own_ref,
    pre_oth_ref,
    stats_own_ref,
    stats_oth_ref,
    back_own_ref,
    back_oth_ref,
    par_own_ref,
    par_oth_ref,
    block_ref,
    peer_ref,
    across_ref,
    corner_ref,
    out_ref,
    keep_ref,
    send_ref,
    d_here_ref,
    pre_here_ref,
    back_here_ref,
    sems,
):
    rows, width = d_own_ref.shape
    arrivals = [
        move(back_oth_ref, back_here_ref, sems, 0),
        move(d_oth_ref, d_here_ref, sems, 1),
        move(pre_oth_ref, pre_here_ref, sems, 2),
    ]
    half = width // 2
    quarter = block_ref.shape[1]
    chan = place_ref[0]
    core, y = chan % 2, chan // 2
    own = None
    for side, grad, pre, stats, back, par in (
        (y, d_own_ref, pre_own_ref, stats_own_ref, back_own_ref, par_own_ref),
        (1 - y, d_here_ref, pre_here_ref, stats_oth_ref, back_here_ref, par_oth_ref),
    ):
        center, rate = norm_stats(*rows_of(stats), count)
        scaled = (pre[...].astype(jnp.float32) - center) * rate
        value = (par[0:1] * rate) * (
            grad[...].astype(jnp.float32) - back[0:1] / count - scaled * (back[1:2] / count)
        )
        value = value.astype(jnp.bfloat16)
        out_ref[:, lane_part(side, width)] = value
        own = value if own is None else own
        for copy in arrivals:
            copy.wait()
        arrivals = []
    mine = block_ref[row_part(core, rows), :]
    for at, piece in enumerate((mine, peer_ref[...], across_ref[...], corner_ref[...])):
        value = lax.dot_general(
            piece, own, (((0,), (0,)), ((), ())), preferred_element_type=jnp.float32
        )
        here = row_part(chan ^ at, quarter)
        low, high = value[:, :half], value[:, half:]
        keep_ref[here, :] = jnp.where(core == 0, low, high)
        send_ref[here, :] = jnp.where(core == 0, high, low).astype(jnp.bfloat16)


def in_back(count, place, d_own, d_oth, pre_own, pre_oth, stats, back, pars, block, pieces):
    rows, width = d_own.shape
    full = 4 * block.shape[1]
    return kernel_call(
        functools.partial(in_back_body, count),
        (
            jax.ShapeDtypeStruct((rows, 2 * width), jnp.bfloat16),
            jax.ShapeDtypeStruct((full, width // 2), jnp.float32),
            jax.ShapeDtypeStruct((full, width // 2), jnp.bfloat16),
        ),
        [scalars, whole, remote, whole, remote, whole, whole, whole, remote] + [whole] * 6,
        (
            pltpu.VMEM((rows, width), jnp.bfloat16),
            pltpu.VMEM((rows, width), jnp.bfloat16),
            pltpu.VMEM(back[1].shape, jnp.float32),
            pltpu.SemaphoreType.DMA((3,)),
        ),
        flops=2 * rows * width * full,
        moved=rows * full * 2,
        held=(1,),
    )(place, d_own, d_oth, pre_own, pre_oth, *stats, *back, *pars, block, *pieces)


def input_grad_body(place_ref, mine_ref, peer_ref, near_ref, far_ref, total_ref, out_ref):
    rows = mine_ref.shape[0]
    width = near_ref.shape[1]
    core, y = place_ref[0] % 2, place_ref[0] // 2
    turned = (((1,), (1,)), ((), ()))
    for side, part in ((core, mine_ref), (1 - core, peer_ref)):
        here = row_part(side, rows)
        value = total_ref[here, :]
        for lanes, weight in ((y, near_ref), (1 - y, far_ref)):
            value += lax.dot_general(
                part[:, lane_part(lanes, width)],
                weight[...],
                turned,
                preferred_element_type=jnp.float32,
            )
        out_ref[here, :] = value.astype(jnp.bfloat16)


def input_grad(place, mine, peer, near, far, total):
    rows, quarter = total.shape
    return kernel_call(
        input_grad_body,
        jax.ShapeDtypeStruct((rows, quarter), jnp.bfloat16),
        [scalars] + [whole] * 5,
        flops=2 * rows * quarter * 2 * near.shape[1],
        moved=rows * quarter * 8,
    )(place, mine, peer, near, far, total)


def pack_body(gain_in, bias_in, gain_mid, bias_mid, gate_bias, near, far, out_ref):
    for at, ref in enumerate((gain_in, bias_in, gain_mid, bias_mid, gate_bias)):
        out_ref[at : at + 1, :] = ref[...]
    out_ref[5:14, :] = near[...]
    out_ref[14:23, :] = far[...]
    out_ref[23:24, :] = jnp.zeros_like(out_ref[23:24, :])


def pack_params(rows, near, far):
    width = near.shape[1]
    return kernel_call(
        pack_body, jax.ShapeDtypeStruct((24, width), jnp.float32), [whole] * 7
    )(*[row.reshape(1, width) for row in rows], near, far)


TAPS = 7
LANES = 16


def exact(left, right, contract):
    return lax.dot_general(
        left, right, (contract, ((), ())), preferred_element_type=jnp.float32
    )


def spot(core, outs, width, part):
    lane = lax.broadcasted_iota(jnp.int32, (outs, width), 1)
    channel = lax.broadcasted_iota(jnp.int32, (outs, width), 0)
    return (lane == core * 2 * outs + part * outs + channel).astype(jnp.float32)


def stem_row(core, width, first, second):
    row = None
    for part, value in enumerate((first, second)):
        column = jnp.sum(jnp.sum(value, 0), 1, keepdims=True)
        term = jnp.sum(column * spot(core, value.shape[1], width, part), 0, keepdims=True)
        row = term if row is None else row + term
    at = lax.broadcasted_iota(jnp.int32, (8, width), 0)
    return jnp.where(at == 2, row, 0.0)


def stem_columns(core, outs, stats_ref):
    row = stats_ref[2:3, :]
    return [
        jnp.sum(row * spot(core, outs, row.shape[1], part), 1, keepdims=True) for part in range(2)
    ]


def upright(row_ref):
    size = row_ref.shape[1]
    at = lax.broadcasted_iota(jnp.int32, (size, size), 0)
    same = at == lax.broadcasted_iota(jnp.int32, (size, size), 1)
    return jnp.sum(jnp.where(same, row_ref[...], 0.0), 1, keepdims=True)


def stem_front_body(
    place_ref, video_ref, weight_ref, pre_out_ref, rows_out_ref, pick_out_ref, extra_ref, flat_ref, parts_ref,
    pre_ref, rows_ref, pick_ref, sems,
):
    segs, colours, size = video_ref.shape
    side = 32
    half = size // 2
    quarter = half // 2
    core = place_ref[0] % 2
    at = lax.broadcasted_iota(jnp.int32, (LANES, size), 0)
    zero = jnp.zeros((LANES - colours, size), jnp.float32)

    def plane_step(seg, _):
        value = jnp.concatenate([video_ref[seg].astype(jnp.float32), zero])
        moving = pltpu.roll(value, LANES - 3, 0) - value
        center = pltpu.roll(value, 6, 0)
        plane = jnp.where(at < 12, moving, jnp.where(at < 15, center, 0.0))
        flat_ref[pl.ds(pl.multiple_of(seg * LANES, LANES), LANES), :] = plane.astype(jnp.bfloat16)
        return 0

    lax.fori_loop(0, segs, plane_step, 0, unroll=4)
    source = lax.broadcasted_iota(jnp.int32, (size, half), 0)
    lane = lax.broadcasted_iota(jnp.int32, (size, half), 1)
    lanes = lax.broadcasted_iota(jnp.int32, (segs * LANES, half), 1)
    for parity in range(2):
        hit = source == 2 * side * (lane // side) + side * parity + lane % side
        rows = jnp.dot(
            flat_ref[...],
            jnp.where(hit, 1.0, 0.0).astype(jnp.bfloat16),
            preferred_element_type=jnp.float32,
        )
        for tap in range(TAPS):
            if (tap - 3) % 2 != parity:
                continue
            shift = (tap - 3 - parity) // 2 * side
            value = rows
            if shift:
                value = pltpu.roll(rows, (-shift) % half, 1)
                inside = lanes < half - shift if shift > 0 else lanes >= -shift
                value = jnp.where(inside, value, 0.0)
            value = value.astype(jnp.bfloat16).reshape(segs, LANES, half)
            rows_ref[:, tap * LANES : (tap + 1) * LANES, :] = value
    weight = weight_ref[...]
    moves = [move(rows_ref, rows_out_ref, sems, 0)]

    def seg_step(seg, _):
        value = jnp.dot(weight, rows_ref[seg], preferred_element_type=jnp.float32)
        value = value.astype(jnp.bfloat16)
        here = pl.ds(pl.multiple_of(seg * LANES, LANES), LANES)
        for tap in range(TAPS):
            parts_ref[tap, here, :] = value[tap * LANES : (tap + 1) * LANES]
        return 0

    lax.fori_loop(0, segs, seg_step, 0, unroll=4)
    source = lax.broadcasted_iota(jnp.int32, (half, quarter), 0)
    lane = lax.broadcasted_iota(jnp.int32, (half, quarter), 1)
    total = None
    for tap in range(TAPS):
        column = 2 * (lane % LANES) + tap - 3
        hit = (source == side * (lane // LANES) + column) & (column >= 0) & (column < side)
        pick = jnp.where(hit, 1.0, 0.0).astype(jnp.bfloat16)
        pick_ref[tap] = pick
        term = jnp.dot(parts_ref[tap], pick, preferred_element_type=jnp.float32)
        total = term if total is None else total + term
    total = total.reshape(segs, LANES, quarter)
    pre_ref[...] = total
    moves += [move(pick_ref, pick_out_ref, sems, 1), move(pre_ref, pre_out_ref, sems, 2)]
    extra_ref[...] = stem_row(core, extra_ref.shape[1], total, total * total)
    for copy in moves:
        copy.wait()


def stem_front(place, video, weight, width):
    segs, _, size = video.shape
    return kernel_call(
        stem_front_body,
        (
            jax.ShapeDtypeStruct((segs, LANES, size // 4), jnp.float32),
            jax.ShapeDtypeStruct((segs, TAPS * LANES, size // 2), jnp.bfloat16),
            jax.ShapeDtypeStruct((TAPS, size // 2, size // 4), jnp.bfloat16),
            jax.ShapeDtypeStruct((8, width), jnp.float32),
        ),
        [scalars, whole, whole],
        (
            pltpu.VMEM((segs * LANES, size), jnp.bfloat16),
            pltpu.VMEM((TAPS, segs * LANES, size // 2), jnp.bfloat16),
            pltpu.VMEM((segs, LANES, size // 4), jnp.float32),
            pltpu.VMEM((segs, TAPS * LANES, size // 2), jnp.bfloat16),
            pltpu.VMEM((TAPS, size // 2, size // 4), jnp.bfloat16),
            pltpu.SemaphoreType.DMA((3,)),
        ),
        away=(0, 1, 2),
        flops=4 * segs * TAPS * LANES * TAPS * LANES * size,
        moved=segs * size * 40,
    )(place, video, weight)


def stem_norm(count, core, pre, stats_ref, gain_ref, bias_ref):
    outs = pre.shape[1]
    center, rate = norm_stats(*stem_columns(core, outs, stats_ref), count)
    scaled = (pre - center) * rate
    return scaled, scaled * upright(gain_ref) + upright(bias_ref), upright(gain_ref) * rate


def stem_out_body(count, place_ref, pre_ref, grad_ref, stats_ref, gain_ref, bias_ref, out_ref, extra_ref):
    core = place_ref[0] % 2
    scaled, normed, _ = stem_norm(count, core, pre_ref[...], stats_ref, gain_ref, bias_ref)
    part = logistic(normed)
    out_ref[...] = (normed * part).astype(jnp.bfloat16)
    value = grad_ref[...].astype(jnp.float32) * (part * (1.0 + normed * (1.0 - part)))
    extra_ref[...] = stem_row(core, extra_ref.shape[1], value, value * scaled)


def stem_output(count, place, pre, grad, stats, gain, bias, width):
    return kernel_call(
        functools.partial(stem_out_body, count),
        (
            jax.ShapeDtypeStruct(pre.shape, jnp.bfloat16),
            jax.ShapeDtypeStruct((8, width), jnp.float32),
        ),
        [scalars] + [whole] * 5,
    )(place, pre, grad, stats, gain.reshape(1, -1), bias.reshape(1, -1))


def stem_back_body(
    count, first, place_ref, pre_ref, grad_ref, stats_ref, back_ref, gain_ref, bias_ref, rows_ref, pick_ref, start_ref, out_ref, slopes_ref,
):
    core = place_ref[0] % 2
    segs, outs, pixels = pre_ref.shape
    scaled, normed, scale = stem_norm(count, core, pre_ref[...], stats_ref, gain_ref, bias_ref)
    bias_grad, gain_grad = stem_columns(core, outs, back_ref)
    value = grad_ref[...].astype(jnp.float32) * silu_slope(normed)
    value = scale * (value - bias_grad / count - scaled * (gain_grad / count))
    value = value.astype(jnp.bfloat16).reshape(segs * outs, pixels)
    half = rows_ref.shape[2]
    for tap in range(TAPS):
        spread = exact(value, pick_ref[tap], ((1,), (1,)))
        slopes_ref[:, tap * LANES : (tap + 1) * LANES, :] = spread.astype(jnp.bfloat16).reshape(
            segs, outs, half
        )
    total = None
    for seg in range(segs):
        term = exact(rows_ref[seg], slopes_ref[seg], ((1,), (1,)))
        total = term if total is None else total + term
    size = TAPS * LANES
    rows = size // 2
    if first:
        out_ref[...] = jnp.zeros_like(out_ref)
    else:
        out_ref[...] = start_ref[...]
    out_ref[:, :size] += total[:rows]
    out_ref[:, 128 : 128 + size] += total[rows:]


def stem_back(count, place, pre, grad, stats, back, gain, bias, rows, pick, start, chunk, chunks):
    segs, outs, pixels = pre.shape
    size = segs // chunks

    def part(*tail):
        return pl.BlockSpec((size,) + tail, lambda at: (chunk, 0, 0))

    def all_of(shape):
        return pl.BlockSpec(shape, lambda at: (0,) * len(shape))

    small = (TAPS * LANES // 2, 256)
    first = start is None
    start = jnp.zeros((8, 256), jnp.float32) if first else start
    return pl.pallas_call(
        functools.partial(stem_back_body, count, first),
        grid=(1,),
        out_shape=jax.ShapeDtypeStruct(small, jnp.float32),
        in_specs=[scalars, part(outs, pixels), part(outs, pixels)]
        + [all_of(stats.shape), all_of(back.shape), all_of((1, outs)), all_of((1, outs))]
        + [part(*rows.shape[1:]), all_of(pick.shape), all_of(start.shape)],
        out_specs=all_of(small),
        scratch_shapes=[pltpu.VMEM((size, TAPS * LANES, rows.shape[2]), jnp.bfloat16)],
        compiler_params=pltpu.CompilerParams(vmem_limit_bytes=vmem_limit),
        cost_estimate=pl.CostEstimate(
            flops=4 * size * (TAPS * LANES) ** 2 * rows.shape[2], bytes_accessed=1 << 20, transcendentals=0
        ),
    )(place, pre, grad, stats, back, gain.reshape(1, -1), bias.reshape(1, -1), rows, pick, start)


def stem_weight(center, diff):
    outs = center.shape[1]
    value = jnp.concatenate([diff, center, jnp.zeros((TAPS * TAPS, outs), center.dtype)])
    value = value.reshape(LANES, TAPS, TAPS, outs)
    return value.transpose(2, 3, 1, 0).reshape(TAPS * outs, TAPS * LANES)


def stem_grads_body(packed_ref, center_ref, diff_ref):
    full = jnp.concatenate([packed_ref[:, :128], packed_ref[:, 128:]])
    for row in range(TAPS):
        value = full[row * LANES : (row + 1) * LANES]
        for col in range(TAPS):
            here = value[:, col * LANES : (col + 1) * LANES]
            at = row * TAPS + col
            diff_ref[pl.ds(at, 12, stride=TAPS * TAPS), :] = here[:12]
            center_ref[pl.ds(at, 3, stride=TAPS * TAPS), :] = here[12:15]


def stem_grads(packed, outs):
    return kernel_call(
        stem_grads_body,
        (
            jax.ShapeDtypeStruct((3 * TAPS * TAPS, outs), jnp.float32),
            jax.ShapeDtypeStruct((12 * TAPS * TAPS, outs), jnp.float32),
        ),
        [whole],
    )(packed)


def after(value, *marks):
    return lax.optimization_barrier((value, marks))[0]


def swap(value, axis, bit):
    size = lax.axis_size(axis)
    return lax.ppermute(value, axis, [(at, at ^ bit) for at in range(size)])


def steps_of(axis):
    size = lax.axis_size(axis)
    assert size & (size - 1) == 0
    return [1 << at for at in range(size.bit_length() - 1)]


def sum_over(value, axis, jobs=()):
    jobs = list(jobs)
    for bit in steps_of(axis):
        got = swap(value, axis, bit)
        if jobs:
            got = after(got, jobs.pop(0)(value))
        value = value + got
    for job in jobs:
        value = after(value, job(value))
    return value


def ordered(second, own, other, axis=0):
    return jnp.where(
        second, jnp.concatenate([other, own], axis), jnp.concatenate([own, other], axis)
    )


def gather_rows(value, axis):
    order = [0]
    for bit in reversed(steps_of(axis)):
        value = jnp.concatenate([value, swap(value, axis, bit)])
        order += [at ^ bit for at in order]
    return value, order


def halve_body(bit, place_ref, keep_ref, got_ref, mine_ref, send_ref):
    size = send_ref.shape[1]
    high = (place_ref[1] // bit) % 2
    for block in range(send_ref.shape[0]):
        for ref, side in ((mine_ref, high), (send_ref, 1 - high)):
            here = pl.ds(pl.multiple_of((2 * block + side) * size, size), size)
            value = keep_ref[here, :]
            if got_ref is not None:
                value = value + got_ref[here, :].astype(jnp.float32)
            ref[block] = value.astype(ref.dtype)


def halve(place, keep, got, axis, bits, at):
    rows, width = keep.shape
    left = sorted(bits, reverse=True)
    outer = 1 << left.index(at)
    inner = rows // (2 * outer)
    if inner % BLOCK:
        total = keep if got is None else keep + got.astype(jnp.float32)
        blocks = total.reshape(outer, 2, inner, width)
        low, high = blocks[:, 0].reshape(-1, width), blocks[:, 1].reshape(-1, width)
        mine = (place[1] // at) % 2 == 0
        return jnp.where(mine, low, high), jnp.where(mine, high, low).astype(jnp.bfloat16)
    shape = (outer, inner, width)
    if got is None:

        def body(place_ref, keep_ref, mine_ref, send_ref):
            halve_body(at, place_ref, keep_ref, None, mine_ref, send_ref)
    else:
        body = functools.partial(halve_body, at)
    mine, send = kernel_call(
        body,
        (jax.ShapeDtypeStruct(shape, jnp.float32), jax.ShapeDtypeStruct(shape, jnp.bfloat16)),
        [scalars] + [whole] * (1 if got is None else 2),
        moved=rows * width * 9,
        held=(0,),
    )(place, keep, *([] if got is None else [got]))
    return mine.reshape(-1, width), send.reshape(-1, width)


def reduce_rows(place, keep, got, axis, bits, jobs=()):
    jobs, left = list(jobs), list(bits)
    while left:
        bit = left[0]
        keep, send = halve(place, keep, got, axis, left, bit)
        left.pop(0)
        got = swap(send, axis, bit)
        if jobs:
            got = after(got, jobs.pop(0)(send))
    for job in jobs:
        got = after(got, job(got))
    return keep + got.astype(jnp.float32)


def transposed(left, right):
    return lax.dot_general(
        left, right, (((1,), (1,)), ((), ())), preferred_element_type=jnp.float32
    )


def weight_grad(left, right):
    return lax.dot_general(
        left, right, (((0,), (0,)), ((), ())), preferred_element_type=jnp.float32
    )


def per_device(
    block_in,
    weight_in,
    weight_mid,
    weight_out,
    gain_in,
    bias_in,
    gain_mid,
    bias_mid,
    gain_out,
    bias_out,
    kernel_near,
    kernel_far,
    gate_bias,
    same_video,
    video,
    stem_center,
    stem_diff,
    stem_gain,
    stem_bias,
    block_grad,
    stem_grad,
):
    groups = lax.axis_size("dp")
    assert lax.axis_size("chan") == 4
    clips = same_video.shape[0]
    rows, quarter = block_in.shape
    half = rows // 2
    narrow = weight_in.shape[1]
    width = 2 * narrow
    count = float(rows * groups)
    segs = video.shape[0]
    stem_count = float(segs * stem_grad.shape[2] * groups)
    chan = lax.axis_index("chan")
    core, y = chan % 2, chan // 2
    place = jnp.stack([chan, lax.axis_index("dp")])

    def my_rows(value, which):
        return lax.dynamic_slice_in_dim(value, which * half, half, 0)

    mine, others = my_rows(block_in, core), my_rows(block_in, 1 - core)
    pieces = [swap(others, "chan", 1), swap(mine, "chan", 2), swap(others, "chan", 3)]

    own_in, order = gather_rows(after(weight_in, mine, others), "dp")
    weights_in = [own_in, swap(own_in, "chan", 1)]
    parts_out = [weight_out[:, at * narrow : (at + 1) * narrow] for at in range(4)]
    packed = jnp.concatenate([weight_mid] + parts_out, 0)
    gathered = lax.all_gather(packed, "dp", axis=0)

    params = pack_params([gain_in, bias_in, gain_mid, bias_mid, gate_bias], kernel_near, kernel_far)
    par_own = ordered(core == 1, params, swap(params, "chan", 1), 1)
    pars = [par_own, swap(par_own, "chan", 2)]
    same = lax.dynamic_slice_in_dim(same_video, core * (clips // 2), clips // 2, 0)
    same = jnp.pad(same, ((0, 0), (0, 1)))
    gain_row, bias_row = gain_out.reshape(1, -1), bias_out.reshape(1, -1)

    outs = stem_grad.shape[1]
    pre_stem, stem_rows, stem_pick, extra = stem_front(
        place, video, stem_weight(stem_center, stem_diff), width
    )

    def both_sums(sums, crossing, jobs=()):
        own = sum_over(sums + swap(sums, "chan", 1), "dp", jobs[:3])
        oth = swap(after(own, crossing), "chan", 2)
        for job in jobs[3:]:
            oth = after(oth, job(own))
        return [own, oth]

    made = {}

    def job(name, work):
        def run(mark):
            made[name] = work(mark)
            return made[name]

        return run

    pre_in, pre_in16, sums_in, full_in = first_conv(
        order, place, block_in, pieces, weights_in, after(extra, pars)
    )
    pre_in_oth = swap(pre_in16, "chan", 2)

    def mid_rows(mark):
        own = after(gathered, mark)[:, : weight_mid.shape[0]].reshape(-1, narrow)
        return [own, swap(own, "chan", 1)]

    def out_rows(mark):
        parts, first, size = after(gathered, mark), weight_mid.shape[0], weight_out.shape[0]
        parts = [parts[:, first + at * size : first + (at + 1) * size] for at in range(4)]
        return jnp.concatenate([part.reshape(-1, narrow) for part in parts], 1)

    stats_in = both_sums(
        sums_in, pre_in_oth, [job("weights_mid", mid_rows), job("full_out", out_rows)]
    )
    weights_mid, full_out = made["weights_mid"], made["full_out"]

    out_across = swap(after(full_out, stats_in), "chan", 2)

    mixed, pre_mid, pre_mid16, sums_mid = gate_mid(
        count, place, same, pre_in, pre_in_oth, *stats_in, *pars, weights_mid
    )
    pre_mid_oth = swap(pre_mid16, "chan", 2)
    stats_stem = after(stats_in[0], sums_mid)

    def stem_half(mark):
        return stem_output(
            stem_count, place, after(pre_stem, mark), stem_grad, stats_stem, stem_gain, stem_bias, quarter
        )

    def slab_of(mark):
        slab = after(weights_mid[0], mark).reshape(9, 2, width, narrow)
        return lax.dynamic_slice_in_dim(slab, 1 - y, 1, 1).reshape(9 * width, narrow)

    stats_mid = both_sums(
        after(sums_mid, out_across),
        pre_mid_oth,
        [job("stem", stem_half), job("slab", slab_of), job("turned", lambda mark: turn(after(mixed, mark)))],
    )
    stem_out, extra = made["stem"]

    second = second_half(count, place, pre_mid, pre_mid_oth, stats_mid, pars)
    second_peer = swap(second, "chan", 1)
    pre_out, sums_out = last_conv(place, second, second_peer, full_out, extra)
    slab_across = swap(after(made["slab"], stats_mid), "chan", 2)
    stats_out = sum_over(sums_out, "dp", [
        job("near_in", lambda mark: lax.dynamic_slice_in_dim(after(full_in, mark), chan * quarter, quarter, 0)),
        job("away_in", lambda mark: lax.dynamic_slice_in_dim(after(full_in, mark), (chan ^ 2) * quarter, quarter, 0)),
    ])
    stats_out = after(stats_out, slab_across)
    out_peers = [swap(after(value, stats_out), "chan", 1) for value in (full_out, out_across)]
    weights_out = [full_out, out_peers[0], out_across, out_peers[1]]
    block_out, grad_total, sums_back, keep, send = out_back(
        count, place, pre_out, block_in, block_grad, stats_out, gain_row, bias_row, full_out
    )
    got = swap(send, "chan", 1)

    def cross(mark):
        return cross_half(place, keep, after(got, mark))

    def stem_part(chunk, start):
        def work(mark):
            return stem_back(
                stem_count, place, after(pre_stem, mark), stem_grad, stats_in[0], stats_out, stem_gain,
                stem_bias, stem_rows, stem_pick, start and made[start], chunk, 4,
            )

        return job(f"stem{chunk}", work)

    back_out = sum_over(
        sums_back, "dp", [job("cross", cross), stem_part(0, None), stem_part(1, "stem0")]
    )
    keep, send = made["cross"]
    got = swap(send, "chan", 2)
    delta = out_delta(count, rows, stats_out, sums_back, back_out, gain_row)
    deltas = [delta, swap(delta, "chan", 1)]
    deltas += [swap(value, "chan", 2) for value in deltas]

    grad_mid, grad_mid16, sums_mid_back = mid_slope(
        count, place, keep, got, second, pre_mid, stats_mid[0], pars[0], deltas, weights_out
    )
    grad_mid_oth = swap(grad_mid16, "chan", 2)

    aways_mid = [slab_across, swap(after(slab_across, sums_mid_back), "chan", 1)]

    def out_part(start, rows_of_second):
        def work(mark):
            return out_weight(
                count, place, rows_of_second, pre_out, grad_total, stats_out, after(back_out, mark),
                gain_row, start and made[start],
            )

        return work

    back_mid = both_sums(sums_mid_back, grad_mid_oth, [
        job("out0", out_part(None, second)),
        job("out1", out_part("out0", second_peer)),
        stem_part(2, "stem1"),
        stem_part(3, "stem2"),
    ])
    bits = steps_of("dp")
    sum_out = reduce_rows(place, made["out1"], None, "dp", bits)
    far_in = swap(made["away_in"], "chan", 2)

    slopes, grad_in, grad_in16, sums_in_back = mid_back(
        count, place, same, grad_mid, grad_mid_oth, pre_mid, pre_mid_oth, stats_mid, back_mid,
        pre_in, stats_in[0], pars, weights_mid, aways_mid,
    )
    grad_in_oth = swap(grad_in16, "chan", 2)

    def mid_part(mark):
        return mid_weight(place, made["turned"], after(slopes, mark))

    def mid_rest(mark):
        keep, send = made["mid"]
        return halve(place, keep, after(swap(send, "chan", 1), mark), "dp", mid_bits, mid_bits[0])

    mid_bits = bits[1:2] + bits[:1] + bits[2:]
    back_in = both_sums(sums_in_back, grad_in_oth, [job("mid", mid_part), job("mid0", mid_rest)])
    mid_got = swap(made["mid0"][1], "dp", mid_bits[0])

    grad_pre, keep, send = in_back(
        count, place, grad_in, grad_in_oth, pre_in, pre_in_oth, stats_in, back_in, pars, block_in,
        pieces,
    )
    grad_peer = swap(grad_pre, "chan", 1)
    got = swap(send, "chan", 1)

    def input_job(mark):
        near = after(made["near_in"], mark)
        return input_grad(place, grad_pre, grad_peer, near, far_in, grad_total)

    def mid_job(at):
        def work(mark):
            made["mid_keep"], send = halve(
                place, after(made["mid_keep"], mark), made["mid_got"], "dp", mid_bits[at:], mid_bits[at]
            )
            made["mid_got"] = swap(send, "dp", mid_bits[at])
            return send

        return work

    made["mid_keep"], made["mid_got"] = made["mid0"][0], mid_got
    many = [mid_job(at) for at in range(1, len(mid_bits))]

    def first_job(mark):
        made["input"] = input_job(many[0](mark))
        return made["input"]

    sum_in = reduce_rows(place, keep, got, "dp", bits, [first_job] + many[1:])
    sum_mid = made["mid_keep"] + made["mid_got"].astype(jnp.float32)
    grad_block_in = made["input"]
    stem_sum = sum_over(made["stem3"], "dp")
    center_grad, diff_grad = stem_grads(after(stem_sum, made["input"]), outs)

    def my_columns(value):
        return lax.dynamic_slice_in_dim(value, core * narrow, narrow, value.ndim - 1)

    def my_stem(value):
        row = lax.dynamic_slice(value, (2, core * 2 * outs), (1, 2 * outs))[0]
        return row[:outs], row[outs:]

    gate_grads = my_columns(back_in[0][8:])
    mid_grads, in_grads = my_columns(back_mid[0]), my_columns(back_in[0])
    stem_bias_grad, stem_gain_grad = my_stem(stats_out)
    return (
        block_out,
        stem_out,
        grad_block_in,
        sum_in,
        sum_mid,
        sum_out,
        in_grads[1],
        in_grads[0],
        mid_grads[1],
        mid_grads[0],
        back_out[1],
        back_out[0],
        gate_grads[1:10],
        gate_grads[10:19],
        gate_grads[0],
        center_grad,
        diff_grad,
        stem_gain_grad,
        stem_bias_grad,
    )


def solution(mesh):
    placed = (
        P("dp", "chan"),
        P("dp", "chan"),
        P("dp", "chan"),
        P("dp", "chan"),
        P("chan"),
        P("chan"),
        P("chan"),
        P("chan"),
        P("chan"),
        P("chan"),
        P(None, "chan"),
        P(None, "chan"),
        P("chan"),
        P("dp", None),
        P("dp", None, None),
        P(None, "chan"),
        P(None, "chan"),
        P("chan"),
        P("chan"),
        P("dp", "chan"),
        P("dp", "chan", None),
    )
    return jax.shard_map(
        per_device,
        mesh=mesh,
        in_specs=placed,
        out_specs=(
            P("dp", "chan"),
            P("dp", "chan", None),
            P("dp", "chan"),
            P("dp", "chan"),
            P("dp", "chan"),
            P("dp", "chan"),
            P("chan"),
            P("chan"),
            P("chan"),
            P("chan"),
            P("chan"),
            P("chan"),
            P(None, "chan"),
            P(None, "chan"),
            P("chan"),
            P(None, "chan"),
            P(None, "chan"),
            P("chan"),
            P("chan"),
        ),
        check_vma=False,
    )
```

```python
import functools

import jax
import jax.numpy as jnp
from jax import lax
from jax.experimental import pallas as pl
from jax.experimental.pallas import tpu as pltpu
from jax.sharding import PartitionSpec as P

SEG = 8
SIDE = 7
FRAMES = 5
PIXELS = SIDE * SIDE
BLOCK = 16
SPAN = SIDE + 2

eps = 1e-05
vmem_limit = 24 * 1024 * 1024
flops_per_us = 0.3e9

whole = pl.BlockSpec(memory_space=pltpu.VMEM)
remote = pl.BlockSpec(memory_space=pltpu.HBM)
scalars = pl.BlockSpec(memory_space=pltpu.SMEM)


def logistic(value):
    return 0.5 * jnp.tanh(0.5 * value) + 0.5


def silu_slope(value):
    part = logistic(value)
    return part * (1.0 + value * (1.0 - part))


def norm_stats(totals, squares, count):
    center = totals / count
    spread = squares / count - center * center
    return (center, lax.rsqrt(spread + eps))


def move(source, target, sems, at):
    copy = pltpu.make_async_copy(source, target, sems.at[at])
    copy.start()
    return copy


def kernel_call(body, out_shape, in_specs, scratch=(), lasts=1.0, away=(), held=()):
    several = isinstance(out_shape, tuple)
    shapes = list(out_shape) if several else [out_shape]
    specs = [remote if at in away else whole for at in range(len(shapes))]
    shapes = [
        (pltpu.HBM if at in away else pltpu.VMEM)(shape.shape, shape.dtype)
        if at in away or at in held
        else shape
        for at, shape in enumerate(shapes)
    ]
    call = pl.pallas_call(
        body,
        out_shape=tuple(shapes) if several else shapes[0],
        in_specs=in_specs,
        out_specs=tuple(specs) if several else specs[0],
        scratch_shapes=list(scratch),
        compiler_params=pltpu.CompilerParams(vmem_limit_bytes=vmem_limit),
        cost_estimate=pl.CostEstimate(
            flops=int(lasts * flops_per_us), bytes_accessed=0, transcendentals=0
        ),
    )

    def run(*args):
        return call(
            *[
                pltpu.with_memory_space_constraint(arg, pltpu.HBM) if spec is remote else arg
                for arg, spec in zip(args, in_specs, strict=True)
            ]
        )

    return run


PAIRS = SEG // 2
CLIP = SEG * PIXELS


def pair_row(clip, pair):
    return pl.multiple_of(BLOCK * (2 + SPAN * (PAIRS * clip + pair)), BLOCK)


def clip_view(ref, clip, extra=0):
    return ref.at[pl.ds(pl.multiple_of(clip * CLIP, 8), CLIP + extra)]


def lane_mask(width):
    return lax.broadcasted_iota(jnp.int32, (1, 8, width), 1)


def load_map(ref, first, lanes):
    return jnp.stack([ref[pl.ds(first + SIDE * at, 8), lanes] for at in range(SIDE)])


def store_map(ref, first, lanes, value):
    for at in range(SIDE):
        ref[pl.ds(first + SIDE * at, SIDE), lanes] = value[at][:SIDE]


def two_maps(early, late):
    both = jnp.stack([early, late], axis=1)
    return both.reshape(SIDE * BLOCK, early.shape[-1])


def down(value, step):
    zeros = jnp.zeros((abs(step),) + value.shape[1:], value.dtype)
    if step > 0:
        return jnp.concatenate([value[step:], zeros])
    if step < 0:
        return jnp.concatenate([zeros, value[:step]])
    return value


def across(value, step, place):
    if step == 0:
        return value
    moved = pltpu.roll(value, (-step) % 8, 1)
    if step == 2:
        return jnp.where(place < 6, moved, 0.0)
    if step == -2:
        return jnp.where(place > 0, moved, 0.0)
    return moved


def taps_of(near, far):
    for step, kernel in ((1, near), (2, far)):
        for row in range(3):
            yield step, row, [kernel[row * 3 + col] for col in range(3)]


def views_of(value, place):
    return {step: across(value, step, place) for step in (-2, -1, 0, 1, 2)}


def gate_score(change, near, far, offset, place):
    views = views_of(change, place)
    score = jnp.broadcast_to(offset, change.shape)
    for step, row, kernel in taps_of(near, far):
        term = sum(kernel[col] * views[step * (col - 1)] for col in range(3))
        score = score + down(term, step * (row - 1))
    return score


def conv_chunk(parts, weights, first, rows, sign):
    total = None
    for col in (1, 0, 2):
        acc = None
        for row in range(3):
            start = pl.multiple_of(first + BLOCK * (1 + sign * (row - 1)), BLOCK)
            for part, weight in zip(parts, weights, strict=True):
                left = part[pl.ds(start, rows), :]
                term = weight(left, row * 3 + col)
                acc = term if acc is None else acc + term
        acc = acc.reshape(rows // 8, 8, acc.shape[-1])
        shift = sign * (col - 1)
        if shift:
            acc = pltpu.roll(acc, (-shift) % 8, 1)
        total = acc if total is None else total + acc
    return total


def lane_part(index, width=128):
    return pl.ds(pl.multiple_of(index * width, width), width)


def row_part(index, size):
    return pl.ds(pl.multiple_of(index * size, size), size)


def rows_of(stats_ref):
    return stats_ref[0:1], stats_ref[1:2]


def put_sums(sums_ref, first, second):
    sums_ref[...] = jnp.zeros_like(sums_ref)
    sums_ref[0:1, :] = first
    sums_ref[1:2, :] = second


def fetch_blocks(sources, core, target_ref, sems, first):
    moves = []
    for side, source in enumerate(sources):
        lanes = lane_part(core if side == 0 else 1 - core)
        blocks = source.shape[0]
        size = target_ref.shape[0] // blocks
        for block in range(blocks):
            here = pl.ds(block * size, size)
            moves.append(
                move(
                    source.at[block, pl.ds(0, size)],
                    target_ref.at[here, lanes],
                    sems,
                    first + side * blocks + block,
                )
            )
    return moves


def gate_half(count, same_ref, pre, stats, par, hidden_ref, mixed_ref, first, gates_ref=None):
    rows, width = pre.shape
    hidden_ref[pl.ds(rows, hidden_ref.shape[0] - rows), :] = jnp.zeros(
        (hidden_ref.shape[0] - rows, width), jnp.float32
    )
    center, rate = norm_stats(*rows_of(stats), count)
    scaled = (pre[...].astype(jnp.float32) - center) * rate
    normed = scaled * par[0:1] + par[1:2]
    hidden_ref[pl.ds(0, rows), :] = normed * logistic(normed)
    at = lane_mask(128)

    def lanes_step(chunk, _):
        lanes = lane_part(chunk)
        target = pl.ds(pl.multiple_of(first + chunk * 128, 128), 128)
        near = [par[5 + tap : 6 + tap, lanes].reshape(1, 1, 128) for tap in range(9)]
        far = [par[14 + tap : 15 + tap, lanes].reshape(1, 1, 128) for tap in range(9)]
        offset = par[4:5, lanes].reshape(1, 1, 128)

        def clip_step(clip, _):
            view = clip_view(hidden_ref, clip, 56)
            for pair in range(PAIRS):
                maps = [load_map(view, PIXELS * (2 * pair + seg), lanes) for seg in range(3)]
                results = []
                for seg in range(2):
                    same = same_ref[clip, 2 * pair + seg].astype(jnp.float32)
                    change = jnp.where(at < SIDE, same * (maps[seg + 1] - maps[seg]), 0.0)
                    gate = logistic(gate_score(change, near, far, offset, at))
                    results.append(jnp.where(at < SIDE, maps[seg] * (1.0 + gate), 0.0))
                    if gates_ref is not None:
                        gates_ref[SEG * clip + 2 * pair + seg, :, :, lanes] = gate
                place = pl.ds(pair_row(clip, pair), SIDE * BLOCK)
                mixed_ref[place, target] = two_maps(*results).astype(jnp.bfloat16)
            return 0

        return lax.fori_loop(0, rows // CLIP, clip_step, 0)

    lax.fori_loop(0, width // 128, lanes_step, 0)


def gate_own_body(
    count, same_ref, own_ref, stats_ref, par_ref, mixed_out_ref, gates_out_ref, hidden_ref, mixed_ref, gates_ref,
    sems,
):
    mixed_ref[...] = jnp.zeros_like(mixed_ref)
    gate_half(count, same_ref, own_ref, stats_ref, par_ref, hidden_ref, mixed_ref, 0, gates_ref)
    moves = [move(mixed_ref, mixed_out_ref, sems, 0), move(gates_ref, gates_out_ref, sems, 1)]
    for copy in moves:
        copy.wait()


def gate_own(count, same, own, stats, par):
    rows, width = own.shape
    shape = (map_rows(rows), width)
    gates = (rows // PIXELS, SIDE, 8, width)
    return kernel_call(
        functools.partial(gate_own_body, count),
        (jax.ShapeDtypeStruct(shape, jnp.bfloat16), jax.ShapeDtypeStruct(gates, jnp.float32)),
        [scalars, whole, whole, whole],
        (
            pltpu.VMEM((rows + 56, width), jnp.float32),
            pltpu.VMEM(shape, jnp.bfloat16),
            pltpu.VMEM(gates, jnp.float32),
            pltpu.SemaphoreType.DMA((2,)),
        ),
        away=(0, 1),
        lasts=3.9,
    )(same, own, stats, par)


def gate_mid_body(
    count,
    place_ref,
    same_ref,
    own_ref,
    oth_ref,
    stats_oth_ref,
    par_oth_ref,
    weight_own_ref,
    weight_peer_ref,
    mixed_out_ref,
    mid_ref,
    mid16_ref,
    sums_ref,
    hidden_ref,
    acc_ref,
    weight_ref,
    oth_here_ref,
    stats_here_ref,
    mixed_ref,
    sems,
):
    rows, width = oth_ref.shape
    clips = rows // CLIP
    core, y = place_ref[0] % 2, place_ref[0] // 2
    arrivals = [
        move(stats_oth_ref, stats_here_ref, sems, 0),
        move(oth_ref, oth_here_ref, sems, 1),
    ]
    weight_moves = [move(own_ref, mixed_ref.at[:, lane_part(y, width)], sems, 2)]
    weight_moves += fetch_blocks((weight_own_ref, weight_peer_ref), core, weight_ref, sems, 5)
    mixed_ref[:, lane_part(1 - y, width)] = jnp.zeros((mixed_ref.shape[0], width), jnp.bfloat16)
    for copy in arrivals:
        copy.wait()
    gate_half(
        count, same_ref, oth_here_ref, stats_here_ref, par_oth_ref, hidden_ref, mixed_ref,
        pl.multiple_of((1 - y) * width, width),
    )
    depth = 2 * width
    for copy in weight_moves:
        copy.wait()
    mixed_move = move(mixed_ref, mixed_out_ref, sems, 3)

    def tap_dot(left, tap):
        return jnp.dot(
            left, weight_ref[tap * depth : (tap + 1) * depth], preferred_element_type=jnp.float32
        )

    def conv_step(clip, _):
        span = PAIRS * SPAN * BLOCK
        total = conv_chunk([mixed_ref], [tap_dot], clip * span, span, 1)
        view = clip_view(acc_ref, clip)
        for seg in range(SEG):
            value = [total[2 * (SPAN * (seg // 2) + 1 + row) + seg % 2] for row in range(SIDE)]
            store_map(view, seg * PIXELS, slice(None), value)
        return 0

    lax.fori_loop(0, clips, conv_step, 0)
    mid_move = move(acc_ref.at[pl.ds(0, rows)], mid_ref, sems, 4)
    result = acc_ref[pl.ds(0, rows), :]
    mid16_ref[...] = result.astype(jnp.bfloat16)
    put_sums(
        sums_ref, jnp.sum(result, 0, keepdims=True), jnp.sum(result * result, 0, keepdims=True)
    )
    mixed_move.wait()
    mid_move.wait()


def map_rows(rows):
    return (rows // (2 * PIXELS) * SPAN + 2) * BLOCK


def gate_mid(count, place, same, own, oth, stats_oth, par_oth, weights):
    rows, width = oth.shape
    spread = map_rows(rows)
    depth = 18 * width
    return kernel_call(
        functools.partial(gate_mid_body, count),
        (
            jax.ShapeDtypeStruct((spread, 2 * width), jnp.bfloat16),
            jax.ShapeDtypeStruct((rows, width), jnp.float32),
            jax.ShapeDtypeStruct((rows, width), jnp.bfloat16),
            jax.ShapeDtypeStruct((8, width), jnp.float32),
        ),
        [scalars, scalars, remote, remote, remote, whole, remote, remote],
        (
            pltpu.VMEM((rows + 56, width), jnp.float32),
            pltpu.VMEM((rows + 8, width), jnp.float32),
            pltpu.VMEM((depth, width), jnp.bfloat16),
            pltpu.VMEM((rows, width), oth.dtype),
            pltpu.VMEM((8, width), jnp.float32),
            pltpu.VMEM((spread, 2 * width), jnp.bfloat16),
            pltpu.SemaphoreType.DMA((5 + 2 * weights[0].shape[0],)),
        ),
        away=(0, 1),
        lasts=8.0,
    )(place, same, own, oth, stats_oth, par_oth, *weights)


def mid_slopes(count, grad, pre, stats, back, par, flat_ref, store):
    rows, width = grad.shape
    flat_ref[pl.ds(rows, flat_ref.shape[0] - rows), :] = jnp.zeros(
        (flat_ref.shape[0] - rows, width), jnp.float32
    )
    center, rate = norm_stats(*rows_of(stats), count)
    scaled = (pre[...].astype(jnp.float32) - center) * rate
    flat_ref[pl.ds(0, rows), :] = (par[2:3] * rate) * (
        grad[...].astype(jnp.float32) - back[0:1] / count - scaled * (back[1:2] / count)
    )
    at = lane_mask(width)

    def clip_step(clip, _):
        view = clip_view(flat_ref, clip, 8)
        for pair in range(PAIRS):
            maps = [
                jnp.where(at < SIDE, load_map(view, PIXELS * (2 * pair + seg), slice(None)), 0.0)
                for seg in range(2)
            ]
            store(pl.ds(pair_row(clip, pair), SIDE * BLOCK), maps, at)
        return 0

    lax.fori_loop(0, rows // CLIP, clip_step, 0)


def mid_own_body(count, d_ref, mid_ref, stats_ref, back_ref, par_ref, slopes_ref, flat_ref, mid_here_ref, sems):
    arrival = move(mid_ref, mid_here_ref, sems, 0)
    slopes_ref[...] = jnp.zeros_like(slopes_ref)

    def store(place, maps, at):
        for col in range(3):
            slopes_ref[col, place, :] = two_maps(
                *[across(value, 1 - col, at) for value in maps]
            ).astype(jnp.bfloat16)

    arrival.wait()
    mid_slopes(count, d_ref, mid_here_ref, stats_ref, back_ref, par_ref, flat_ref, store)


def mid_own(count, d_own, mid, stats, back, par):
    rows, width = d_own.shape
    return kernel_call(
        functools.partial(mid_own_body, count),
        jax.ShapeDtypeStruct((3, map_rows(rows), width), jnp.bfloat16),
        [whole, remote, whole, whole, whole],
        (
            pltpu.VMEM((rows + 56, width), jnp.float32),
            pltpu.VMEM((rows, width), jnp.float32),
            pltpu.SemaphoreType.DMA((1,)),
        ),
        held=(0,),
        lasts=1.7,
    )(d_own, mid, stats, back, par)


def mid_back_body(
    count,
    place_ref,
    same_ref,
    slopes_ref,
    d_oth_ref,
    mid_oth_ref,
    stats_oth_ref,
    back_oth_ref,
    pre_ref,
    gates_ref,
    stats_in_ref,
    par_own_ref,
    par_oth_ref,
    weight_own_ref,
    weight_peer_ref,
    away_own_ref,
    away_peer_ref,
    d_in_out_ref,
    d_in16_ref,
    sums_ref,
    flat_ref,
    oth_ref,
    dmix_ref,
    scaled_ref,
    parts_ref,
    weight_ref,
    weight_oth_ref,
    d_here_ref,
    mid_here_ref,
    back_here_ref,
    pre_here_ref,
    gates_here_ref,
    sems,
):
    rows, width = d_oth_ref.shape
    clips = rows // CLIP
    core, y = place_ref[0] % 2, place_ref[0] // 2
    arrivals = [
        move(back_oth_ref, back_here_ref, sems, 0),
        move(d_oth_ref, d_here_ref, sems, 1),
        move(mid_oth_ref, mid_here_ref, sems, 2),
    ]
    weight_moves = fetch_blocks((weight_own_ref, weight_peer_ref), core, weight_ref, sems, 10)
    weight_moves += [
        move(away_own_ref, weight_oth_ref.at[:, lane_part(core)], sems, 3),
        move(away_peer_ref, weight_oth_ref.at[:, lane_part(1 - core)], sems, 4),
    ]
    pre_moves = [
        move(pre_ref, pre_here_ref, sems, 7),
        move(gates_ref, gates_here_ref, sems, 9),
    ]
    oth_ref[...] = jnp.zeros_like(oth_ref)

    def store(place, maps, _):
        oth_ref[place, :] = two_maps(*maps).astype(jnp.bfloat16)

    for copy in arrivals:
        copy.wait()
    mid_slopes(count, d_here_ref, mid_here_ref, stats_oth_ref, back_here_ref, par_oth_ref, flat_ref, store)
    depth = 2 * width
    turned = (((1,), (1,)), ((), ()))
    for copy in weight_moves:
        copy.wait()

    def own_dot(left, tap):
        start = pl.multiple_of(tap * depth + y * width, width)
        return lax.dot_general(
            left, weight_ref[pl.ds(start, width), :], turned, preferred_element_type=jnp.float32
        )

    def oth_dot(left, tap):
        return lax.dot_general(
            left,
            weight_oth_ref[tap * width : (tap + 1) * width],
            turned,
            preferred_element_type=jnp.float32,
        )

    def conv_step(clip, _):
        span = PAIRS * SPAN * BLOCK
        total = conv_chunk([slopes_ref.at[1], oth_ref], [own_dot, oth_dot], clip * span, span, -1)
        dmix_ref[pl.ds(clip * (span // 8), span // 8)] = total
        return 0

    lax.fori_loop(0, clips, conv_step, 0)

    center, rate = norm_stats(*rows_of(stats_in_ref), count)
    for copy in pre_moves:
        copy.wait()
    scaled_ref[pl.ds(0, rows), :] = (pre_here_ref[...] - center) * rate
    scaled_ref[pl.ds(rows, scaled_ref.shape[0] - rows), :] = jnp.zeros(
        (scaled_ref.shape[0] - rows, width), jnp.float32
    )
    parts_ref[...] = jnp.zeros_like(parts_ref)
    at = lane_mask(128)

    def lanes_step(chunk, _):
        lanes = pl.ds(pl.multiple_of(chunk * 128, 128), 128)

        def row_of(index):
            return par_own_ref[index : index + 1, lanes].reshape(1, 1, 128)

        near = [row_of(5 + tap) for tap in range(9)]
        far = [row_of(14 + tap) for tap in range(9)]
        gain, bias = row_of(0), row_of(1)

        def add_part(index, value):
            here = pl.ds(8 * index, 8)
            parts_ref[here, lanes] += jnp.sum(value, 0)

        def clip_step(clip, carry):
            view = clip_view(scaled_ref, clip, 56)
            target = clip_view(flat_ref, clip)
            for pair in range(PAIRS):
                carry = pair_step(clip, pair, carry, view, target)
            return carry

        def pair_step(clip, pair, carry, view, target):
            normed = [
                load_map(view, PIXELS * (2 * pair + seg), lanes) * gain + bias for seg in range(3)
            ]
            parts = [logistic(value) for value in normed]
            hidden = [value * part for value, part in zip(normed, parts, strict=True)]
            for seg in range(2):
                same = same_ref[clip, 2 * pair + seg].astype(jnp.float32)
                change = jnp.where(at < SIDE, same * (hidden[seg + 1] - hidden[seg]), 0.0)
                views = views_of(change, at)
                gate = gates_here_ref[SEG * clip + 2 * pair + seg, :, :, lanes]
                start = 2 * (SPAN * (PAIRS * clip + pair) + 1) + seg
                d_mixed = jnp.stack([dmix_ref[start + 2 * row, :, lanes] for row in range(SIDE)])
                d_mixed = jnp.where(at < SIDE, d_mixed, 0.0)
                d_score = d_mixed * hidden[seg] * (gate * (1.0 - gate))
                add_part(0, d_score)
                backs = {step: across(d_score, step, at) for step in (-2, -1, 0, 1, 2)}
                d_change = None
                for index, (step, row, kernel) in enumerate(taps_of(near, far)):
                    here = down(d_score, -step * (row - 1))
                    for col in range(3):
                        if index != 4 or col != 1:
                            add_part(1 + 3 * index + col, here * views[step * (col - 1)])
                    term = sum(kernel[col] * backs[-step * (col - 1)] for col in range(3))
                    term = down(term, -step * (row - 1))
                    d_change = term if d_change is None else d_change + term
                d_change = jnp.where(at < SIDE, same * d_change, 0.0)
                d_hidden = d_mixed * (1.0 + gate) - d_change + carry
                carry = d_change
                slope = parts[seg] * (1.0 + normed[seg] * (1.0 - parts[seg]))
                store_map(target, PIXELS * (2 * pair + seg), lanes, d_hidden * slope)
            return carry

        lax.fori_loop(0, clips, clip_step, jnp.zeros((SIDE, 8, 128), jnp.float32))
        return 0

    lax.fori_loop(0, width // 128, lanes_step, 0)
    d_in_move = move(flat_ref.at[pl.ds(0, rows)], d_in_out_ref, sems, 8)
    result = flat_ref[pl.ds(0, rows), :]
    d_in16_ref[...] = result.astype(jnp.bfloat16)
    put_sums(
        sums_ref,
        jnp.sum(result, 0, keepdims=True),
        jnp.sum(result * scaled_ref[pl.ds(0, rows), :], 0, keepdims=True),
    )
    parts_ref[pl.ds(8 * 14, 8), :] = parts_ref[pl.ds(8 * 5, 8), :]
    sums_ref[8:32, :] = jnp.sum(parts_ref[...].reshape(24, 8, width), 1)
    d_in_move.wait()


def mid_back(
    count, place, same, slopes, d_oth, mid_oth, stats_oth, back_oth, pre, gates, stats_in, pars, weights, aways
):
    rows, width = d_oth.shape
    spread = map_rows(rows)
    depth = 18 * width
    return kernel_call(
        functools.partial(mid_back_body, count),
        (
            jax.ShapeDtypeStruct((rows, width), jnp.float32),
            jax.ShapeDtypeStruct((rows, width), jnp.bfloat16),
            jax.ShapeDtypeStruct((32, width), jnp.float32),
        ),
        [scalars, scalars, whole, remote, remote, whole, remote, remote, remote]
        + [whole] * 3
        + [remote] * 4,
        (
            pltpu.VMEM((rows + 56, width), jnp.float32),
            pltpu.VMEM((spread, width), jnp.bfloat16),
            pltpu.VMEM((spread // 8, 8, width), jnp.float32),
            pltpu.VMEM((rows + 56, width), jnp.float32),
            pltpu.VMEM((24 * 8, width), jnp.float32),
            pltpu.VMEM((depth, width), jnp.bfloat16),
            pltpu.VMEM((depth // 2, width), jnp.bfloat16),
            pltpu.VMEM((rows, width), jnp.bfloat16),
            pltpu.VMEM((rows, width), jnp.bfloat16),
            pltpu.VMEM((8, width), jnp.float32),
            pltpu.VMEM((rows, width), jnp.float32),
            pltpu.VMEM(gates.shape, jnp.float32),
            pltpu.SemaphoreType.DMA((10 + 2 * weights[0].shape[0],)),
        ),
        away=(0,),
        lasts=11.5,
    )(
        place, same, slopes, d_oth, mid_oth, stats_oth, back_oth, pre, gates, stats_in, *pars, *weights,
        *aways,
    )


def turn_body(mixed_ref, out_ref, mixed_here_ref, sems):
    move(mixed_ref, mixed_here_ref, sems, 0).wait()
    out_ref[...] = mixed_here_ref[pl.ds(BLOCK, out_ref.shape[1]), :].T


def turn(mixed):
    spread, depth = mixed.shape
    return kernel_call(
        turn_body,
        jax.ShapeDtypeStruct((depth, spread - 2 * BLOCK), jnp.bfloat16),
        [remote],
        (pltpu.VMEM(mixed.shape, jnp.bfloat16), pltpu.SemaphoreType.DMA((1,))),
        held=(0,),
        lasts=1.6,
    )(mixed)


def mid_weight_body(place_ref, turned_ref, slopes_ref, keep_ref, early_ref, late_ref, keep_here_ref, sems):
    depth, rows = turned_ref.shape
    half = keep_ref.shape[1]
    cut = early_ref.shape[0]
    first = place_ref[0] % 2 == 0
    moves = []
    for tap in range(9):
        row, col = tap // 3, tap % 3
        right = slopes_ref[col, pl.ds(BLOCK * (2 - row), rows), :]
        value = jnp.dot(turned_ref[...], right, preferred_element_type=jnp.float32)
        low, high = value[:, :half], value[:, half:]
        here = pl.ds(tap * depth, depth)
        keep_here_ref[here, :] = jnp.where(first, low, high)
        moves.append(move(keep_here_ref.at[here], keep_ref.at[here], sems, tap))
        send = jnp.where(first, high, low).astype(jnp.bfloat16)
        middle = min(max(cut - tap * depth, 0), depth)
        if middle > 0:
            early_ref[tap * depth : tap * depth + middle] = send[:middle]
        if middle < depth:
            late_ref[tap * depth + middle - cut : (tap + 1) * depth - cut] = send[middle:]
    for copy in moves:
        copy.wait()


def mid_weight(place, turned, slopes):
    depth, rows = turned.shape
    width = slopes.shape[2]
    part = jax.ShapeDtypeStruct((9 * depth // 2, width // 2), jnp.bfloat16)
    return kernel_call(
        mid_weight_body,
        (jax.ShapeDtypeStruct((9 * depth, width // 2), jnp.float32), part, part),
        [scalars, whole, whole],
        (pltpu.VMEM((9 * depth, width // 2), jnp.float32), pltpu.SemaphoreType.DMA((9,))),
        away=(0,),
        lasts=4.8,
    )(place, turned, slopes)


def first_conv_body(
    order,
    place_ref,
    block_ref,
    peer_ref,
    across_ref,
    corner_ref,
    own_ref,
    other_ref,
    extra_ref,
    pre_out_ref,
    sums_ref,
    weight_out_ref,
    pre_ref,
    weight_ref,
    sems,
):
    rows = peer_ref.shape[0]
    quarter = block_ref.shape[1]
    chan, group = place_ref[0], place_ref[1]
    core = chan % 2
    size = own_ref.shape[0] // len(order)
    for at, bits in enumerate(order):
        here = row_part(group ^ bits, size)
        weight_ref[here, lane_part(core)] = own_ref[at * size : (at + 1) * size]
        weight_ref[here, lane_part(1 - core)] = other_ref[at * size : (at + 1) * size]
    weight_move = move(weight_ref, weight_out_ref, sems, 0)
    mine = block_ref[row_part(core, rows), :]
    total = None
    for at, piece in enumerate((mine, peer_ref[...], across_ref[...], corner_ref[...])):
        weight = weight_ref[row_part(chan ^ at, quarter), :]
        term = jnp.dot(piece, weight, preferred_element_type=jnp.float32)
        total = term if total is None else total + term
    pre_ref[...] = total
    pre_move = move(pre_ref, pre_out_ref, sems, 1)
    sums_ref[...] = extra_ref[...]
    sums_ref[0:1, :] = jnp.sum(total, 0, keepdims=True)
    sums_ref[1:2, :] = jnp.sum(total * total, 0, keepdims=True)
    weight_move.wait()
    pre_move.wait()


def first_conv(order, place, block, pieces, weights, extra):
    rows, quarter = pieces[0].shape
    width = 2 * weights[0].shape[1]
    return kernel_call(
        functools.partial(first_conv_body, order),
        (
            jax.ShapeDtypeStruct((rows, width), jnp.float32),
            jax.ShapeDtypeStruct((8, width), jnp.float32),
            jax.ShapeDtypeStruct((4 * quarter, width), jnp.bfloat16),
        ),
        [scalars] + [whole] * 7,
        (
            pltpu.VMEM((rows, width), jnp.float32),
            pltpu.VMEM((4 * quarter, width), jnp.bfloat16),
            pltpu.SemaphoreType.DMA((2,)),
        ),
        away=(0, 2),
        lasts=4.0,
    )(place, block, *pieces, *weights, extra)


def second_body(
    count, place_ref, own_ref, oth_ref, stats_own_ref, stats_oth_ref, par_own_ref, par_oth_ref, out_ref,
    oth_here_ref, stats_here_ref, sems,
):
    width = own_ref.shape[1]
    y = place_ref[0] // 2
    arrivals = [
        move(stats_oth_ref, stats_here_ref, sems, 0),
        move(oth_ref, oth_here_ref, sems, 1),
    ]
    for side, pre, stats, par in (
        (y, own_ref, stats_own_ref, par_own_ref),
        (1 - y, oth_here_ref, stats_here_ref, par_oth_ref),
    ):
        center, rate = norm_stats(*rows_of(stats), count)
        normed = (pre[...].astype(jnp.float32) - center) * rate * par[2:3] + par[3:4]
        out_ref[:, lane_part(side, width)] = (normed * logistic(normed)).astype(jnp.bfloat16)
        for copy in arrivals:
            copy.wait()
        arrivals = []


def second_half(count, place, own, oth, stats, pars):
    rows, width = own.shape
    return kernel_call(
        functools.partial(second_body, count),
        jax.ShapeDtypeStruct((rows, 2 * width), jnp.bfloat16),
        [scalars, whole, remote, whole, remote, whole, whole],
        (
            pltpu.VMEM((rows, width), jnp.bfloat16),
            pltpu.VMEM((8, width), jnp.float32),
            pltpu.SemaphoreType.DMA((2,)),
        ),
        lasts=1.9,
    )(place, own, oth, *stats, *pars)


def last_conv_body(place_ref, mine_ref, peer_ref, weight_ref, extra_ref, out_ref, sums_ref):
    rows = mine_ref.shape[0]
    core = place_ref[0] % 2
    sums = squares = 0.0
    for side, part in ((core, mine_ref), (1 - core, peer_ref)):
        value = jnp.dot(part[...], weight_ref[...], preferred_element_type=jnp.float32)
        out_ref[row_part(side, rows), :] = value
        sums += jnp.sum(value, 0, keepdims=True)
        squares += jnp.sum(value * value, 0, keepdims=True)
    sums_ref[...] = extra_ref[...]
    sums_ref[0:1, :] = sums
    sums_ref[1:2, :] = squares


def last_conv(place, mine, peer, weight, extra):
    rows, depth = mine.shape
    width = weight.shape[1]
    return kernel_call(
        last_conv_body,
        (
            jax.ShapeDtypeStruct((2 * rows, width), jnp.float32),
            jax.ShapeDtypeStruct((8, width), jnp.float32),
        ),
        [scalars] + [whole] * 4,
        lasts=2.3,
    )(place, mine, peer, weight, extra)


def out_back_body(
    count,
    place_ref,
    pre_ref,
    block_ref,
    grad_ref,
    stats_ref,
    gain_ref,
    bias_ref,
    weight_ref,
    out_ref,
    total_out_ref,
    sums_ref,
    keep_ref,
    send_ref,
    total_ref,
    sems,
):
    rows = keep_ref.shape[0]
    core = place_ref[0] % 2
    center, rate = norm_stats(*rows_of(stats_ref), count)
    gain, bias = gain_ref[...], bias_ref[...]
    step = rows // 7

    def add_step(at, sums):
        here = row_part(at, step)
        scaled = (pre_ref[here, :] - center) * rate
        total = scaled * gain + bias + block_ref[here, :].astype(jnp.float32)
        part = logistic(total)
        out_ref[here, :] = (total * part).astype(jnp.bfloat16)
        value = grad_ref[here, :].astype(jnp.float32) * (part * (1.0 + total * (1.0 - part)))
        total_ref[here, :] = value
        return (
            sums[0] + jnp.sum(value, 0, keepdims=True),
            sums[1] + jnp.sum(value * scaled, 0, keepdims=True),
        )

    zero = jnp.zeros((1, pre_ref.shape[1]), jnp.float32)
    sums, products = lax.fori_loop(0, 14, add_step, (zero, zero))
    put_sums(sums_ref, sums, products)
    total_move = move(total_ref, total_out_ref, sems, 0)
    local = 1.0 / (2 * rows)

    def slope_rows(side):
        here = row_part(side, rows)
        scaled = (pre_ref[here, :] - center) * rate
        value = gain * rate * (total_ref[here, :] - sums * local - scaled * (products * local))
        return lax.dot_general(
            value.astype(jnp.bfloat16),
            weight_ref[...],
            (((1,), (1,)), ((), ())),
            preferred_element_type=jnp.float32,
        )

    send_ref[...] = slope_rows(1 - core).astype(jnp.bfloat16)
    keep_ref[...] = slope_rows(core)
    total_move.wait()


def out_back(count, place, pre, block, grad, stats, gain, bias, weight):
    rows, width = pre.shape
    depth = weight.shape[0]
    return kernel_call(
        functools.partial(out_back_body, count),
        (
            jax.ShapeDtypeStruct((rows, width), jnp.bfloat16),
            jax.ShapeDtypeStruct((rows, width), jnp.float32),
            jax.ShapeDtypeStruct((8, width), jnp.float32),
            jax.ShapeDtypeStruct((rows // 2, depth), jnp.float32),
            jax.ShapeDtypeStruct((rows // 2, depth), jnp.bfloat16),
        ),
        [scalars] + [whole] * 7,
        (pltpu.VMEM((rows, width), jnp.float32), pltpu.SemaphoreType.DMA((1,))),
        away=(1,),
        lasts=7.5,
    )(place, pre, block, grad, stats, gain, bias, weight)


def cross_body(place_ref, keep_ref, got_ref, own_ref, send_ref):
    width = own_ref.shape[1]
    y = place_ref[0] // 2
    for lanes, ref in ((1 - y, send_ref), (y, own_ref)):
        here = lane_part(lanes, width)
        value = keep_ref[:, here] + got_ref[:, here].astype(jnp.float32)
        ref[...] = value.astype(ref.dtype)


def cross_half(place, keep, got):
    rows, width = keep.shape[0], keep.shape[1] // 2
    return kernel_call(
        cross_body,
        (
            jax.ShapeDtypeStruct((rows, width), jnp.float32),
            jax.ShapeDtypeStruct((rows, width), jnp.bfloat16),
        ),
        [scalars, whole, whole],
        lasts=0.7,
    )(place, keep, got)


def out_delta_body(count, local, stats_ref, sums_ref, back_ref, gain_ref, out_ref):
    center, rate = norm_stats(*rows_of(stats_ref), count)
    scale = gain_ref[...] * rate
    first = scale * (back_ref[0:1] / count - sums_ref[0:1] * local)
    second = scale * rate * (back_ref[1:2] / count - sums_ref[1:2] * local)
    put_sums(out_ref, first - second * center, second)


def out_delta(count, rows, stats, sums, back, gain):
    return kernel_call(
        functools.partial(out_delta_body, count, 1.0 / rows),
        jax.ShapeDtypeStruct(stats.shape, jnp.float32),
        [whole] * 4,
    )(stats, sums, back, gain)


def mid_slope_body(
    count,
    place_ref,
    keep_ref,
    got_ref,
    second_ref,
    mid_ref,
    stats_ref,
    par_ref,
    deltas0_ref,
    deltas1_ref,
    deltas2_ref,
    deltas3_ref,
    weights0_ref,
    weights1_ref,
    weights2_ref,
    weights3_ref,
    out_ref,
    out16_ref,
    sums_ref,
):
    width = mid_ref.shape[1]
    y = place_ref[0] // 2
    turned = (((1,), (1,)), ((), ()))
    factor, offset = None, None
    for deltas, weights in (
        (deltas0_ref, weights0_ref),
        (deltas1_ref, weights1_ref),
        (deltas2_ref, weights2_ref),
        (deltas3_ref, weights3_ref),
    ):
        own = weights[row_part(y, width), :]
        left = (weights[...].astype(jnp.float32) * deltas[1:2]).astype(jnp.bfloat16)
        term = lax.dot_general(left, own, turned, preferred_element_type=jnp.float32)
        factor = term if factor is None else factor + term
        high = deltas[0:1].astype(jnp.bfloat16).astype(jnp.float32)
        both = jnp.concatenate([high, deltas[0:1] - high, jnp.zeros_like(deltas[2:8])])
        term = lax.dot_general(
            both.astype(jnp.bfloat16), own, turned, preferred_element_type=jnp.float32
        )
        term = term[0:1] + term[1:2]
        offset = term if offset is None else offset + term
    high = factor.astype(jnp.bfloat16)
    low = (factor - high.astype(jnp.float32)).astype(jnp.bfloat16)
    delta = jnp.dot(second_ref[...], high, preferred_element_type=jnp.float32)
    delta += jnp.dot(second_ref[...], low, preferred_element_type=jnp.float32)
    grad = keep_ref[...] + got_ref[...].astype(jnp.float32) - delta - offset
    center, rate = norm_stats(*rows_of(stats_ref), count)
    scaled = (mid_ref[...] - center) * rate
    normed = scaled * par_ref[2:3] + par_ref[3:4]
    result = grad * silu_slope(normed)
    out_ref[...] = result
    out16_ref[...] = result.astype(jnp.bfloat16)
    put_sums(
        sums_ref, jnp.sum(result, 0, keepdims=True), jnp.sum(result * scaled, 0, keepdims=True)
    )


def mid_slope(count, place, keep, got, second, mid, stats, par, deltas, weights):
    rows, width = mid.shape
    return kernel_call(
        functools.partial(mid_slope_body, count),
        (
            jax.ShapeDtypeStruct((rows, width), jnp.float32),
            jax.ShapeDtypeStruct((rows, width), jnp.bfloat16),
            jax.ShapeDtypeStruct((8, width), jnp.float32),
        ),
        [scalars] + [whole] * 14,
        held=(0,),
        lasts=3.3,
    )(place, keep, got, second, mid, stats, par, *deltas, *weights)


def out_weight_body(
    count, part, place_ref, rows_ref, pre_ref, total_ref, stats_ref, back_ref, gain_ref, *refs
):
    rows = rows_ref.shape[0]
    core = place_ref[0] % 2
    center, rate = norm_stats(*rows_of(stats_ref), count)
    here = row_part(1 - core if part else core, rows)
    scaled = (pre_ref[here, :] - center) * rate
    value = (gain_ref[...] * rate) * (
        total_ref[here, :] - back_ref[0:1] / count - scaled * (back_ref[1:2] / count)
    )
    result = exact(rows_ref[...], value.astype(jnp.bfloat16), ((0,), (0,)))
    refs[-1][...] = refs[0][...] + result if part else result


def out_weight(count, place, second, pre, total, stats, back, gain, start=None):
    rows, depth = second.shape
    width = pre.shape[1]
    part = 0 if start is None else 1
    return kernel_call(
        functools.partial(out_weight_body, count, part),
        jax.ShapeDtypeStruct((depth, width), jnp.float32),
        [scalars] + [whole] * (6 + part),
        lasts=1.7,
    )(place, second, pre, total, stats, back, gain, *([start] if part else []))


def in_slopes(count, grad, pre, stats, back, par):
    center, rate = norm_stats(*rows_of(stats), count)
    scaled = (pre[...].astype(jnp.float32) - center) * rate
    value = (par[0:1] * rate) * (
        grad[...].astype(jnp.float32) - back[0:1] / count - scaled * (back[1:2] / count)
    )
    return value.astype(jnp.bfloat16)


def in_own_body(
    count, place_ref, d_ref, pre_ref, stats_ref, back_ref, par_ref, block_ref, peer_ref, across_ref, corner_ref,
    out_ref, keep_ref, send_ref, d_here_ref, pre_here_ref, keep_here_ref, pieces_ref, sems,
):
    rows, width = d_ref.shape
    arrivals = [move(d_ref, d_here_ref, sems, 0), move(pre_ref, pre_here_ref, sems, 1)]
    half = width // 2
    quarter = block_ref.shape[1]
    chan = place_ref[0]
    core = chan % 2
    sources = (block_ref.at[row_part(core, rows)], peer_ref, across_ref, corner_ref)
    pieces = [
        move(source, pieces_ref.at[at], sems, 6 + at) for at, source in enumerate(sources)
    ]
    for copy in arrivals:
        copy.wait()
    own = in_slopes(count, d_here_ref, pre_here_ref, stats_ref, back_ref, par_ref)
    out_ref[...] = own
    moves = []
    for at, arrival in enumerate(pieces):
        arrival.wait()
        value = lax.dot_general(
            pieces_ref[at], own, (((0,), (0,)), ((), ())), preferred_element_type=jnp.float32
        )
        here = row_part(chan ^ at, quarter)
        low, high = value[:, :half], value[:, half:]
        keep_here_ref[here, :] = jnp.where(core == 0, low, high)
        moves.append(move(keep_here_ref.at[here], keep_ref.at[here], sems, 2 + at))
        send_ref[here, :] = jnp.where(core == 0, high, low).astype(jnp.bfloat16)
    for copy in moves:
        copy.wait()


def in_own(count, place, d_own, pre, stats, back, par, block, pieces):
    rows, width = d_own.shape
    full = 4 * block.shape[1]
    return kernel_call(
        functools.partial(in_own_body, count),
        (
            jax.ShapeDtypeStruct((rows, width), jnp.bfloat16),
            jax.ShapeDtypeStruct((full, width // 2), jnp.float32),
            jax.ShapeDtypeStruct((full, width // 2), jnp.bfloat16),
        ),
        [scalars, remote, remote] + [whole] * 3 + [remote] * 4,
        (
            pltpu.VMEM((rows, width), jnp.float32),
            pltpu.VMEM((rows, width), jnp.float32),
            pltpu.VMEM((full, width // 2), jnp.float32),
            pltpu.VMEM((4, rows, block.shape[1]), block.dtype),
            pltpu.SemaphoreType.DMA((10,)),
        ),
        away=(1,),
        lasts=4.5,
    )(place, d_own, pre, stats, back, par, block, *pieces)


def in_other_body(
    count, place_ref, own_ref, d_ref, pre_ref, stats_ref, back_ref, par_ref, out_ref,
    d_here_ref, pre_here_ref, back_here_ref, sems,
):
    width = d_ref.shape[1]
    y = place_ref[0] // 2
    arrivals = [
        move(back_ref, back_here_ref, sems, 0),
        move(d_ref, d_here_ref, sems, 1),
        move(pre_ref, pre_here_ref, sems, 2),
    ]
    out_ref[:, lane_part(y, width)] = own_ref[...]
    for copy in arrivals:
        copy.wait()
    value = in_slopes(count, d_here_ref, pre_here_ref, stats_ref, back_here_ref, par_ref)
    out_ref[:, lane_part(1 - y, width)] = value


def in_other(count, place, own, d_oth, pre_oth, stats, back, par):
    rows, width = d_oth.shape
    return kernel_call(
        functools.partial(in_other_body, count),
        jax.ShapeDtypeStruct((rows, 2 * width), jnp.bfloat16),
        [scalars, whole, remote, remote, whole, remote, whole],
        (
            pltpu.VMEM((rows, width), d_oth.dtype),
            pltpu.VMEM((rows, width), pre_oth.dtype),
            pltpu.VMEM(back.shape, jnp.float32),
            pltpu.SemaphoreType.DMA((3,)),
        ),
        lasts=2.0,
    )(place, own, d_oth, pre_oth, stats, back, par)


def input_grad_body(place_ref, mine_ref, peer_ref, near_ref, far_ref, total_ref, out_ref):
    rows = mine_ref.shape[0]
    width = near_ref.shape[1]
    core, y = place_ref[0] % 2, place_ref[0] // 2
    turned = (((1,), (1,)), ((), ()))
    for side, part in ((core, mine_ref), (1 - core, peer_ref)):
        here = row_part(side, rows)
        value = total_ref[here, :]
        for lanes, weight in ((y, near_ref), (1 - y, far_ref)):
            value += lax.dot_general(
                part[:, lane_part(lanes, width)],
                weight[...],
                turned,
                preferred_element_type=jnp.float32,
            )
        out_ref[here, :] = value.astype(jnp.bfloat16)


def input_grad(place, mine, peer, near, far, total):
    rows, quarter = total.shape
    return kernel_call(
        input_grad_body,
        jax.ShapeDtypeStruct((rows, quarter), jnp.bfloat16),
        [scalars] + [whole] * 5,
        lasts=2.8,
    )(place, mine, peer, near, far, total)


def pack_weights_body(mid_ref, out_ref, packed_ref):
    rows, width = mid_ref.shape
    size = out_ref.shape[0]
    packed_ref[0:rows, :] = mid_ref[...]
    for at in range(4):
        packed_ref[rows + at * size : rows + (at + 1) * size, :] = out_ref[
            :, at * width : (at + 1) * width
        ]


def pack_weights(mid, out):
    rows, width = mid.shape
    size = out.shape[0]
    if size % BLOCK or rows % BLOCK:
        parts = [out[:, at * width : (at + 1) * width] for at in range(4)]
        return jnp.concatenate([mid] + parts, 0)
    return kernel_call(
        pack_weights_body,
        jax.ShapeDtypeStruct((rows + 4 * size, width), mid.dtype),
        [whole, whole],
    )(mid, out)


def pack_body(gain_in, bias_in, gain_mid, bias_mid, gate_bias, near, far, out_ref):
    for at, ref in enumerate((gain_in, bias_in, gain_mid, bias_mid, gate_bias)):
        out_ref[at : at + 1, :] = ref[...]
    out_ref[5:14, :] = near[...]
    out_ref[14:23, :] = far[...]
    out_ref[23:24, :] = jnp.zeros_like(out_ref[23:24, :])


def pack_params(rows, near, far):
    width = near.shape[1]
    return kernel_call(
        pack_body, jax.ShapeDtypeStruct((24, width), jnp.float32), [whole] * 7
    )(*[row.reshape(1, width) for row in rows], near, far)


TAPS = 7
LANES = 16


def exact(left, right, contract):
    return lax.dot_general(
        left, right, (contract, ((), ())), preferred_element_type=jnp.float32
    )


def spot(core, outs, width, part):
    lane = lax.broadcasted_iota(jnp.int32, (outs, width), 1)
    channel = lax.broadcasted_iota(jnp.int32, (outs, width), 0)
    return (lane == core * 2 * outs + part * outs + channel).astype(jnp.float32)


def stem_row(core, width, first, second):
    row = None
    for part, value in enumerate((first, second)):
        column = jnp.sum(jnp.sum(value, 0), 1, keepdims=True)
        term = jnp.sum(column * spot(core, value.shape[1], width, part), 0, keepdims=True)
        row = term if row is None else row + term
    at = lax.broadcasted_iota(jnp.int32, (8, width), 0)
    return jnp.where(at == 2, row, 0.0)


def stem_columns(core, outs, stats_ref):
    row = stats_ref[2:3, :]
    return [
        jnp.sum(row * spot(core, outs, row.shape[1], part), 1, keepdims=True) for part in range(2)
    ]


def upright(row_ref):
    size = row_ref.shape[1]
    at = lax.broadcasted_iota(jnp.int32, (size, size), 0)
    same = at == lax.broadcasted_iota(jnp.int32, (size, size), 1)
    return jnp.sum(jnp.where(same, row_ref[...], 0.0), 1, keepdims=True)


def stem_front_body(
    place_ref, video_ref, weight_ref, pre_out_ref, rows_out_ref, pick_out_ref, extra_ref, flat_ref, parts_ref,
    pre_ref, rows_ref, pick_ref, sems,
):
    segs, colours, size = video_ref.shape
    side = 32
    half = size // 2
    quarter = half // 2
    core = place_ref[0] % 2
    at = lax.broadcasted_iota(jnp.int32, (LANES, size), 0)
    zero = jnp.zeros((LANES - colours, size), jnp.float32)

    def plane_step(seg, _):
        value = jnp.concatenate([video_ref[seg].astype(jnp.float32), zero])
        moving = pltpu.roll(value, LANES - 3, 0) - value
        center = pltpu.roll(value, 6, 0)
        plane = jnp.where(at < 12, moving, jnp.where(at < 15, center, 0.0))
        flat_ref[pl.ds(pl.multiple_of(seg * LANES, LANES), LANES), :] = plane.astype(jnp.bfloat16)
        return 0

    lax.fori_loop(0, segs, plane_step, 0, unroll=4)
    source = lax.broadcasted_iota(jnp.int32, (size, half), 0)
    lane = lax.broadcasted_iota(jnp.int32, (size, half), 1)
    lanes = lax.broadcasted_iota(jnp.int32, (segs * LANES, half), 1)
    for parity in range(2):
        hit = source == 2 * side * (lane // side) + side * parity + lane % side
        rows = jnp.dot(
            flat_ref[...],
            jnp.where(hit, 1.0, 0.0).astype(jnp.bfloat16),
            preferred_element_type=jnp.float32,
        )
        for tap in range(TAPS):
            if (tap - 3) % 2 != parity:
                continue
            shift = (tap - 3 - parity) // 2 * side
            value = rows
            if shift:
                value = pltpu.roll(rows, (-shift) % half, 1)
                inside = lanes < half - shift if shift > 0 else lanes >= -shift
                value = jnp.where(inside, value, 0.0)
            value = value.astype(jnp.bfloat16).reshape(segs, LANES, half)
            rows_ref[:, tap * LANES : (tap + 1) * LANES, :] = value
    weight = weight_ref[...]
    moves = [move(rows_ref, rows_out_ref, sems, 0)]

    def seg_step(seg, _):
        value = jnp.dot(weight, rows_ref[seg], preferred_element_type=jnp.float32)
        value = value.astype(jnp.bfloat16)
        here = pl.ds(pl.multiple_of(seg * LANES, LANES), LANES)
        for tap in range(TAPS):
            parts_ref[tap, here, :] = value[tap * LANES : (tap + 1) * LANES]
        return 0

    lax.fori_loop(0, segs, seg_step, 0, unroll=4)
    source = lax.broadcasted_iota(jnp.int32, (half, quarter), 0)
    lane = lax.broadcasted_iota(jnp.int32, (half, quarter), 1)
    total = None
    for tap in range(TAPS):
        column = 2 * (lane % LANES) + tap - 3
        hit = (source == side * (lane // LANES) + column) & (column >= 0) & (column < side)
        pick = jnp.where(hit, 1.0, 0.0).astype(jnp.bfloat16)
        pick_ref[tap] = pick
        term = jnp.dot(parts_ref[tap], pick, preferred_element_type=jnp.float32)
        total = term if total is None else total + term
    total = total.reshape(segs, LANES, quarter)
    pre_ref[...] = total
    moves += [move(pick_ref, pick_out_ref, sems, 1), move(pre_ref, pre_out_ref, sems, 2)]
    extra_ref[...] = stem_row(core, extra_ref.shape[1], total, total * total)
    for copy in moves:
        copy.wait()


def stem_front(place, video, weight, width):
    segs, _, size = video.shape
    return kernel_call(
        stem_front_body,
        (
            jax.ShapeDtypeStruct((segs, LANES, size // 4), jnp.float32),
            jax.ShapeDtypeStruct((segs, TAPS * LANES, size // 2), jnp.bfloat16),
            jax.ShapeDtypeStruct((TAPS, size // 2, size // 4), jnp.bfloat16),
            jax.ShapeDtypeStruct((8, width), jnp.float32),
        ),
        [scalars, whole, whole],
        (
            pltpu.VMEM((segs * LANES, size), jnp.bfloat16),
            pltpu.VMEM((TAPS, segs * LANES, size // 2), jnp.bfloat16),
            pltpu.VMEM((segs, LANES, size // 4), jnp.float32),
            pltpu.VMEM((segs, TAPS * LANES, size // 2), jnp.bfloat16),
            pltpu.VMEM((TAPS, size // 2, size // 4), jnp.bfloat16),
            pltpu.SemaphoreType.DMA((3,)),
        ),
        away=(0, 1, 2),
        lasts=0.0,
    )(place, video, weight)


def stem_norm(count, core, pre, stats_ref, gain_ref, bias_ref):
    outs = pre.shape[1]
    center, rate = norm_stats(*stem_columns(core, outs, stats_ref), count)
    scaled = (pre - center) * rate
    return scaled, scaled * upright(gain_ref) + upright(bias_ref), upright(gain_ref) * rate


def stem_out_body(count, place_ref, pre_ref, grad_ref, stats_ref, gain_ref, bias_ref, out_ref, extra_ref):
    core = place_ref[0] % 2
    scaled, normed, _ = stem_norm(count, core, pre_ref[...], stats_ref, gain_ref, bias_ref)
    part = logistic(normed)
    out_ref[...] = (normed * part).astype(jnp.bfloat16)
    value = grad_ref[...].astype(jnp.float32) * (part * (1.0 + normed * (1.0 - part)))
    extra_ref[...] = stem_row(core, extra_ref.shape[1], value, value * scaled)


def stem_output(count, place, pre, grad, stats, gain, bias, width):
    return kernel_call(
        functools.partial(stem_out_body, count),
        (
            jax.ShapeDtypeStruct(pre.shape, jnp.bfloat16),
            jax.ShapeDtypeStruct((8, width), jnp.float32),
        ),
        [scalars] + [whole] * 5,
        lasts=1.8,
    )(place, pre, grad, stats, gain.reshape(1, -1), bias.reshape(1, -1))


def stem_back_body(
    count, first, place_ref, pre_ref, grad_ref, stats_ref, back_ref, gain_ref, bias_ref, rows_ref, pick_ref, start_ref, out_ref, slopes_ref,
):
    core = place_ref[0] % 2
    segs, outs, pixels = pre_ref.shape
    scaled, normed, scale = stem_norm(count, core, pre_ref[...], stats_ref, gain_ref, bias_ref)
    bias_grad, gain_grad = stem_columns(core, outs, back_ref)
    value = grad_ref[...].astype(jnp.float32) * silu_slope(normed)
    value = scale * (value - bias_grad / count - scaled * (gain_grad / count))
    value = value.astype(jnp.bfloat16).reshape(segs * outs, pixels)
    half = rows_ref.shape[2]
    for tap in range(TAPS):
        spread = exact(value, pick_ref[tap], ((1,), (1,)))
        slopes_ref[:, tap * LANES : (tap + 1) * LANES, :] = spread.astype(jnp.bfloat16).reshape(
            segs, outs, half
        )
    total = None
    for seg in range(segs):
        term = exact(rows_ref[seg], slopes_ref[seg], ((1,), (1,)))
        total = term if total is None else total + term
    size = TAPS * LANES
    rows = size // 2
    if first:
        out_ref[...] = jnp.zeros_like(out_ref)
    else:
        out_ref[...] = start_ref[...]
    out_ref[:, :size] += total[:rows]
    out_ref[:, 128 : 128 + size] += total[rows:]


def stem_back(count, place, pre, grad, stats, back, gain, bias, rows, pick, start, chunk, chunks):
    segs, outs, pixels = pre.shape
    size = segs // chunks

    def part(*tail):
        return pl.BlockSpec((size,) + tail, lambda at: (chunk, 0, 0))

    def all_of(shape):
        return pl.BlockSpec(shape, lambda at: (0,) * len(shape))

    small = (TAPS * LANES // 2, 256)
    first = start is None
    start = jnp.zeros((8, 256), jnp.float32) if first else start
    return pl.pallas_call(
        functools.partial(stem_back_body, count, first),
        grid=(1,),
        out_shape=jax.ShapeDtypeStruct(small, jnp.float32),
        in_specs=[scalars, part(outs, pixels), part(outs, pixels)]
        + [all_of(stats.shape), all_of(back.shape), all_of((1, outs)), all_of((1, outs))]
        + [part(*rows.shape[1:]), all_of(pick.shape), all_of(start.shape)],
        out_specs=all_of(small),
        scratch_shapes=[pltpu.VMEM((size, TAPS * LANES, rows.shape[2]), jnp.bfloat16)],
        compiler_params=pltpu.CompilerParams(vmem_limit_bytes=vmem_limit),
        cost_estimate=pl.CostEstimate(
            flops=int(1.7 * flops_per_us), bytes_accessed=0, transcendentals=0
        ),
    )(place, pre, grad, stats, back, gain.reshape(1, -1), bias.reshape(1, -1), rows, pick, start)


def stem_weight(center, diff):
    outs = center.shape[1]
    value = jnp.concatenate([diff, center, jnp.zeros((TAPS * TAPS, outs), center.dtype)])
    value = value.reshape(LANES, TAPS, TAPS, outs)
    return value.transpose(2, 3, 1, 0).reshape(TAPS * outs, TAPS * LANES)


def stem_grads_body(packed_ref, center_ref, diff_ref):
    full = jnp.concatenate([packed_ref[:, :128], packed_ref[:, 128:]])
    for row in range(TAPS):
        value = full[row * LANES : (row + 1) * LANES]
        for col in range(TAPS):
            here = value[:, col * LANES : (col + 1) * LANES]
            at = row * TAPS + col
            diff_ref[pl.ds(at, 12, stride=TAPS * TAPS), :] = here[:12]
            center_ref[pl.ds(at, 3, stride=TAPS * TAPS), :] = here[12:15]


def stem_grads(packed, outs):
    return kernel_call(
        stem_grads_body,
        (
            jax.ShapeDtypeStruct((3 * TAPS * TAPS, outs), jnp.float32),
            jax.ShapeDtypeStruct((12 * TAPS * TAPS, outs), jnp.float32),
        ),
        [whole],
    )(packed)


def after(value, *marks):
    return lax.optimization_barrier((value, marks))[0]


def swap(value, axis, bit):
    size = lax.axis_size(axis)
    return lax.ppermute(value, axis, [(at, at ^ bit) for at in range(size)])


def steps_of(axis):
    size = lax.axis_size(axis)
    assert size & (size - 1) == 0
    return [1 << at for at in range(size.bit_length() - 1)]


def sum_over(value, axis, jobs=()):
    jobs = list(jobs)
    for bit in steps_of(axis):
        got = swap(value, axis, bit)
        if jobs:
            got = after(got, jobs.pop(0)(value))
        value = value + got
    for job in jobs:
        value = after(value, job(value))
    return value


def ordered(second, own, other, axis=0):
    return jnp.where(
        second, jnp.concatenate([other, own], axis), jnp.concatenate([own, other], axis)
    )


def gather_rows(value, axis):
    order = [0]
    for bit in reversed(steps_of(axis)):
        value = jnp.concatenate([value, swap(value, axis, bit)])
        order += [at ^ bit for at in order]
    return value, order


def halve_body(bit, parts, far, place_ref, keep_ref, *refs):
    got_refs, refs = refs[:parts], refs[parts:]
    mine_ref, send_ref = refs[:2]
    count, size = send_ref.shape[:2]
    high = (place_ref[1] // bit) % 2
    source, places, moves = keep_ref, [], []
    for block in range(count):
        for side in (1 - high, high):
            here = pl.ds(pl.multiple_of((2 * block + side) * size, size), size)
            places.append((block, side, here))
    if far:
        source, sems = refs[2:]
        moves = [
            move(keep_ref.at[here], source.at[here], sems, at)
            for at, (_, _, here) in enumerate(places)
        ]
    for at, (block, side, here) in enumerate(places):
        if far:
            moves[at].wait()
        value = source[here, :]
        if parts:
            part = block * parts // count
            first = 2 * (block - part * count // parts) + side
            got = got_refs[part][pl.ds(pl.multiple_of(first * size, size), size), :]
            value = value + got.astype(jnp.float32)
        ref = mine_ref if at % 2 else send_ref
        ref[block] = value.astype(ref.dtype)


def halve(place, keep, got, bits, at, far=False):
    rows, width = keep.shape
    left = sorted(bits, reverse=True)
    outer = 1 << left.index(at)
    inner = rows // (2 * outer)
    if inner % BLOCK or outer % max(len(got), 1):
        total = keep + jnp.concatenate(got).astype(jnp.float32) if got else keep
        blocks = total.reshape(outer, 2, inner, width)
        low, high = blocks[:, 0].reshape(-1, width), blocks[:, 1].reshape(-1, width)
        mine = (place[1] // at) % 2 == 0
        return jnp.where(mine, low, high), jnp.where(mine, high, low).astype(jnp.bfloat16)
    shape = (outer, inner, width)
    scratch = [pltpu.VMEM(keep.shape, keep.dtype), pltpu.SemaphoreType.DMA((2 * outer,))]
    mine, send = kernel_call(
        functools.partial(halve_body, at, len(got), far),
        (jax.ShapeDtypeStruct(shape, jnp.float32), jax.ShapeDtypeStruct(shape, jnp.bfloat16)),
        [scalars, remote if far else whole] + [whole] * len(got),
        scratch if far else [],
        lasts=2.0 if far else 0.7,
    )(place, keep, *got)
    return mine.reshape(-1, width), send.reshape(-1, width)


def transposed(left, right):
    return lax.dot_general(
        left, right, (((1,), (1,)), ((), ())), preferred_element_type=jnp.float32
    )


def weight_grad(left, right):
    return lax.dot_general(
        left, right, (((0,), (0,)), ((), ())), preferred_element_type=jnp.float32
    )


def per_device(
    block_in,
    weight_in,
    weight_mid,
    weight_out,
    gain_in,
    bias_in,
    gain_mid,
    bias_mid,
    gain_out,
    bias_out,
    kernel_near,
    kernel_far,
    gate_bias,
    same_video,
    video,
    stem_center,
    stem_diff,
    stem_gain,
    stem_bias,
    block_grad,
    stem_grad,
):
    groups = lax.axis_size("dp")
    assert lax.axis_size("chan") == 4
    clips = same_video.shape[0]
    rows, quarter = block_in.shape
    half = rows // 2
    narrow = weight_in.shape[1]
    width = 2 * narrow
    count = float(rows * groups)
    segs = video.shape[0]
    stem_count = float(segs * stem_grad.shape[2] * groups)
    chan = lax.axis_index("chan")
    core, y = chan % 2, chan // 2
    place = jnp.stack([chan, lax.axis_index("dp")])

    def my_rows(value, which):
        return lax.dynamic_slice_in_dim(value, which * half, half, 0)

    packed = pack_weights(weight_mid, weight_out)
    block_in = after(block_in, packed)
    mine, others = my_rows(block_in, core), my_rows(block_in, 1 - core)
    pieces = [swap(others, "chan", 1), swap(mine, "chan", 2)]
    pieces.append(swap(after(others, pieces[1]), "chan", 3))

    own_in, order = gather_rows(after(weight_in, mine, others), "dp")
    weights_in = [own_in, swap(own_in, "chan", 1)]
    gathered = lax.all_gather(packed, "dp", axis=0)

    params = pack_params([gain_in, bias_in, gain_mid, bias_mid, gate_bias], kernel_near, kernel_far)
    par_own = ordered(core == 1, params, swap(params, "chan", 1), 1)
    pars = [par_own]
    same = lax.dynamic_slice_in_dim(same_video, core * (clips // 2), clips // 2, 0)
    same = jnp.pad(same, ((0, 0), (0, 1)))
    gain_row, bias_row = gain_out.reshape(1, -1), bias_out.reshape(1, -1)

    outs = stem_grad.shape[1]
    pre_stem, stem_rows, stem_pick, extra = stem_front(
        place, video, stem_weight(stem_center, stem_diff), width
    )

    def both_sums(sums, jobs=()):
        jobs = [run or (lambda mark: mark) for run in jobs]
        got = swap(sums, "chan", 1)
        if jobs:
            got = after(got, jobs[0](sums))
        own = sum_over(sums + got, "dp", jobs[1:4])
        oth = swap(own, "chan", 2)
        for run in jobs[4:]:
            oth = after(oth, run(own))
        return [own, oth]

    made = {}

    def in_turn(*works):
        def run(mark):
            results = []
            for work in works:
                results.append(work((mark, results) if results else mark))
            return results

        return run

    def job(name, work):
        def run(mark):
            made[name] = work(mark)
            return made[name]

        return run

    pre_in, sums_in, full_in = first_conv(
        order, place, block_in, pieces, weights_in, after(extra, par_own)
    )
    pre_in_oth = swap(pre_in, "chan", 2)

    blocks = gathered
    if weight_mid.shape[0] % BLOCK:
        blocks = gathered[:, : weight_mid.shape[0]].reshape(1, -1, narrow)
    blocks = after(blocks, sums_in)
    weights_mid = [blocks, swap(blocks, "chan", 1)]

    def out_rows(mark):
        parts, first, size = after(gathered, mark), weight_mid.shape[0], weight_out.shape[0]
        parts = [parts[:, first + at * size : first + (at + 1) * size] for at in range(4)]
        return jnp.concatenate([part.reshape(-1, narrow) for part in parts], 1)

    def own_gate(mark):
        return gate_own(count, same, pre_in, mark, pars[0])

    stats_in = both_sums(
        sums_in,
        [None, None, job("full_out", out_rows), None, job("own", own_gate)],
    )
    pars.append(swap(after(par_own, stats_in[0]), "chan", 2))
    full_out = made["full_out"]

    out_across = swap(after(full_out, stats_in), "chan", 2)

    mixed, pre_mid, pre_mid16, sums_mid = gate_mid(
        count, place, same, made["own"][0], pre_in_oth, stats_in[1], pars[1], weights_mid
    )
    pre_mid_oth = swap(pre_mid16, "chan", 2)
    stats_stem = after(stats_in[0], sums_mid)

    def stem_half(mark):
        return stem_output(
            stem_count, place, after(pre_stem, mark), stem_grad, stats_stem, stem_gain, stem_bias, quarter
        )

    def slab_of(mark):
        slab = after(gathered, mark)[:, : weight_mid.shape[0]].reshape(9, 2, width, narrow)
        return lax.dynamic_slice_in_dim(slab, 1 - y, 1, 1).reshape(9 * width, narrow)

    stats_mid = both_sums(
        sums_mid,
        [
            None,
            job("stem", stem_half),
            in_turn(job("slab", slab_of), lambda mark: out_across),
            job("turned", lambda mark: turn(after(mixed, mark))),
            lambda mark: pre_mid_oth,
        ],
    )
    stem_out, extra = made["stem"]

    second = second_half(count, place, pre_mid, pre_mid_oth, stats_mid, pars)
    second_peer = swap(second, "chan", 1)
    pre_out, sums_out = last_conv(place, second, second_peer, full_out, extra)
    slab_across = swap(after(made["slab"], stats_mid), "chan", 2)
    stats_out = sum_over(sums_out, "dp", [
        job("near_in", lambda mark: lax.dynamic_slice_in_dim(after(full_in, mark), chan * quarter, quarter, 0)),
        job("away_in", lambda mark: lax.dynamic_slice_in_dim(after(full_in, mark), (chan ^ 2) * quarter, quarter, 0)),
    ])
    stats_out = after(stats_out, slab_across)
    out_peers = [swap(after(value, stats_out), "chan", 1) for value in (full_out, out_across)]
    weights_out = [full_out, out_peers[0], out_across, out_peers[1]]
    block_out, grad_total, sums_back, keep, send = out_back(
        count, place, pre_out, block_in, block_grad, stats_out, gain_row, bias_row, full_out
    )
    got = swap(send, "chan", 1)

    def cross(mark):
        return cross_half(place, keep, after(got, mark))

    def stem_part(chunk, start):
        def work(mark):
            return stem_back(
                stem_count, place, after(pre_stem, mark), stem_grad, stats_in[0], stats_out, stem_gain,
                stem_bias, stem_rows, stem_pick, start and made[start], chunk, 4,
            )

        return job(f"stem{chunk}", work)

    back_out = sum_over(
        sums_back, "dp", [stem_part(0, None), job("cross", cross), stem_part(1, "stem0")]
    )
    keep, send = made["cross"]
    got = swap(send, "chan", 2)
    delta = out_delta(count, rows, stats_out, sums_back, back_out, gain_row)
    deltas = [delta] + [swap(delta, "chan", at) for at in (1, 2, 3)]

    grad_mid, grad_mid16, sums_mid_back = mid_slope(
        count, place, keep, got, second, pre_mid, stats_mid[0], pars[0], deltas, weights_out
    )
    grad_mid_oth = swap(grad_mid16, "chan", 2)

    aways_mid = [slab_across, swap(after(slab_across, sums_mid_back), "chan", 1)]

    def out_part(start, rows_of_second):
        def work(mark):
            return out_weight(
                count, place, rows_of_second, pre_out, grad_total, stats_out, after(back_out, mark),
                gain_row, start and made[start],
            )

        return work

    def own_slopes(mark):
        return mid_own(count, grad_mid, pre_mid, stats_mid[0], mark, pars[0])

    bits = steps_of("dp")

    back_mid = both_sums(sums_mid_back, [
        None,
        job("out0", out_part(None, second)),
        job("out1", out_part("out0", second_peer)),
        stem_part(2, "stem1"),
        in_turn(job("slopes", own_slopes), stem_part(3, "stem2")),
    ])
    slopes = made["slopes"]
    sum_out = lax.psum_scatter(made["out1"], "dp", scatter_dimension=0, tiled=True)
    stem_first = swap(made["stem3"], "dp", bits[0])
    far_in = swap(made["away_in"], "chan", 2)

    grad_in, grad_in16, sums_in_back = mid_back(
        count, place, same, slopes, grad_mid_oth, pre_mid_oth, stats_mid[1], back_mid[1], pre_in,
        made["own"][1], stats_in[0], pars, weights_mid, aways_mid,
    )
    grad_in_oth = swap(grad_in16, "chan", 2)

    def mid_part(mark):
        return mid_weight(place, made["turned"], after(slopes, mark))

    def mid_rest(mark):
        keep, *sends = made["mid"]
        got = [after(swap(send, "chan", 1), mark) for send in sends]
        return halve(place, keep, got, mid_bits, mid_bits[0], True)

    mid_bits = bits

    def mid_step(at):
        def work(mark):
            keep, got = made["keep"], after(swap(made["send"], "dp", mid_bits[at - 1]), mark)
            made["keep"], made["send"] = halve(place, keep, [got], mid_bits[at:], mid_bits[at])
            return made["send"]

        return work

    def mid_first(mark):
        made["keep"], made["send"] = mid_rest(mark)
        return made["send"]

    def own_in_back(mark):
        return in_own(
            count, place, grad_in, pre_in, stats_in[0], mark, pars[0], block_in, pieces
        )

    back_in = both_sums(
        sums_in_back,
        [
            lambda mark: stem_first,
            job("mid", mid_part),
            None,
            mid_first,
            job("in", own_in_back),
        ],
    )

    grad_own, keep, send = made["in"]
    got = swap(send, "chan", 1)
    grad_pre = in_other(
        count, place, after(grad_own, send), grad_in_oth, pre_in_oth, stats_in[1], back_in[1], pars[1]
    )
    grad_peer = swap(grad_pre, "chan", 1)
    mark, stem_total, stem_got = grad_pre, made["stem3"], stem_first
    assert len(bits) > 1
    last = len(bits) - 1
    for at, bit in enumerate(bits):
        got = after(got, mark, sum_out) if at == 1 else after(got, mark)
        keep, send = halve(place, keep, [got], bits[at:], bit, at == 0)
        got = swap(send, "dp", bit)
        if at < last:
            mark = mid_step(at + 1)(send)
            if at == 0:
                near = after(made["near_in"], mark)
                mark = grad_block_in = input_grad(
                    place, grad_pre, grad_peer, near, far_in, grad_total
                )
            mark = stem_total = after(stem_total, mark) + stem_got
            stem_got = swap(stem_total, "dp", bits[at + 1])
    sum_mid = after(made["keep"], send) + swap(made["send"], "dp", bit).astype(jnp.float32)
    stem_total = after(stem_total, sum_mid) + stem_got
    sum_in = keep + after(got, stem_total).astype(jnp.float32)
    center_grad, diff_grad = stem_grads(stem_total, outs)

    def my_columns(value):
        return lax.dynamic_slice_in_dim(value, core * narrow, narrow, value.ndim - 1)

    def my_stem(value):
        row = lax.dynamic_slice(value, (2, core * 2 * outs), (1, 2 * outs))[0]
        return row[:outs], row[outs:]

    gate_grads = my_columns(back_in[0][8:])
    mid_grads, in_grads = my_columns(back_mid[0]), my_columns(back_in[0])
    stem_bias_grad, stem_gain_grad = my_stem(stats_out)
    return (
        block_out,
        stem_out,
        grad_block_in,
        sum_in,
        sum_mid,
        sum_out,
        in_grads[1],
        in_grads[0],
        mid_grads[1],
        mid_grads[0],
        back_out[1],
        back_out[0],
        gate_grads[1:10],
        gate_grads[10:19],
        gate_grads[0],
        center_grad,
        diff_grad,
        stem_gain_grad,
        stem_bias_grad,
    )


def solution(mesh):
    placed = (
        P("dp", "chan"),
        P("dp", "chan"),
        P("dp", "chan"),
        P("dp", "chan"),
        P("chan"),
        P("chan"),
        P("chan"),
        P("chan"),
        P("chan"),
        P("chan"),
        P(None, "chan"),
        P(None, "chan"),
        P("chan"),
        P("dp", None),
        P("dp", None, None),
        P(None, "chan"),
        P(None, "chan"),
        P("chan"),
        P("chan"),
        P("dp", "chan"),
        P("dp", "chan", None),
    )
    return jax.shard_map(
        per_device,
        mesh=mesh,
        in_specs=placed,
        out_specs=(
            P("dp", "chan"),
            P("dp", "chan", None),
            P("dp", "chan"),
            P("dp", "chan"),
            P("dp", "chan"),
            P("dp", "chan"),
            P("chan"),
            P("chan"),
            P("chan"),
            P("chan"),
            P("chan"),
            P("chan"),
            P(None, "chan"),
            P(None, "chan"),
            P("chan"),
            P(None, "chan"),
            P(None, "chan"),
            P("chan"),
            P("chan"),
        ),
        check_vma=False,
    )
```

```python
import functools

import jax
import jax.numpy as jnp
from jax import lax
from jax.experimental import pallas as pl
from jax.experimental.pallas import tpu as pltpu
from jax.sharding import PartitionSpec as P

SEG = 8
SIDE = 7
FRAMES = 5
PIXELS = SIDE * SIDE
BLOCK = 16
SPAN = SIDE + 2

eps = 1e-05
vmem_limit = 24 * 1024 * 1024
flops_per_us = 0.3e9

whole = pl.BlockSpec(memory_space=pltpu.VMEM)
remote = pl.BlockSpec(memory_space=pltpu.HBM)
scalars = pl.BlockSpec(memory_space=pltpu.SMEM)


def logistic(value):
    return 0.5 * jnp.tanh(0.5 * value) + 0.5


def silu_slope(value):
    part = logistic(value)
    return part * (1.0 + value * (1.0 - part))


def norm_stats(totals, squares, count):
    center = totals / count
    spread = squares / count - center * center
    return (center, lax.rsqrt(spread + eps))


def move(source, target, sems, at):
    copy = pltpu.make_async_copy(source, target, sems.at[at])
    copy.start()
    return copy


def kernel_call(body, out_shape, in_specs, scratch=(), lasts=1.0, away=(), held=()):
    several = isinstance(out_shape, tuple)
    shapes = list(out_shape) if several else [out_shape]
    specs = [remote if at in away else whole for at in range(len(shapes))]
    shapes = [
        (pltpu.HBM if at in away else pltpu.VMEM)(shape.shape, shape.dtype)
        if at in away or at in held
        else shape
        for at, shape in enumerate(shapes)
    ]
    call = pl.pallas_call(
        body,
        out_shape=tuple(shapes) if several else shapes[0],
        in_specs=in_specs,
        out_specs=tuple(specs) if several else specs[0],
        scratch_shapes=list(scratch),
        compiler_params=pltpu.CompilerParams(vmem_limit_bytes=vmem_limit),
        cost_estimate=pl.CostEstimate(
            flops=int(lasts * flops_per_us), bytes_accessed=0, transcendentals=0
        ),
    )

    def run(*args):
        return call(
            *[
                pltpu.with_memory_space_constraint(arg, pltpu.HBM) if spec is remote else arg
                for arg, spec in zip(args, in_specs, strict=True)
            ]
        )

    return run


PAIRS = SEG // 2
CLIP = SEG * PIXELS


def pair_row(clip, pair):
    return pl.multiple_of(BLOCK * (2 + SPAN * (PAIRS * clip + pair)), BLOCK)


def clip_view(ref, clip, extra=0):
    return ref.at[pl.ds(pl.multiple_of(clip * CLIP, 8), CLIP + extra)]


def lane_mask(width):
    return lax.broadcasted_iota(jnp.int32, (1, 8, width), 1)


def load_map(ref, first, lanes):
    return jnp.stack([ref[pl.ds(first + SIDE * at, 8), lanes] for at in range(SIDE)])


def store_map(ref, first, lanes, value):
    for at in range(SIDE):
        ref[pl.ds(first + SIDE * at, SIDE), lanes] = value[at][:SIDE]


def two_maps(early, late):
    both = jnp.stack([early, late], axis=1)
    return both.reshape(SIDE * BLOCK, early.shape[-1])


def down(value, step):
    zeros = jnp.zeros((abs(step),) + value.shape[1:], value.dtype)
    if step > 0:
        return jnp.concatenate([value[step:], zeros])
    if step < 0:
        return jnp.concatenate([zeros, value[:step]])
    return value


def across(value, step, place):
    if step == 0:
        return value
    moved = pltpu.roll(value, (-step) % 8, 1)
    if step == 2:
        return jnp.where(place < 6, moved, 0.0)
    if step == -2:
        return jnp.where(place > 0, moved, 0.0)
    return moved


def taps_of(near, far):
    for step, kernel in ((1, near), (2, far)):
        for row in range(3):
            yield step, row, [kernel[row * 3 + col] for col in range(3)]


def views_of(value, place):
    return {step: across(value, step, place) for step in (-2, -1, 0, 1, 2)}


def gate_score(change, near, far, offset, place):
    views = views_of(change, place)
    score = jnp.broadcast_to(offset, change.shape)
    for step, row, kernel in taps_of(near, far):
        term = sum(kernel[col] * views[step * (col - 1)] for col in range(3))
        score = score + down(term, step * (row - 1))
    return score


def conv_chunk(parts, weights, first, rows, sign):
    total = None
    for col in (1, 0, 2):
        acc = None
        for row in range(3):
            start = pl.multiple_of(first + BLOCK * (1 + sign * (row - 1)), BLOCK)
            for part, weight in zip(parts, weights, strict=True):
                left = part[pl.ds(start, rows), :]
                term = weight(left, row * 3 + col)
                acc = term if acc is None else acc + term
        acc = acc.reshape(rows // 8, 8, acc.shape[-1])
        shift = sign * (col - 1)
        if shift:
            acc = pltpu.roll(acc, (-shift) % 8, 1)
        total = acc if total is None else total + acc
    return total


def lane_part(index, width=128):
    return pl.ds(pl.multiple_of(index * width, width), width)


def row_part(index, size):
    return pl.ds(pl.multiple_of(index * size, size), size)


def after_sums(ref):
    return ref.at[pl.ds(8, 24)]


def rows_of(stats_ref, first=0):
    return stats_ref[first : first + 1], stats_ref[first + 1 : first + 2]


def put_sums(sums_ref, first, second):
    sums_ref[...] = jnp.zeros_like(sums_ref)
    sums_ref[0:1, :] = first
    sums_ref[1:2, :] = second


def fetch_blocks(sources, core, target_ref, sems, first):
    moves = []
    for side, source in enumerate(sources):
        lanes = lane_part(core if side == 0 else 1 - core)
        blocks = source.shape[0]
        size = target_ref.shape[0] // blocks
        for block in range(blocks):
            here = pl.ds(block * size, size)
            moves.append(
                move(
                    source.at[block, pl.ds(0, size)],
                    target_ref.at[here, lanes],
                    sems,
                    first + side * blocks + block,
                )
            )
    return moves


def gate_half(count, same_ref, pre, stats, par, hidden_ref, mixed_ref, first, gates_ref=None):
    rows, width = pre.shape
    hidden_ref[pl.ds(rows, hidden_ref.shape[0] - rows), :] = jnp.zeros(
        (hidden_ref.shape[0] - rows, width), jnp.float32
    )
    center, rate = norm_stats(*stats, count)
    scaled = (pre[...].astype(jnp.float32) - center) * rate
    normed = scaled * par[0:1] + par[1:2]
    hidden_ref[pl.ds(0, rows), :] = normed * logistic(normed)
    at = lane_mask(128)

    def lanes_step(chunk, _):
        lanes = lane_part(chunk)
        target = pl.ds(pl.multiple_of(first + chunk * 128, 128), 128)
        near = [par[5 + tap : 6 + tap, lanes].reshape(1, 1, 128) for tap in range(9)]
        far = [par[14 + tap : 15 + tap, lanes].reshape(1, 1, 128) for tap in range(9)]
        offset = par[4:5, lanes].reshape(1, 1, 128)

        def clip_step(clip, _):
            view = clip_view(hidden_ref, clip, 56)
            for pair in range(PAIRS):
                maps = [load_map(view, PIXELS * (2 * pair + seg), lanes) for seg in range(3)]
                results = []
                for seg in range(2):
                    same = same_ref[clip, 2 * pair + seg].astype(jnp.float32)
                    change = jnp.where(at < SIDE, same * (maps[seg + 1] - maps[seg]), 0.0)
                    gate = logistic(gate_score(change, near, far, offset, at))
                    results.append(jnp.where(at < SIDE, maps[seg] * (1.0 + gate), 0.0))
                    if gates_ref is not None:
                        gates_ref[SEG * clip + 2 * pair + seg, :, :, lanes] = gate
                place = pl.ds(pair_row(clip, pair), SIDE * BLOCK)
                mixed_ref[place, target] = two_maps(*results).astype(jnp.bfloat16)
            return 0

        return lax.fori_loop(0, rows // CLIP, clip_step, 0)

    lax.fori_loop(0, width // 128, lanes_step, 0)


def gate_mid_body(
    count,
    place_ref,
    same_ref,
    own_ref,
    oth_ref,
    stats_ref,
    par_own_ref,
    par_oth_ref,
    weight_own_ref,
    weight_peer_ref,
    mixed_out_ref,
    gates_out_ref,
    mid_ref,
    mid16_ref,
    sums_ref,
    hidden_ref,
    acc_ref,
    weight_ref,
    own_here_ref,
    mixed_ref,
    gates_ref,
    sems,
):
    rows, width = oth_ref.shape
    clips = rows // CLIP
    core, y = place_ref[0] % 2, place_ref[0] // 2
    arrival = move(own_ref, own_here_ref, sems, 0)
    weight_moves = fetch_blocks((weight_own_ref, weight_peer_ref), core, weight_ref, sems, 5)
    mixed_ref[...] = jnp.zeros_like(mixed_ref)
    arrival.wait()
    gate_half(
        count, same_ref, own_here_ref, rows_of(stats_ref), par_own_ref, hidden_ref, mixed_ref,
        pl.multiple_of(y * width, width), gates_ref,
    )
    gates_move = move(gates_ref, gates_out_ref, sems, 2)
    gate_half(
        count, same_ref, oth_ref, rows_of(stats_ref, 4), after_sums(par_oth_ref), hidden_ref, mixed_ref,
        pl.multiple_of((1 - y) * width, width),
    )
    depth = 2 * width
    for copy in weight_moves:
        copy.wait()
    mixed_move = move(mixed_ref, mixed_out_ref, sems, 3)

    def tap_dot(left, tap):
        return jnp.dot(
            left, weight_ref[tap * depth : (tap + 1) * depth], preferred_element_type=jnp.float32
        )

    def conv_step(clip, _):
        span = PAIRS * SPAN * BLOCK
        total = conv_chunk([mixed_ref], [tap_dot], clip * span, span, 1)
        view = clip_view(acc_ref, clip)
        for seg in range(SEG):
            value = [total[2 * (SPAN * (seg // 2) + 1 + row) + seg % 2] for row in range(SIDE)]
            store_map(view, seg * PIXELS, slice(None), value)
        return 0

    lax.fori_loop(0, clips, conv_step, 0)
    mid_move = move(acc_ref.at[pl.ds(0, rows)], mid_ref, sems, 4)
    result = acc_ref[pl.ds(0, rows), :]
    mid16_ref[...] = result.astype(jnp.bfloat16)
    put_sums(
        sums_ref, jnp.sum(result, 0, keepdims=True), jnp.sum(result * result, 0, keepdims=True)
    )
    for copy in (gates_move, mixed_move, mid_move):
        copy.wait()


def map_rows(rows):
    return (rows // (2 * PIXELS) * SPAN + 2) * BLOCK


def gate_mid(count, place, same, own, oth, stats, pars, weights):
    rows, width = oth.shape
    spread = map_rows(rows)
    depth = 18 * width
    gates = (rows // PIXELS, SIDE, 8, width)
    return kernel_call(
        functools.partial(gate_mid_body, count),
        (
            jax.ShapeDtypeStruct((spread, 2 * width), jnp.bfloat16),
            jax.ShapeDtypeStruct(gates, jnp.float32),
            jax.ShapeDtypeStruct((rows, width), jnp.float32),
            jax.ShapeDtypeStruct((rows, width), jnp.bfloat16),
            jax.ShapeDtypeStruct((8, width), jnp.float32),
        ),
        [scalars, scalars, remote, whole, whole, whole, whole, remote, remote],
        (
            pltpu.VMEM((rows + 56, width), jnp.float32),
            pltpu.VMEM((rows + 8, width), jnp.float32),
            pltpu.VMEM((depth, width), jnp.bfloat16),
            pltpu.VMEM((rows, width), own.dtype),
            pltpu.VMEM((spread, 2 * width), jnp.bfloat16),
            pltpu.VMEM(gates, jnp.float32),
            pltpu.SemaphoreType.DMA((5 + 2 * weights[0].shape[0],)),
        ),
        away=(0, 1, 2),
        lasts=12.0,
    )(place, same, own, oth, stats, *pars, *weights)


def mid_slopes(count, grad, pre, stats, back, par, flat_ref, store):
    rows, width = grad.shape
    flat_ref[pl.ds(rows, flat_ref.shape[0] - rows), :] = jnp.zeros(
        (flat_ref.shape[0] - rows, width), jnp.float32
    )
    center, rate = norm_stats(*rows_of(stats), count)
    scaled = (pre[...].astype(jnp.float32) - center) * rate
    flat_ref[pl.ds(0, rows), :] = (par[2:3] * rate) * (
        grad[...].astype(jnp.float32) - back[0:1] / count - scaled * (back[1:2] / count)
    )
    at = lane_mask(width)

    def clip_step(clip, _):
        view = clip_view(flat_ref, clip, 8)
        for pair in range(PAIRS):
            maps = [
                jnp.where(at < SIDE, load_map(view, PIXELS * (2 * pair + seg), slice(None)), 0.0)
                for seg in range(2)
            ]
            store(pl.ds(pair_row(clip, pair), SIDE * BLOCK), maps, at)
        return 0

    lax.fori_loop(0, rows // CLIP, clip_step, 0)


def mid_own_body(count, d_ref, mid_ref, stats_ref, back_ref, par_ref, slopes_ref, flat_ref, mid_here_ref, d_here_ref, sems):
    arrivals = [move(mid_ref, mid_here_ref, sems, 0), move(d_ref, d_here_ref, sems, 1)]
    slopes_ref[...] = jnp.zeros_like(slopes_ref)

    def store(place, maps, at):
        for col in range(3):
            slopes_ref[col, place, :] = two_maps(
                *[across(value, 1 - col, at) for value in maps]
            ).astype(jnp.bfloat16)

    for copy in arrivals:
        copy.wait()
    mid_slopes(count, d_here_ref, mid_here_ref, stats_ref, back_ref, par_ref, flat_ref, store)


def mid_own(count, d_own, mid, stats, back, par):
    rows, width = d_own.shape
    return kernel_call(
        functools.partial(mid_own_body, count),
        jax.ShapeDtypeStruct((3, map_rows(rows), width), jnp.bfloat16),
        [remote, remote, whole, whole, whole],
        (
            pltpu.VMEM((rows + 56, width), jnp.float32),
            pltpu.VMEM((rows, width), jnp.float32),
            pltpu.VMEM((rows, width), jnp.float32),
            pltpu.SemaphoreType.DMA((2,)),
        ),
        held=(0,),
        lasts=1.7,
    )(d_own, mid, stats, back, par)


def mid_back_body(
    count,
    place_ref,
    same_ref,
    slopes_ref,
    d_oth_ref,
    mid_oth_ref,
    stats_oth_ref,
    back_oth_ref,
    pre_ref,
    gates_ref,
    stats_in_ref,
    par_own_ref,
    par_oth_ref,
    weight_own_ref,
    weight_peer_ref,
    away_own_ref,
    away_peer_ref,
    d_in_out_ref,
    d_in16_ref,
    sums_ref,
    flat_ref,
    oth_ref,
    dmix_ref,
    scaled_ref,
    parts_ref,
    weight_ref,
    weight_oth_ref,
    d_here_ref,
    mid_here_ref,
    pre_here_ref,
    gates_here_ref,
    sems,
):
    rows, width = d_oth_ref.shape
    clips = rows // CLIP
    core, y = place_ref[0] % 2, place_ref[0] // 2
    arrivals = [
        move(d_oth_ref, d_here_ref, sems, 1),
        move(mid_oth_ref, mid_here_ref, sems, 2),
    ]
    weight_moves = fetch_blocks((weight_own_ref, weight_peer_ref), core, weight_ref, sems, 10)
    weight_moves += [
        move(away_own_ref, weight_oth_ref.at[:, lane_part(core)], sems, 3),
        move(away_peer_ref, weight_oth_ref.at[:, lane_part(1 - core)], sems, 4),
    ]
    pre_moves = [
        move(pre_ref, pre_here_ref, sems, 7),
        move(gates_ref, gates_here_ref, sems, 9),
    ]
    oth_ref[...] = jnp.zeros_like(oth_ref)

    def store(place, maps, _):
        oth_ref[place, :] = two_maps(*maps).astype(jnp.bfloat16)

    for copy in arrivals:
        copy.wait()
    mid_slopes(count, d_here_ref, mid_here_ref, stats_oth_ref, back_oth_ref, after_sums(par_oth_ref), flat_ref, store)
    depth = 2 * width
    turned = (((1,), (1,)), ((), ()))
    for copy in weight_moves:
        copy.wait()

    def own_dot(left, tap):
        start = pl.multiple_of(tap * depth + y * width, width)
        return lax.dot_general(
            left, weight_ref[pl.ds(start, width), :], turned, preferred_element_type=jnp.float32
        )

    def oth_dot(left, tap):
        return lax.dot_general(
            left,
            weight_oth_ref[tap * width : (tap + 1) * width],
            turned,
            preferred_element_type=jnp.float32,
        )

    def conv_step(clip, _):
        span = PAIRS * SPAN * BLOCK
        total = conv_chunk([slopes_ref.at[1], oth_ref], [own_dot, oth_dot], clip * span, span, -1)
        dmix_ref[pl.ds(clip * (span // 8), span // 8)] = total
        return 0

    lax.fori_loop(0, clips, conv_step, 0)

    center, rate = norm_stats(*rows_of(stats_in_ref), count)
    for copy in pre_moves:
        copy.wait()
    scaled_ref[pl.ds(0, rows), :] = (pre_here_ref[...] - center) * rate
    scaled_ref[pl.ds(rows, scaled_ref.shape[0] - rows), :] = jnp.zeros(
        (scaled_ref.shape[0] - rows, width), jnp.float32
    )
    parts_ref[...] = jnp.zeros_like(parts_ref)
    at = lane_mask(128)

    def lanes_step(chunk, _):
        lanes = pl.ds(pl.multiple_of(chunk * 128, 128), 128)

        def row_of(index):
            return par_own_ref[index : index + 1, lanes].reshape(1, 1, 128)

        near = [row_of(5 + tap) for tap in range(9)]
        far = [row_of(14 + tap) for tap in range(9)]
        gain, bias = row_of(0), row_of(1)

        def add_part(index, value):
            here = pl.ds(8 * index, 8)
            parts_ref[here, lanes] += jnp.sum(value, 0)

        def clip_step(clip, carry):
            view = clip_view(scaled_ref, clip, 56)
            target = clip_view(flat_ref, clip)
            for pair in range(PAIRS):
                carry = pair_step(clip, pair, carry, view, target)
            return carry

        def pair_step(clip, pair, carry, view, target):
            normed = [
                load_map(view, PIXELS * (2 * pair + seg), lanes) * gain + bias for seg in range(3)
            ]
            parts = [logistic(value) for value in normed]
            hidden = [value * part for value, part in zip(normed, parts, strict=True)]
            for seg in range(2):
                same = same_ref[clip, 2 * pair + seg].astype(jnp.float32)
                change = jnp.where(at < SIDE, same * (hidden[seg + 1] - hidden[seg]), 0.0)
                views = views_of(change, at)
                gate = gates_here_ref[SEG * clip + 2 * pair + seg, :, :, lanes]
                start = 2 * (SPAN * (PAIRS * clip + pair) + 1) + seg
                d_mixed = jnp.stack([dmix_ref[start + 2 * row, :, lanes] for row in range(SIDE)])
                d_mixed = jnp.where(at < SIDE, d_mixed, 0.0)
                d_score = d_mixed * hidden[seg] * (gate * (1.0 - gate))
                add_part(0, d_score)
                backs = {step: across(d_score, step, at) for step in (-2, -1, 0, 1, 2)}
                d_change = None
                for index, (step, row, kernel) in enumerate(taps_of(near, far)):
                    here = down(d_score, -step * (row - 1))
                    for col in range(3):
                        if index != 4 or col != 1:
                            add_part(1 + 3 * index + col, here * views[step * (col - 1)])
                    term = sum(kernel[col] * backs[-step * (col - 1)] for col in range(3))
                    term = down(term, -step * (row - 1))
                    d_change = term if d_change is None else d_change + term
                d_change = jnp.where(at < SIDE, same * d_change, 0.0)
                d_hidden = d_mixed * (1.0 + gate) - d_change + carry
                carry = d_change
                slope = parts[seg] * (1.0 + normed[seg] * (1.0 - parts[seg]))
                store_map(target, PIXELS * (2 * pair + seg), lanes, d_hidden * slope)
            return carry

        lax.fori_loop(0, clips, clip_step, jnp.zeros((SIDE, 8, 128), jnp.float32))
        return 0

    lax.fori_loop(0, width // 128, lanes_step, 0)
    d_in_move = move(flat_ref.at[pl.ds(0, rows)], d_in_out_ref, sems, 8)
    result = flat_ref[pl.ds(0, rows), :]
    d_in16_ref[...] = result.astype(jnp.bfloat16)
    put_sums(
        sums_ref,
        jnp.sum(result, 0, keepdims=True),
        jnp.sum(result * scaled_ref[pl.ds(0, rows), :], 0, keepdims=True),
    )
    parts_ref[pl.ds(8 * 14, 8), :] = parts_ref[pl.ds(8 * 5, 8), :]
    sums_ref[8:32, :] = jnp.sum(parts_ref[...].reshape(24, 8, width), 1)
    d_in_move.wait()


def mid_back(
    count, place, same, slopes, d_oth, mid_oth, stats_oth, back_oth, pre, gates, stats_in, pars, weights, aways
):
    rows, width = d_oth.shape
    spread = map_rows(rows)
    depth = 18 * width
    return kernel_call(
        functools.partial(mid_back_body, count),
        (
            jax.ShapeDtypeStruct((rows, width), jnp.float32),
            jax.ShapeDtypeStruct((rows, width), jnp.bfloat16),
            jax.ShapeDtypeStruct((32, width), jnp.float32),
        ),
        [scalars, scalars, whole, remote, remote, whole, whole, remote, remote]
        + [whole] * 3
        + [remote] * 4,
        (
            pltpu.VMEM((rows + 56, width), jnp.float32),
            pltpu.VMEM((spread, width), jnp.bfloat16),
            pltpu.VMEM((spread // 8, 8, width), jnp.float32),
            pltpu.VMEM((rows + 56, width), jnp.float32),
            pltpu.VMEM((24 * 8, width), jnp.float32),
            pltpu.VMEM((depth, width), jnp.bfloat16),
            pltpu.VMEM((depth // 2, width), jnp.bfloat16),
            pltpu.VMEM((rows, width), jnp.bfloat16),
            pltpu.VMEM((rows, width), jnp.bfloat16),
            pltpu.VMEM((rows, width), jnp.float32),
            pltpu.VMEM(gates.shape, jnp.float32),
            pltpu.SemaphoreType.DMA((10 + 2 * weights[0].shape[0],)),
        ),
        away=(0,),
        lasts=11.5,
    )(
        place, same, slopes, d_oth, mid_oth, stats_oth, back_oth, pre, gates, stats_in, *pars, *weights,
        *aways,
    )


def turn_body(mixed_ref, out_ref, mixed_here_ref, sems):
    move(mixed_ref, mixed_here_ref, sems, 0).wait()
    out_ref[...] = mixed_here_ref[pl.ds(BLOCK, out_ref.shape[1]), :].T


def turn(mixed):
    spread, depth = mixed.shape
    return kernel_call(
        turn_body,
        jax.ShapeDtypeStruct((depth, spread - 2 * BLOCK), jnp.bfloat16),
        [remote],
        (pltpu.VMEM(mixed.shape, jnp.bfloat16), pltpu.SemaphoreType.DMA((1,))),
        held=(0,),
        lasts=1.6,
    )(mixed)


def mid_weight_body(place_ref, turned_ref, slopes_ref, keep_ref, early_ref, late_ref, keep_here_ref, sems):
    depth, rows = turned_ref.shape
    half = keep_ref.shape[1]
    cut = early_ref.shape[0]
    first = place_ref[0] % 2 == 0
    moves = []
    for tap in range(9):
        row, col = tap // 3, tap % 3
        right = slopes_ref[col, pl.ds(BLOCK * (2 - row), rows), :]
        value = jnp.dot(turned_ref[...], right, preferred_element_type=jnp.float32)
        low, high = value[:, :half], value[:, half:]
        here = pl.ds(tap * depth, depth)
        keep_here_ref[here, :] = jnp.where(first, low, high)
        moves.append(move(keep_here_ref.at[here], keep_ref.at[here], sems, tap))
        send = jnp.where(first, high, low).astype(jnp.bfloat16)
        middle = min(max(cut - tap * depth, 0), depth)
        if middle > 0:
            early_ref[tap * depth : tap * depth + middle] = send[:middle]
        if middle < depth:
            late_ref[tap * depth + middle - cut : (tap + 1) * depth - cut] = send[middle:]
    for copy in moves:
        copy.wait()


def mid_weight(place, turned, slopes):
    depth, rows = turned.shape
    width = slopes.shape[2]
    part = jax.ShapeDtypeStruct((9 * depth // 2, width // 2), jnp.bfloat16)
    return kernel_call(
        mid_weight_body,
        (jax.ShapeDtypeStruct((9 * depth, width // 2), jnp.float32), part, part),
        [scalars, whole, whole],
        (pltpu.VMEM((9 * depth, width // 2), jnp.float32), pltpu.SemaphoreType.DMA((9,))),
        away=(0,),
        lasts=4.8,
    )(place, turned, slopes)


def first_conv_body(
    order,
    place_ref,
    block_ref,
    peer_ref,
    across_ref,
    corner_ref,
    own_ref,
    other_ref,
    extra_ref,
    par_ref,
    pre_out_ref,
    pre16_ref,
    sums_ref,
    cross_ref,
    near_ref,
    away_ref,
    pre_ref,
    weight_ref,
    pieces_ref,
    sems,
):
    rows = peer_ref.shape[0]
    quarter = block_ref.shape[1]
    chan, group = place_ref[0], place_ref[1]
    core = chan % 2
    sources = (block_ref.at[row_part(core, rows)], peer_ref, across_ref)
    arrivals = [
        move(source, pieces_ref.at[at], sems, 3 + at) for at, source in enumerate(sources)
    ]
    size = own_ref.shape[0] // len(order)
    for at, bits in enumerate(order):
        here = row_part(group ^ bits, size)
        weight_ref[here, lane_part(core)] = own_ref[at * size : (at + 1) * size]
        weight_ref[here, lane_part(1 - core)] = other_ref[at * size : (at + 1) * size]
    weight_moves = [
        move(weight_ref.at[row_part(chan, quarter)], near_ref, sems, 0),
        move(weight_ref.at[row_part(chan ^ 2, quarter)], away_ref, sems, 2),
    ]
    total = None
    for at in range(4):
        if at < 3:
            arrivals[at].wait()
        piece = pieces_ref[at] if at < 3 else corner_ref[...]
        weight = weight_ref[row_part(chan ^ at, quarter), :]
        term = jnp.dot(piece, weight, preferred_element_type=jnp.float32)
        total = term if total is None else total + term
    pre_ref[...] = total
    pre_move = move(pre_ref, pre_out_ref, sems, 1)
    pre16_ref[...] = total.astype(jnp.bfloat16)
    sums_ref[...] = extra_ref[...]
    cross_ref[0:8, :] = jnp.zeros((8, cross_ref.shape[1]), jnp.float32)
    cross_ref[8:32, :] = par_ref[...]
    for at, value in enumerate((total, total * total)):
        row = jnp.sum(value, 0, keepdims=True)
        sums_ref[at : at + 1, :] = row
        cross_ref[4 + at : 5 + at, :] = row
    for copy in weight_moves:
        copy.wait()
    pre_move.wait()


def first_conv(order, place, block, pieces, weights, extra, par):
    rows, quarter = pieces[0].shape
    width = 2 * weights[0].shape[1]
    return kernel_call(
        functools.partial(first_conv_body, order),
        (
            jax.ShapeDtypeStruct((rows, width), jnp.float32),
            jax.ShapeDtypeStruct((rows, width), jnp.bfloat16),
            jax.ShapeDtypeStruct((8, width), jnp.float32),
            jax.ShapeDtypeStruct((32, width), jnp.float32),
            jax.ShapeDtypeStruct((quarter, width), jnp.bfloat16),
            jax.ShapeDtypeStruct((quarter, width), jnp.bfloat16),
        ),
        [scalars, remote, remote, remote] + [whole] * 5,
        (
            pltpu.VMEM((rows, width), jnp.float32),
            pltpu.VMEM((4 * quarter, width), jnp.bfloat16),
            pltpu.VMEM((3, rows, quarter), jnp.bfloat16),
            pltpu.SemaphoreType.DMA((6,)),
        ),
        away=(0, 4, 5),
        lasts=4.0,
    )(place, block, *pieces, *weights, extra, par)


def second_body(
    count, place_ref, own_ref, oth_ref, stats_own_ref, stats_oth_ref, par_own_ref, par_oth_ref, out_ref,
    oth_here_ref, sems,
):
    width = own_ref.shape[1]
    y = place_ref[0] // 2
    arrivals = [move(oth_ref, oth_here_ref, sems, 0)]
    for side, pre, stats, par in (
        (y, own_ref, stats_own_ref, par_own_ref),
        (1 - y, oth_here_ref, stats_oth_ref, after_sums(par_oth_ref)),
    ):
        center, rate = norm_stats(*rows_of(stats), count)
        normed = (pre[...].astype(jnp.float32) - center) * rate * par[2:3] + par[3:4]
        out_ref[:, lane_part(side, width)] = (normed * logistic(normed)).astype(jnp.bfloat16)
        for copy in arrivals:
            copy.wait()
        arrivals = []


def second_half(count, place, own, oth, stats, pars):
    rows, width = own.shape
    return kernel_call(
        functools.partial(second_body, count),
        jax.ShapeDtypeStruct((rows, 2 * width), jnp.bfloat16),
        [scalars, whole, remote, whole, whole, whole, whole],
        (
            pltpu.VMEM((rows, width), jnp.bfloat16),
            pltpu.SemaphoreType.DMA((1,)),
        ),
        lasts=1.9,
    )(place, own, oth, *stats, *pars)


def last_conv_body(place_ref, mine_ref, peer_ref, weight_ref, extra_ref, out_ref, sums_ref):
    rows = mine_ref.shape[0]
    core = place_ref[0] % 2
    sums = squares = 0.0
    for side, part in ((core, mine_ref), (1 - core, peer_ref)):
        value = jnp.dot(part[...], weight_ref[...], preferred_element_type=jnp.float32)
        out_ref[row_part(side, rows), :] = value
        sums += jnp.sum(value, 0, keepdims=True)
        squares += jnp.sum(value * value, 0, keepdims=True)
    sums_ref[...] = extra_ref[...]
    sums_ref[0:1, :] = sums
    sums_ref[1:2, :] = squares


def last_conv(place, mine, peer, weight, extra):
    rows, depth = mine.shape
    width = weight.shape[1]
    return kernel_call(
        last_conv_body,
        (
            jax.ShapeDtypeStruct((2 * rows, width), jnp.float32),
            jax.ShapeDtypeStruct((8, width), jnp.float32),
        ),
        [scalars] + [whole] * 4,
        lasts=2.3,
    )(place, mine, peer, weight, extra)


def out_back_body(
    count,
    place_ref,
    pre_ref,
    block_ref,
    grad_ref,
    stats_ref,
    gain_ref,
    bias_ref,
    weight_ref,
    out_ref,
    total_out_ref,
    sums_ref,
    keep_ref,
    send_ref,
    total_ref,
    weight_here_ref,
    sems,
):
    rows = keep_ref.shape[0]
    weight_move = move(weight_ref, weight_here_ref, sems, 1)
    core = place_ref[0] % 2
    center, rate = norm_stats(*rows_of(stats_ref), count)
    gain, bias = gain_ref[...], bias_ref[...]
    step = rows // 7

    def add_step(at, sums):
        here = row_part(at, step)
        scaled = (pre_ref[here, :] - center) * rate
        total = scaled * gain + bias + block_ref[here, :].astype(jnp.float32)
        part = logistic(total)
        out_ref[here, :] = (total * part).astype(jnp.bfloat16)
        value = grad_ref[here, :].astype(jnp.float32) * (part * (1.0 + total * (1.0 - part)))
        total_ref[here, :] = value
        return (
            sums[0] + jnp.sum(value, 0, keepdims=True),
            sums[1] + jnp.sum(value * scaled, 0, keepdims=True),
        )

    zero = jnp.zeros((1, pre_ref.shape[1]), jnp.float32)
    sums, products = lax.fori_loop(0, 14, add_step, (zero, zero))
    put_sums(sums_ref, sums, products)
    total_move = move(total_ref, total_out_ref, sems, 0)
    local = 1.0 / (2 * rows)
    weight_move.wait()

    def slope_rows(side):
        here = row_part(side, rows)
        scaled = (pre_ref[here, :] - center) * rate
        value = gain * rate * (total_ref[here, :] - sums * local - scaled * (products * local))
        return lax.dot_general(
            value.astype(jnp.bfloat16),
            weight_here_ref[...],
            (((1,), (1,)), ((), ())),
            preferred_element_type=jnp.float32,
        )

    send_ref[...] = slope_rows(1 - core).astype(jnp.bfloat16)
    keep_ref[...] = slope_rows(core)
    total_move.wait()


def out_back(count, place, pre, block, grad, stats, gain, bias, weight):
    rows, width = pre.shape
    depth = weight.shape[0]
    return kernel_call(
        functools.partial(out_back_body, count),
        (
            jax.ShapeDtypeStruct((rows, width), jnp.bfloat16),
            jax.ShapeDtypeStruct((rows, width), jnp.float32),
            jax.ShapeDtypeStruct((8, width), jnp.float32),
            jax.ShapeDtypeStruct((rows // 2, depth), jnp.float32),
            jax.ShapeDtypeStruct((rows // 2, depth), jnp.bfloat16),
        ),
        [scalars] + [whole] * 6 + [remote],
        (
            pltpu.VMEM((rows, width), jnp.float32),
            pltpu.VMEM(weight.shape, weight.dtype),
            pltpu.SemaphoreType.DMA((2,)),
        ),
        away=(1,),
        lasts=7.5,
    )(place, pre, block, grad, stats, gain, bias, weight)


def cross_body(place_ref, keep_ref, got_ref, own_ref, send_ref):
    width = own_ref.shape[1]
    y = place_ref[0] // 2
    for lanes, ref in ((1 - y, send_ref), (y, own_ref)):
        here = lane_part(lanes, width)
        value = keep_ref[:, here] + got_ref[:, here].astype(jnp.float32)
        ref[...] = value.astype(ref.dtype)


def cross_half(place, keep, got):
    rows, width = keep.shape[0], keep.shape[1] // 2
    return kernel_call(
        cross_body,
        (
            jax.ShapeDtypeStruct((rows, width), jnp.float32),
            jax.ShapeDtypeStruct((rows, width), jnp.bfloat16),
        ),
        [scalars, whole, whole],
        lasts=0.7,
    )(place, keep, got)


def out_delta_body(count, local, stats_ref, sums_ref, back_ref, gain_ref, out_ref):
    center, rate = norm_stats(*rows_of(stats_ref), count)
    scale = gain_ref[...] * rate
    first = scale * (back_ref[0:1] / count - sums_ref[0:1] * local)
    second = scale * rate * (back_ref[1:2] / count - sums_ref[1:2] * local)
    put_sums(out_ref, first - second * center, second)


def out_delta(count, rows, stats, sums, back, gain):
    return kernel_call(
        functools.partial(out_delta_body, count, 1.0 / rows),
        jax.ShapeDtypeStruct(stats.shape, jnp.float32),
        [whole] * 4,
    )(stats, sums, back, gain)


def mid_slope_body(
    count,
    place_ref,
    keep_ref,
    got_ref,
    second_ref,
    mid_ref,
    stats_ref,
    par_ref,
    deltas0_ref,
    deltas1_ref,
    deltas2_ref,
    deltas3_ref,
    weights0_ref,
    weights1_ref,
    weights2_ref,
    weights3_ref,
    out_ref,
    out16_ref,
    sums_ref,
    here_ref,
    sems,
):
    width = mid_ref.shape[1]
    y = place_ref[0] // 2
    turned = (((1,), (1,)), ((), ()))
    factor, offset = None, None
    for deltas, weights in (
        (deltas0_ref, weights0_ref),
        (deltas1_ref, weights1_ref),
        (deltas2_ref, weights2_ref),
        (deltas3_ref, weights3_ref),
    ):
        own = weights[row_part(y, width), :]
        left = (weights[...].astype(jnp.float32) * deltas[1:2]).astype(jnp.bfloat16)
        term = lax.dot_general(left, own, turned, preferred_element_type=jnp.float32)
        factor = term if factor is None else factor + term
        high = deltas[0:1].astype(jnp.bfloat16).astype(jnp.float32)
        both = jnp.concatenate([high, deltas[0:1] - high, jnp.zeros_like(deltas[2:8])])
        term = lax.dot_general(
            both.astype(jnp.bfloat16), own, turned, preferred_element_type=jnp.float32
        )
        term = term[0:1] + term[1:2]
        offset = term if offset is None else offset + term
    high = factor.astype(jnp.bfloat16)
    low = (factor - high.astype(jnp.float32)).astype(jnp.bfloat16)
    delta = jnp.dot(second_ref[...], high, preferred_element_type=jnp.float32)
    delta += jnp.dot(second_ref[...], low, preferred_element_type=jnp.float32)
    grad = keep_ref[...] + got_ref[...].astype(jnp.float32) - delta - offset
    center, rate = norm_stats(*rows_of(stats_ref), count)
    scaled = (mid_ref[...] - center) * rate
    normed = scaled * par_ref[2:3] + par_ref[3:4]
    result = grad * silu_slope(normed)
    here_ref[...] = result
    out_move = move(here_ref, out_ref, sems, 0)
    out16_ref[...] = result.astype(jnp.bfloat16)
    put_sums(
        sums_ref, jnp.sum(result, 0, keepdims=True), jnp.sum(result * scaled, 0, keepdims=True)
    )
    out_move.wait()


def mid_slope(count, place, keep, got, second, mid, stats, par, deltas, weights):
    rows, width = mid.shape
    return kernel_call(
        functools.partial(mid_slope_body, count),
        (
            jax.ShapeDtypeStruct((rows, width), jnp.float32),
            jax.ShapeDtypeStruct((rows, width), jnp.bfloat16),
            jax.ShapeDtypeStruct((8, width), jnp.float32),
        ),
        [scalars] + [whole] * 14,
        (pltpu.VMEM((rows, width), jnp.float32), pltpu.SemaphoreType.DMA((1,))),
        away=(0,),
        lasts=3.3,
    )(place, keep, got, second, mid, stats, par, *deltas, *weights)


def out_weight_body(
    count, part, place_ref, rows_ref, pre_ref, total_ref, stats_ref, back_ref, gain_ref, *refs
):
    rows = rows_ref.shape[0]
    core = place_ref[0] % 2
    center, rate = norm_stats(*rows_of(stats_ref), count)
    here = row_part(1 - core if part else core, rows)
    scaled = (pre_ref[here, :] - center) * rate
    value = (gain_ref[...] * rate) * (
        total_ref[here, :] - back_ref[0:1] / count - scaled * (back_ref[1:2] / count)
    )
    result = exact(rows_ref[...], value.astype(jnp.bfloat16), ((0,), (0,)))
    if part:
        start_ref, out_ref, here_ref, sems = refs
        here_ref[...] = start_ref[...] + result
        move(here_ref, out_ref, sems, 0).wait()
    else:
        refs[0][...] = result


def out_weight(count, place, second, pre, total, stats, back, gain, start=None):
    rows, depth = second.shape
    width = pre.shape[1]
    part = 0 if start is None else 1
    return kernel_call(
        functools.partial(out_weight_body, count, part),
        jax.ShapeDtypeStruct((depth, width), jnp.float32),
        [scalars] + [whole] * (6 + part),
        (pltpu.VMEM((depth, width), jnp.float32), pltpu.SemaphoreType.DMA((1,))) if part else (),
        away=(0,) if part else (),
        lasts=1.7,
    )(place, second, pre, total, stats, back, gain, *([start] if part else []))


def in_slopes(count, grad, pre, stats, back, par):
    center, rate = norm_stats(*stats, count)
    scaled = (pre[...].astype(jnp.float32) - center) * rate
    value = (par[0:1] * rate) * (
        grad[...].astype(jnp.float32) - back[0:1] / count - scaled * (back[1:2] / count)
    )
    return value.astype(jnp.bfloat16)


def in_own_body(
    count, place_ref, d_ref, pre_ref, stats_ref, back_ref, par_ref, block_ref, peer_ref, across_ref, corner_ref,
    out_ref, keep_ref, send_ref, d_here_ref, pre_here_ref, keep_here_ref, pieces_ref, sems,
):
    rows, width = d_ref.shape
    arrivals = [move(d_ref, d_here_ref, sems, 0), move(pre_ref, pre_here_ref, sems, 1)]
    half = width // 2
    quarter = block_ref.shape[1]
    chan = place_ref[0]
    core = chan % 2
    sources = (block_ref.at[row_part(core, rows)], peer_ref, across_ref, corner_ref)
    pieces = [
        move(source, pieces_ref.at[at], sems, 6 + at) for at, source in enumerate(sources)
    ]
    for copy in arrivals:
        copy.wait()
    own = in_slopes(count, d_here_ref, pre_here_ref, rows_of(stats_ref), back_ref, par_ref)
    out_ref[...] = own
    moves = []
    for at, arrival in enumerate(pieces):
        arrival.wait()
        value = lax.dot_general(
            pieces_ref[at], own, (((0,), (0,)), ((), ())), preferred_element_type=jnp.float32
        )
        here = row_part(chan ^ at, quarter)
        low, high = value[:, :half], value[:, half:]
        keep_here_ref[here, :] = jnp.where(core == 0, low, high)
        moves.append(move(keep_here_ref.at[here], keep_ref.at[here], sems, 2 + at))
        send_ref[here, :] = jnp.where(core == 0, high, low).astype(jnp.bfloat16)
    for copy in moves:
        copy.wait()


def in_own(count, place, d_own, pre, stats, back, par, block, pieces):
    rows, width = d_own.shape
    full = 4 * block.shape[1]
    return kernel_call(
        functools.partial(in_own_body, count),
        (
            jax.ShapeDtypeStruct((rows, width), jnp.bfloat16),
            jax.ShapeDtypeStruct((full, width // 2), jnp.float32),
            jax.ShapeDtypeStruct((full, width // 2), jnp.bfloat16),
        ),
        [scalars, remote, remote] + [whole] * 3 + [remote] * 4,
        (
            pltpu.VMEM((rows, width), jnp.float32),
            pltpu.VMEM((rows, width), jnp.float32),
            pltpu.VMEM((full, width // 2), jnp.float32),
            pltpu.VMEM((4, rows, block.shape[1]), block.dtype),
            pltpu.SemaphoreType.DMA((10,)),
        ),
        away=(1,),
        lasts=4.5,
    )(place, d_own, pre, stats, back, par, block, *pieces)


def in_other_body(
    count, place_ref, own_ref, d_ref, pre_ref, stats_ref, back_ref, par_ref, out_ref, pre_here_ref, sems
):
    width = d_ref.shape[1]
    y = place_ref[0] // 2
    arrival = move(pre_ref, pre_here_ref, sems, 0)
    out_ref[:, lane_part(y, width)] = own_ref[...]
    arrival.wait()
    value = in_slopes(count, d_ref, pre_here_ref, rows_of(stats_ref, 4), back_ref, after_sums(par_ref))
    out_ref[:, lane_part(1 - y, width)] = value


def in_other(count, place, own, d_oth, pre_oth, stats, back, par):
    rows, width = d_oth.shape
    return kernel_call(
        functools.partial(in_other_body, count),
        jax.ShapeDtypeStruct((rows, 2 * width), jnp.bfloat16),
        [scalars, whole, whole, remote, whole, whole, whole],
        (pltpu.VMEM((rows, width), pre_oth.dtype), pltpu.SemaphoreType.DMA((1,))),
        lasts=2.0,
    )(place, own, d_oth, pre_oth, stats, back, par)


def input_grad_body(place_ref, mine_ref, peer_ref, near_ref, far_ref, total_ref, out_ref):
    rows = mine_ref.shape[0]
    width = near_ref.shape[1]
    core, y = place_ref[0] % 2, place_ref[0] // 2
    turned = (((1,), (1,)), ((), ()))
    for side, part in ((core, mine_ref), (1 - core, peer_ref)):
        here = row_part(side, rows)
        value = total_ref[here, :]
        for lanes, weight in ((y, near_ref), (1 - y, far_ref)):
            value += lax.dot_general(
                part[:, lane_part(lanes, width)],
                weight[...],
                turned,
                preferred_element_type=jnp.float32,
            )
        out_ref[here, :] = value.astype(jnp.bfloat16)


def input_grad(place, mine, peer, near, far, total):
    rows, quarter = total.shape
    return kernel_call(
        input_grad_body,
        jax.ShapeDtypeStruct((rows, quarter), jnp.bfloat16),
        [scalars] + [whole] * 5,
        lasts=2.8,
    )(place, mine, peer, near, far, total)


def opening_body(
    place_ref, block_ref, mid_ref, out_ref, mine_ref, others_ref, packed_ref, rows_ref, small_ref, sems
):
    rows = mine_ref.shape[0]
    core = place_ref[0] % 2
    count, width = mid_ref.shape
    size = out_ref.shape[0]
    sources = [(block_ref.at[row_part(side, rows)], rows_ref.at[at]) for at, side in ((0, core), (1, 1 - core))]
    sources.append((mid_ref, small_ref.at[pl.ds(0, count)]))
    for at in range(4):
        here = small_ref.at[pl.ds(count + at * size, size)]
        sources.append((out_ref.at[:, pl.ds(at * width, width)], here))
    arrivals = [move(*pair, sems, at) for at, pair in enumerate(sources)]
    moves = []
    for at, target in enumerate((mine_ref, others_ref)):
        arrivals[at].wait()
        moves.append(move(rows_ref.at[at], target, sems, 7 + at))
    for copy in arrivals[2:]:
        copy.wait()
    moves.append(move(small_ref, packed_ref, sems, 9))
    for copy in moves:
        copy.wait()


def opening(place, block, mid, out):
    half = block.shape[0] // 2
    rows, width = mid.shape
    size = out.shape[0]
    if size % BLOCK or rows % BLOCK:
        parts = [out[:, at * width : (at + 1) * width] for at in range(4)]
        core = place[0] % 2
        halves = [
            lax.dynamic_slice_in_dim(block, side * half, half, 0) for side in (core, 1 - core)
        ]
        return (*halves, jnp.concatenate([mid] + parts, 0))
    rows_shape = jax.ShapeDtypeStruct((half, block.shape[1]), block.dtype)
    return kernel_call(
        opening_body,
        (rows_shape, rows_shape, jax.ShapeDtypeStruct((rows + 4 * size, width), mid.dtype)),
        [scalars, remote, remote, remote],
        (
            pltpu.VMEM((2, half, block.shape[1]), block.dtype),
            pltpu.VMEM((rows + 4 * size, width), mid.dtype),
            pltpu.SemaphoreType.DMA((10,)),
        ),
        away=(0, 1, 2),
    )(place, block, mid, out)


def pack_body(gain_in, bias_in, gain_mid, bias_mid, gate_bias, near, far, stem_gain, stem_bias, out_ref, stem_ref):
    stem_ref[...] = jnp.zeros_like(stem_ref)
    stem_ref[0:1, :] = stem_gain[...]
    stem_ref[1:2, :] = stem_bias[...]
    for at, ref in enumerate((gain_in, bias_in, gain_mid, bias_mid, gate_bias)):
        out_ref[at : at + 1, :] = ref[...]
    out_ref[5:14, :] = near[...]
    out_ref[14:23, :] = far[...]
    out_ref[23:24, :] = jnp.zeros_like(out_ref[23:24, :])


def pack_params(rows, near, far, stem):
    width, outs = near.shape[1], stem[0].shape[0]
    return kernel_call(
        pack_body,
        (
            jax.ShapeDtypeStruct((24, width), jnp.float32),
            jax.ShapeDtypeStruct((8, outs), jnp.float32),
        ),
        [whole] * 9,
    )(*[row.reshape(1, width) for row in rows], near, far, *[row.reshape(1, outs) for row in stem])


TAPS = 7
LANES = 16


def exact(left, right, contract):
    return lax.dot_general(
        left, right, (contract, ((), ())), preferred_element_type=jnp.float32
    )


def spot(core, outs, width, part):
    lane = lax.broadcasted_iota(jnp.int32, (outs, width), 1)
    channel = lax.broadcasted_iota(jnp.int32, (outs, width), 0)
    return (lane == core * 2 * outs + part * outs + channel).astype(jnp.float32)


def stem_row(core, width, first, second):
    row = None
    for part, value in enumerate((first, second)):
        column = jnp.sum(jnp.sum(value, 0), 1, keepdims=True)
        term = jnp.sum(column * spot(core, value.shape[1], width, part), 0, keepdims=True)
        row = term if row is None else row + term
    at = lax.broadcasted_iota(jnp.int32, (8, width), 0)
    return jnp.where(at == 2, row, 0.0)


def stem_columns(core, outs, stats_ref):
    row = stats_ref[2:3, :]
    return [
        jnp.sum(row * spot(core, outs, row.shape[1], part), 1, keepdims=True) for part in range(2)
    ]


def upright(row):
    size = row.shape[1]
    at = lax.broadcasted_iota(jnp.int32, (size, size), 0)
    same = at == lax.broadcasted_iota(jnp.int32, (size, size), 1)
    return jnp.sum(jnp.where(same, row, 0.0), 1, keepdims=True)


def stem_front_body(
    place_ref, video_ref, weight_ref, pre_out_ref, rows_out_ref, pick_out_ref, extra_ref, flat_ref, parts_ref,
    pre_ref, rows_ref, pick_ref, sems,
):
    segs, colours, size = video_ref.shape
    side = 32
    half = size // 2
    quarter = half // 2
    core = place_ref[0] % 2
    at = lax.broadcasted_iota(jnp.int32, (LANES, size), 0)
    zero = jnp.zeros((LANES - colours, size), jnp.float32)

    def plane_step(seg, _):
        value = jnp.concatenate([video_ref[seg].astype(jnp.float32), zero])
        moving = pltpu.roll(value, LANES - 3, 0) - value
        center = pltpu.roll(value, 6, 0)
        plane = jnp.where(at < 12, moving, jnp.where(at < 15, center, 0.0))
        flat_ref[pl.ds(pl.multiple_of(seg * LANES, LANES), LANES), :] = plane.astype(jnp.bfloat16)
        return 0

    lax.fori_loop(0, segs, plane_step, 0, unroll=4)
    source = lax.broadcasted_iota(jnp.int32, (size, half), 0)
    lane = lax.broadcasted_iota(jnp.int32, (size, half), 1)
    lanes = lax.broadcasted_iota(jnp.int32, (segs * LANES, half), 1)
    for parity in range(2):
        hit = source == 2 * side * (lane // side) + side * parity + lane % side
        rows = jnp.dot(
            flat_ref[...],
            jnp.where(hit, 1.0, 0.0).astype(jnp.bfloat16),
            preferred_element_type=jnp.float32,
        )
        for tap in range(TAPS):
            if (tap - 3) % 2 != parity:
                continue
            shift = (tap - 3 - parity) // 2 * side
            value = rows
            if shift:
                value = pltpu.roll(rows, (-shift) % half, 1)
                inside = lanes < half - shift if shift > 0 else lanes >= -shift
                value = jnp.where(inside, value, 0.0)
            value = value.astype(jnp.bfloat16).reshape(segs, LANES, half)
            rows_ref[:, tap * LANES : (tap + 1) * LANES, :] = value
    weight = weight_ref[...]
    moves = [move(rows_ref, rows_out_ref, sems, 0)]

    def seg_step(seg, _):
        value = jnp.dot(weight, rows_ref[seg], preferred_element_type=jnp.float32)
        value = value.astype(jnp.bfloat16)
        here = pl.ds(pl.multiple_of(seg * LANES, LANES), LANES)
        for tap in range(TAPS):
            parts_ref[tap, here, :] = value[tap * LANES : (tap + 1) * LANES]
        return 0

    lax.fori_loop(0, segs, seg_step, 0, unroll=4)
    source = lax.broadcasted_iota(jnp.int32, (half, quarter), 0)
    lane = lax.broadcasted_iota(jnp.int32, (half, quarter), 1)
    total = None
    for tap in range(TAPS):
        column = 2 * (lane % LANES) + tap - 3
        hit = (source == side * (lane // LANES) + column) & (column >= 0) & (column < side)
        pick = jnp.where(hit, 1.0, 0.0).astype(jnp.bfloat16)
        pick_ref[tap] = pick
        term = jnp.dot(parts_ref[tap], pick, preferred_element_type=jnp.float32)
        total = term if total is None else total + term
    total = total.reshape(segs, LANES, quarter)
    pre_ref[...] = total
    moves += [move(pick_ref, pick_out_ref, sems, 1), move(pre_ref, pre_out_ref, sems, 2)]
    extra_ref[...] = stem_row(core, extra_ref.shape[1], total, total * total)
    for copy in moves:
        copy.wait()


def stem_front(place, video, weight, width):
    segs, _, size = video.shape
    return kernel_call(
        stem_front_body,
        (
            jax.ShapeDtypeStruct((segs, LANES, size // 4), jnp.float32),
            jax.ShapeDtypeStruct((segs, TAPS * LANES, size // 2), jnp.bfloat16),
            jax.ShapeDtypeStruct((TAPS, size // 2, size // 4), jnp.bfloat16),
            jax.ShapeDtypeStruct((8, width), jnp.float32),
        ),
        [scalars, whole, whole],
        (
            pltpu.VMEM((segs * LANES, size), jnp.bfloat16),
            pltpu.VMEM((TAPS, segs * LANES, size // 2), jnp.bfloat16),
            pltpu.VMEM((segs, LANES, size // 4), jnp.float32),
            pltpu.VMEM((segs, TAPS * LANES, size // 2), jnp.bfloat16),
            pltpu.VMEM((TAPS, size // 2, size // 4), jnp.bfloat16),
            pltpu.SemaphoreType.DMA((3,)),
        ),
        away=(0, 1, 2),
        lasts=0.0,
    )(place, video, weight)


def stem_norm(count, core, pre, stats_ref, par_ref):
    outs = pre.shape[1]
    center, rate = norm_stats(*stem_columns(core, outs, stats_ref), count)
    scaled = (pre - center) * rate
    gain, bias = upright(par_ref[0:1]), upright(par_ref[1:2])
    return scaled, scaled * gain + bias, gain * rate


def stem_out_body(count, place_ref, pre_ref, grad_ref, stats_ref, par_ref, out_ref, extra_ref):
    core = place_ref[0] % 2
    scaled, normed, _ = stem_norm(count, core, pre_ref[...], stats_ref, par_ref)
    part = logistic(normed)
    out_ref[...] = (normed * part).astype(jnp.bfloat16)
    value = grad_ref[...].astype(jnp.float32) * (part * (1.0 + normed * (1.0 - part)))
    extra_ref[...] = stem_row(core, extra_ref.shape[1], value, value * scaled)


def stem_output(count, place, pre, grad, stats, par, width):
    return kernel_call(
        functools.partial(stem_out_body, count),
        (
            jax.ShapeDtypeStruct(pre.shape, jnp.bfloat16),
            jax.ShapeDtypeStruct((8, width), jnp.float32),
        ),
        [scalars] + [whole] * 4,
        lasts=1.8,
    )(place, pre, grad, stats, par)


def stem_back_body(
    count, first, place_ref, pre_ref, grad_ref, stats_ref, back_ref, par_ref, rows_ref, pick_ref, start_ref, out_ref, slopes_ref,
):
    core = place_ref[0] % 2
    segs, outs, pixels = pre_ref.shape
    scaled, normed, scale = stem_norm(count, core, pre_ref[...], stats_ref, par_ref)
    bias_grad, gain_grad = stem_columns(core, outs, back_ref)
    value = grad_ref[...].astype(jnp.float32) * silu_slope(normed)
    value = scale * (value - bias_grad / count - scaled * (gain_grad / count))
    value = value.astype(jnp.bfloat16).reshape(segs * outs, pixels)
    half = rows_ref.shape[2]
    for tap in range(TAPS):
        spread = exact(value, pick_ref[tap], ((1,), (1,)))
        slopes_ref[:, tap * LANES : (tap + 1) * LANES, :] = spread.astype(jnp.bfloat16).reshape(
            segs, outs, half
        )
    total = None
    for seg in range(segs):
        term = exact(rows_ref[seg], slopes_ref[seg], ((1,), (1,)))
        total = term if total is None else total + term
    size = TAPS * LANES
    rows = size // 2
    if first:
        out_ref[...] = jnp.zeros_like(out_ref)
    else:
        out_ref[...] = start_ref[...]
    out_ref[:, :size] += total[:rows]
    out_ref[:, 128 : 128 + size] += total[rows:]


def stem_back(count, place, pre, grad, stats, back, par, rows, pick, start, chunk, chunks):
    segs, outs, pixels = pre.shape
    size = segs // chunks

    def part(*tail):
        return pl.BlockSpec((size,) + tail, lambda at: (chunk, 0, 0))

    def all_of(shape):
        return pl.BlockSpec(shape, lambda at: (0,) * len(shape))

    small = (TAPS * LANES // 2, 256)
    first = start is None
    start = jnp.zeros((8, 256), jnp.float32) if first else start
    return pl.pallas_call(
        functools.partial(stem_back_body, count, first),
        grid=(1,),
        out_shape=jax.ShapeDtypeStruct(small, jnp.float32),
        in_specs=[scalars, part(outs, pixels), part(outs, pixels)]
        + [all_of(stats.shape), all_of(back.shape), all_of(par.shape)]
        + [part(*rows.shape[1:]), all_of(pick.shape), all_of(start.shape)],
        out_specs=all_of(small),
        scratch_shapes=[pltpu.VMEM((size, TAPS * LANES, rows.shape[2]), jnp.bfloat16)],
        compiler_params=pltpu.CompilerParams(vmem_limit_bytes=vmem_limit),
        cost_estimate=pl.CostEstimate(
            flops=int(1.7 * flops_per_us), bytes_accessed=0, transcendentals=0
        ),
    )(place, pre, grad, stats, back, par, pltpu.with_memory_space_constraint(rows, pltpu.HBM), pick, start)


def stem_weight(center, diff):
    outs = center.shape[1]
    value = jnp.concatenate([diff, center, jnp.zeros((TAPS * TAPS, outs), center.dtype)])
    value = value.reshape(LANES, TAPS, TAPS, outs)
    return value.transpose(2, 3, 1, 0).reshape(TAPS * outs, TAPS * LANES)


def stem_grads_body(packed_ref, center_ref, diff_ref):
    full = jnp.concatenate([packed_ref[:, :128], packed_ref[:, 128:]])
    for row in range(TAPS):
        value = full[row * LANES : (row + 1) * LANES]
        for col in range(TAPS):
            here = value[:, col * LANES : (col + 1) * LANES]
            at = row * TAPS + col
            diff_ref[pl.ds(at, 12, stride=TAPS * TAPS), :] = here[:12]
            center_ref[pl.ds(at, 3, stride=TAPS * TAPS), :] = here[12:15]


def stem_grads(packed, outs):
    return kernel_call(
        stem_grads_body,
        (
            jax.ShapeDtypeStruct((3 * TAPS * TAPS, outs), jnp.float32),
            jax.ShapeDtypeStruct((12 * TAPS * TAPS, outs), jnp.float32),
        ),
        [whole],
    )(packed)


def after(value, *marks):
    return lax.optimization_barrier((value, marks))[0]


def swap(value, axis, bit):
    size = lax.axis_size(axis)
    return lax.ppermute(value, axis, [(at, at ^ bit) for at in range(size)])


def steps_of(axis):
    size = lax.axis_size(axis)
    assert size & (size - 1) == 0
    return [1 << at for at in range(size.bit_length() - 1)]


def sum_over(value, axis, jobs=()):
    jobs = list(jobs)
    jobs = [job or (lambda mark: mark) for job in jobs]
    for bit in steps_of(axis):
        got = swap(value, axis, bit)
        if jobs:
            got = after(got, jobs.pop(0)(value))
        value = value + got
    for job in jobs:
        value = after(value, job(value))
    return value


def ordered(second, own, other, axis=0):
    return jnp.where(
        second, jnp.concatenate([other, own], axis), jnp.concatenate([own, other], axis)
    )


def gather_rows(value, axis):
    order = [0]
    for bit in reversed(steps_of(axis)):
        value = jnp.concatenate([value, swap(value, axis, bit)])
        order += [at ^ bit for at in order]
    return value, order


def halve_body(bit, parts, far, place_ref, keep_ref, *refs):
    got_refs, refs = refs[:parts], refs[parts:]
    mine_ref, send_ref = refs[:2]
    count, size = send_ref.shape[:2]
    high = (place_ref[1] // bit) % 2
    source, places, moves = keep_ref, [], []
    for block in range(count):
        for side in (1 - high, high):
            here = pl.ds(pl.multiple_of((2 * block + side) * size, size), size)
            places.append((block, side, here))
    if far:
        source, sems = refs[2:]
        moves = [
            move(keep_ref.at[here], source.at[here], sems, at)
            for at, (_, _, here) in enumerate(places)
        ]
    for at, (block, side, here) in enumerate(places):
        if far:
            moves[at].wait()
        value = source[here, :]
        if parts:
            part = block * parts // count
            first = 2 * (block - part * count // parts) + side
            got = got_refs[part][pl.ds(pl.multiple_of(first * size, size), size), :]
            value = value + got.astype(jnp.float32)
        ref = mine_ref if at % 2 else send_ref
        ref[block] = value.astype(ref.dtype)


def halve(place, keep, got, bits, at, far=False):
    rows, width = keep.shape
    left = sorted(bits, reverse=True)
    outer = 1 << left.index(at)
    inner = rows // (2 * outer)
    if inner % BLOCK or outer % max(len(got), 1):
        total = keep + jnp.concatenate(got).astype(jnp.float32) if got else keep
        blocks = total.reshape(outer, 2, inner, width)
        low, high = blocks[:, 0].reshape(-1, width), blocks[:, 1].reshape(-1, width)
        mine = (place[1] // at) % 2 == 0
        return jnp.where(mine, low, high), jnp.where(mine, high, low).astype(jnp.bfloat16)
    shape = (outer, inner, width)
    scratch = [pltpu.VMEM(keep.shape, keep.dtype), pltpu.SemaphoreType.DMA((2 * outer,))]
    mine, send = kernel_call(
        functools.partial(halve_body, at, len(got), far),
        (jax.ShapeDtypeStruct(shape, jnp.float32), jax.ShapeDtypeStruct(shape, jnp.bfloat16)),
        [scalars, remote if far else whole] + [whole] * len(got),
        scratch if far else [],
        lasts=2.0 if far else 0.7,
    )(place, keep, *got)
    return mine.reshape(-1, width), send.reshape(-1, width)


def transposed(left, right):
    return lax.dot_general(
        left, right, (((1,), (1,)), ((), ())), preferred_element_type=jnp.float32
    )


def weight_grad(left, right):
    return lax.dot_general(
        left, right, (((0,), (0,)), ((), ())), preferred_element_type=jnp.float32
    )


def per_device(
    block_in,
    weight_in,
    weight_mid,
    weight_out,
    gain_in,
    bias_in,
    gain_mid,
    bias_mid,
    gain_out,
    bias_out,
    kernel_near,
    kernel_far,
    gate_bias,
    same_video,
    video,
    stem_center,
    stem_diff,
    stem_gain,
    stem_bias,
    block_grad,
    stem_grad,
):
    groups = lax.axis_size("dp")
    assert lax.axis_size("chan") == 4
    clips = same_video.shape[0]
    rows, quarter = block_in.shape
    half = rows // 2
    narrow = weight_in.shape[1]
    width = 2 * narrow
    count = float(rows * groups)
    segs = video.shape[0]
    stem_count = float(segs * stem_grad.shape[2] * groups)
    chan = lax.axis_index("chan")
    core, y = chan % 2, chan // 2
    place = jnp.stack([chan, lax.axis_index("dp")])

    mine, others, packed = opening(place, block_in, weight_mid, weight_out)
    pieces = [swap(others, "chan", 1), swap(mine, "chan", 2)]
    pieces.append(swap(after(others, pieces[1]), "chan", 3))

    own_in, order = gather_rows(after(weight_in, mine, others), "dp")
    weights_in = [own_in, swap(own_in, "chan", 1)]
    gathered = lax.all_gather(packed, "dp", axis=0)

    params, stem_par = pack_params(
        [gain_in, bias_in, gain_mid, bias_mid, gate_bias],
        kernel_near,
        kernel_far,
        [stem_gain, stem_bias],
    )
    par_own = ordered(core == 1, params, swap(params, "chan", 1), 1)
    pars = [par_own]
    same = lax.dynamic_slice_in_dim(same_video, core * (clips // 2), clips // 2, 0)
    same = jnp.pad(same, ((0, 0), (0, 1)))
    gain_row, bias_row = gain_out.reshape(1, -1), bias_out.reshape(1, -1)

    outs = stem_grad.shape[1]
    pre_stem, stem_rows, stem_pick, extra = stem_front(
        place, video, stem_weight(stem_center, stem_diff), width
    )

    def both_sums(sums, jobs=()):
        jobs = [run or (lambda mark: mark) for run in jobs]
        got = swap(sums, "chan", 1)
        if jobs:
            got = after(got, jobs[0](sums))
        own = sum_over(sums + got, "dp", jobs[1:4])
        oth = swap(own, "chan", 2)
        for run in jobs[4:]:
            oth = after(oth, run(own))
        return [own, oth]

    made = {}

    def in_turn(*works):
        def run(mark):
            results = []
            for work in works:
                results.append(work((mark, results) if results else mark))
            return results

        return run

    def job(name, work):
        def run(mark):
            made[name] = work(mark)
            return made[name]

        return run

    pre_in, pre_in16, sums_in, cross_in, near_in, away_in = first_conv(
        order, place, block_in, pieces, weights_in, extra, par_own
    )

    blocks = gathered
    if weight_mid.shape[0] % BLOCK:
        blocks = gathered[:, : weight_mid.shape[0]].reshape(1, -1, narrow)

    def mid_blocks(mark):
        own = after(blocks, mark)
        return [own, swap(own, "chan", 1)]


    def out_rows(mark):
        parts, first, size = after(gathered, mark), weight_mid.shape[0], weight_out.shape[0]
        parts = [parts[:, first + at * size : first + (at + 1) * size] for at in range(4)]
        return jnp.concatenate([part.reshape(-1, narrow) for part in parts], 1)

    cross_got = swap(cross_in, "chan", 2)
    pre_in_oth = swap(after(pre_in16, cross_got), "chan", 2)
    sums_in = sums_in + cross_got[:8]
    stats_in = sum_over(
        sums_in + swap(sums_in, "chan", 1),
        "dp",
        [
            None,
            in_turn(job("weights_mid", mid_blocks), job("full_out", out_rows)),
        ],
    )
    pars.append(cross_got)
    weights_mid = made["weights_mid"]
    full_out = made["full_out"]

    out_across = swap(after(full_out, stats_in), "chan", 2)

    mixed, gates, pre_mid, pre_mid16, sums_mid = gate_mid(
        count, place, same, pre_in, pre_in_oth, stats_in, pars, weights_mid
    )
    pre_mid_oth = swap(pre_mid16, "chan", 2)
    stats_stem = after(stats_in, sums_mid)

    def stem_half(mark):
        return stem_output(
            stem_count, place, after(pre_stem, mark), stem_grad, stats_stem, stem_par, quarter
        )

    def slab_of(mark):
        slab = after(gathered, mark)[:, : weight_mid.shape[0]].reshape(9, 2, width, narrow)
        return lax.dynamic_slice_in_dim(slab, 1 - y, 1, 1).reshape(9 * width, narrow)

    stats_mid = both_sums(
        sums_mid,
        [
            None,
            job("stem", stem_half),
            in_turn(job("slab", slab_of), lambda mark: out_across),
            job("turned", lambda mark: turn(after(mixed, mark))),
            lambda mark: pre_mid_oth,
        ],
    )
    stem_out, extra = made["stem"]

    second = second_half(count, place, pre_mid, pre_mid_oth, stats_mid, pars)
    second_peer = swap(second, "chan", 1)
    pre_out, sums_out = last_conv(place, second, second_peer, full_out, extra)
    slab_across = swap(after(made["slab"], stats_mid), "chan", 2)
    stats_out = sum_over(sums_out, "dp")
    stats_out = after(stats_out, slab_across)
    out_peers = [swap(after(value, stats_out), "chan", 1) for value in (full_out, out_across)]
    weights_out = [full_out, out_peers[0], out_across, out_peers[1]]
    block_out, grad_total, sums_back, keep, send = out_back(
        count, place, pre_out, block_in, block_grad, stats_out, gain_row, bias_row, full_out
    )
    got = swap(send, "chan", 1)

    def cross(mark):
        return cross_half(place, keep, after(got, mark))

    def stem_part(chunk, start):
        def work(mark):
            return stem_back(
                stem_count, place, after(pre_stem, mark), stem_grad, stats_in, stats_out,
                stem_par, stem_rows, stem_pick, start and made[start], chunk, 4,
            )

        return job(f"stem{chunk}", work)

    back_out = sum_over(
        sums_back, "dp", [stem_part(0, None), job("cross", cross), stem_part(1, "stem0")]
    )
    keep, send = made["cross"]
    got = swap(send, "chan", 2)
    delta = out_delta(count, rows, stats_out, sums_back, back_out, gain_row)
    deltas = [delta] + [swap(delta, "chan", at) for at in (1, 2, 3)]

    grad_mid, grad_mid16, sums_mid_back = mid_slope(
        count, place, keep, got, second, pre_mid, stats_mid[0], pars[0], deltas, weights_out
    )
    grad_mid_oth = swap(grad_mid16, "chan", 2)

    aways_mid = [slab_across, swap(after(slab_across, sums_mid_back), "chan", 1)]

    def out_part(start, rows_of_second):
        def work(mark):
            return out_weight(
                count, place, rows_of_second, pre_out, grad_total, stats_out, after(back_out, mark),
                gain_row, start and made[start],
            )

        return work

    def own_slopes(mark):
        return mid_own(count, grad_mid, pre_mid, stats_mid[0], mark, pars[0])

    bits = steps_of("dp")

    back_mid = both_sums(sums_mid_back, [
        None,
        job("out0", out_part(None, second)),
        job("out1", out_part("out0", second_peer)),
        stem_part(2, "stem1"),
        in_turn(job("slopes", own_slopes), stem_part(3, "stem2")),
    ])
    slopes = made["slopes"]
    sum_out = lax.psum_scatter(made["out1"], "dp", scatter_dimension=0, tiled=True)
    stem_first = swap(made["stem3"], "dp", bits[0])
    far_in = swap(after(away_in, sums_mid_back), "chan", 2)

    grad_in, grad_in16, sums_in_back = mid_back(
        count, place, same, slopes, grad_mid_oth, pre_mid_oth, stats_mid[1], back_mid[1], pre_in,
        gates, stats_in, pars, weights_mid, aways_mid,
    )
    grad_in_oth = swap(grad_in16, "chan", 2)

    def mid_part(mark):
        return mid_weight(place, made["turned"], after(slopes, mark))

    def mid_rest(mark):
        keep, *sends = made["mid"]
        got = [after(swap(send, "chan", 1), mark) for send in sends]
        return halve(place, keep, got, mid_bits, mid_bits[0], True)

    mid_bits = bits

    def mid_step(at):
        def work(mark):
            keep, got = made["keep"], after(swap(made["send"], "dp", mid_bits[at - 1]), mark)
            made["keep"], made["send"] = halve(place, keep, [got], mid_bits[at:], mid_bits[at])
            return made["send"]

        return work

    def mid_first(mark):
        made["keep"], made["send"] = mid_rest(mark)
        return made["send"]

    def own_in_back(mark):
        return in_own(
            count, place, grad_in, pre_in, stats_in, mark, pars[0], block_in, pieces
        )

    def stem_next(mark):
        return made["stem3"] + after(stem_first, mark)

    back_in = both_sums(
        sums_in_back,
        [
            None,
            job("mid", mid_part),
            job("stem_total", stem_next),
            in_turn(mid_first, lambda mark: grad_in_oth),
            job("in", own_in_back),
        ],
    )

    grad_own, keep, send = made["in"]
    got = swap(send, "chan", 1)
    grad_pre = in_other(
        count, place, after(grad_own, send), grad_in_oth, pre_in_oth, stats_in, back_in[1], pars[1]
    )
    grad_peer = swap(grad_pre, "chan", 1)
    mark, stem_total = grad_pre, made["stem_total"]
    assert len(bits) > 1
    last = len(bits) - 1
    for at, bit in enumerate(bits):
        got = after(got, mark, sum_out) if at == 1 else after(got, mark)
        keep, send = halve(place, keep, [got], bits[at:], bit, at == 0)
        got = swap(send, "dp", bit)
        mark = send
        if at < last:
            mark = mid_step(at + 1)(mark)
            if at == 0:
                near = after(near_in, mark)
                mark = grad_block_in = input_grad(
                    place, grad_pre, grad_peer, near, far_in, grad_total
                )
            stem_got = swap(stem_total, "dp", bits[at + 1])
            mark = stem_total = after(stem_total, mark) + stem_got
    sum_mid = after(made["keep"], send) + swap(made["send"], "dp", bit).astype(jnp.float32)
    sum_in = keep + after(got, sum_mid).astype(jnp.float32)
    center_grad, diff_grad = stem_grads(stem_total, outs)

    def my_columns(value):
        return lax.dynamic_slice_in_dim(value, core * narrow, narrow, value.ndim - 1)

    def my_stem(value):
        row = lax.dynamic_slice(value, (2, core * 2 * outs), (1, 2 * outs))[0]
        return row[:outs], row[outs:]

    gate_grads = my_columns(back_in[0][8:])
    mid_grads, in_grads = my_columns(back_mid[0]), my_columns(back_in[0])
    stem_bias_grad, stem_gain_grad = my_stem(stats_out)
    return (
        block_out,
        stem_out,
        grad_block_in,
        sum_in,
        sum_mid,
        sum_out,
        in_grads[1],
        in_grads[0],
        mid_grads[1],
        mid_grads[0],
        back_out[1],
        back_out[0],
        gate_grads[1:10],
        gate_grads[10:19],
        gate_grads[0],
        center_grad,
        diff_grad,
        stem_gain_grad,
        stem_bias_grad,
    )


def solution(mesh):
    placed = (
        P("dp", "chan"),
        P("dp", "chan"),
        P("dp", "chan"),
        P("dp", "chan"),
        P("chan"),
        P("chan"),
        P("chan"),
        P("chan"),
        P("chan"),
        P("chan"),
        P(None, "chan"),
        P(None, "chan"),
        P("chan"),
        P("dp", None),
        P("dp", None, None),
        P(None, "chan"),
        P(None, "chan"),
        P("chan"),
        P("chan"),
        P("dp", "chan"),
        P("dp", "chan", None),
    )
    return jax.shard_map(
        per_device,
        mesh=mesh,
        in_specs=placed,
        out_specs=(
            P("dp", "chan"),
            P("dp", "chan", None),
            P("dp", "chan"),
            P("dp", "chan"),
            P("dp", "chan"),
            P("dp", "chan"),
            P("chan"),
            P("chan"),
            P("chan"),
            P("chan"),
            P("chan"),
            P("chan"),
            P(None, "chan"),
            P(None, "chan"),
            P("chan"),
            P(None, "chan"),
            P(None, "chan"),
            P("chan"),
            P("chan"),
        ),
        check_vma=False,
    )
```

```python
import functools

import jax
import jax.numpy as jnp
from jax import lax
from jax.experimental import pallas as pl
from jax.experimental.pallas import tpu as pltpu
from jax.sharding import PartitionSpec as P

SEG = 8
SIDE = 7
FRAMES = 5
PIXELS = SIDE * SIDE
BLOCK = 16
SPAN = SIDE + 2

eps = 1e-05
vmem_limit = 32 * 1024 * 1024
flops_per_us = 0.3e9

whole = pl.BlockSpec(memory_space=pltpu.VMEM)
remote = pl.BlockSpec(memory_space=pltpu.HBM)
scalars = pl.BlockSpec(memory_space=pltpu.SMEM)


def logistic(value):
    return 0.5 * jnp.tanh(0.5 * value) + 0.5


def silu_slope(value):
    part = logistic(value)
    return part * (1.0 + value * (1.0 - part))


def norm_stats(totals, squares, count):
    center = totals / count
    spread = squares / count - center * center
    return (center, lax.rsqrt(spread + eps))


def move(source, target, sems, at):
    copy = pltpu.make_async_copy(source, target, sems.at[at])
    copy.start()
    return copy


def kernel_call(body, out_shape, in_specs, scratch=(), lasts=1.0, away=(), held=()):
    several = isinstance(out_shape, tuple)
    shapes = list(out_shape) if several else [out_shape]
    specs = [remote if at in away else whole for at in range(len(shapes))]
    shapes = [
        (pltpu.HBM if at in away else pltpu.VMEM)(shape.shape, shape.dtype)
        if at in away or at in held
        else shape
        for at, shape in enumerate(shapes)
    ]
    call = pl.pallas_call(
        body,
        out_shape=tuple(shapes) if several else shapes[0],
        in_specs=in_specs,
        out_specs=tuple(specs) if several else specs[0],
        scratch_shapes=list(scratch),
        compiler_params=pltpu.CompilerParams(vmem_limit_bytes=vmem_limit),
        cost_estimate=pl.CostEstimate(
            flops=int(lasts * flops_per_us), bytes_accessed=0, transcendentals=0
        ),
    )

    def run(*args):
        return call(
            *[
                pltpu.with_memory_space_constraint(arg, pltpu.HBM) if spec is remote else arg
                for arg, spec in zip(args, in_specs, strict=True)
            ]
        )

    return run


PAIRS = SEG // 2
CLIP = SEG * PIXELS


def pair_row(clip, pair):
    return pl.multiple_of(BLOCK * (2 + SPAN * (PAIRS * clip + pair)), BLOCK)


def clip_view(ref, clip, extra=0):
    return ref.at[pl.ds(pl.multiple_of(clip * CLIP, 8), CLIP + extra)]


def lane_mask(width):
    return lax.broadcasted_iota(jnp.int32, (1, 8, width), 1)


def load_map(ref, first, lanes):
    return jnp.stack([ref[pl.ds(first + SIDE * at, 8), lanes] for at in range(SIDE)])


def store_map(ref, first, lanes, value):
    for at in range(SIDE):
        ref[pl.ds(first + SIDE * at, SIDE), lanes] = value[at][:SIDE]


def two_maps(early, late):
    both = jnp.stack([early, late], axis=1)
    return both.reshape(SIDE * BLOCK, early.shape[-1])


def load_rows(ref, first, lanes):
    return [ref[pl.ds(first + SIDE * at, 8), lanes] for at in range(SIDE)]


def store_rows(ref, first, lanes, rows):
    for at in range(SIDE):
        ref[pl.ds(first + SIDE * at, SIDE), lanes] = rows[at][:SIDE]


def across(value, step, place):
    if step == 0:
        return value
    moved = pltpu.roll(value, (-step) % 8, 1)
    if step == 2:
        return jnp.where(place < 6, moved, 0.0)
    if step == -2:
        return jnp.where(place > 0, moved, 0.0)
    return moved


def taps_of(near, far):
    for step, kernel in ((1, near), (2, far)):
        for row in range(3):
            yield step, row, [kernel[row * 3 + col] for col in range(3)]


def row_views(value, place):
    views = {0: value}
    for step in (-2, -1, 1, 2):
        moved = pltpu.roll(value, (-step) % 8, 0)
        if step == 2:
            moved = jnp.where(place < 6, moved, 0.0)
        if step == -2:
            moved = jnp.where(place > 0, moved, 0.0)
        views[step] = moved
    return views


def weighted(kernel, views, step):
    return sum(kernel[col] * views[step * (col - 1)] for col in range(3))


def gate_scores(change, near, far, offset, place):
    scores = [offset] * SIDE
    for at in range(SIDE):
        views = row_views(change[at], place)
        for step, row, kernel in taps_of(near, far):
            target = at - step * (row - 1)
            if 0 <= target < SIDE:
                scores[target] = scores[target] + weighted(kernel, views, step)
    return scores


def conv_chunk(parts, weights, first, rows, sign):
    total = None
    for col in (1, 0, 2):
        acc = None
        for row in range(3):
            start = pl.multiple_of(first + BLOCK * (1 + sign * (row - 1)), BLOCK)
            for part, weight in zip(parts, weights, strict=True):
                left = part[pl.ds(start, rows), :]
                term = weight(left, row * 3 + col)
                acc = term if acc is None else acc + term
        acc = acc.reshape(rows // 8, 8, acc.shape[-1])
        shift = sign * (col - 1)
        if shift:
            acc = pltpu.roll(acc, (-shift) % 8, 1)
        total = acc if total is None else total + acc
    return total


def lane_part(index, width=128):
    return pl.ds(pl.multiple_of(index * width, width), width)


def row_part(index, size):
    return pl.ds(pl.multiple_of(index * size, size), size)


def after_sums(ref):
    return ref.at[pl.ds(8, 24)]


def rows_of(stats_ref, first=0):
    return stats_ref[first : first + 1], stats_ref[first + 1 : first + 2]


def put_sums(sums_ref, first, second):
    sums_ref[...] = jnp.zeros_like(sums_ref)
    sums_ref[0:1, :] = first
    sums_ref[1:2, :] = second


def fetch_blocks(sources, core, target_ref, sems, first):
    moves = []
    for side, source in enumerate(sources):
        lanes = lane_part(core if side == 0 else 1 - core)
        blocks = source.shape[0]
        size = target_ref.shape[0] // blocks
        for block in range(blocks):
            here = pl.ds(block * size, size)
            moves.append(
                move(
                    source.at[block, pl.ds(0, size)],
                    target_ref.at[here, lanes],
                    sems,
                    first + side * blocks + block,
                )
            )
    return moves


def gate_half(count, same_ref, pre, stats, par, hidden_ref, mixed_ref, first, gates_ref=None):
    rows, width = pre.shape
    hidden_ref[pl.ds(rows, hidden_ref.shape[0] - rows), :] = jnp.zeros(
        (hidden_ref.shape[0] - rows, width), jnp.float32
    )
    center, rate = norm_stats(*stats, count)
    scaled = (pre[...].astype(jnp.float32) - center) * rate
    normed = scaled * par[0:1] + par[1:2]
    hidden_ref[pl.ds(0, rows), :] = normed * logistic(normed)
    place = lax.broadcasted_iota(jnp.int32, (8, 128), 0)

    def lanes_step(chunk, _):
        lanes = lane_part(chunk)
        target = pl.ds(pl.multiple_of(first + chunk * 128, 128), 128)
        near = [par[5 + tap : 6 + tap, lanes] for tap in range(9)]
        far = [par[14 + tap : 15 + tap, lanes] for tap in range(9)]
        offset = par[4:5, lanes]

        def clip_step(clip, _):
            view = clip_view(hidden_ref, clip, 56)
            for pair in range(PAIRS):
                maps = [load_rows(view, PIXELS * (2 * pair + seg), lanes) for seg in range(3)]
                results = []
                for seg in range(2):
                    same = same_ref[clip, 2 * pair + seg].astype(jnp.float32)
                    change = [
                        jnp.where(place < SIDE, same * (later - now), 0.0)
                        for now, later in zip(maps[seg], maps[seg + 1], strict=True)
                    ]
                    scores = gate_scores(change, near, far, offset, place)
                    gates = [logistic(score) for score in scores]
                    results.append(
                        [
                            jnp.where(place < SIDE, now * (1.0 + gate), 0.0)
                            for now, gate in zip(maps[seg], gates, strict=True)
                        ]
                    )
                    if gates_ref is not None:
                        for row in range(SIDE):
                            gates_ref[SEG * clip + 2 * pair + seg, row, :, lanes] = gates[row]
                here = pl.ds(pair_row(clip, pair), SIDE * BLOCK)
                blocks = [results[seg][row] for row in range(SIDE) for seg in range(2)]
                mixed_ref[here, target] = jnp.concatenate(blocks).astype(jnp.bfloat16)
            return 0

        return lax.fori_loop(0, rows // CLIP, clip_step, 0)

    lax.fori_loop(0, width // 128, lanes_step, 0)


def gate_mid_body(
    count,
    place_ref,
    same_ref,
    own_ref,
    oth_ref,
    first_ref,
    second_ref,
    par_own_ref,
    par_oth_ref,
    weight_own_ref,
    weight_peer_ref,
    mixed_out_ref,
    gates_out_ref,
    mid_ref,
    mid16_ref,
    sums_ref,
    hidden_ref,
    acc_ref,
    weight_ref,
    own_here_ref,
    mixed_ref,
    gates_ref,
    sems,
):
    rows, width = oth_ref.shape
    clips = rows // CLIP
    core, y = place_ref[0] % 2, place_ref[0] // 2
    arrival = move(own_ref, own_here_ref, sems, 0)
    stats = first_ref[...] + second_ref[...]
    weight_moves = fetch_blocks((weight_own_ref, weight_peer_ref), core, weight_ref, sems, 5)
    mixed_ref[...] = jnp.zeros_like(mixed_ref)
    gate_half(
        count, same_ref, oth_ref, rows_of(stats, 4), after_sums(par_oth_ref), hidden_ref, mixed_ref,
        pl.multiple_of((1 - y) * width, width),
    )
    arrival.wait()
    gate_half(
        count, same_ref, own_here_ref, rows_of(stats), par_own_ref, hidden_ref, mixed_ref,
        pl.multiple_of(y * width, width), gates_ref,
    )
    gates_move = move(gates_ref, gates_out_ref, sems, 2)
    depth = 2 * width
    for copy in weight_moves:
        copy.wait()
    mixed_move = move(mixed_ref, mixed_out_ref, sems, 3)

    def tap_dot(left, tap):
        return jnp.dot(
            left, weight_ref[tap * depth : (tap + 1) * depth], preferred_element_type=jnp.float32
        )

    def conv_step(clip, _):
        span = PAIRS * SPAN * BLOCK
        total = conv_chunk([mixed_ref], [tap_dot], clip * span, span, 1)
        view = clip_view(acc_ref, clip)
        for seg in range(SEG):
            value = [total[2 * (SPAN * (seg // 2) + 1 + row) + seg % 2] for row in range(SIDE)]
            store_map(view, seg * PIXELS, slice(None), value)
        return 0

    lax.fori_loop(0, clips, conv_step, 0)
    mid_move = move(acc_ref.at[pl.ds(0, rows)], mid_ref, sems, 4)
    result = acc_ref[pl.ds(0, rows), :]
    mid16_ref[...] = result.astype(jnp.bfloat16)
    put_sums(
        sums_ref, jnp.sum(result, 0, keepdims=True), jnp.sum(result * result, 0, keepdims=True)
    )
    for copy in (gates_move, mixed_move, mid_move):
        copy.wait()


def map_rows(rows):
    return (rows // (2 * PIXELS) * SPAN + 2) * BLOCK


def gate_mid(count, place, same, own, oth, stats, pars, weights):
    rows, width = oth.shape
    spread = map_rows(rows)
    depth = 18 * width
    gates = (rows // PIXELS, SIDE, 8, width)
    return kernel_call(
        functools.partial(gate_mid_body, count),
        (
            jax.ShapeDtypeStruct((spread, 2 * width), jnp.bfloat16),
            jax.ShapeDtypeStruct(gates, jnp.float32),
            jax.ShapeDtypeStruct((rows, width), jnp.float32),
            jax.ShapeDtypeStruct((rows, width), jnp.bfloat16),
            jax.ShapeDtypeStruct((8, width), jnp.float32),
        ),
        [scalars, scalars, remote] + [whole] * 5 + [remote, remote],
        (
            pltpu.VMEM((rows + 56, width), jnp.float32),
            pltpu.VMEM((rows + 8, width), jnp.float32),
            pltpu.VMEM((depth, width), jnp.bfloat16),
            pltpu.VMEM((rows, width), own.dtype),
            pltpu.VMEM((spread, 2 * width), jnp.bfloat16),
            pltpu.VMEM(gates, jnp.float32),
            pltpu.SemaphoreType.DMA((5 + 2 * weights[0].shape[0],)),
        ),
        away=(0, 1, 2),
        lasts=12.0,
    )(place, same, own, oth, *stats, *pars, *weights)


def mid_slopes(count, grad, pre, stats, back, par, flat_ref, store):
    rows, width = grad.shape
    flat_ref[pl.ds(rows, flat_ref.shape[0] - rows), :] = jnp.zeros(
        (flat_ref.shape[0] - rows, width), jnp.float32
    )
    center, rate = norm_stats(*rows_of(stats), count)
    scaled = (pre[...].astype(jnp.float32) - center) * rate
    flat_ref[pl.ds(0, rows), :] = (par[2:3] * rate) * (
        grad[...].astype(jnp.float32) - back[0:1] / count - scaled * (back[1:2] / count)
    )
    at = lane_mask(width)

    def clip_step(clip, _):
        view = clip_view(flat_ref, clip, 8)
        for pair in range(PAIRS):
            maps = [
                jnp.where(at < SIDE, load_map(view, PIXELS * (2 * pair + seg), slice(None)), 0.0)
                for seg in range(2)
            ]
            store(pl.ds(pair_row(clip, pair), SIDE * BLOCK), maps, at)
        return 0

    lax.fori_loop(0, rows // CLIP, clip_step, 0)


def mid_own_body(count, d_ref, mid_ref, stats_ref, back_ref, par_ref, slopes_ref, flat_ref, mid_here_ref, d_here_ref, sems):
    arrivals = [move(mid_ref, mid_here_ref, sems, 0), move(d_ref, d_here_ref, sems, 1)]
    slopes_ref[...] = jnp.zeros_like(slopes_ref)

    def store(place, maps, at):
        for col in range(3):
            slopes_ref[col, place, :] = two_maps(
                *[across(value, 1 - col, at) for value in maps]
            ).astype(jnp.bfloat16)

    for copy in arrivals:
        copy.wait()
    mid_slopes(count, d_here_ref, mid_here_ref, stats_ref, back_ref, par_ref, flat_ref, store)


def mid_own(count, d_own, mid, stats, back, par):
    rows, width = d_own.shape
    return kernel_call(
        functools.partial(mid_own_body, count),
        jax.ShapeDtypeStruct((3, map_rows(rows), width), jnp.bfloat16),
        [remote, remote, whole, whole, whole],
        (
            pltpu.VMEM((rows + 56, width), jnp.float32),
            pltpu.VMEM((rows, width), jnp.float32),
            pltpu.VMEM((rows, width), jnp.float32),
            pltpu.SemaphoreType.DMA((2,)),
        ),
        held=(0,),
        lasts=1.7,
    )(d_own, mid, stats, back, par)


def mid_back_body(
    count,
    place_ref,
    same_ref,
    slopes_ref,
    d_oth_ref,
    mid_oth_ref,
    stats_oth_ref,
    back_oth_ref,
    pre_ref,
    gates_ref,
    stats_in_ref,
    par_own_ref,
    par_oth_ref,
    weight_own_ref,
    weight_peer_ref,
    away_own_ref,
    away_peer_ref,
    d_in_out_ref,
    d_in16_ref,
    sums_ref,
    flat_ref,
    oth_ref,
    dmix_ref,
    scaled_ref,
    parts_ref,
    weight_ref,
    weight_oth_ref,
    d_here_ref,
    mid_here_ref,
    pre_here_ref,
    gates_here_ref,
    sems,
):
    rows, width = d_oth_ref.shape
    clips = rows // CLIP
    core, y = place_ref[0] % 2, place_ref[0] // 2
    arrivals = [move(d_oth_ref, d_here_ref, sems, 1), move(mid_oth_ref, mid_here_ref, sems, 2)]
    weight_moves = fetch_blocks((weight_own_ref, weight_peer_ref), core, weight_ref, sems, 10)
    weight_moves += [
        move(away_own_ref, weight_oth_ref.at[:, lane_part(core)], sems, 3),
        move(away_peer_ref, weight_oth_ref.at[:, lane_part(1 - core)], sems, 4),
    ]
    pre_moves = [
        move(pre_ref, pre_here_ref, sems, 7),
        move(gates_ref, gates_here_ref, sems, 9),
    ]
    oth_ref[...] = jnp.zeros_like(oth_ref)

    def store(place, maps, _):
        oth_ref[place, :] = two_maps(*maps).astype(jnp.bfloat16)

    for copy in arrivals:
        copy.wait()
    mid_slopes(count, d_here_ref, mid_here_ref, stats_oth_ref, back_oth_ref, after_sums(par_oth_ref), flat_ref, store)
    depth = 2 * width
    turned = (((1,), (1,)), ((), ()))
    for copy in weight_moves:
        copy.wait()

    def own_dot(left, tap):
        start = pl.multiple_of(tap * depth + y * width, width)
        return lax.dot_general(
            left, weight_ref[pl.ds(start, width), :], turned, preferred_element_type=jnp.float32
        )

    def oth_dot(left, tap):
        return lax.dot_general(
            left,
            weight_oth_ref[tap * width : (tap + 1) * width],
            turned,
            preferred_element_type=jnp.float32,
        )

    def conv_step(clip, _):
        span = PAIRS * SPAN * BLOCK
        total = conv_chunk([slopes_ref.at[1], oth_ref], [own_dot, oth_dot], clip * span, span, -1)
        dmix_ref[pl.ds(clip * (span // 8), span // 8)] = total
        return 0

    lax.fori_loop(0, clips, conv_step, 0)

    center, rate = norm_stats(*rows_of(stats_in_ref), count)
    for copy in pre_moves:
        copy.wait()
    scaled_ref[pl.ds(0, rows), :] = (pre_here_ref[...] - center) * rate
    scaled_ref[pl.ds(rows, scaled_ref.shape[0] - rows), :] = jnp.zeros(
        (scaled_ref.shape[0] - rows, width), jnp.float32
    )
    parts_ref[...] = jnp.zeros_like(parts_ref)
    place = lax.broadcasted_iota(jnp.int32, (8, 128), 0)
    inside = place < SIDE

    def lanes_step(chunk, _):
        lanes = lane_part(chunk)

        def row_of(index):
            return par_own_ref[index : index + 1, lanes]

        near = [row_of(5 + tap) for tap in range(9)]
        far = [row_of(14 + tap) for tap in range(9)]
        gain, bias = row_of(0), row_of(1)

        def add_part(index, value):
            parts_ref[pl.ds(8 * index, 8), lanes] += value

        def clip_step(clip, carry):
            view = clip_view(scaled_ref, clip, 56)
            target = clip_view(flat_ref, clip)
            for pair in range(PAIRS):
                carry = pair_step(clip, pair, carry, view, target)
            return carry

        def pair_step(clip, pair, carry, view, target):
            normed = [
                [value * gain + bias for value in load_rows(view, PIXELS * (2 * pair + seg), lanes)]
                for seg in range(3)
            ]
            parts = [[logistic(value) for value in rows] for rows in normed]
            hidden = [
                [value * part for value, part in zip(*both, strict=True)]
                for both in zip(normed, parts, strict=True)
            ]
            for seg in range(2):
                same = same_ref[clip, 2 * pair + seg].astype(jnp.float32)
                start = 2 * (SPAN * (PAIRS * clip + pair) + 1) + seg
                d_mixed, gates, d_score = [], [], []
                for row in range(SIDE):
                    gate = gates_here_ref[SEG * clip + 2 * pair + seg, row, :, lanes]
                    grad = jnp.where(inside, dmix_ref[start + 2 * row, :, lanes], 0.0)
                    gates.append(gate)
                    d_mixed.append(grad)
                    d_score.append(grad * hidden[seg][row] * (gate * (1.0 - gate)))
                add_part(0, sum(d_score[1:], d_score[0]))
                sums = [None] * 18
                d_change = [None] * SIDE
                for row in range(SIDE):
                    change = hidden[seg + 1][row] - hidden[seg][row]
                    views = row_views(jnp.where(inside, same * change, 0.0), place)
                    backs = row_views(d_score[row], place)
                    for index, (step, tap_row, kernel) in enumerate(taps_of(near, far)):
                        other = row - step * (tap_row - 1)
                        if 0 <= other < SIDE:
                            for col in range(3):
                                if index == 4 and col == 1:
                                    continue
                                term = d_score[other] * views[step * (col - 1)]
                                at = 3 * index + col
                                sums[at] = term if sums[at] is None else sums[at] + term
                        other = row + step * (tap_row - 1)
                        if 0 <= other < SIDE:
                            term = weighted(kernel, backs, -step)
                            before = d_change[other]
                            d_change[other] = term if before is None else before + term
                for at, value in enumerate(sums):
                    if value is not None:
                        add_part(1 + at, value)
                d_change = [jnp.where(inside, same * value, 0.0) for value in d_change]
                results = []
                for row in range(SIDE):
                    d_hidden = d_mixed[row] * (1.0 + gates[row]) - d_change[row] + carry[row]
                    part, value = parts[seg][row], normed[seg][row]
                    results.append(d_hidden * (part * (1.0 + value * (1.0 - part))))
                carry = d_change
                store_rows(target, PIXELS * (2 * pair + seg), lanes, results)
            return carry

        lax.fori_loop(0, clips, clip_step, [jnp.zeros((8, 128), jnp.float32)] * SIDE)
        return 0

    lax.fori_loop(0, width // 128, lanes_step, 0)
    d_in_move = move(flat_ref.at[pl.ds(0, rows)], d_in_out_ref, sems, 8)
    result = flat_ref[pl.ds(0, rows), :]
    d_in16_ref[...] = result.astype(jnp.bfloat16)
    put_sums(
        sums_ref,
        jnp.sum(result, 0, keepdims=True),
        jnp.sum(result * scaled_ref[pl.ds(0, rows), :], 0, keepdims=True),
    )
    parts_ref[pl.ds(8 * 14, 8), :] = parts_ref[pl.ds(8 * 5, 8), :]
    sums_ref[8:32, :] = jnp.sum(parts_ref[...].reshape(24, 8, width), 1)
    d_in_move.wait()


def mid_back(
    count, place, same, slopes, d_oth, mid_oth, stats_oth, back_oth, pre, gates, stats_in, pars, weights, aways
):
    rows, width = d_oth.shape
    spread = map_rows(rows)
    depth = 18 * width
    return kernel_call(
        functools.partial(mid_back_body, count),
        (
            jax.ShapeDtypeStruct((rows, width), jnp.float32),
            jax.ShapeDtypeStruct((rows, width), jnp.bfloat16),
            jax.ShapeDtypeStruct((32, width), jnp.float32),
        ),
        [scalars, scalars, whole, remote, remote, whole, whole, remote, remote]
        + [whole] * 3
        + [remote] * 4,
        (
            pltpu.VMEM((rows + 56, width), jnp.float32),
            pltpu.VMEM((spread, width), jnp.bfloat16),
            pltpu.VMEM((spread // 8, 8, width), jnp.float32),
            pltpu.VMEM((rows + 56, width), jnp.float32),
            pltpu.VMEM((24 * 8, width), jnp.float32),
            pltpu.VMEM((depth, width), jnp.bfloat16),
            pltpu.VMEM((depth // 2, width), jnp.bfloat16),
            pltpu.VMEM((rows, width), jnp.bfloat16),
            pltpu.VMEM((rows, width), jnp.bfloat16),
            pltpu.VMEM((rows, width), jnp.float32),
            pltpu.VMEM(gates.shape, jnp.float32),
            pltpu.SemaphoreType.DMA((10 + 2 * weights[0].shape[0],)),
        ),
        away=(0,),
        lasts=11.5,
    )(
        place, same, slopes, d_oth, mid_oth, stats_oth, back_oth, pre, gates, stats_in, *pars, *weights,
        *aways,
    )


def turn_body(mixed_ref, out_ref, mixed_here_ref, sems):
    move(mixed_ref, mixed_here_ref, sems, 0).wait()
    out_ref[...] = mixed_here_ref[pl.ds(BLOCK, out_ref.shape[1]), :].T


def turn(mixed):
    spread, depth = mixed.shape
    return kernel_call(
        turn_body,
        jax.ShapeDtypeStruct((depth, spread - 2 * BLOCK), jnp.bfloat16),
        [remote],
        (pltpu.VMEM(mixed.shape, jnp.bfloat16), pltpu.SemaphoreType.DMA((1,))),
        held=(0,),
        lasts=1.6,
    )(mixed)


def mid_weight_body(place_ref, turned_ref, slopes_ref, keep_ref, early_ref, late_ref, keep_here_ref, sems):
    depth, rows = turned_ref.shape
    half = keep_ref.shape[1]
    cut = early_ref.shape[0]
    first = place_ref[0] % 2 == 0
    moves = []
    for tap in range(9):
        row, col = tap // 3, tap % 3
        right = slopes_ref[col, pl.ds(BLOCK * (2 - row), rows), :]
        value = jnp.dot(turned_ref[...], right, preferred_element_type=jnp.float32)
        low, high = value[:, :half], value[:, half:]
        here = pl.ds(tap * depth, depth)
        keep_here_ref[here, :] = jnp.where(first, low, high)
        moves.append(move(keep_here_ref.at[here], keep_ref.at[here], sems, tap))
        send = jnp.where(first, high, low).astype(jnp.bfloat16)
        middle = min(max(cut - tap * depth, 0), depth)
        if middle > 0:
            early_ref[tap * depth : tap * depth + middle] = send[:middle]
        if middle < depth:
            late_ref[tap * depth + middle - cut : (tap + 1) * depth - cut] = send[middle:]
    for copy in moves:
        copy.wait()


def mid_weight(place, turned, slopes):
    depth, rows = turned.shape
    width = slopes.shape[2]
    part = jax.ShapeDtypeStruct((9 * depth // 2, width // 2), jnp.bfloat16)
    return kernel_call(
        mid_weight_body,
        (jax.ShapeDtypeStruct((9 * depth, width // 2), jnp.float32), part, part),
        [scalars, whole, whole],
        (pltpu.VMEM((9 * depth, width // 2), jnp.float32), pltpu.SemaphoreType.DMA((9,))),
        away=(0,),
        lasts=4.8,
    )(place, turned, slopes)


def first_conv_body(
    order,
    place_ref,
    block_ref,
    peer_ref,
    across_ref,
    corner_ref,
    own_ref,
    other_ref,
    extra_ref,
    par_ref,
    pre_out_ref,
    pre16_ref,
    sums_ref,
    cross_ref,
    near_ref,
    away_ref,
    pre_ref,
    weight_ref,
    pieces_ref,
    sems,
):
    rows = peer_ref.shape[0]
    quarter = block_ref.shape[1]
    chan, group = place_ref[0], place_ref[1]
    core = chan % 2
    sources = (block_ref.at[row_part(core, rows)], peer_ref, across_ref)
    arrivals = [
        move(source, pieces_ref.at[at], sems, 3 + at) for at, source in enumerate(sources)
    ]
    size = own_ref.shape[0] // len(order)
    for at, bits in enumerate(order):
        here = row_part(group ^ bits, size)
        weight_ref[here, lane_part(core)] = own_ref[at * size : (at + 1) * size]
        weight_ref[here, lane_part(1 - core)] = other_ref[at * size : (at + 1) * size]
    weight_moves = [
        move(weight_ref.at[row_part(chan, quarter)], near_ref, sems, 0),
        move(weight_ref.at[row_part(chan ^ 2, quarter)], away_ref, sems, 2),
    ]
    total = None
    for at in (3, 0, 1, 2):
        if at < 3:
            arrivals[at].wait()
        piece = pieces_ref[at] if at < 3 else corner_ref[...]
        weight = weight_ref[row_part(chan ^ at, quarter), :]
        term = jnp.dot(piece, weight, preferred_element_type=jnp.float32)
        total = term if total is None else total + term
    pre_ref[...] = total
    pre_move = move(pre_ref, pre_out_ref, sems, 1)
    pre16_ref[...] = total.astype(jnp.bfloat16)
    sums_ref[...] = extra_ref[...]
    cross_ref[0:8, :] = jnp.zeros((8, cross_ref.shape[1]), jnp.float32)
    cross_ref[8:32, :] = par_ref[...]
    for at, value in enumerate((total, total * total)):
        row = jnp.sum(value, 0, keepdims=True)
        sums_ref[at : at + 1, :] = row
        cross_ref[4 + at : 5 + at, :] = row
    for copy in weight_moves:
        copy.wait()
    pre_move.wait()


def first_conv(order, place, block, pieces, weights, extra, par):
    rows, quarter = pieces[0].shape
    width = 2 * weights[0].shape[1]
    return kernel_call(
        functools.partial(first_conv_body, order),
        (
            jax.ShapeDtypeStruct((rows, width), jnp.float32),
            jax.ShapeDtypeStruct((rows, width), jnp.bfloat16),
            jax.ShapeDtypeStruct((8, width), jnp.float32),
            jax.ShapeDtypeStruct((32, width), jnp.float32),
            jax.ShapeDtypeStruct((quarter, width), jnp.bfloat16),
            jax.ShapeDtypeStruct((quarter, width), jnp.bfloat16),
        ),
        [scalars, remote, remote, remote] + [whole] * 5,
        (
            pltpu.VMEM((rows, width), jnp.float32),
            pltpu.VMEM((4 * quarter, width), jnp.bfloat16),
            pltpu.VMEM((3, rows, quarter), jnp.bfloat16),
            pltpu.SemaphoreType.DMA((6,)),
        ),
        away=(0, 4, 5),
        lasts=4.0,
    )(place, block, *pieces, *weights, extra, par)


def second_body(
    count, place_ref, own_ref, oth_ref, stats_own_ref, stats_oth_ref, par_own_ref, par_oth_ref, out_ref,
    oth_here_ref, sems,
):
    width = own_ref.shape[1]
    y = place_ref[0] // 2
    arrivals = [move(oth_ref, oth_here_ref, sems, 0)]
    for side, pre, stats, par in (
        (y, own_ref, stats_own_ref, par_own_ref),
        (1 - y, oth_here_ref, stats_oth_ref, after_sums(par_oth_ref)),
    ):
        center, rate = norm_stats(*rows_of(stats), count)
        normed = (pre[...].astype(jnp.float32) - center) * rate * par[2:3] + par[3:4]
        out_ref[:, lane_part(side, width)] = (normed * logistic(normed)).astype(jnp.bfloat16)
        for copy in arrivals:
            copy.wait()
        arrivals = []


def second_half(count, place, own, oth, stats, pars):
    rows, width = own.shape
    return kernel_call(
        functools.partial(second_body, count),
        jax.ShapeDtypeStruct((rows, 2 * width), jnp.bfloat16),
        [scalars, whole, remote, whole, whole, whole, whole],
        (
            pltpu.VMEM((rows, width), jnp.bfloat16),
            pltpu.SemaphoreType.DMA((1,)),
        ),
        lasts=1.9,
    )(place, own, oth, *stats, *pars)


def last_conv_body(place_ref, mine_ref, peer_ref, weight_ref, extra_ref, out_ref, sums_ref):
    rows = mine_ref.shape[0]
    core = place_ref[0] % 2
    sums = squares = 0.0
    for side, part in ((core, mine_ref), (1 - core, peer_ref)):
        value = jnp.dot(part[...], weight_ref[...], preferred_element_type=jnp.float32)
        out_ref[row_part(side, rows), :] = value
        sums += jnp.sum(value, 0, keepdims=True)
        squares += jnp.sum(value * value, 0, keepdims=True)
    sums_ref[...] = extra_ref[...]
    sums_ref[0:1, :] = sums
    sums_ref[1:2, :] = squares


def last_conv(place, mine, peer, weight, extra):
    rows, depth = mine.shape
    width = weight.shape[1]
    return kernel_call(
        last_conv_body,
        (
            jax.ShapeDtypeStruct((2 * rows, width), jnp.float32),
            jax.ShapeDtypeStruct((8, width), jnp.float32),
        ),
        [scalars] + [whole] * 4,
        lasts=2.3,
    )(place, mine, peer, weight, extra)


def out_back_body(
    count,
    place_ref,
    pre_ref,
    block_ref,
    grad_ref,
    first_ref,
    second_ref,
    gain_ref,
    bias_ref,
    weight_ref,
    out_ref,
    total_out_ref,
    sums_ref,
    keep_ref,
    send_ref,
    total_ref,
    weight_here_ref,
    sems,
):
    rows = keep_ref.shape[0]
    weight_move = move(weight_ref, weight_here_ref, sems, 1)
    core = place_ref[0] % 2
    center, rate = norm_stats(*rows_of(first_ref[...] + second_ref[...]), count)
    gain, bias = gain_ref[...], bias_ref[...]
    step = rows // 7

    def add_step(at, sums):
        here = row_part(at, step)
        scaled = (pre_ref[here, :] - center) * rate
        total = scaled * gain + bias + block_ref[here, :].astype(jnp.float32)
        part = logistic(total)
        out_ref[here, :] = (total * part).astype(jnp.bfloat16)
        value = grad_ref[here, :].astype(jnp.float32) * (part * (1.0 + total * (1.0 - part)))
        total_ref[here, :] = value
        return (
            sums[0] + jnp.sum(value, 0, keepdims=True),
            sums[1] + jnp.sum(value * scaled, 0, keepdims=True),
        )

    zero = jnp.zeros((1, pre_ref.shape[1]), jnp.float32)
    sums, products = lax.fori_loop(0, 14, add_step, (zero, zero))
    put_sums(sums_ref, sums, products)
    total_move = move(total_ref, total_out_ref, sems, 0)
    local = 1.0 / (2 * rows)
    weight_move.wait()
    scale = gain * rate
    factor = scale * rate * (products * local)
    offset = scale * (sums * local) - factor * center

    def slope_rows(side):
        here = row_part(side, rows)
        value = scale * total_ref[here, :] - (factor * pre_ref[here, :] + offset)
        return lax.dot_general(
            value.astype(jnp.bfloat16),
            weight_here_ref[...],
            (((1,), (1,)), ((), ())),
            preferred_element_type=jnp.float32,
        )

    send_ref[...] = slope_rows(1 - core).astype(jnp.bfloat16)
    keep_ref[...] = slope_rows(core)
    total_move.wait()


def out_back(count, place, pre, block, grad, stats, gain, bias, weight):
    rows, width = pre.shape
    depth = weight.shape[0]
    return kernel_call(
        functools.partial(out_back_body, count),
        (
            jax.ShapeDtypeStruct((rows, width), jnp.bfloat16),
            jax.ShapeDtypeStruct((rows, width), jnp.float32),
            jax.ShapeDtypeStruct((8, width), jnp.float32),
            jax.ShapeDtypeStruct((rows // 2, depth), jnp.float32),
            jax.ShapeDtypeStruct((rows // 2, depth), jnp.bfloat16),
        ),
        [scalars] + [whole] * 7 + [remote],
        (
            pltpu.VMEM((rows, width), jnp.float32),
            pltpu.VMEM(weight.shape, weight.dtype),
            pltpu.SemaphoreType.DMA((2,)),
        ),
        away=(1,),
        lasts=7.5,
    )(place, pre, block, grad, *stats, gain, bias, weight)


def cross_body(place_ref, keep_ref, got_ref, own_ref, send_ref):
    width = own_ref.shape[1]
    y = place_ref[0] // 2
    for lanes, ref in ((1 - y, send_ref), (y, own_ref)):
        here = lane_part(lanes, width)
        value = keep_ref[:, here] + got_ref[:, here].astype(jnp.float32)
        ref[...] = value.astype(ref.dtype)


def cross_half(place, keep, got):
    rows, width = keep.shape[0], keep.shape[1] // 2
    return kernel_call(
        cross_body,
        (
            jax.ShapeDtypeStruct((rows, width), jnp.float32),
            jax.ShapeDtypeStruct((rows, width), jnp.bfloat16),
        ),
        [scalars, whole, whole],
        lasts=0.7,
    )(place, keep, got)


def out_delta_body(count, local, stats_ref, sums_ref, first_ref, second_ref, gain_ref, out_ref):
    center, rate = norm_stats(*rows_of(stats_ref), count)
    back = first_ref[...] + second_ref[...]
    scale = gain_ref[...] * rate
    first = scale * (back[0:1] / count - sums_ref[0:1] * local)
    second = scale * rate * (back[1:2] / count - sums_ref[1:2] * local)
    put_sums(out_ref, first - second * center, second)


def out_delta(count, rows, stats, sums, back, gain):
    return kernel_call(
        functools.partial(out_delta_body, count, 1.0 / rows),
        jax.ShapeDtypeStruct(stats.shape, jnp.float32),
        [whole] * 5,
    )(stats, sums, *back, gain)


def mid_slope_body(
    count,
    place_ref,
    keep_ref,
    got_ref,
    second_ref,
    mid_ref,
    stats_ref,
    par_ref,
    deltas0_ref,
    deltas1_ref,
    deltas2_ref,
    deltas3_ref,
    weights0_ref,
    weights1_ref,
    weights2_ref,
    weights3_ref,
    out_ref,
    out16_ref,
    sums_ref,
    here_ref,
    sems,
):
    width = mid_ref.shape[1]
    y = place_ref[0] // 2
    turned = (((1,), (1,)), ((), ()))
    factor, offset = None, None
    for deltas, weights in (
        (deltas0_ref, weights0_ref),
        (deltas1_ref, weights1_ref),
        (deltas2_ref, weights2_ref),
        (deltas3_ref, weights3_ref),
    ):
        own = weights[row_part(y, width), :]
        left = (weights[...].astype(jnp.float32) * deltas[1:2]).astype(jnp.bfloat16)
        term = lax.dot_general(left, own, turned, preferred_element_type=jnp.float32)
        factor = term if factor is None else factor + term
        high = deltas[0:1].astype(jnp.bfloat16).astype(jnp.float32)
        both = jnp.concatenate([high, deltas[0:1] - high, jnp.zeros_like(deltas[2:8])])
        term = lax.dot_general(
            both.astype(jnp.bfloat16), own, turned, preferred_element_type=jnp.float32
        )
        term = term[0:1] + term[1:2]
        offset = term if offset is None else offset + term
    high = factor.astype(jnp.bfloat16)
    low = (factor - high.astype(jnp.float32)).astype(jnp.bfloat16)
    delta = jnp.dot(second_ref[...], high, preferred_element_type=jnp.float32)
    delta += jnp.dot(second_ref[...], low, preferred_element_type=jnp.float32)
    grad = keep_ref[...] + got_ref[...].astype(jnp.float32) - delta - offset
    center, rate = norm_stats(*rows_of(stats_ref), count)
    scaled = (mid_ref[...] - center) * rate
    normed = scaled * par_ref[2:3] + par_ref[3:4]
    result = grad * silu_slope(normed)
    here_ref[...] = result
    out_move = move(here_ref, out_ref, sems, 0)
    out16_ref[...] = result.astype(jnp.bfloat16)
    put_sums(
        sums_ref, jnp.sum(result, 0, keepdims=True), jnp.sum(result * scaled, 0, keepdims=True)
    )
    out_move.wait()


def mid_slope(count, place, keep, got, second, mid, stats, par, deltas, weights):
    rows, width = mid.shape
    return kernel_call(
        functools.partial(mid_slope_body, count),
        (
            jax.ShapeDtypeStruct((rows, width), jnp.float32),
            jax.ShapeDtypeStruct((rows, width), jnp.bfloat16),
            jax.ShapeDtypeStruct((8, width), jnp.float32),
        ),
        [scalars] + [whole] * 14,
        (pltpu.VMEM((rows, width), jnp.float32), pltpu.SemaphoreType.DMA((1,))),
        away=(0,),
        lasts=3.3,
    )(place, keep, got, second, mid, stats, par, *deltas, *weights)


def out_weight_body(
    count, part, place_ref, rows_ref, pre_ref, total_ref, stats_ref, back_ref, gain_ref, *refs
):
    rows = rows_ref.shape[0]
    core = place_ref[0] % 2
    center, rate = norm_stats(*rows_of(stats_ref), count)
    here = row_part(1 - core if part else core, rows)
    scaled = (pre_ref[here, :] - center) * rate
    value = (gain_ref[...] * rate) * (
        total_ref[here, :] - back_ref[0:1] / count - scaled * (back_ref[1:2] / count)
    )
    result = exact(rows_ref[...], value.astype(jnp.bfloat16), ((0,), (0,)))
    if part:
        start_ref, out_ref, here_ref, sems = refs
        here_ref[...] = start_ref[...] + result
        move(here_ref, out_ref, sems, 0).wait()
    else:
        refs[0][...] = result


def out_weight(count, place, second, pre, total, stats, back, gain, start=None):
    rows, depth = second.shape
    width = pre.shape[1]
    part = 0 if start is None else 1
    return kernel_call(
        functools.partial(out_weight_body, count, part),
        jax.ShapeDtypeStruct((depth, width), jnp.float32),
        [scalars] + [whole] * (6 + part),
        (pltpu.VMEM((depth, width), jnp.float32), pltpu.SemaphoreType.DMA((1,))) if part else (),
        away=(0,) if part else (),
        lasts=1.7,
    )(place, second, pre, total, stats, back, gain, *([start] if part else []))


def in_slopes(count, grad, pre, stats, back, par):
    center, rate = norm_stats(*stats, count)
    scaled = (pre[...].astype(jnp.float32) - center) * rate
    value = (par[0:1] * rate) * (
        grad[...].astype(jnp.float32) - back[0:1] / count - scaled * (back[1:2] / count)
    )
    return value.astype(jnp.bfloat16)


def in_own_body(
    count, place_ref, d_ref, pre_ref, stats_ref, back_ref, par_ref, block_ref, peer_ref, across_ref, corner_ref,
    out_ref, keep_ref, send_ref, d_here_ref, pre_here_ref, keep_here_ref, pieces_ref, sems,
):
    rows, width = d_ref.shape
    arrivals = [move(d_ref, d_here_ref, sems, 0), move(pre_ref, pre_here_ref, sems, 1)]
    half = width // 2
    quarter = block_ref.shape[1]
    chan = place_ref[0]
    core = chan % 2
    sources = (block_ref.at[row_part(core, rows)], peer_ref, across_ref, corner_ref)
    pieces = [
        move(source, pieces_ref.at[at], sems, 6 + at) for at, source in enumerate(sources)
    ]
    for copy in arrivals:
        copy.wait()
    own = in_slopes(count, d_here_ref, pre_here_ref, rows_of(stats_ref), back_ref, par_ref)
    out_ref[...] = own
    moves = []
    for at, arrival in enumerate(pieces):
        arrival.wait()
        value = lax.dot_general(
            pieces_ref[at], own, (((0,), (0,)), ((), ())), preferred_element_type=jnp.float32
        )
        here = row_part(chan ^ at, quarter)
        low, high = value[:, :half], value[:, half:]
        keep_here_ref[here, :] = jnp.where(core == 0, low, high)
        moves.append(move(keep_here_ref.at[here], keep_ref.at[here], sems, 2 + at))
        send_ref[here, :] = jnp.where(core == 0, high, low).astype(jnp.bfloat16)
    for copy in moves:
        copy.wait()


def in_own(count, place, d_own, pre, stats, back, par, block, pieces):
    rows, width = d_own.shape
    full = 4 * block.shape[1]
    return kernel_call(
        functools.partial(in_own_body, count),
        (
            jax.ShapeDtypeStruct((rows, width), jnp.bfloat16),
            jax.ShapeDtypeStruct((full, width // 2), jnp.float32),
            jax.ShapeDtypeStruct((full, width // 2), jnp.bfloat16),
        ),
        [scalars, remote, remote] + [whole] * 3 + [remote] * 4,
        (
            pltpu.VMEM((rows, width), jnp.float32),
            pltpu.VMEM((rows, width), jnp.float32),
            pltpu.VMEM((full, width // 2), jnp.float32),
            pltpu.VMEM((4, rows, block.shape[1]), block.dtype),
            pltpu.SemaphoreType.DMA((10,)),
        ),
        away=(1,),
        lasts=4.5,
    )(place, d_own, pre, stats, back, par, block, *pieces)


def in_other_body(
    count, place_ref, own_ref, d_ref, pre_ref, stats_ref, back_ref, par_ref, out_ref, pre_here_ref, sems
):
    width = d_ref.shape[1]
    y = place_ref[0] // 2
    arrival = move(pre_ref, pre_here_ref, sems, 0)
    out_ref[:, lane_part(y, width)] = own_ref[...]
    arrival.wait()
    value = in_slopes(count, d_ref, pre_here_ref, rows_of(stats_ref, 4), back_ref, after_sums(par_ref))
    out_ref[:, lane_part(1 - y, width)] = value


def in_other(count, place, own, d_oth, pre_oth, stats, back, par):
    rows, width = d_oth.shape
    return kernel_call(
        functools.partial(in_other_body, count),
        jax.ShapeDtypeStruct((rows, 2 * width), jnp.bfloat16),
        [scalars, whole, whole, remote, whole, whole, whole],
        (pltpu.VMEM((rows, width), pre_oth.dtype), pltpu.SemaphoreType.DMA((1,))),
        lasts=2.0,
    )(place, own, d_oth, pre_oth, stats, back, par)


def input_grad_body(place_ref, mine_ref, peer_ref, near_ref, far_ref, total_ref, out_ref):
    rows = mine_ref.shape[0]
    width = near_ref.shape[1]
    core, y = place_ref[0] % 2, place_ref[0] // 2
    turned = (((1,), (1,)), ((), ()))
    for side, part in ((core, mine_ref), (1 - core, peer_ref)):
        here = row_part(side, rows)
        value = total_ref[here, :]
        for lanes, weight in ((y, near_ref), (1 - y, far_ref)):
            value += lax.dot_general(
                part[:, lane_part(lanes, width)],
                weight[...],
                turned,
                preferred_element_type=jnp.float32,
            )
        out_ref[here, :] = value.astype(jnp.bfloat16)


def input_grad(place, mine, peer, near, far, total):
    rows, quarter = total.shape
    return kernel_call(
        input_grad_body,
        jax.ShapeDtypeStruct((rows, quarter), jnp.bfloat16),
        [scalars] + [whole] * 5,
        lasts=2.8,
    )(place, mine, peer, near, far, total)


def opening_body(
    place_ref, block_ref, mid_ref, out_ref, mine_ref, others_ref, packed_ref, rows_ref, small_ref, sems
):
    rows = mine_ref.shape[0]
    core = place_ref[0] % 2
    count, width = mid_ref.shape
    size = out_ref.shape[0]
    sources = [(block_ref.at[row_part(side, rows)], rows_ref.at[at]) for at, side in ((0, core), (1, 1 - core))]
    sources.append((mid_ref, small_ref.at[pl.ds(0, count)]))
    for at in range(4):
        here = small_ref.at[pl.ds(count + at * size, size)]
        sources.append((out_ref.at[:, pl.ds(at * width, width)], here))
    arrivals = [move(*pair, sems, at) for at, pair in enumerate(sources)]
    moves = []
    for at, target in enumerate((mine_ref, others_ref)):
        arrivals[at].wait()
        moves.append(move(rows_ref.at[at], target, sems, 7 + at))
    for copy in arrivals[2:]:
        copy.wait()
    moves.append(move(small_ref, packed_ref, sems, 9))
    for copy in moves:
        copy.wait()


def opening(place, block, mid, out):
    half = block.shape[0] // 2
    rows, width = mid.shape
    size = out.shape[0]
    if size % BLOCK or rows % BLOCK:
        parts = [out[:, at * width : (at + 1) * width] for at in range(4)]
        core = place[0] % 2
        halves = [
            lax.dynamic_slice_in_dim(block, side * half, half, 0) for side in (core, 1 - core)
        ]
        return (*halves, jnp.concatenate([mid] + parts, 0))
    rows_shape = jax.ShapeDtypeStruct((half, block.shape[1]), block.dtype)
    return kernel_call(
        opening_body,
        (rows_shape, rows_shape, jax.ShapeDtypeStruct((rows + 4 * size, width), mid.dtype)),
        [scalars, remote, remote, remote],
        (
            pltpu.VMEM((2, half, block.shape[1]), block.dtype),
            pltpu.VMEM((rows + 4 * size, width), mid.dtype),
            pltpu.SemaphoreType.DMA((10,)),
        ),
        away=(0, 1, 2),
    )(place, block, mid, out)


def pack_body(gain_in, bias_in, gain_mid, bias_mid, gate_bias, near, far, stem_gain, stem_bias, out_ref, stem_ref):
    stem_ref[...] = jnp.zeros_like(stem_ref)
    stem_ref[0:1, :] = stem_gain[...]
    stem_ref[1:2, :] = stem_bias[...]
    for at, ref in enumerate((gain_in, bias_in, gain_mid, bias_mid, gate_bias)):
        out_ref[at : at + 1, :] = ref[...]
    out_ref[5:14, :] = near[...]
    out_ref[14:23, :] = far[...]
    out_ref[23:24, :] = jnp.zeros_like(out_ref[23:24, :])


def pack_params(rows, near, far, stem):
    width, outs = near.shape[1], stem[0].shape[0]
    return kernel_call(
        pack_body,
        (
            jax.ShapeDtypeStruct((24, width), jnp.float32),
            jax.ShapeDtypeStruct((8, outs), jnp.float32),
        ),
        [whole] * 9,
    )(*[row.reshape(1, width) for row in rows], near, far, *[row.reshape(1, outs) for row in stem])


TAPS = 7
LANES = 16


def exact(left, right, contract):
    return lax.dot_general(
        left, right, (contract, ((), ())), preferred_element_type=jnp.float32
    )


def spot(core, outs, width, part):
    lane = lax.broadcasted_iota(jnp.int32, (outs, width), 1)
    channel = lax.broadcasted_iota(jnp.int32, (outs, width), 0)
    return (lane == core * 2 * outs + part * outs + channel).astype(jnp.float32)


def stem_row(core, width, first, second):
    row = None
    for part, value in enumerate((first, second)):
        column = jnp.sum(jnp.sum(value, 0), 1, keepdims=True)
        term = jnp.sum(column * spot(core, value.shape[1], width, part), 0, keepdims=True)
        row = term if row is None else row + term
    at = lax.broadcasted_iota(jnp.int32, (8, width), 0)
    return jnp.where(at == 2, row, 0.0)


def stem_columns(core, outs, stats_ref):
    row = stats_ref[2:3, :]
    return [
        jnp.sum(row * spot(core, outs, row.shape[1], part), 1, keepdims=True) for part in range(2)
    ]


def upright(row):
    size = row.shape[1]
    at = lax.broadcasted_iota(jnp.int32, (size, size), 0)
    same = at == lax.broadcasted_iota(jnp.int32, (size, size), 1)
    return jnp.sum(jnp.where(same, row, 0.0), 1, keepdims=True)


def stem_front_body(
    place_ref, video_ref, weight_ref, pre_out_ref, rows_out_ref, pick_out_ref, extra_ref, flat_ref, parts_ref,
    pre_ref, rows_ref, pick_ref, sems,
):
    segs, colours, size = video_ref.shape
    side = 32
    half = size // 2
    quarter = half // 2
    core = place_ref[0] % 2
    at = lax.broadcasted_iota(jnp.int32, (LANES, size), 0)
    zero = jnp.zeros((LANES - colours, size), jnp.float32)

    def plane_step(seg, _):
        value = jnp.concatenate([video_ref[seg].astype(jnp.float32), zero])
        moving = pltpu.roll(value, LANES - 3, 0) - value
        center = pltpu.roll(value, 6, 0)
        plane = jnp.where(at < 12, moving, jnp.where(at < 15, center, 0.0))
        flat_ref[pl.ds(pl.multiple_of(seg * LANES, LANES), LANES), :] = plane.astype(jnp.bfloat16)
        return 0

    lax.fori_loop(0, segs, plane_step, 0, unroll=4)
    source = lax.broadcasted_iota(jnp.int32, (size, half), 0)
    lane = lax.broadcasted_iota(jnp.int32, (size, half), 1)
    lanes = lax.broadcasted_iota(jnp.int32, (segs * LANES, half), 1)
    for parity in range(2):
        hit = source == 2 * side * (lane // side) + side * parity + lane % side
        rows = jnp.dot(
            flat_ref[...],
            jnp.where(hit, 1.0, 0.0).astype(jnp.bfloat16),
            preferred_element_type=jnp.float32,
        )
        for tap in range(TAPS):
            if (tap - 3) % 2 != parity:
                continue
            shift = (tap - 3 - parity) // 2 * side
            value = rows
            if shift:
                value = pltpu.roll(rows, (-shift) % half, 1)
                inside = lanes < half - shift if shift > 0 else lanes >= -shift
                value = jnp.where(inside, value, 0.0)
            value = value.astype(jnp.bfloat16).reshape(segs, LANES, half)
            rows_ref[:, tap * LANES : (tap + 1) * LANES, :] = value
    weight = weight_ref[...]
    moves = [move(rows_ref, rows_out_ref, sems, 0)]

    def seg_step(seg, _):
        value = jnp.dot(weight, rows_ref[seg], preferred_element_type=jnp.float32)
        value = value.astype(jnp.bfloat16)
        here = pl.ds(pl.multiple_of(seg * LANES, LANES), LANES)
        for tap in range(TAPS):
            parts_ref[tap, here, :] = value[tap * LANES : (tap + 1) * LANES]
        return 0

    lax.fori_loop(0, segs, seg_step, 0, unroll=4)
    source = lax.broadcasted_iota(jnp.int32, (half, quarter), 0)
    lane = lax.broadcasted_iota(jnp.int32, (half, quarter), 1)
    total = None
    for tap in range(TAPS):
        column = 2 * (lane % LANES) + tap - 3
        hit = (source == side * (lane // LANES) + column) & (column >= 0) & (column < side)
        pick = jnp.where(hit, 1.0, 0.0).astype(jnp.bfloat16)
        pick_ref[tap] = pick
        term = jnp.dot(parts_ref[tap], pick, preferred_element_type=jnp.float32)
        total = term if total is None else total + term
    total = total.reshape(segs, LANES, quarter)
    pre_ref[...] = total
    moves += [move(pick_ref, pick_out_ref, sems, 1), move(pre_ref, pre_out_ref, sems, 2)]
    extra_ref[...] = stem_row(core, extra_ref.shape[1], total, total * total)
    for copy in moves:
        copy.wait()


def stem_front(place, video, weight, width):
    segs, _, size = video.shape
    return kernel_call(
        stem_front_body,
        (
            jax.ShapeDtypeStruct((segs, LANES, size // 4), jnp.float32),
            jax.ShapeDtypeStruct((segs, TAPS * LANES, size // 2), jnp.bfloat16),
            jax.ShapeDtypeStruct((TAPS, size // 2, size // 4), jnp.bfloat16),
            jax.ShapeDtypeStruct((8, width), jnp.float32),
        ),
        [scalars, whole, whole],
        (
            pltpu.VMEM((segs * LANES, size), jnp.bfloat16),
            pltpu.VMEM((TAPS, segs * LANES, size // 2), jnp.bfloat16),
            pltpu.VMEM((segs, LANES, size // 4), jnp.float32),
            pltpu.VMEM((segs, TAPS * LANES, size // 2), jnp.bfloat16),
            pltpu.VMEM((TAPS, size // 2, size // 4), jnp.bfloat16),
            pltpu.SemaphoreType.DMA((3,)),
        ),
        away=(0, 1, 2),
        lasts=0.0,
    )(place, video, weight)


def stem_norm(count, core, pre, stats_ref, par_ref):
    outs = pre.shape[1]
    center, rate = norm_stats(*stem_columns(core, outs, stats_ref), count)
    scaled = (pre - center) * rate
    gain, bias = upright(par_ref[0:1]), upright(par_ref[1:2])
    return scaled, scaled * gain + bias, gain * rate


def stem_out_body(count, place_ref, pre_ref, grad_ref, stats_ref, par_ref, out_ref, extra_ref):
    core = place_ref[0] % 2
    scaled, normed, _ = stem_norm(count, core, pre_ref[...], stats_ref, par_ref)
    part = logistic(normed)
    out_ref[...] = (normed * part).astype(jnp.bfloat16)
    value = grad_ref[...].astype(jnp.float32) * (part * (1.0 + normed * (1.0 - part)))
    extra_ref[...] = stem_row(core, extra_ref.shape[1], value, value * scaled)


def stem_output(count, place, pre, grad, stats, par, width):
    return kernel_call(
        functools.partial(stem_out_body, count),
        (
            jax.ShapeDtypeStruct(pre.shape, jnp.bfloat16),
            jax.ShapeDtypeStruct((8, width), jnp.float32),
        ),
        [scalars] + [whole] * 4,
        lasts=1.8,
    )(place, pre, grad, stats, par)


def stem_back_body(
    count, first, place_ref, pre_ref, grad_ref, stats_ref, back_ref, par_ref, rows_ref, pick_ref, start_ref, out_ref, slopes_ref,
):
    core = place_ref[0] % 2
    segs, outs, pixels = pre_ref.shape
    scaled, normed, scale = stem_norm(count, core, pre_ref[...], stats_ref, par_ref)
    bias_grad, gain_grad = stem_columns(core, outs, back_ref)
    value = grad_ref[...].astype(jnp.float32) * silu_slope(normed)
    value = scale * (value - bias_grad / count - scaled * (gain_grad / count))
    value = value.astype(jnp.bfloat16).reshape(segs * outs, pixels)
    half = rows_ref.shape[2]
    for tap in range(TAPS):
        spread = exact(value, pick_ref[tap], ((1,), (1,)))
        slopes_ref[:, tap * LANES : (tap + 1) * LANES, :] = spread.astype(jnp.bfloat16).reshape(
            segs, outs, half
        )
    total = None
    for seg in range(segs):
        term = exact(rows_ref[seg], slopes_ref[seg], ((1,), (1,)))
        total = term if total is None else total + term
    size = TAPS * LANES
    rows = size // 2
    if first:
        out_ref[...] = jnp.zeros_like(out_ref)
    else:
        out_ref[...] = start_ref[...]
    out_ref[:, :size] += total[:rows]
    out_ref[:, 128 : 128 + size] += total[rows:]


def stem_back(count, place, pre, grad, stats, back, par, rows, pick, start, chunk, chunks):
    segs, outs, pixels = pre.shape
    size = segs // chunks

    def part(*tail):
        return pl.BlockSpec((size,) + tail, lambda at: (chunk, 0, 0))

    def all_of(shape):
        return pl.BlockSpec(shape, lambda at: (0,) * len(shape))

    small = (TAPS * LANES // 2, 256)
    first = start is None
    start = jnp.zeros((8, 256), jnp.float32) if first else start
    return pl.pallas_call(
        functools.partial(stem_back_body, count, first),
        grid=(1,),
        out_shape=jax.ShapeDtypeStruct(small, jnp.float32),
        in_specs=[scalars, part(outs, pixels), part(outs, pixels)]
        + [all_of(stats.shape), all_of(back.shape), all_of(par.shape)]
        + [part(*rows.shape[1:]), all_of(pick.shape), all_of(start.shape)],
        out_specs=all_of(small),
        scratch_shapes=[pltpu.VMEM((size, TAPS * LANES, rows.shape[2]), jnp.bfloat16)],
        compiler_params=pltpu.CompilerParams(vmem_limit_bytes=vmem_limit),
        cost_estimate=pl.CostEstimate(
            flops=int(1.7 * flops_per_us), bytes_accessed=0, transcendentals=0
        ),
    )(place, pre, grad, stats, back, par, pltpu.with_memory_space_constraint(rows, pltpu.HBM), pick, start)


def stem_weight(center, diff):
    outs = center.shape[1]
    value = jnp.concatenate([diff, center, jnp.zeros((TAPS * TAPS, outs), center.dtype)])
    value = value.reshape(LANES, TAPS, TAPS, outs)
    return value.transpose(2, 3, 1, 0).reshape(TAPS * outs, TAPS * LANES)


def stem_grads_body(packed_ref, center_ref, diff_ref):
    full = jnp.concatenate([packed_ref[:, :128], packed_ref[:, 128:]])
    for row in range(TAPS):
        value = full[row * LANES : (row + 1) * LANES]
        for col in range(TAPS):
            here = value[:, col * LANES : (col + 1) * LANES]
            at = row * TAPS + col
            diff_ref[pl.ds(at, 12, stride=TAPS * TAPS), :] = here[:12]
            center_ref[pl.ds(at, 3, stride=TAPS * TAPS), :] = here[12:15]


def stem_grads(packed, outs):
    return kernel_call(
        stem_grads_body,
        (
            jax.ShapeDtypeStruct((3 * TAPS * TAPS, outs), jnp.float32),
            jax.ShapeDtypeStruct((12 * TAPS * TAPS, outs), jnp.float32),
        ),
        [whole],
    )(packed)


def after(value, *marks):
    return lax.optimization_barrier((value, marks))[0]


def swap(value, axis, bit):
    size = lax.axis_size(axis)
    return lax.ppermute(value, axis, [(at, at ^ bit) for at in range(size)])


def steps_of(axis):
    size = lax.axis_size(axis)
    assert size & (size - 1) == 0
    return [1 << at for at in range(size.bit_length() - 1)]


def sum_over(value, axis, jobs=()):
    jobs = list(jobs)
    value, got = open_sum(value, axis, jobs)
    return value + got


def open_sum(value, axis, jobs=()):
    jobs = [job or (lambda mark: mark) for job in jobs]
    bits = steps_of(axis)
    for bit in bits:
        got = swap(value, axis, bit)
        if jobs:
            got = after(got, jobs.pop(0)(value))
        if bit != bits[-1]:
            value = value + got
    for job in jobs:
        got = after(got, job(value))
    return value, got


def ordered(second, own, other, axis=0):
    return jnp.where(
        second, jnp.concatenate([other, own], axis), jnp.concatenate([own, other], axis)
    )


def gather_rows(value, axis):
    order = [0]
    for bit in reversed(steps_of(axis)):
        value = jnp.concatenate([value, swap(value, axis, bit)])
        order += [at ^ bit for at in order]
    return value, order


def halve_body(bit, parts, far, place_ref, keep_ref, *refs):
    got_refs, refs = refs[:parts], refs[parts:]
    mine_ref, send_ref = refs[:2]
    count, size = send_ref.shape[:2]
    high = (place_ref[1] // bit) % 2
    source, places, moves = keep_ref, [], []
    for block in range(count):
        for side in (1 - high, high):
            here = pl.ds(pl.multiple_of((2 * block + side) * size, size), size)
            places.append((block, side, here))
    if far:
        source, sems = refs[2:]
        moves = [
            move(keep_ref.at[here], source.at[here], sems, at)
            for at, (_, _, here) in enumerate(places)
        ]
    for at, (block, side, here) in enumerate(places):
        if far:
            moves[at].wait()
        value = source[here, :]
        if parts:
            part = block * parts // count
            first = 2 * (block - part * count // parts) + side
            got = got_refs[part][pl.ds(pl.multiple_of(first * size, size), size), :]
            value = value + got.astype(jnp.float32)
        ref = mine_ref if at % 2 else send_ref
        ref[block] = value.astype(ref.dtype)


def halve(place, keep, got, bits, at, far=False):
    rows, width = keep.shape
    left = sorted(bits, reverse=True)
    outer = 1 << left.index(at)
    inner = rows // (2 * outer)
    if inner % BLOCK or outer % max(len(got), 1):
        total = keep + jnp.concatenate(got).astype(jnp.float32) if got else keep
        blocks = total.reshape(outer, 2, inner, width)
        low, high = blocks[:, 0].reshape(-1, width), blocks[:, 1].reshape(-1, width)
        mine = (place[1] // at) % 2 == 0
        return jnp.where(mine, low, high), jnp.where(mine, high, low).astype(jnp.bfloat16)
    shape = (outer, inner, width)
    scratch = [pltpu.VMEM(keep.shape, keep.dtype), pltpu.SemaphoreType.DMA((2 * outer,))]
    mine, send = kernel_call(
        functools.partial(halve_body, at, len(got), far),
        (jax.ShapeDtypeStruct(shape, jnp.float32), jax.ShapeDtypeStruct(shape, jnp.bfloat16)),
        [scalars, remote if far else whole] + [whole] * len(got),
        scratch if far else [],
        lasts=2.0 if far else 0.7,
    )(place, keep, *got)
    return mine.reshape(-1, width), send.reshape(-1, width)


def transposed(left, right):
    return lax.dot_general(
        left, right, (((1,), (1,)), ((), ())), preferred_element_type=jnp.float32
    )


def weight_grad(left, right):
    return lax.dot_general(
        left, right, (((0,), (0,)), ((), ())), preferred_element_type=jnp.float32
    )


def per_device(
    block_in,
    weight_in,
    weight_mid,
    weight_out,
    gain_in,
    bias_in,
    gain_mid,
    bias_mid,
    gain_out,
    bias_out,
    kernel_near,
    kernel_far,
    gate_bias,
    same_video,
    video,
    stem_center,
    stem_diff,
    stem_gain,
    stem_bias,
    block_grad,
    stem_grad,
):
    groups = lax.axis_size("dp")
    assert lax.axis_size("chan") == 4
    clips = same_video.shape[0]
    rows, quarter = block_in.shape
    half = rows // 2
    narrow = weight_in.shape[1]
    width = 2 * narrow
    count = float(rows * groups)
    segs = video.shape[0]
    stem_count = float(segs * stem_grad.shape[2] * groups)
    chan = lax.axis_index("chan")
    core, y = chan % 2, chan // 2
    place = jnp.stack([chan, lax.axis_index("dp")])

    mine, others, packed = opening(place, block_in, weight_mid, weight_out)
    pieces = [swap(others, "chan", 1), swap(mine, "chan", 2)]
    pieces.append(swap(after(others, pieces[1]), "chan", 3))

    own_in, order = gather_rows(after(weight_in, mine, others), "dp")
    weights_in = [own_in, swap(own_in, "chan", 1)]
    gathered = lax.all_gather(packed, "dp", axis=0)

    params, stem_par = pack_params(
        [gain_in, bias_in, gain_mid, bias_mid, gate_bias],
        kernel_near,
        kernel_far,
        [stem_gain, stem_bias],
    )
    par_own = ordered(core == 1, params, swap(params, "chan", 1), 1)
    pars = [par_own]
    same = lax.dynamic_slice_in_dim(same_video, core * (clips // 2), clips // 2, 0)
    same = jnp.pad(same, ((0, 0), (0, 1)))
    gain_row, bias_row = gain_out.reshape(1, -1), bias_out.reshape(1, -1)

    outs = stem_grad.shape[1]
    pre_stem, stem_rows, stem_pick, extra = stem_front(
        place, video, stem_weight(stem_center, stem_diff), width
    )

    def both_sums(sums, jobs=()):
        jobs = [run or (lambda mark: mark) for run in jobs]
        got = swap(sums, "chan", 1)
        if jobs:
            got = after(got, jobs[0](sums))
        own = sum_over(sums + got, "dp", jobs[1:4])
        oth = swap(own, "chan", 2)
        for run in jobs[4:]:
            oth = after(oth, run(own))
        return [own, oth]

    made = {}

    def in_turn(*works):
        def run(mark):
            results = []
            for work in works:
                results.append(work((mark, results) if results else mark))
            return results

        return run

    def job(name, work):
        def run(mark):
            made[name] = work(mark)
            return made[name]

        return run

    pre_in, pre_in16, sums_in, cross_in, near_in, away_in = first_conv(
        order, place, block_in, pieces, weights_in, extra, par_own
    )

    blocks = gathered
    if weight_mid.shape[0] % BLOCK:
        blocks = gathered[:, : weight_mid.shape[0]].reshape(1, -1, narrow)

    def mid_blocks(mark):
        own = after(blocks, mark)
        return [own, swap(own, "chan", 1)]


    def out_rows(mark):
        parts, first, size = after(gathered, mark), weight_mid.shape[0], weight_out.shape[0]
        parts = [parts[:, first + at * size : first + (at + 1) * size] for at in range(4)]
        return jnp.concatenate([part.reshape(-1, narrow) for part in parts], 1)

    cross_got = swap(cross_in, "chan", 2)
    corner_got = swap(cross_in[:8], "chan", 3)
    pre_in_oth = swap(after(pre_in16, cross_got), "chan", 2)
    sums_in = sums_in + swap(sums_in, "chan", 1) + cross_got[:8] + corner_got
    open_in = open_sum(
        sums_in, "dp", [None, in_turn(job("weights_mid", mid_blocks), job("full_out", out_rows))]
    )
    pars.append(cross_got)
    weights_mid = made["weights_mid"]
    full_out = made["full_out"]

    out_across = swap(after(full_out, open_in), "chan", 2)

    mixed, gates, pre_mid, pre_mid16, sums_mid = gate_mid(
        count, place, same, pre_in, pre_in_oth, open_in, pars, weights_mid
    )
    pre_mid_oth = swap(pre_mid16, "chan", 2)
    first, second_part = after(open_in, sums_mid)
    stats_stem = stats_in = first + second_part

    def stem_half(mark):
        return stem_output(
            stem_count, place, after(pre_stem, mark), stem_grad, stats_stem, stem_par, quarter
        )

    def slab_of(mark):
        slab = after(gathered, mark)[:, : weight_mid.shape[0]].reshape(9, 2, width, narrow)
        return lax.dynamic_slice_in_dim(slab, 1 - y, 1, 1).reshape(9 * width, narrow)

    stats_mid = both_sums(
        sums_mid,
        [
            None,
            job("stem", stem_half),
            in_turn(job("slab", slab_of), lambda mark: out_across),
            job("turned", lambda mark: turn(after(mixed, mark))),
            lambda mark: pre_mid_oth,
        ],
    )
    stem_out, extra = made["stem"]

    second = second_half(count, place, pre_mid, pre_mid_oth, stats_mid, pars)
    second_peer = swap(second, "chan", 1)
    pre_out, sums_out = last_conv(place, second, second_peer, full_out, extra)
    slab_across = swap(after(made["slab"], stats_mid), "chan", 2)
    open_out = after(open_sum(sums_out, "dp"), slab_across)
    out_peers = [swap(after(value, open_out), "chan", 1) for value in (full_out, out_across)]
    weights_out = [full_out, out_peers[0], out_across, out_peers[1]]
    block_out, grad_total, sums_back, keep, send = out_back(
        count, place, pre_out, block_in, block_grad, open_out, gain_row, bias_row, full_out
    )
    first, second_part = after(open_out, sums_back)
    stats_out = first + second_part
    got = swap(send, "chan", 1)

    def cross(mark):
        return cross_half(place, keep, after(got, mark))

    def stem_part(chunk, start):
        def work(mark):
            return stem_back(
                stem_count, place, after(pre_stem, mark), stem_grad, stats_in, stats_out,
                stem_par, stem_rows, stem_pick, start and made[start], chunk, 4,
            )

        return job(f"stem{chunk}", work)

    open_back = open_sum(
        sums_back, "dp", [stem_part(0, None), job("cross", cross), stem_part(1, "stem0")]
    )
    keep, send = made["cross"]
    got = swap(send, "chan", 2)
    delta = out_delta(count, rows, stats_out, sums_back, open_back, gain_row)
    deltas = [delta] + [swap(delta, "chan", at) for at in (1, 2, 3)]

    grad_mid, grad_mid16, sums_mid_back = mid_slope(
        count, place, keep, got, second, pre_mid, stats_mid[0], pars[0], deltas, weights_out
    )
    grad_mid_oth = swap(grad_mid16, "chan", 2)
    first, second_part = after(open_back, sums_mid_back)
    back_out = first + second_part

    aways_mid = [slab_across, swap(after(slab_across, sums_mid_back), "chan", 1)]

    def out_part(start, rows_of_second):
        def work(mark):
            return out_weight(
                count, place, rows_of_second, pre_out, grad_total, stats_out, after(back_out, mark),
                gain_row, start and made[start],
            )

        return work

    def own_slopes(mark):
        return mid_own(count, grad_mid, pre_mid, stats_mid[0], mark, pars[0])

    bits = steps_of("dp")

    back_mid = both_sums(sums_mid_back, [
        None,
        job("out0", out_part(None, second)),
        job("out1", out_part("out0", second_peer)),
        stem_part(2, "stem1"),
        in_turn(job("slopes", own_slopes), stem_part(3, "stem2")),
    ])
    slopes = made["slopes"]
    sum_out = lax.psum_scatter(made["out1"], "dp", scatter_dimension=0, tiled=True)
    stem_first = swap(made["stem3"], "dp", bits[0])
    far_in = swap(after(away_in, sums_mid_back), "chan", 2)

    grad_in, grad_in16, sums_in_back = mid_back(
        count, place, same, slopes, grad_mid_oth, pre_mid_oth, stats_mid[1], back_mid[1], pre_in,
        gates, stats_in, pars, weights_mid, aways_mid,
    )
    grad_in_oth = swap(grad_in16, "chan", 2)

    def mid_part(mark):
        return mid_weight(place, made["turned"], after(slopes, mark))

    def mid_rest(mark):
        keep, *sends = made["mid"]
        got = [after(swap(send, "chan", 1), mark) for send in sends]
        return halve(place, keep, got, mid_bits, mid_bits[0], True)

    mid_bits = bits

    def mid_step(at):
        def work(mark):
            keep, got = made["keep"], after(swap(made["send"], "dp", mid_bits[at - 1]), mark)
            made["keep"], made["send"] = halve(place, keep, [got], mid_bits[at:], mid_bits[at])
            return made["send"]

        return work

    def mid_first(mark):
        made["keep"], made["send"] = mid_rest(mark)
        return made["send"]

    def own_in_back(mark):
        return in_own(
            count, place, grad_in, pre_in, stats_in, mark, pars[0], block_in, pieces
        )

    def stem_next(mark):
        return made["stem3"] + after(stem_first, mark)

    back_in = both_sums(
        sums_in_back,
        [
            None,
            job("mid", mid_part),
            job("stem_total", stem_next),
            in_turn(mid_first, lambda mark: grad_in_oth),
            job("in", own_in_back),
        ],
    )

    grad_own, keep, send = made["in"]
    got = swap(send, "chan", 1)
    grad_pre = in_other(
        count, place, after(grad_own, send), grad_in_oth, pre_in_oth, stats_in, back_in[1], pars[1]
    )
    grad_peer = swap(grad_pre, "chan", 1)
    mark, stem_total = grad_pre, made["stem_total"]
    assert len(bits) > 1
    last = len(bits) - 1
    for at, bit in enumerate(bits):
        got = after(got, mark, sum_out) if at == 1 else after(got, mark)
        keep, send = halve(place, keep, [got], bits[at:], bit, at == 0)
        got = swap(send, "dp", bit)
        mark = send
        if at < last:
            mark = mid_step(at + 1)(mark)
            if at == 0:
                near = after(near_in, mark)
                mark = grad_block_in = input_grad(
                    place, grad_pre, grad_peer, near, far_in, grad_total
                )
            stem_got = swap(stem_total, "dp", bits[at + 1])
            mark = stem_total = after(stem_total, mark) + stem_got
    sum_mid = after(made["keep"], send) + swap(made["send"], "dp", bit).astype(jnp.float32)
    sum_in = keep + after(got, sum_mid).astype(jnp.float32)
    center_grad, diff_grad = stem_grads(stem_total, outs)

    def my_columns(value):
        return lax.dynamic_slice_in_dim(value, core * narrow, narrow, value.ndim - 1)

    def my_stem(value):
        row = lax.dynamic_slice(value, (2, core * 2 * outs), (1, 2 * outs))[0]
        return row[:outs], row[outs:]

    gate_grads = my_columns(back_in[0][8:])
    mid_grads, in_grads = my_columns(back_mid[0]), my_columns(back_in[0])
    stem_bias_grad, stem_gain_grad = my_stem(stats_out)
    return (
        block_out,
        stem_out,
        grad_block_in,
        sum_in,
        sum_mid,
        sum_out,
        in_grads[1],
        in_grads[0],
        mid_grads[1],
        mid_grads[0],
        back_out[1],
        back_out[0],
        gate_grads[1:10],
        gate_grads[10:19],
        gate_grads[0],
        center_grad,
        diff_grad,
        stem_gain_grad,
        stem_bias_grad,
    )


def solution(mesh):
    placed = (
        P("dp", "chan"),
        P("dp", "chan"),
        P("dp", "chan"),
        P("dp", "chan"),
        P("chan"),
        P("chan"),
        P("chan"),
        P("chan"),
        P("chan"),
        P("chan"),
        P(None, "chan"),
        P(None, "chan"),
        P("chan"),
        P("dp", None),
        P("dp", None, None),
        P(None, "chan"),
        P(None, "chan"),
        P("chan"),
        P("chan"),
        P("dp", "chan"),
        P("dp", "chan", None),
    )
    return jax.shard_map(
        per_device,
        mesh=mesh,
        in_specs=placed,
        out_specs=(
            P("dp", "chan"),
            P("dp", "chan", None),
            P("dp", "chan"),
            P("dp", "chan"),
            P("dp", "chan"),
            P("dp", "chan"),
            P("chan"),
            P("chan"),
            P("chan"),
            P("chan"),
            P("chan"),
            P("chan"),
            P(None, "chan"),
            P(None, "chan"),
            P("chan"),
            P(None, "chan"),
            P(None, "chan"),
            P("chan"),
            P("chan"),
        ),
        check_vma=False,
    )
```

```python
import functools

import jax
import jax.numpy as jnp
from jax import lax
from jax.experimental import pallas as pl
from jax.experimental.pallas import tpu as pltpu
from jax.sharding import PartitionSpec as P

SEG = 8
SIDE = 7
FRAMES = 5
PIXELS = SIDE * SIDE
BLOCK = 16
SPAN = SIDE + 2

eps = 1e-05
vmem_limit = 32 * 1024 * 1024
flops_per_us = 0.3e9

whole = pl.BlockSpec(memory_space=pltpu.VMEM)
remote = pl.BlockSpec(memory_space=pltpu.HBM)
scalars = pl.BlockSpec(memory_space=pltpu.SMEM)


def logistic(value):
    return 0.5 * jnp.tanh(0.5 * value) + 0.5


def silu_slope(value):
    part = logistic(value)
    return part * (1.0 + value * (1.0 - part))


def norm_stats(totals, squares, count):
    center = totals / count
    spread = squares / count - center * center
    return (center, lax.rsqrt(spread + eps))


def move(source, target, sems, at):
    copy = pltpu.make_async_copy(source, target, sems.at[at])
    copy.start()
    return copy


def kernel_call(body, out_shape, in_specs, scratch=(), lasts=1.0, away=(), held=()):
    several = isinstance(out_shape, tuple)
    shapes = list(out_shape) if several else [out_shape]
    specs = [remote if at in away else whole for at in range(len(shapes))]
    shapes = [
        (pltpu.HBM if at in away else pltpu.VMEM)(shape.shape, shape.dtype)
        if at in away or at in held
        else shape
        for at, shape in enumerate(shapes)
    ]
    call = pl.pallas_call(
        body,
        out_shape=tuple(shapes) if several else shapes[0],
        in_specs=in_specs,
        out_specs=tuple(specs) if several else specs[0],
        scratch_shapes=list(scratch),
        compiler_params=pltpu.CompilerParams(vmem_limit_bytes=vmem_limit),
        cost_estimate=pl.CostEstimate(
            flops=int(lasts * flops_per_us), bytes_accessed=0, transcendentals=0
        ),
    )

    def run(*args):
        return call(
            *[
                pltpu.with_memory_space_constraint(arg, pltpu.HBM) if spec is remote else arg
                for arg, spec in zip(args, in_specs, strict=True)
            ]
        )

    return run


PAIRS = SEG // 2
CLIP = SEG * PIXELS


def pair_row(clip, pair):
    return pl.multiple_of(BLOCK * (2 + SPAN * (PAIRS * clip + pair)), BLOCK)


def clip_view(ref, clip, extra=0):
    return ref.at[pl.ds(pl.multiple_of(clip * CLIP, 8), CLIP + extra)]


def lane_mask(width):
    return lax.broadcasted_iota(jnp.int32, (1, 8, width), 1)


def load_map(ref, first, lanes):
    return jnp.stack([ref[pl.ds(first + SIDE * at, 8), lanes] for at in range(SIDE)])


def store_map(ref, first, lanes, value):
    for at in range(SIDE):
        ref[pl.ds(first + SIDE * at, SIDE), lanes] = value[at][:SIDE]


def two_maps(early, late):
    both = jnp.stack([early, late], axis=1)
    return both.reshape(SIDE * BLOCK, early.shape[-1])


def load_rows(ref, first, lanes):
    return [ref[pl.ds(first + SIDE * at, 8), lanes] for at in range(SIDE)]


def store_rows(ref, first, lanes, rows):
    for at in range(SIDE):
        ref[pl.ds(first + SIDE * at, SIDE), lanes] = rows[at][:SIDE]


def across(value, step, place):
    if step == 0:
        return value
    moved = pltpu.roll(value, (-step) % 8, 1)
    if step == 2:
        return jnp.where(place < 6, moved, 0.0)
    if step == -2:
        return jnp.where(place > 0, moved, 0.0)
    return moved


def taps_of(near, far):
    for step, kernel in ((1, near), (2, far)):
        for row in range(3):
            yield step, row, [kernel[row * 3 + col] for col in range(3)]


def row_views(value, place):
    views = {0: value}
    for step in (-2, -1, 1, 2):
        moved = pltpu.roll(value, (-step) % 8, 0)
        if step == 2:
            moved = jnp.where(place < 6, moved, 0.0)
        if step == -2:
            moved = jnp.where(place > 0, moved, 0.0)
        views[step] = moved
    return views


def weighted(kernel, views, step):
    return sum(kernel[col] * views[step * (col - 1)] for col in range(3))


def gate_scores(change, near, far, offset, place):
    scores = [offset] * SIDE
    for at in range(SIDE):
        views = row_views(change[at], place)
        for step, row, kernel in taps_of(near, far):
            target = at - step * (row - 1)
            if 0 <= target < SIDE:
                scores[target] = scores[target] + weighted(kernel, views, step)
    return scores


def conv_chunk(parts, weights, first, rows, sign):
    total = None
    for col in (1, 0, 2):
        acc = None
        for row in range(3):
            start = pl.multiple_of(first + BLOCK * (1 + sign * (row - 1)), BLOCK)
            for part, weight in zip(parts, weights, strict=True):
                left = part[pl.ds(start, rows), :]
                term = weight(left, row * 3 + col)
                acc = term if acc is None else acc + term
        acc = acc.reshape(rows // 8, 8, acc.shape[-1])
        shift = sign * (col - 1)
        if shift:
            acc = pltpu.roll(acc, (-shift) % 8, 1)
        total = acc if total is None else total + acc
    return total


def lane_part(index, width=128):
    return pl.ds(pl.multiple_of(index * width, width), width)


def row_part(index, size):
    return pl.ds(pl.multiple_of(index * size, size), size)


def after_sums(ref):
    return ref.at[pl.ds(8, 24)]


def rows_of(stats_ref, first=0):
    return stats_ref[first : first + 1], stats_ref[first + 1 : first + 2]


def put_sums(sums_ref, first, second):
    sums_ref[...] = jnp.zeros_like(sums_ref)
    sums_ref[0:1, :] = first
    sums_ref[1:2, :] = second


def fetch_blocks(sources, core, target_ref, sems, first):
    moves = []
    for side, source in enumerate(sources):
        lanes = lane_part(core if side == 0 else 1 - core)
        blocks = source.shape[0]
        size = target_ref.shape[0] // blocks
        for block in range(blocks):
            here = pl.ds(block * size, size)
            moves.append(
                move(
                    source.at[block, pl.ds(0, size)],
                    target_ref.at[here, lanes],
                    sems,
                    first + side * blocks + block,
                )
            )
    return moves


def gate_half(count, same_ref, pre, stats, par, hidden_ref, mixed_ref, first, gates_ref=None):
    rows, width = pre.shape
    hidden_ref[pl.ds(rows, hidden_ref.shape[0] - rows), :] = jnp.zeros(
        (hidden_ref.shape[0] - rows, width), jnp.float32
    )
    center, rate = norm_stats(*stats, count)
    scaled = (pre[...].astype(jnp.float32) - center) * rate
    normed = scaled * par[0:1] + par[1:2]
    hidden_ref[pl.ds(0, rows), :] = normed * logistic(normed)
    place = lax.broadcasted_iota(jnp.int32, (8, 128), 0)

    def lanes_step(chunk, _):
        lanes = lane_part(chunk)
        target = pl.ds(pl.multiple_of(first + chunk * 128, 128), 128)
        near = [par[5 + tap : 6 + tap, lanes] for tap in range(9)]
        far = [par[14 + tap : 15 + tap, lanes] for tap in range(9)]
        offset = par[4:5, lanes]

        def clip_step(clip, _):
            view = clip_view(hidden_ref, clip, 56)
            for pair in range(PAIRS):
                maps = [load_rows(view, PIXELS * (2 * pair + seg), lanes) for seg in range(3)]
                results = []
                for seg in range(2):
                    same = same_ref[clip, 2 * pair + seg].astype(jnp.float32)
                    change = [
                        jnp.where(place < SIDE, same * (later - now), 0.0)
                        for now, later in zip(maps[seg], maps[seg + 1], strict=True)
                    ]
                    scores = gate_scores(change, near, far, offset, place)
                    gates = [logistic(score) for score in scores]
                    results.append(
                        [
                            jnp.where(place < SIDE, now * (1.0 + gate), 0.0)
                            for now, gate in zip(maps[seg], gates, strict=True)
                        ]
                    )
                    if gates_ref is not None:
                        for row in range(SIDE):
                            gates_ref[SEG * clip + 2 * pair + seg, row, :, lanes] = gates[row]
                here = pl.ds(pair_row(clip, pair), SIDE * BLOCK)
                blocks = [results[seg][row] for row in range(SIDE) for seg in range(2)]
                mixed_ref[here, target] = jnp.concatenate(blocks).astype(jnp.bfloat16)
            return 0

        return lax.fori_loop(0, rows // CLIP, clip_step, 0)

    lax.fori_loop(0, width // 128, lanes_step, 0)


def gate_mid_body(
    count,
    place_ref,
    same_ref,
    own_ref,
    oth_ref,
    first_ref,
    second_ref,
    par_own_ref,
    par_oth_ref,
    weight_own_ref,
    weight_peer_ref,
    mixed_out_ref,
    gates_out_ref,
    mid_ref,
    mid16_ref,
    sums_ref,
    hidden_ref,
    acc_ref,
    weight_ref,
    own_here_ref,
    mixed_ref,
    gates_ref,
    sems,
):
    rows, width = oth_ref.shape
    clips = rows // CLIP
    core, y = place_ref[0] % 2, place_ref[0] // 2
    arrival = move(own_ref, own_here_ref, sems, 0)
    stats = first_ref[...] + second_ref[...]
    weight_moves = fetch_blocks((weight_own_ref, weight_peer_ref), core, weight_ref, sems, 5)
    mixed_ref[...] = jnp.zeros_like(mixed_ref)
    gate_half(
        count, same_ref, oth_ref, rows_of(stats, 4), after_sums(par_oth_ref), hidden_ref, mixed_ref,
        pl.multiple_of((1 - y) * width, width),
    )
    arrival.wait()
    gate_half(
        count, same_ref, own_here_ref, rows_of(stats), par_own_ref, hidden_ref, mixed_ref,
        pl.multiple_of(y * width, width), gates_ref,
    )
    gates_move = move(gates_ref, gates_out_ref, sems, 2)
    depth = 2 * width
    for copy in weight_moves:
        copy.wait()
    mixed_move = move(mixed_ref, mixed_out_ref, sems, 3)

    def tap_dot(left, tap):
        return jnp.dot(
            left, weight_ref[tap * depth : (tap + 1) * depth], preferred_element_type=jnp.float32
        )

    first_mid = 5 + len(weight_moves)

    def conv_step(clip, _):
        span = PAIRS * SPAN * BLOCK
        total = conv_chunk([mixed_ref], [tap_dot], clip * span, span, 1)
        view = clip_view(acc_ref, clip)
        for seg in range(SEG):
            value = [total[2 * (SPAN * (seg // 2) + 1 + row) + seg % 2] for row in range(SIDE)]
            store_map(view, seg * PIXELS, slice(None), value)
        here = row_part(clip, CLIP)
        move(acc_ref.at[here], mid_ref.at[here], sems, first_mid + clip)
        return 0

    lax.fori_loop(0, clips, conv_step, 0)
    result = acc_ref[pl.ds(0, rows), :]
    mid16_ref[...] = result.astype(jnp.bfloat16)
    put_sums(
        sums_ref, jnp.sum(result, 0, keepdims=True), jnp.sum(result * result, 0, keepdims=True)
    )
    for copy in (gates_move, mixed_move):
        copy.wait()
    for clip in range(clips):
        here = pl.ds(clip * CLIP, CLIP)
        pltpu.make_async_copy(
            acc_ref.at[here], mid_ref.at[here], sems.at[first_mid + clip]
        ).wait()


def map_rows(rows):
    return (rows // (2 * PIXELS) * SPAN + 2) * BLOCK


def gate_mid(count, place, same, own, oth, stats, pars, weights):
    rows, width = oth.shape
    spread = map_rows(rows)
    depth = 18 * width
    gates = (rows // PIXELS, SIDE, 8, width)
    return kernel_call(
        functools.partial(gate_mid_body, count),
        (
            jax.ShapeDtypeStruct((spread, 2 * width), jnp.bfloat16),
            jax.ShapeDtypeStruct(gates, jnp.float32),
            jax.ShapeDtypeStruct((rows, width), jnp.float32),
            jax.ShapeDtypeStruct((rows, width), jnp.bfloat16),
            jax.ShapeDtypeStruct((8, width), jnp.float32),
        ),
        [scalars, scalars, remote] + [whole] * 5 + [remote, remote],
        (
            pltpu.VMEM((rows + 56, width), jnp.float32),
            pltpu.VMEM((rows + 8, width), jnp.float32),
            pltpu.VMEM((depth, width), jnp.bfloat16),
            pltpu.VMEM((rows, width), own.dtype),
            pltpu.VMEM((spread, 2 * width), jnp.bfloat16),
            pltpu.VMEM(gates, jnp.float32),
            pltpu.SemaphoreType.DMA((5 + 2 * weights[0].shape[0] + rows // CLIP,)),
        ),
        away=(0, 1, 2),
        lasts=12.0,
    )(place, same, own, oth, *stats, *pars, *weights)


def mid_slopes(count, grad, pre, stats, back, par, flat_ref, store):
    rows, width = grad.shape
    flat_ref[pl.ds(rows, flat_ref.shape[0] - rows), :] = jnp.zeros(
        (flat_ref.shape[0] - rows, width), jnp.float32
    )
    center, rate = norm_stats(*rows_of(stats), count)
    scaled = (pre[...].astype(jnp.float32) - center) * rate
    flat_ref[pl.ds(0, rows), :] = (par[2:3] * rate) * (
        grad[...].astype(jnp.float32) - back[0:1] / count - scaled * (back[1:2] / count)
    )
    at = lane_mask(width)

    def clip_step(clip, _):
        view = clip_view(flat_ref, clip, 8)
        for pair in range(PAIRS):
            maps = [
                jnp.where(at < SIDE, load_map(view, PIXELS * (2 * pair + seg), slice(None)), 0.0)
                for seg in range(2)
            ]
            store(pl.ds(pair_row(clip, pair), SIDE * BLOCK), maps, at)
        return 0

    lax.fori_loop(0, rows // CLIP, clip_step, 0)


def mid_own_body(count, d_ref, mid_ref, stats_ref, back_ref, par_ref, slopes_ref, flat_ref, mid_here_ref, d_here_ref, sems):
    arrivals = [move(mid_ref, mid_here_ref, sems, 0), move(d_ref, d_here_ref, sems, 1)]
    slopes_ref[...] = jnp.zeros_like(slopes_ref)

    def store(place, maps, at):
        for col in range(3):
            slopes_ref[col, place, :] = two_maps(
                *[across(value, 1 - col, at) for value in maps]
            ).astype(jnp.bfloat16)

    for copy in arrivals:
        copy.wait()
    mid_slopes(count, d_here_ref, mid_here_ref, stats_ref, back_ref, par_ref, flat_ref, store)


def mid_own(count, d_own, mid, stats, back, par):
    rows, width = d_own.shape
    return kernel_call(
        functools.partial(mid_own_body, count),
        jax.ShapeDtypeStruct((3, map_rows(rows), width), jnp.bfloat16),
        [remote, remote, whole, whole, whole],
        (
            pltpu.VMEM((rows + 56, width), jnp.float32),
            pltpu.VMEM((rows, width), jnp.float32),
            pltpu.VMEM((rows, width), jnp.float32),
            pltpu.SemaphoreType.DMA((2,)),
        ),
        held=(0,),
        lasts=1.7,
    )(d_own, mid, stats, back, par)


def mid_back_body(
    count,
    place_ref,
    same_ref,
    slopes_ref,
    d_oth_ref,
    mid_oth_ref,
    stats_oth_ref,
    back_oth_ref,
    pre_ref,
    gates_ref,
    stats_in_ref,
    par_own_ref,
    par_oth_ref,
    weight_own_ref,
    weight_peer_ref,
    away_own_ref,
    away_peer_ref,
    d_in_out_ref,
    d_in16_ref,
    sums_ref,
    flat_ref,
    oth_ref,
    dmix_ref,
    scaled_ref,
    parts_ref,
    weight_ref,
    weight_oth_ref,
    d_here_ref,
    mid_here_ref,
    pre_here_ref,
    gates_here_ref,
    sems,
):
    rows, width = d_oth_ref.shape
    clips = rows // CLIP
    core, y = place_ref[0] % 2, place_ref[0] // 2
    arrivals = [move(d_oth_ref, d_here_ref, sems, 1), move(mid_oth_ref, mid_here_ref, sems, 2)]
    weight_moves = fetch_blocks((weight_own_ref, weight_peer_ref), core, weight_ref, sems, 10)
    weight_moves += [
        move(away_own_ref, weight_oth_ref.at[:, lane_part(core)], sems, 3),
        move(away_peer_ref, weight_oth_ref.at[:, lane_part(1 - core)], sems, 4),
    ]
    pre_moves = [
        move(pre_ref, pre_here_ref, sems, 7),
        move(gates_ref, gates_here_ref, sems, 9),
    ]
    oth_ref[...] = jnp.zeros_like(oth_ref)

    def store(place, maps, _):
        oth_ref[place, :] = two_maps(*maps).astype(jnp.bfloat16)

    for copy in arrivals:
        copy.wait()
    mid_slopes(count, d_here_ref, mid_here_ref, stats_oth_ref, back_oth_ref, after_sums(par_oth_ref), flat_ref, store)
    depth = 2 * width
    turned = (((1,), (1,)), ((), ()))
    for copy in weight_moves:
        copy.wait()

    def own_dot(left, tap):
        start = pl.multiple_of(tap * depth + y * width, width)
        return lax.dot_general(
            left, weight_ref[pl.ds(start, width), :], turned, preferred_element_type=jnp.float32
        )

    def oth_dot(left, tap):
        return lax.dot_general(
            left,
            weight_oth_ref[tap * width : (tap + 1) * width],
            turned,
            preferred_element_type=jnp.float32,
        )

    def conv_step(clip, _):
        span = PAIRS * SPAN * BLOCK
        total = conv_chunk([slopes_ref.at[1], oth_ref], [own_dot, oth_dot], clip * span, span, -1)
        dmix_ref[pl.ds(clip * (span // 8), span // 8)] = total
        return 0

    lax.fori_loop(0, clips, conv_step, 0)

    center, rate = norm_stats(*rows_of(stats_in_ref), count)
    for copy in pre_moves:
        copy.wait()
    scaled_ref[pl.ds(0, rows), :] = (pre_here_ref[...] - center) * rate
    scaled_ref[pl.ds(rows, scaled_ref.shape[0] - rows), :] = jnp.zeros(
        (scaled_ref.shape[0] - rows, width), jnp.float32
    )
    parts_ref[...] = jnp.zeros_like(parts_ref)
    place = lax.broadcasted_iota(jnp.int32, (8, 128), 0)
    inside = place < SIDE

    def lanes_step(chunk, _):
        lanes = lane_part(chunk)

        def row_of(index):
            return par_own_ref[index : index + 1, lanes]

        near = [row_of(5 + tap) for tap in range(9)]
        far = [row_of(14 + tap) for tap in range(9)]
        gain, bias = row_of(0), row_of(1)

        def add_part(index, value):
            parts_ref[pl.ds(8 * index, 8), lanes] += value

        def clip_step(clip, carry):
            view = clip_view(scaled_ref, clip, 56)
            target = clip_view(flat_ref, clip)
            for pair in range(PAIRS):
                carry = pair_step(clip, pair, carry, view, target)
            return carry

        def pair_step(clip, pair, carry, view, target):
            normed = [
                [value * gain + bias for value in load_rows(view, PIXELS * (2 * pair + seg), lanes)]
                for seg in range(3)
            ]
            parts = [[logistic(value) for value in rows] for rows in normed]
            hidden = [
                [value * part for value, part in zip(*both, strict=True)]
                for both in zip(normed, parts, strict=True)
            ]
            for seg in range(2):
                same = same_ref[clip, 2 * pair + seg].astype(jnp.float32)
                start = 2 * (SPAN * (PAIRS * clip + pair) + 1) + seg
                d_mixed, gates, d_score = [], [], []
                for row in range(SIDE):
                    gate = gates_here_ref[SEG * clip + 2 * pair + seg, row, :, lanes]
                    grad = jnp.where(inside, dmix_ref[start + 2 * row, :, lanes], 0.0)
                    gates.append(gate)
                    d_mixed.append(grad)
                    d_score.append(grad * hidden[seg][row] * (gate * (1.0 - gate)))
                add_part(0, sum(d_score[1:], d_score[0]))
                sums = [None] * 18
                d_change = [None] * SIDE
                for row in range(SIDE):
                    change = hidden[seg + 1][row] - hidden[seg][row]
                    views = row_views(jnp.where(inside, same * change, 0.0), place)
                    backs = row_views(d_score[row], place)
                    for index, (step, tap_row, kernel) in enumerate(taps_of(near, far)):
                        other = row - step * (tap_row - 1)
                        if 0 <= other < SIDE:
                            for col in range(3):
                                if index == 4 and col == 1:
                                    continue
                                term = d_score[other] * views[step * (col - 1)]
                                at = 3 * index + col
                                sums[at] = term if sums[at] is None else sums[at] + term
                        other = row + step * (tap_row - 1)
                        if 0 <= other < SIDE:
                            term = weighted(kernel, backs, -step)
                            before = d_change[other]
                            d_change[other] = term if before is None else before + term
                for at, value in enumerate(sums):
                    if value is not None:
                        add_part(1 + at, value)
                d_change = [jnp.where(inside, same * value, 0.0) for value in d_change]
                results = []
                for row in range(SIDE):
                    d_hidden = d_mixed[row] * (1.0 + gates[row]) - d_change[row] + carry[row]
                    part, value = parts[seg][row], normed[seg][row]
                    results.append(d_hidden * (part * (1.0 + value * (1.0 - part))))
                carry = d_change
                store_rows(target, PIXELS * (2 * pair + seg), lanes, results)
            return carry

        lax.fori_loop(0, clips, clip_step, [jnp.zeros((8, 128), jnp.float32)] * SIDE)
        return 0

    lax.fori_loop(0, width // 128, lanes_step, 0)
    d_in_move = move(flat_ref.at[pl.ds(0, rows)], d_in_out_ref, sems, 8)
    result = flat_ref[pl.ds(0, rows), :]
    d_in16_ref[...] = result.astype(jnp.bfloat16)
    put_sums(
        sums_ref,
        jnp.sum(result, 0, keepdims=True),
        jnp.sum(result * scaled_ref[pl.ds(0, rows), :], 0, keepdims=True),
    )
    parts_ref[pl.ds(8 * 14, 8), :] = parts_ref[pl.ds(8 * 5, 8), :]
    sums_ref[8:32, :] = jnp.sum(parts_ref[...].reshape(24, 8, width), 1)
    d_in_move.wait()


def mid_back(
    count, place, same, slopes, d_oth, mid_oth, stats_oth, back_oth, pre, gates, stats_in, pars, weights, aways
):
    rows, width = d_oth.shape
    spread = map_rows(rows)
    depth = 18 * width
    return kernel_call(
        functools.partial(mid_back_body, count),
        (
            jax.ShapeDtypeStruct((rows, width), jnp.float32),
            jax.ShapeDtypeStruct((rows, width), jnp.bfloat16),
            jax.ShapeDtypeStruct((32, width), jnp.float32),
        ),
        [scalars, scalars, whole, remote, remote, whole, whole, remote, remote]
        + [whole] * 3
        + [remote] * 4,
        (
            pltpu.VMEM((rows + 56, width), jnp.float32),
            pltpu.VMEM((spread, width), jnp.bfloat16),
            pltpu.VMEM((spread // 8, 8, width), jnp.float32),
            pltpu.VMEM((rows + 56, width), jnp.float32),
            pltpu.VMEM((24 * 8, width), jnp.float32),
            pltpu.VMEM((depth, width), jnp.bfloat16),
            pltpu.VMEM((depth // 2, width), jnp.bfloat16),
            pltpu.VMEM((rows, width), jnp.bfloat16),
            pltpu.VMEM((rows, width), jnp.bfloat16),
            pltpu.VMEM((rows, width), jnp.float32),
            pltpu.VMEM(gates.shape, jnp.float32),
            pltpu.SemaphoreType.DMA((10 + 2 * weights[0].shape[0],)),
        ),
        away=(0,),
        lasts=11.5,
    )(
        place, same, slopes, d_oth, mid_oth, stats_oth, back_oth, pre, gates, stats_in, *pars, *weights,
        *aways,
    )


def turn_body(mixed_ref, out_ref, mixed_here_ref, sems):
    move(mixed_ref, mixed_here_ref, sems, 0).wait()
    out_ref[...] = mixed_here_ref[pl.ds(BLOCK, out_ref.shape[1]), :].T


def turn(mixed):
    spread, depth = mixed.shape
    return kernel_call(
        turn_body,
        jax.ShapeDtypeStruct((depth, spread - 2 * BLOCK), jnp.bfloat16),
        [remote],
        (pltpu.VMEM(mixed.shape, jnp.bfloat16), pltpu.SemaphoreType.DMA((1,))),
        held=(0,),
        lasts=1.6,
    )(mixed)


def mid_weight_body(place_ref, turned_ref, slopes_ref, keep_ref, early_ref, late_ref, keep_here_ref, sems):
    depth, rows = turned_ref.shape
    half = keep_ref.shape[1]
    cut = early_ref.shape[0]
    first = place_ref[0] % 2 == 0
    moves = []
    for tap in range(9):
        row, col = tap // 3, tap % 3
        right = slopes_ref[col, pl.ds(BLOCK * (2 - row), rows), :]
        value = jnp.dot(turned_ref[...], right, preferred_element_type=jnp.float32)
        low, high = value[:, :half], value[:, half:]
        here = pl.ds(tap * depth, depth)
        keep_here_ref[here, :] = jnp.where(first, low, high)
        moves.append(move(keep_here_ref.at[here], keep_ref.at[here], sems, tap))
        send = jnp.where(first, high, low).astype(jnp.bfloat16)
        middle = min(max(cut - tap * depth, 0), depth)
        if middle > 0:
            early_ref[tap * depth : tap * depth + middle] = send[:middle]
        if middle < depth:
            late_ref[tap * depth + middle - cut : (tap + 1) * depth - cut] = send[middle:]
    for copy in moves:
        copy.wait()


def mid_weight(place, turned, slopes):
    depth, rows = turned.shape
    width = slopes.shape[2]
    part = jax.ShapeDtypeStruct((9 * depth // 2, width // 2), jnp.bfloat16)
    return kernel_call(
        mid_weight_body,
        (jax.ShapeDtypeStruct((9 * depth, width // 2), jnp.float32), part, part),
        [scalars, whole, whole],
        (pltpu.VMEM((9 * depth, width // 2), jnp.float32), pltpu.SemaphoreType.DMA((9,))),
        away=(0,),
        lasts=4.8,
    )(place, turned, slopes)


def first_conv_body(
    order,
    place_ref,
    block_ref,
    peer_ref,
    across_ref,
    corner_ref,
    own_ref,
    other_ref,
    extra_ref,
    par_ref,
    pre_out_ref,
    pre16_ref,
    sums_ref,
    cross_ref,
    near_ref,
    away_ref,
    pre_ref,
    weight_ref,
    pieces_ref,
    sems,
):
    rows = peer_ref.shape[0]
    quarter = block_ref.shape[1]
    chan, group = place_ref[0], place_ref[1]
    core = chan % 2
    sources = (block_ref.at[row_part(core, rows)], peer_ref, across_ref)
    arrivals = [
        move(source, pieces_ref.at[at], sems, 3 + at) for at, source in enumerate(sources)
    ]
    size = own_ref.shape[0] // len(order)
    for at, bits in enumerate(order):
        here = row_part(group ^ bits, size)
        weight_ref[here, lane_part(core)] = own_ref[at * size : (at + 1) * size]
        weight_ref[here, lane_part(1 - core)] = other_ref[at * size : (at + 1) * size]
    weight_moves = [
        move(weight_ref.at[row_part(chan, quarter)], near_ref, sems, 0),
        move(weight_ref.at[row_part(chan ^ 2, quarter)], away_ref, sems, 2),
    ]
    total = None
    for at in (3, 0, 1, 2):
        if at < 3:
            arrivals[at].wait()
        piece = pieces_ref[at] if at < 3 else corner_ref[...]
        weight = weight_ref[row_part(chan ^ at, quarter), :]
        term = jnp.dot(piece, weight, preferred_element_type=jnp.float32)
        total = term if total is None else total + term
    pre_ref[...] = total
    pre_move = move(pre_ref, pre_out_ref, sems, 1)
    pre16_ref[...] = total.astype(jnp.bfloat16)
    sums_ref[...] = extra_ref[...]
    cross_ref[0:8, :] = jnp.zeros((8, cross_ref.shape[1]), jnp.float32)
    cross_ref[8:32, :] = par_ref[...]
    for at, value in enumerate((total, total * total)):
        row = jnp.sum(value, 0, keepdims=True)
        sums_ref[at : at + 1, :] = row
        cross_ref[4 + at : 5 + at, :] = row
    for copy in weight_moves:
        copy.wait()
    pre_move.wait()


def first_conv(order, place, block, pieces, weights, extra, par):
    rows, quarter = pieces[0].shape
    width = 2 * weights[0].shape[1]
    return kernel_call(
        functools.partial(first_conv_body, order),
        (
            jax.ShapeDtypeStruct((rows, width), jnp.float32),
            jax.ShapeDtypeStruct((rows, width), jnp.bfloat16),
            jax.ShapeDtypeStruct((8, width), jnp.float32),
            jax.ShapeDtypeStruct((32, width), jnp.float32),
            jax.ShapeDtypeStruct((quarter, width), jnp.bfloat16),
            jax.ShapeDtypeStruct((quarter, width), jnp.bfloat16),
        ),
        [scalars, remote, remote, remote] + [whole] * 5,
        (
            pltpu.VMEM((rows, width), jnp.float32),
            pltpu.VMEM((4 * quarter, width), jnp.bfloat16),
            pltpu.VMEM((3, rows, quarter), jnp.bfloat16),
            pltpu.SemaphoreType.DMA((6,)),
        ),
        away=(0, 4, 5),
        lasts=4.0,
    )(place, block, *pieces, *weights, extra, par)


def second_body(
    count, place_ref, own_ref, oth_ref, stats_own_ref, stats_oth_ref, par_own_ref, par_oth_ref, out_ref,
    oth_here_ref, sems,
):
    width = own_ref.shape[1]
    y = place_ref[0] // 2
    arrivals = [move(oth_ref, oth_here_ref, sems, 0)]
    for side, pre, stats, par in (
        (y, own_ref, stats_own_ref, par_own_ref),
        (1 - y, oth_here_ref, stats_oth_ref, after_sums(par_oth_ref)),
    ):
        center, rate = norm_stats(*rows_of(stats), count)
        normed = (pre[...].astype(jnp.float32) - center) * rate * par[2:3] + par[3:4]
        out_ref[:, lane_part(side, width)] = (normed * logistic(normed)).astype(jnp.bfloat16)
        for copy in arrivals:
            copy.wait()
        arrivals = []


def second_half(count, place, own, oth, stats, pars):
    rows, width = own.shape
    return kernel_call(
        functools.partial(second_body, count),
        jax.ShapeDtypeStruct((rows, 2 * width), jnp.bfloat16),
        [scalars, whole, remote, whole, whole, whole, whole],
        (
            pltpu.VMEM((rows, width), jnp.bfloat16),
            pltpu.SemaphoreType.DMA((1,)),
        ),
        lasts=1.9,
    )(place, own, oth, *stats, *pars)


def last_conv_body(place_ref, mine_ref, peer_ref, weight_ref, extra_ref, out_ref, sums_ref):
    rows = mine_ref.shape[0]
    core = place_ref[0] % 2
    sums = squares = 0.0
    for side, part in ((core, mine_ref), (1 - core, peer_ref)):
        value = jnp.dot(part[...], weight_ref[...], preferred_element_type=jnp.float32)
        out_ref[row_part(side, rows), :] = value
        sums += jnp.sum(value, 0, keepdims=True)
        squares += jnp.sum(value * value, 0, keepdims=True)
    sums_ref[...] = extra_ref[...]
    sums_ref[0:1, :] = sums
    sums_ref[1:2, :] = squares


def last_conv(place, mine, peer, weight, extra):
    rows, depth = mine.shape
    width = weight.shape[1]
    return kernel_call(
        last_conv_body,
        (
            jax.ShapeDtypeStruct((2 * rows, width), jnp.float32),
            jax.ShapeDtypeStruct((8, width), jnp.float32),
        ),
        [scalars] + [whole] * 4,
        lasts=2.3,
    )(place, mine, peer, weight, extra)


def out_back_body(
    count,
    place_ref,
    pre_ref,
    block_ref,
    grad_ref,
    first_ref,
    second_ref,
    gain_ref,
    bias_ref,
    weight_ref,
    out_ref,
    total_out_ref,
    sums_ref,
    keep_ref,
    send_ref,
    total_ref,
    weight_here_ref,
    sems,
):
    rows = keep_ref.shape[0]
    weight_move = move(weight_ref, weight_here_ref, sems, 1)
    core = place_ref[0] % 2
    center, rate = norm_stats(*rows_of(first_ref[...] + second_ref[...]), count)
    gain, bias = gain_ref[...], bias_ref[...]
    step = rows // 7

    def add_step(at, sums):
        here = row_part(at, step)
        scaled = (pre_ref[here, :] - center) * rate
        total = scaled * gain + bias + block_ref[here, :].astype(jnp.float32)
        part = logistic(total)
        out_ref[here, :] = (total * part).astype(jnp.bfloat16)
        value = grad_ref[here, :].astype(jnp.float32) * (part * (1.0 + total * (1.0 - part)))
        total_ref[here, :] = value
        return (
            sums[0] + jnp.sum(value, 0, keepdims=True),
            sums[1] + jnp.sum(value * scaled, 0, keepdims=True),
        )

    zero = jnp.zeros((1, pre_ref.shape[1]), jnp.float32)
    sums, products = lax.fori_loop(0, 14, add_step, (zero, zero))
    put_sums(sums_ref, sums, products)
    total_move = move(total_ref, total_out_ref, sems, 0)
    local = 1.0 / (2 * rows)
    weight_move.wait()
    scale = gain * rate
    factor = scale * rate * (products * local)
    offset = scale * (sums * local) - factor * center

    def slope_rows(side):
        here = row_part(side, rows)
        value = scale * total_ref[here, :] - (factor * pre_ref[here, :] + offset)
        return lax.dot_general(
            value.astype(jnp.bfloat16),
            weight_here_ref[...],
            (((1,), (1,)), ((), ())),
            preferred_element_type=jnp.float32,
        )

    send_ref[...] = slope_rows(1 - core).astype(jnp.bfloat16)
    keep_ref[...] = slope_rows(core)
    total_move.wait()


def out_back(count, place, pre, block, grad, stats, gain, bias, weight):
    rows, width = pre.shape
    depth = weight.shape[0]
    return kernel_call(
        functools.partial(out_back_body, count),
        (
            jax.ShapeDtypeStruct((rows, width), jnp.bfloat16),
            jax.ShapeDtypeStruct((rows, width), jnp.float32),
            jax.ShapeDtypeStruct((8, width), jnp.float32),
            jax.ShapeDtypeStruct((rows // 2, depth), jnp.float32),
            jax.ShapeDtypeStruct((rows // 2, depth), jnp.bfloat16),
        ),
        [scalars] + [whole] * 7 + [remote],
        (
            pltpu.VMEM((rows, width), jnp.float32),
            pltpu.VMEM(weight.shape, weight.dtype),
            pltpu.SemaphoreType.DMA((2,)),
        ),
        away=(1,),
        lasts=7.5,
    )(place, pre, block, grad, *stats, gain, bias, weight)


def cross_body(place_ref, keep_ref, got_ref, own_ref, send_ref):
    width = own_ref.shape[1]
    y = place_ref[0] // 2
    for lanes, ref in ((1 - y, send_ref), (y, own_ref)):
        here = lane_part(lanes, width)
        value = keep_ref[:, here] + got_ref[:, here].astype(jnp.float32)
        ref[...] = value.astype(ref.dtype)


def cross_half(place, keep, got):
    rows, width = keep.shape[0], keep.shape[1] // 2
    return kernel_call(
        cross_body,
        (
            jax.ShapeDtypeStruct((rows, width), jnp.float32),
            jax.ShapeDtypeStruct((rows, width), jnp.bfloat16),
        ),
        [scalars, whole, whole],
        lasts=0.7,
    )(place, keep, got)


def out_delta_body(count, local, stats_ref, sums_ref, first_ref, second_ref, gain_ref, out_ref):
    center, rate = norm_stats(*rows_of(stats_ref), count)
    back = first_ref[...] + second_ref[...]
    scale = gain_ref[...] * rate
    first = scale * (back[0:1] / count - sums_ref[0:1] * local)
    second = scale * rate * (back[1:2] / count - sums_ref[1:2] * local)
    put_sums(out_ref, first - second * center, second)


def out_delta(count, rows, stats, sums, back, gain):
    return kernel_call(
        functools.partial(out_delta_body, count, 1.0 / rows),
        jax.ShapeDtypeStruct(stats.shape, jnp.float32),
        [whole] * 5,
    )(stats, sums, *back, gain)


def mid_slope_body(
    count,
    place_ref,
    keep_ref,
    got_ref,
    second_ref,
    mid_ref,
    stats_ref,
    par_ref,
    deltas0_ref,
    deltas1_ref,
    deltas2_ref,
    deltas3_ref,
    weights0_ref,
    weights1_ref,
    weights2_ref,
    weights3_ref,
    out_ref,
    out16_ref,
    sums_ref,
    here_ref,
    sems,
):
    width = mid_ref.shape[1]
    y = place_ref[0] // 2
    turned = (((1,), (1,)), ((), ()))
    factor, offset = None, None
    for deltas, weights in (
        (deltas0_ref, weights0_ref),
        (deltas1_ref, weights1_ref),
        (deltas2_ref, weights2_ref),
        (deltas3_ref, weights3_ref),
    ):
        own = weights[row_part(y, width), :]
        left = (weights[...].astype(jnp.float32) * deltas[1:2]).astype(jnp.bfloat16)
        term = lax.dot_general(left, own, turned, preferred_element_type=jnp.float32)
        factor = term if factor is None else factor + term
        high = deltas[0:1].astype(jnp.bfloat16).astype(jnp.float32)
        both = jnp.concatenate([high, deltas[0:1] - high, jnp.zeros_like(deltas[2:8])])
        term = lax.dot_general(
            both.astype(jnp.bfloat16), own, turned, preferred_element_type=jnp.float32
        )
        term = term[0:1] + term[1:2]
        offset = term if offset is None else offset + term
    high = factor.astype(jnp.bfloat16)
    low = (factor - high.astype(jnp.float32)).astype(jnp.bfloat16)
    delta = jnp.dot(second_ref[...], high, preferred_element_type=jnp.float32)
    delta += jnp.dot(second_ref[...], low, preferred_element_type=jnp.float32)
    grad = keep_ref[...] + got_ref[...].astype(jnp.float32) - delta - offset
    center, rate = norm_stats(*rows_of(stats_ref), count)
    scaled = (mid_ref[...] - center) * rate
    normed = scaled * par_ref[2:3] + par_ref[3:4]
    result = grad * silu_slope(normed)
    here_ref[...] = result
    out_move = move(here_ref, out_ref, sems, 0)
    out16_ref[...] = result.astype(jnp.bfloat16)
    put_sums(
        sums_ref, jnp.sum(result, 0, keepdims=True), jnp.sum(result * scaled, 0, keepdims=True)
    )
    out_move.wait()


def mid_slope(count, place, keep, got, second, mid, stats, par, deltas, weights):
    rows, width = mid.shape
    return kernel_call(
        functools.partial(mid_slope_body, count),
        (
            jax.ShapeDtypeStruct((rows, width), jnp.float32),
            jax.ShapeDtypeStruct((rows, width), jnp.bfloat16),
            jax.ShapeDtypeStruct((8, width), jnp.float32),
        ),
        [scalars] + [whole] * 14,
        (pltpu.VMEM((rows, width), jnp.float32), pltpu.SemaphoreType.DMA((1,))),
        away=(0,),
        lasts=3.3,
    )(place, keep, got, second, mid, stats, par, *deltas, *weights)


def out_weight_body(
    count, part, place_ref, rows_ref, pre_ref, total_ref, stats_ref, back_ref, gain_ref, *refs
):
    rows = rows_ref.shape[0]
    core = place_ref[0] % 2
    center, rate = norm_stats(*rows_of(stats_ref), count)
    here = row_part(1 - core if part else core, rows)
    scaled = (pre_ref[here, :] - center) * rate
    value = (gain_ref[...] * rate) * (
        total_ref[here, :] - back_ref[0:1] / count - scaled * (back_ref[1:2] / count)
    )
    result = exact(rows_ref[...], value.astype(jnp.bfloat16), ((0,), (0,)))
    if part:
        start_ref, out_ref, here_ref, sems = refs
        here_ref[...] = start_ref[...] + result
        move(here_ref, out_ref, sems, 0).wait()
    else:
        refs[0][...] = result


def out_weight(count, place, second, pre, total, stats, back, gain, start=None):
    rows, depth = second.shape
    width = pre.shape[1]
    part = 0 if start is None else 1
    return kernel_call(
        functools.partial(out_weight_body, count, part),
        jax.ShapeDtypeStruct((depth, width), jnp.float32),
        [scalars] + [whole] * (6 + part),
        (pltpu.VMEM((depth, width), jnp.float32), pltpu.SemaphoreType.DMA((1,))) if part else (),
        away=(0,) if part else (),
        lasts=1.7,
    )(place, second, pre, total, stats, back, gain, *([start] if part else []))


def in_slopes(count, grad, pre, stats, back, par):
    center, rate = norm_stats(*stats, count)
    scaled = (pre[...].astype(jnp.float32) - center) * rate
    value = (par[0:1] * rate) * (
        grad[...].astype(jnp.float32) - back[0:1] / count - scaled * (back[1:2] / count)
    )
    return value.astype(jnp.bfloat16)


def in_own_body(
    count, place_ref, d_ref, pre_ref, stats_ref, back_ref, par_ref, block_ref, peer_ref, across_ref, corner_ref,
    out_ref, keep_ref, send_ref, d_here_ref, pre_here_ref, keep_here_ref, pieces_ref, sems,
):
    rows, width = d_ref.shape
    arrivals = [move(d_ref, d_here_ref, sems, 0), move(pre_ref, pre_here_ref, sems, 1)]
    half = width // 2
    quarter = block_ref.shape[1]
    chan = place_ref[0]
    core = chan % 2
    sources = (block_ref.at[row_part(core, rows)], peer_ref, across_ref, corner_ref)
    pieces = [
        move(source, pieces_ref.at[at], sems, 6 + at) for at, source in enumerate(sources)
    ]
    for copy in arrivals:
        copy.wait()
    own = in_slopes(count, d_here_ref, pre_here_ref, rows_of(stats_ref), back_ref, par_ref)
    out_ref[...] = own
    moves = []
    for at, arrival in enumerate(pieces):
        arrival.wait()
        value = lax.dot_general(
            pieces_ref[at], own, (((0,), (0,)), ((), ())), preferred_element_type=jnp.float32
        )
        here = row_part(chan ^ at, quarter)
        low, high = value[:, :half], value[:, half:]
        keep_here_ref[here, :] = jnp.where(core == 0, low, high)
        moves.append(move(keep_here_ref.at[here], keep_ref.at[here], sems, 2 + at))
        send_ref[here, :] = jnp.where(core == 0, high, low).astype(jnp.bfloat16)
    for copy in moves:
        copy.wait()


def in_own(count, place, d_own, pre, stats, back, par, block, pieces):
    rows, width = d_own.shape
    full = 4 * block.shape[1]
    return kernel_call(
        functools.partial(in_own_body, count),
        (
            jax.ShapeDtypeStruct((rows, width), jnp.bfloat16),
            jax.ShapeDtypeStruct((full, width // 2), jnp.float32),
            jax.ShapeDtypeStruct((full, width // 2), jnp.bfloat16),
        ),
        [scalars, remote, remote] + [whole] * 3 + [remote] * 4,
        (
            pltpu.VMEM((rows, width), jnp.float32),
            pltpu.VMEM((rows, width), jnp.float32),
            pltpu.VMEM((full, width // 2), jnp.float32),
            pltpu.VMEM((4, rows, block.shape[1]), block.dtype),
            pltpu.SemaphoreType.DMA((10,)),
        ),
        away=(1,),
        lasts=4.5,
    )(place, d_own, pre, stats, back, par, block, *pieces)


def in_other_body(
    count, place_ref, own_ref, d_ref, pre_ref, stats_ref, back_ref, par_ref, out_ref, pre_here_ref, sems
):
    width = d_ref.shape[1]
    y = place_ref[0] // 2
    arrival = move(pre_ref, pre_here_ref, sems, 0)
    out_ref[:, lane_part(y, width)] = own_ref[...]
    arrival.wait()
    value = in_slopes(count, d_ref, pre_here_ref, rows_of(stats_ref, 4), back_ref, after_sums(par_ref))
    out_ref[:, lane_part(1 - y, width)] = value


def in_other(count, place, own, d_oth, pre_oth, stats, back, par):
    rows, width = d_oth.shape
    return kernel_call(
        functools.partial(in_other_body, count),
        jax.ShapeDtypeStruct((rows, 2 * width), jnp.bfloat16),
        [scalars, whole, whole, remote, whole, whole, whole],
        (pltpu.VMEM((rows, width), pre_oth.dtype), pltpu.SemaphoreType.DMA((1,))),
        lasts=2.0,
    )(place, own, d_oth, pre_oth, stats, back, par)


def input_grad_body(place_ref, mine_ref, peer_ref, near_ref, far_ref, total_ref, out_ref):
    rows = mine_ref.shape[0]
    width = near_ref.shape[1]
    core, y = place_ref[0] % 2, place_ref[0] // 2
    turned = (((1,), (1,)), ((), ()))
    for side, part in ((core, mine_ref), (1 - core, peer_ref)):
        here = row_part(side, rows)
        value = total_ref[here, :]
        for lanes, weight in ((y, near_ref), (1 - y, far_ref)):
            value += lax.dot_general(
                part[:, lane_part(lanes, width)],
                weight[...],
                turned,
                preferred_element_type=jnp.float32,
            )
        out_ref[here, :] = value.astype(jnp.bfloat16)


def input_grad(place, mine, peer, near, far, total):
    rows, quarter = total.shape
    return kernel_call(
        input_grad_body,
        jax.ShapeDtypeStruct((rows, quarter), jnp.bfloat16),
        [scalars] + [whole] * 5,
        lasts=2.8,
    )(place, mine, peer, near, far, total)


def opening_body(
    place_ref, block_ref, mid_ref, out_ref, mine_ref, others_ref, packed_ref, rows_ref, small_ref, sems
):
    rows = mine_ref.shape[0]
    core = place_ref[0] % 2
    count, width = mid_ref.shape
    size = out_ref.shape[0]
    sources = [(block_ref.at[row_part(side, rows)], rows_ref.at[at]) for at, side in ((0, core), (1, 1 - core))]
    sources.append((mid_ref, small_ref.at[pl.ds(0, count)]))
    for at in range(4):
        here = small_ref.at[pl.ds(count + at * size, size)]
        sources.append((out_ref.at[:, pl.ds(at * width, width)], here))
    arrivals = [move(*pair, sems, at) for at, pair in enumerate(sources)]
    moves = []
    for at, target in enumerate((mine_ref, others_ref)):
        arrivals[at].wait()
        moves.append(move(rows_ref.at[at], target, sems, 7 + at))
    for copy in arrivals[2:]:
        copy.wait()
    moves.append(move(small_ref, packed_ref, sems, 9))
    for copy in moves:
        copy.wait()


def opening(place, block, mid, out):
    half = block.shape[0] // 2
    rows, width = mid.shape
    size = out.shape[0]
    if size % BLOCK or rows % BLOCK:
        parts = [out[:, at * width : (at + 1) * width] for at in range(4)]
        core = place[0] % 2
        halves = [
            lax.dynamic_slice_in_dim(block, side * half, half, 0) for side in (core, 1 - core)
        ]
        return (*halves, jnp.concatenate([mid] + parts, 0))
    rows_shape = jax.ShapeDtypeStruct((half, block.shape[1]), block.dtype)
    return kernel_call(
        opening_body,
        (rows_shape, rows_shape, jax.ShapeDtypeStruct((rows + 4 * size, width), mid.dtype)),
        [scalars, remote, remote, remote],
        (
            pltpu.VMEM((2, half, block.shape[1]), block.dtype),
            pltpu.VMEM((rows + 4 * size, width), mid.dtype),
            pltpu.SemaphoreType.DMA((10,)),
        ),
        away=(0, 1, 2),
    )(place, block, mid, out)


def pack_body(gain_in, bias_in, gain_mid, bias_mid, gate_bias, near, far, stem_gain, stem_bias, out_ref, stem_ref):
    stem_ref[...] = jnp.zeros_like(stem_ref)
    stem_ref[0:1, :] = stem_gain[...]
    stem_ref[1:2, :] = stem_bias[...]
    for at, ref in enumerate((gain_in, bias_in, gain_mid, bias_mid, gate_bias)):
        out_ref[at : at + 1, :] = ref[...]
    out_ref[5:14, :] = near[...]
    out_ref[14:23, :] = far[...]
    out_ref[23:24, :] = jnp.zeros_like(out_ref[23:24, :])


def pack_params(rows, near, far, stem):
    width, outs = near.shape[1], stem[0].shape[0]
    return kernel_call(
        pack_body,
        (
            jax.ShapeDtypeStruct((24, width), jnp.float32),
            jax.ShapeDtypeStruct((8, outs), jnp.float32),
        ),
        [whole] * 9,
    )(*[row.reshape(1, width) for row in rows], near, far, *[row.reshape(1, outs) for row in stem])


TAPS = 7
LANES = 16


def exact(left, right, contract):
    return lax.dot_general(
        left, right, (contract, ((), ())), preferred_element_type=jnp.float32
    )


def spot(core, outs, width, part):
    lane = lax.broadcasted_iota(jnp.int32, (outs, width), 1)
    channel = lax.broadcasted_iota(jnp.int32, (outs, width), 0)
    return (lane == core * 2 * outs + part * outs + channel).astype(jnp.float32)


def stem_row(core, width, first, second):
    row = None
    for part, value in enumerate((first, second)):
        column = jnp.sum(jnp.sum(value, 0), 1, keepdims=True)
        term = jnp.sum(column * spot(core, value.shape[1], width, part), 0, keepdims=True)
        row = term if row is None else row + term
    at = lax.broadcasted_iota(jnp.int32, (8, width), 0)
    return jnp.where(at == 2, row, 0.0)


def stem_columns(core, outs, stats_ref):
    row = stats_ref[2:3, :]
    return [
        jnp.sum(row * spot(core, outs, row.shape[1], part), 1, keepdims=True) for part in range(2)
    ]


def upright(row):
    size = row.shape[1]
    at = lax.broadcasted_iota(jnp.int32, (size, size), 0)
    same = at == lax.broadcasted_iota(jnp.int32, (size, size), 1)
    return jnp.sum(jnp.where(same, row, 0.0), 1, keepdims=True)


def stem_front_body(
    place_ref, video_ref, weight_ref, pre_out_ref, rows_out_ref, pick_out_ref, extra_ref, flat_ref, parts_ref,
    pre_ref, rows_ref, pick_ref, sems,
):
    segs, colours, size = video_ref.shape
    side = 32
    half = size // 2
    quarter = half // 2
    core = place_ref[0] % 2
    at = lax.broadcasted_iota(jnp.int32, (LANES, size), 0)
    zero = jnp.zeros((LANES - colours, size), jnp.float32)

    def plane_step(seg, _):
        value = jnp.concatenate([video_ref[seg].astype(jnp.float32), zero])
        moving = pltpu.roll(value, LANES - 3, 0) - value
        center = pltpu.roll(value, 6, 0)
        plane = jnp.where(at < 12, moving, jnp.where(at < 15, center, 0.0))
        flat_ref[pl.ds(pl.multiple_of(seg * LANES, LANES), LANES), :] = plane.astype(jnp.bfloat16)
        return 0

    lax.fori_loop(0, segs, plane_step, 0, unroll=4)
    source = lax.broadcasted_iota(jnp.int32, (size, half), 0)
    lane = lax.broadcasted_iota(jnp.int32, (size, half), 1)
    lanes = lax.broadcasted_iota(jnp.int32, (segs * LANES, half), 1)
    for parity in range(2):
        hit = source == 2 * side * (lane // side) + side * parity + lane % side
        rows = jnp.dot(
            flat_ref[...],
            jnp.where(hit, 1.0, 0.0).astype(jnp.bfloat16),
            preferred_element_type=jnp.float32,
        )
        for tap in range(TAPS):
            if (tap - 3) % 2 != parity:
                continue
            shift = (tap - 3 - parity) // 2 * side
            value = rows
            if shift:
                value = pltpu.roll(rows, (-shift) % half, 1)
                inside = lanes < half - shift if shift > 0 else lanes >= -shift
                value = jnp.where(inside, value, 0.0)
            value = value.astype(jnp.bfloat16).reshape(segs, LANES, half)
            rows_ref[:, tap * LANES : (tap + 1) * LANES, :] = value
    weight = weight_ref[...]
    moves = [move(rows_ref, rows_out_ref, sems, 0)]

    def seg_step(seg, _):
        value = jnp.dot(weight, rows_ref[seg], preferred_element_type=jnp.float32)
        value = value.astype(jnp.bfloat16)
        here = pl.ds(pl.multiple_of(seg * LANES, LANES), LANES)
        for tap in range(TAPS):
            parts_ref[tap, here, :] = value[tap * LANES : (tap + 1) * LANES]
        return 0

    lax.fori_loop(0, segs, seg_step, 0, unroll=4)
    source = lax.broadcasted_iota(jnp.int32, (half, quarter), 0)
    lane = lax.broadcasted_iota(jnp.int32, (half, quarter), 1)
    total = None
    for tap in range(TAPS):
        column = 2 * (lane % LANES) + tap - 3
        hit = (source == side * (lane // LANES) + column) & (column >= 0) & (column < side)
        pick = jnp.where(hit, 1.0, 0.0).astype(jnp.bfloat16)
        pick_ref[tap] = pick
        term = jnp.dot(parts_ref[tap], pick, preferred_element_type=jnp.float32)
        total = term if total is None else total + term
    total = total.reshape(segs, LANES, quarter)
    pre_ref[...] = total
    moves += [move(pick_ref, pick_out_ref, sems, 1), move(pre_ref, pre_out_ref, sems, 2)]
    extra_ref[...] = stem_row(core, extra_ref.shape[1], total, total * total)
    for copy in moves:
        copy.wait()


def stem_front(place, video, weight, width):
    segs, _, size = video.shape
    return kernel_call(
        stem_front_body,
        (
            jax.ShapeDtypeStruct((segs, LANES, size // 4), jnp.float32),
            jax.ShapeDtypeStruct((segs, TAPS * LANES, size // 2), jnp.bfloat16),
            jax.ShapeDtypeStruct((TAPS, size // 2, size // 4), jnp.bfloat16),
            jax.ShapeDtypeStruct((8, width), jnp.float32),
        ),
        [scalars, whole, whole],
        (
            pltpu.VMEM((segs * LANES, size), jnp.bfloat16),
            pltpu.VMEM((TAPS, segs * LANES, size // 2), jnp.bfloat16),
            pltpu.VMEM((segs, LANES, size // 4), jnp.float32),
            pltpu.VMEM((segs, TAPS * LANES, size // 2), jnp.bfloat16),
            pltpu.VMEM((TAPS, size // 2, size // 4), jnp.bfloat16),
            pltpu.SemaphoreType.DMA((3,)),
        ),
        away=(0, 1, 2),
        lasts=0.0,
    )(place, video, weight)


def stem_norm(count, core, pre, stats_ref, par_ref):
    outs = pre.shape[1]
    center, rate = norm_stats(*stem_columns(core, outs, stats_ref), count)
    scaled = (pre - center) * rate
    gain, bias = upright(par_ref[0:1]), upright(par_ref[1:2])
    return scaled, scaled * gain + bias, gain * rate


def stem_out_body(count, place_ref, pre_ref, grad_ref, stats_ref, par_ref, out_ref, extra_ref):
    core = place_ref[0] % 2
    scaled, normed, _ = stem_norm(count, core, pre_ref[...], stats_ref, par_ref)
    part = logistic(normed)
    out_ref[...] = (normed * part).astype(jnp.bfloat16)
    value = grad_ref[...].astype(jnp.float32) * (part * (1.0 + normed * (1.0 - part)))
    extra_ref[...] = stem_row(core, extra_ref.shape[1], value, value * scaled)


def stem_output(count, place, pre, grad, stats, par, width):
    return kernel_call(
        functools.partial(stem_out_body, count),
        (
            jax.ShapeDtypeStruct(pre.shape, jnp.bfloat16),
            jax.ShapeDtypeStruct((8, width), jnp.float32),
        ),
        [scalars] + [whole] * 4,
        lasts=1.8,
    )(place, pre, grad, stats, par)


def stem_back_body(
    count, first, place_ref, pre_ref, grad_ref, stats_ref, back_ref, par_ref, rows_ref, pick_ref, start_ref, out_ref, slopes_ref,
):
    core = place_ref[0] % 2
    segs, outs, pixels = pre_ref.shape
    scaled, normed, scale = stem_norm(count, core, pre_ref[...], stats_ref, par_ref)
    bias_grad, gain_grad = stem_columns(core, outs, back_ref)
    value = grad_ref[...].astype(jnp.float32) * silu_slope(normed)
    value = scale * (value - bias_grad / count - scaled * (gain_grad / count))
    value = value.astype(jnp.bfloat16).reshape(segs * outs, pixels)
    half = rows_ref.shape[2]
    for tap in range(TAPS):
        spread = exact(value, pick_ref[tap], ((1,), (1,)))
        slopes_ref[:, tap * LANES : (tap + 1) * LANES, :] = spread.astype(jnp.bfloat16).reshape(
            segs, outs, half
        )
    total = None
    for seg in range(segs):
        term = exact(rows_ref[seg], slopes_ref[seg], ((1,), (1,)))
        total = term if total is None else total + term
    size = TAPS * LANES
    rows = size // 2
    if first:
        out_ref[...] = jnp.zeros_like(out_ref)
    else:
        out_ref[...] = start_ref[...]
    out_ref[:, :size] += total[:rows]
    out_ref[:, 128 : 128 + size] += total[rows:]


def stem_back(count, place, pre, grad, stats, back, par, rows, pick, start, chunk, chunks):
    segs, outs, pixels = pre.shape
    size = segs // chunks

    def part(*tail):
        return pl.BlockSpec((size,) + tail, lambda at: (chunk, 0, 0))

    def all_of(shape):
        return pl.BlockSpec(shape, lambda at: (0,) * len(shape))

    small = (TAPS * LANES // 2, 256)
    first = start is None
    start = jnp.zeros((8, 256), jnp.float32) if first else start
    return pl.pallas_call(
        functools.partial(stem_back_body, count, first),
        grid=(1,),
        out_shape=jax.ShapeDtypeStruct(small, jnp.float32),
        in_specs=[scalars, part(outs, pixels), part(outs, pixels)]
        + [all_of(stats.shape), all_of(back.shape), all_of(par.shape)]
        + [part(*rows.shape[1:]), all_of(pick.shape), all_of(start.shape)],
        out_specs=all_of(small),
        scratch_shapes=[pltpu.VMEM((size, TAPS * LANES, rows.shape[2]), jnp.bfloat16)],
        compiler_params=pltpu.CompilerParams(vmem_limit_bytes=vmem_limit),
        cost_estimate=pl.CostEstimate(
            flops=int(1.7 * flops_per_us), bytes_accessed=0, transcendentals=0
        ),
    )(place, pre, grad, stats, back, par, pltpu.with_memory_space_constraint(rows, pltpu.HBM), pick, start)


def stem_weight(center, diff):
    outs = center.shape[1]
    value = jnp.concatenate([diff, center, jnp.zeros((TAPS * TAPS, outs), center.dtype)])
    value = value.reshape(LANES, TAPS, TAPS, outs)
    return value.transpose(2, 3, 1, 0).reshape(TAPS * outs, TAPS * LANES)


def stem_grads_body(packed_ref, center_ref, diff_ref):
    full = jnp.concatenate([packed_ref[:, :128], packed_ref[:, 128:]])
    for row in range(TAPS):
        value = full[row * LANES : (row + 1) * LANES]
        for col in range(TAPS):
            here = value[:, col * LANES : (col + 1) * LANES]
            at = row * TAPS + col
            diff_ref[pl.ds(at, 12, stride=TAPS * TAPS), :] = here[:12]
            center_ref[pl.ds(at, 3, stride=TAPS * TAPS), :] = here[12:15]


def stem_grads(packed, outs):
    return kernel_call(
        stem_grads_body,
        (
            jax.ShapeDtypeStruct((3 * TAPS * TAPS, outs), jnp.float32),
            jax.ShapeDtypeStruct((12 * TAPS * TAPS, outs), jnp.float32),
        ),
        [whole],
    )(packed)


def after(value, *marks):
    return lax.optimization_barrier((value, marks))[0]


def swap(value, axis, bit):
    size = lax.axis_size(axis)
    return lax.ppermute(value, axis, [(at, at ^ bit) for at in range(size)])


def steps_of(axis):
    size = lax.axis_size(axis)
    assert size & (size - 1) == 0
    return [1 << at for at in range(size.bit_length() - 1)]


def sum_over(value, axis, jobs=()):
    jobs = list(jobs)
    value, got = open_sum(value, axis, jobs)
    return value + got


def open_sum(value, axis, jobs=()):
    jobs = [job or (lambda mark: mark) for job in jobs]
    bits = steps_of(axis)
    for bit in bits:
        got = swap(value, axis, bit)
        if jobs:
            got = after(got, jobs.pop(0)(value))
        if bit != bits[-1]:
            value = value + got
    for job in jobs:
        got = after(got, job(value))
    return value, got


def ordered(second, own, other, axis=0):
    return jnp.where(
        second, jnp.concatenate([other, own], axis), jnp.concatenate([own, other], axis)
    )


def gather_rows(value, axis):
    order = [0]
    for bit in reversed(steps_of(axis)):
        value = jnp.concatenate([value, swap(value, axis, bit)])
        order += [at ^ bit for at in order]
    return value, order


def halve_body(bit, parts, far, place_ref, keep_ref, *refs):
    got_refs, refs = refs[:parts], refs[parts:]
    mine_ref, send_ref = refs[:2]
    count, size = send_ref.shape[:2]
    high = (place_ref[1] // bit) % 2
    source, places, moves = keep_ref, [], []
    for block in range(count):
        for side in (1 - high, high):
            here = pl.ds(pl.multiple_of((2 * block + side) * size, size), size)
            places.append((block, side, here))
    if far:
        source, sems = refs[2:]
        moves = [
            move(keep_ref.at[here], source.at[here], sems, at)
            for at, (_, _, here) in enumerate(places)
        ]
    for at, (block, side, here) in enumerate(places):
        if far:
            moves[at].wait()
        value = source[here, :]
        if parts:
            part = block * parts // count
            first = 2 * (block - part * count // parts) + side
            got = got_refs[part][pl.ds(pl.multiple_of(first * size, size), size), :]
            value = value + got.astype(jnp.float32)
        ref = mine_ref if at % 2 else send_ref
        ref[block] = value.astype(ref.dtype)


def halve(place, keep, got, bits, at, far=False):
    rows, width = keep.shape
    left = sorted(bits, reverse=True)
    outer = 1 << left.index(at)
    inner = rows // (2 * outer)
    if inner % BLOCK or outer % max(len(got), 1):
        total = keep + jnp.concatenate(got).astype(jnp.float32) if got else keep
        blocks = total.reshape(outer, 2, inner, width)
        low, high = blocks[:, 0].reshape(-1, width), blocks[:, 1].reshape(-1, width)
        mine = (place[1] // at) % 2 == 0
        return jnp.where(mine, low, high), jnp.where(mine, high, low).astype(jnp.bfloat16)
    shape = (outer, inner, width)
    scratch = [pltpu.VMEM(keep.shape, keep.dtype), pltpu.SemaphoreType.DMA((2 * outer,))]
    mine, send = kernel_call(
        functools.partial(halve_body, at, len(got), far),
        (jax.ShapeDtypeStruct(shape, jnp.float32), jax.ShapeDtypeStruct(shape, jnp.bfloat16)),
        [scalars, remote if far else whole] + [whole] * len(got),
        scratch if far else [],
        lasts=2.0 if far else 0.7,
    )(place, keep, *got)
    return mine.reshape(-1, width), send.reshape(-1, width)


def transposed(left, right):
    return lax.dot_general(
        left, right, (((1,), (1,)), ((), ())), preferred_element_type=jnp.float32
    )


def weight_grad(left, right):
    return lax.dot_general(
        left, right, (((0,), (0,)), ((), ())), preferred_element_type=jnp.float32
    )


def per_device(
    block_in,
    weight_in,
    weight_mid,
    weight_out,
    gain_in,
    bias_in,
    gain_mid,
    bias_mid,
    gain_out,
    bias_out,
    kernel_near,
    kernel_far,
    gate_bias,
    same_video,
    video,
    stem_center,
    stem_diff,
    stem_gain,
    stem_bias,
    block_grad,
    stem_grad,
):
    groups = lax.axis_size("dp")
    assert lax.axis_size("chan") == 4
    clips = same_video.shape[0]
    rows, quarter = block_in.shape
    half = rows // 2
    narrow = weight_in.shape[1]
    width = 2 * narrow
    count = float(rows * groups)
    segs = video.shape[0]
    stem_count = float(segs * stem_grad.shape[2] * groups)
    chan = lax.axis_index("chan")
    core, y = chan % 2, chan // 2
    place = jnp.stack([chan, lax.axis_index("dp")])

    mine, others, packed = opening(place, block_in, weight_mid, weight_out)
    pieces = [swap(others, "chan", 1), swap(mine, "chan", 2)]
    pieces.append(swap(after(others, pieces[1]), "chan", 3))

    own_in, order = gather_rows(after(weight_in, mine, others), "dp")
    weights_in = [own_in, swap(own_in, "chan", 1)]
    gathered = lax.all_gather(packed, "dp", axis=0)

    params, stem_par = pack_params(
        [gain_in, bias_in, gain_mid, bias_mid, gate_bias],
        kernel_near,
        kernel_far,
        [stem_gain, stem_bias],
    )
    par_own = ordered(core == 1, params, swap(params, "chan", 1), 1)
    pars = [par_own]
    same = lax.dynamic_slice_in_dim(same_video, core * (clips // 2), clips // 2, 0)
    same = jnp.pad(same, ((0, 0), (0, 1)))
    gain_row, bias_row = gain_out.reshape(1, -1), bias_out.reshape(1, -1)

    outs = stem_grad.shape[1]
    pre_stem, stem_rows, stem_pick, extra = stem_front(
        place, video, stem_weight(stem_center, stem_diff), width
    )

    def both_sums(sums, jobs=()):
        jobs = [run or (lambda mark: mark) for run in jobs]
        got = swap(sums, "chan", 1)
        if jobs:
            got = after(got, jobs[0](sums))
        own = sum_over(sums + got, "dp", jobs[1:4])
        oth = swap(own, "chan", 2)
        for run in jobs[4:]:
            oth = after(oth, run(own))
        return [own, oth]

    made = {}

    def in_turn(*works):
        def run(mark):
            results = []
            for work in works:
                results.append(work((mark, results) if results else mark))
            return results

        return run

    def job(name, work):
        def run(mark):
            made[name] = work(mark)
            return made[name]

        return run

    pre_in, pre_in16, sums_in, cross_in, near_in, away_in = first_conv(
        order, place, block_in, pieces, weights_in, extra, par_own
    )

    blocks = gathered
    if weight_mid.shape[0] % BLOCK:
        blocks = gathered[:, : weight_mid.shape[0]].reshape(1, -1, narrow)

    def mid_blocks(mark):
        own = after(blocks, mark)
        return [own, swap(own, "chan", 1)]


    def out_rows(mark):
        parts, first, size = after(gathered, mark), weight_mid.shape[0], weight_out.shape[0]
        parts = [parts[:, first + at * size : first + (at + 1) * size] for at in range(4)]
        return jnp.concatenate([part.reshape(-1, narrow) for part in parts], 1)

    cross_got = swap(cross_in, "chan", 2)
    corner_got = swap(cross_in[:8], "chan", 3)
    pre_in_oth = swap(after(pre_in16, cross_got), "chan", 2)
    sums_in = sums_in + swap(sums_in, "chan", 1) + cross_got[:8] + corner_got
    open_in = open_sum(
        sums_in, "dp", [None, in_turn(job("weights_mid", mid_blocks), job("full_out", out_rows))]
    )
    pars.append(cross_got)
    weights_mid = made["weights_mid"]
    full_out = made["full_out"]

    out_across = swap(after(full_out, open_in), "chan", 2)

    mixed, gates, pre_mid, pre_mid16, sums_mid = gate_mid(
        count, place, same, pre_in, pre_in_oth, open_in, pars, weights_mid
    )
    pre_mid_oth = swap(pre_mid16, "chan", 2)
    first, second_part = after(open_in, sums_mid)
    stats_stem = stats_in = first + second_part

    def stem_half(mark):
        return stem_output(
            stem_count, place, after(pre_stem, mark), stem_grad, stats_stem, stem_par, quarter
        )

    def slab_of(mark):
        slab = after(gathered, mark)[:, : weight_mid.shape[0]].reshape(9, 2, width, narrow)
        return lax.dynamic_slice_in_dim(slab, 1 - y, 1, 1).reshape(9 * width, narrow)

    stats_mid = both_sums(
        sums_mid,
        [
            None,
            job("stem", stem_half),
            in_turn(job("slab", slab_of), lambda mark: out_across),
            job("turned", lambda mark: turn(after(mixed, mark))),
            lambda mark: pre_mid_oth,
        ],
    )
    stem_out, extra = made["stem"]

    second = second_half(count, place, pre_mid, pre_mid_oth, stats_mid, pars)
    second_peer = swap(second, "chan", 1)
    pre_out, sums_out = last_conv(place, second, second_peer, full_out, extra)
    slab_across = swap(after(made["slab"], stats_mid), "chan", 2)
    open_out = after(open_sum(sums_out, "dp"), slab_across)
    out_peers = [swap(after(value, open_out), "chan", 1) for value in (full_out, out_across)]
    weights_out = [full_out, out_peers[0], out_across, out_peers[1]]
    block_out, grad_total, sums_back, keep, send = out_back(
        count, place, pre_out, block_in, block_grad, open_out, gain_row, bias_row, full_out
    )
    first, second_part = after(open_out, sums_back)
    stats_out = first + second_part
    got = swap(send, "chan", 1)

    def cross(mark):
        return cross_half(place, keep, after(got, mark))

    def stem_part(chunk, start):
        def work(mark):
            return stem_back(
                stem_count, place, after(pre_stem, mark), stem_grad, stats_in, stats_out,
                stem_par, stem_rows, stem_pick, start and made[start], chunk, 4,
            )

        return job(f"stem{chunk}", work)

    open_back = open_sum(
        sums_back, "dp", [stem_part(0, None), job("cross", cross), stem_part(1, "stem0")]
    )
    keep, send = made["cross"]
    got = swap(send, "chan", 2)
    delta = out_delta(count, rows, stats_out, sums_back, open_back, gain_row)
    deltas = [delta] + [swap(delta, "chan", at) for at in (1, 2, 3)]

    grad_mid, grad_mid16, sums_mid_back = mid_slope(
        count, place, keep, got, second, pre_mid, stats_mid[0], pars[0], deltas, weights_out
    )
    grad_mid_oth = swap(grad_mid16, "chan", 2)
    first, second_part = after(open_back, sums_mid_back)
    back_out = first + second_part

    aways_mid = [slab_across, swap(after(slab_across, sums_mid_back), "chan", 1)]

    def out_part(start, rows_of_second):
        def work(mark):
            return out_weight(
                count, place, rows_of_second, pre_out, grad_total, stats_out, after(back_out, mark),
                gain_row, start and made[start],
            )

        return work

    def own_slopes(mark):
        return mid_own(count, grad_mid, pre_mid, stats_mid[0], mark, pars[0])

    bits = steps_of("dp")

    back_mid = both_sums(sums_mid_back, [
        None,
        job("out0", out_part(None, second)),
        job("out1", out_part("out0", second_peer)),
        stem_part(2, "stem1"),
        in_turn(job("slopes", own_slopes), stem_part(3, "stem2")),
    ])
    slopes = made["slopes"]
    sum_out = lax.psum_scatter(made["out1"], "dp", scatter_dimension=0, tiled=True)
    stem_first = swap(made["stem3"], "dp", bits[0])
    far_in = swap(after(away_in, sums_mid_back), "chan", 2)

    grad_in, grad_in16, sums_in_back = mid_back(
        count, place, same, slopes, grad_mid_oth, pre_mid_oth, stats_mid[1], back_mid[1], pre_in,
        gates, stats_in, pars, weights_mid, aways_mid,
    )
    grad_in_oth = swap(grad_in16, "chan", 2)

    def mid_part(mark):
        return mid_weight(place, made["turned"], after(slopes, mark))

    def mid_rest(mark):
        keep, *sends = made["mid"]
        got = [after(swap(send, "chan", 1), mark) for send in sends]
        return halve(place, keep, got, mid_bits, mid_bits[0], True)

    mid_bits = bits

    def mid_step(at):
        def work(mark):
            keep, got = made["keep"], after(swap(made["send"], "dp", mid_bits[at - 1]), mark)
            made["keep"], made["send"] = halve(place, keep, [got], mid_bits[at:], mid_bits[at])
            return made["send"]

        return work

    def mid_first(mark):
        made["keep"], made["send"] = mid_rest(mark)
        return made["send"]

    def own_in_back(mark):
        return in_own(
            count, place, grad_in, pre_in, stats_in, mark, pars[0], block_in, pieces
        )

    def stem_next(mark):
        return made["stem3"] + after(stem_first, mark)

    back_in = both_sums(
        sums_in_back,
        [
            None,
            job("mid", mid_part),
            job("stem_total", stem_next),
            in_turn(mid_first, lambda mark: grad_in_oth),
            job("in", own_in_back),
        ],
    )

    grad_own, keep, send = made["in"]
    got = swap(send, "chan", 1)
    grad_pre = in_other(
        count, place, after(grad_own, send), grad_in_oth, pre_in_oth, stats_in, back_in[1], pars[1]
    )
    grad_peer = swap(grad_pre, "chan", 1)
    mark, stem_total = grad_pre, made["stem_total"]
    assert len(bits) > 1
    last = len(bits) - 1
    for at, bit in enumerate(bits):
        got = after(got, mark, sum_out) if at == 1 else after(got, mark)
        keep, send = halve(place, keep, [got], bits[at:], bit, at == 0)
        got = swap(send, "dp", bit)
        mark = send
        if at < last:
            mark = mid_step(at + 1)(mark)
            if at == 0:
                near = after(near_in, mark)
                mark = grad_block_in = input_grad(
                    place, grad_pre, grad_peer, near, far_in, grad_total
                )
            stem_got = swap(stem_total, "dp", bits[at + 1])
            mark = stem_total = after(stem_total, mark) + stem_got
    sum_mid = after(made["keep"], send) + swap(made["send"], "dp", bit).astype(jnp.float32)
    sum_in = keep + after(got, sum_mid).astype(jnp.float32)
    center_grad, diff_grad = stem_grads(stem_total, outs)

    def my_columns(value):
        return lax.dynamic_slice_in_dim(value, core * narrow, narrow, value.ndim - 1)

    def my_stem(value):
        row = lax.dynamic_slice(value, (2, core * 2 * outs), (1, 2 * outs))[0]
        return row[:outs], row[outs:]

    gate_grads = my_columns(back_in[0][8:])
    mid_grads, in_grads = my_columns(back_mid[0]), my_columns(back_in[0])
    stem_bias_grad, stem_gain_grad = my_stem(stats_out)
    return (
        block_out,
        stem_out,
        grad_block_in,
        sum_in,
        sum_mid,
        sum_out,
        in_grads[1],
        in_grads[0],
        mid_grads[1],
        mid_grads[0],
        back_out[1],
        back_out[0],
        gate_grads[1:10],
        gate_grads[10:19],
        gate_grads[0],
        center_grad,
        diff_grad,
        stem_gain_grad,
        stem_bias_grad,
    )


def solution(mesh):
    placed = (
        P("dp", "chan"),
        P("dp", "chan"),
        P("dp", "chan"),
        P("dp", "chan"),
        P("chan"),
        P("chan"),
        P("chan"),
        P("chan"),
        P("chan"),
        P("chan"),
        P(None, "chan"),
        P(None, "chan"),
        P("chan"),
        P("dp", None),
        P("dp", None, None),
        P(None, "chan"),
        P(None, "chan"),
        P("chan"),
        P("chan"),
        P("dp", "chan"),
        P("dp", "chan", None),
    )
    return jax.shard_map(
        per_device,
        mesh=mesh,
        in_specs=placed,
        out_specs=(
            P("dp", "chan"),
            P("dp", "chan", None),
            P("dp", "chan"),
            P("dp", "chan"),
            P("dp", "chan"),
            P("dp", "chan"),
            P("chan"),
            P("chan"),
            P("chan"),
            P("chan"),
            P("chan"),
            P("chan"),
            P(None, "chan"),
            P(None, "chan"),
            P("chan"),
            P(None, "chan"),
            P(None, "chan"),
            P("chan"),
            P("chan"),
        ),
        check_vma=False,
    )
```
